32 devices in a mesh: fsdp: 4 (over x, core), seq: 8 (over z, y).
Axes of the slice: x: 2, y: 2, z: 4, core: 2. Of those that a mesh axis runs over, the one named last changes fastest.
Arguments:
- layer_input: bfloat16 [2, 4096, 2048], P(None, ('fsdp', 'seq')), may hold values from -6 to 6
- cotangent: bfloat16 [2, 4096, 2048], P(None, ('fsdp', 'seq')), may hold values from -6 to 6
- segments: int32 [2, 4096], P(None, 'fsdp'), may hold values from 0 to 31, as said below
- routes: int32 [2, 4096, 8], P(None, ('fsdp', 'seq')), may hold values from 0 to 31, all different within a row; in each aligned block of 128 rows (0 to 127, 128 to 255, ..., all dimensions but the last counted through in order) at most 48 rows name the same one
- route_weights: float32 [2, 4096, 8], P(None, ('fsdp', 'seq')), may hold values from 0.1 to 0.3
- gain_attention: bfloat16 [2048], P('fsdp'), may hold values from 0.5 to 1.5
- gain_experts: bfloat16 [2048], P('fsdp'), may hold values from 0.5 to 1.5
- query_proj: bfloat16 [2048, 2048], P('fsdp'), may hold values from -0.125 to 0.125
- key_proj: bfloat16 [2048, 2048], P('fsdp'), may hold values from -0.125 to 0.125
- value_proj: bfloat16 [2048, 2048], P('fsdp'), may hold values from -0.125 to 0.125
- output_proj: bfloat16 [2048, 2048], P('fsdp'), may hold values from -1 to 1
- head_gains: bfloat16 [2, 128], replicated, may hold values from 0.5 to 1.5
- expert_gate: bfloat16 [32, 2048, 1024], P('seq', 'fsdp'), may hold values from -0.125 to 0.125
- expert_up: bfloat16 [32, 2048, 1024], P('seq', 'fsdp'), may hold values from -0.125 to 0.125
- expert_down: bfloat16 [32, 2048, 1024], P('seq', 'fsdp'), may hold values from -0.375 to 0.375
Outputs:
- layer_output: bfloat16 [2, 4096, 2048], P(None, ('fsdp', 'seq'))
- input_grad: float32 [2, 4096, 2048], P(None, ('fsdp', 'seq'))
- grad_gain_attention: float32 [2048], P(('fsdp', 'seq'))
- grad_gain_experts: float32 [2048], P(('fsdp', 'seq'))
- grad_query: float32 [2048, 2048], P(('fsdp', 'seq'))
- grad_key: float32 [2048, 2048], P(('fsdp', 'seq'))
- grad_value: float32 [2048, 2048], P(('fsdp', 'seq'))
- grad_output: float32 [2048, 2048], P(('fsdp', 'seq'))
- grad_head_gains: float32 [2, 128], replicated
- grad_expert_gate: float32 [32, 2048, 1024], P('seq', 'fsdp')
- grad_expert_up: float32 [32, 2048, 1024], P('seq', 'fsdp')
- grad_expert_down: float32 [32, 2048, 1024], P('seq', 'fsdp')
The draws below stay inside these ranges and needn't reach their ends.
Inputs may be any that keep to these rules, and one draw needn't show every extreme that they name: `routes`: in each aligned block of 128 rows (one device's tokens of one micro-batch) no expert is named more than 48 times, and some expert exactly that often; a row names 8 different experts. `segments`: numbers never fall along a micro-batch; each document lies inside one 1024-token sequence, which holds 2 to 4 documents of 204 tokens or more, the last sequence exactly 4; sequence j of all (micro-batches first) numbers its documents 4 * j, 4 * j + 1 and so on.
All inputs are finite; a program needn't handle non-finite values.
Results may differ from the reference program's by a relative error of at most 0.015.
Values may be sent and summed in bfloat16 or wider, within the bound.
No kernel may reach another device: no remote copies, remote signals or barrier semaphores. Data moves between devices by JAX's collectives and lax.ppermute only.
A program may use at most 448 MiB of HBM per device.

```python
import math
import jax
import jax.numpy as jnp
import numpy as np
from jax import lax

D = 2048
H = 16
HD = 128
FFE = 1024
TOP = 8
SEQ_LEN = 1024
MICRO = 2
SEQS = 1
EXPERTS = 32
TOK_DEV = 128
ROWS = 4096
CAPACITY = 48
N_FSDP = 4
N_SEQ = 8


def draw_segments(key, part):
    key = jax.random.fold_in(key, 11)
    doc_key, share_key = jax.random.split(key)
    sequence_count = MICRO * N_FSDP * SEQS
    doc_count = jax.random.randint(doc_key, (sequence_count,), 2, 5)
    doc_count = doc_count.at[sequence_count - 1].set(4)
    slot_ids = jnp.arange(4)
    active = (slot_ids[None, :] < doc_count[:, None]).astype(jnp.int32)
    shares = jax.random.randint(share_key, (sequence_count, 4), 1, 101) * active
    shortest = SEQ_LEN // 5
    spare_len = SEQ_LEN - shortest * doc_count
    extra_len = spare_len[:, None] * shares // jnp.sum(shares, axis=1, keepdims=True)
    extra_len = extra_len.at[:, 0].add(spare_len - jnp.sum(extra_len, axis=1))
    lengths = (shortest + extra_len) * active
    end_points = jnp.cumsum(lengths, axis=1)
    places = jnp.arange(SEQ_LEN)
    local_doc = jnp.sum((places[None, :, None] >= end_points[:, None, :]).astype(jnp.int32), axis=2)
    numbers = jnp.arange(sequence_count)[:, None] * 4 + local_doc
    return numbers.reshape(MICRO, N_FSDP * SEQS * SEQ_LEN).astype(jnp.int32)


def steps_of(own_key, shape, cuts, smallest, largest):
    def one(dim, blocks):
        heights = jax.random.uniform(jax.random.fold_in(jax.random.fold_in(own_key, 6), dim), (blocks,), jnp.float32, smallest / len(cuts), largest / len(cuts))
        return jnp.repeat(jnp.exp(heights), shape[dim] // blocks).reshape((-1,) + (1,) * (len(shape) - dim - 1))

    gain = one(*cuts[0])
    for cut in cuts[1:]:
        gain = gain * one(*cut)
    return gain


def deal_out(own_key, own, number, rows, amount, top, reach, slope):
    order = jax.random.permutation(own_key, amount)
    crowded, usual = portions_of(amount, rows * top, reach, slope, True), portions_of(amount, rows * top, reach, slope, False)
    places = jnp.arange(amount)

    def named(tallies, turn):
        used = int((tallies > 0).sum())
        fixed = max(1, used // 4)
        shifted = fixed + (places - fixed + turn * (used - fixed)) % max(1, amount - fixed)
        return jnp.zeros((amount,), jnp.int32).at[order[jnp.where(places < fixed, places, shifted)]].set(jnp.asarray(tallies, jnp.int32))

    tallies = jnp.where(number % 4 == 0, named(crowded, number // 4), named(usual, number - number // 4 - 1))
    mixed = jax.random.permutation(jax.random.fold_in(own, 3), amount)
    giver, taker = mixed[0:amount // 2 * 2:2], mixed[1:amount // 2 * 2:2]
    slack = jnp.minimum(tallies[giver] - 1, reach - tallies[taker]) // 2
    slack = jnp.where((giver == order[0]) | (taker == order[0]) | (tallies[taker] == 0), 0, jnp.maximum(slack, 0))
    shifted = jax.random.randint(jax.random.fold_in(own, 4), (amount // 2,), 0, 1 << 20) % (slack + 1)
    tallies = tallies.at[giver].add(-shifted).at[taker].add(shifted)
    labels = jnp.searchsorted(jnp.cumsum(tallies), jnp.arange(rows * top), side="right").astype(jnp.int32)
    table = labels.reshape(top, rows).T
    table = table[jax.random.permutation(jax.random.fold_in(own, 1), rows)]
    turn = jax.random.randint(jax.random.fold_in(own, 2), (rows, 1), 0, top)
    return jnp.take_along_axis(table, (jnp.arange(top)[None, :] + turn) % top, axis=1)


def portions_of(count, total, limit, slope, full):
    weights = [(1 << 20) // math.isqrt(standing ** slope) + 1 for standing in range(1, count + 1)]
    largest = limit if full else min(limit, max(-(-total // count), total * weights[0] // sum(weights)))
    least = 1 if total - largest >= count - 1 else 0
    holding, spare = [largest] + [least] * (count - 1), total - largest - least * (count - 1)
    while spare > 0:
        movable = [i for i in range(1, count) if holding[i] < largest] or [i for i in range(1, count) if holding[i] < limit]
        pool, budget = sum([weights[i] for i in movable]), spare
        for i in movable:
            more = min(limit - holding[i], max(1, budget * weights[i] // pool), spare)
            holding[i] = holding[i] + more
            spare = spare - more
    return np.array(holding)


def normal_values(own_key, shape, spread, bound, shards=(), kind=jnp.bfloat16):
    factor_of = steps_of(own_key, shape, shards, -0.22, 0.18) if shards else 1.0
    values = jax.random.normal(own_key, shape, jnp.float32) * spread * factor_of
    return jnp.minimum(jnp.maximum(values, -bound), bound).astype(kind)


def setup_inputs(seed: int = 0) -> dict:
    streams_of = jax.random.split(jax.random.key(seed), 16)
    layer_input = normal_values(streams_of[0], (MICRO, ROWS, D), 1.0, 6.0, ((1, 32),))
    cotangent = normal_values(streams_of[1], (MICRO, ROWS, D), 1.0, 6.0, ((1, 32),))
    segments = draw_segments(jax.random.fold_in(streams_of[15], 71), 0)
    routes_keys = jax.random.split(jax.random.fold_in(streams_of[3], 1), MICRO * ROWS // TOK_DEV)
    routes_turns = jax.random.permutation(jax.random.fold_in(streams_of[3], 3), MICRO * ROWS // TOK_DEV)
    routes = jax.vmap(lambda own, number: deal_out(jax.random.fold_in(streams_of[3], 2), own, number, TOK_DEV, EXPERTS, TOP, CAPACITY, 1))(routes_keys, routes_turns).reshape((MICRO, ROWS, TOP))
    route_weights = jnp.clip(0.1 + 0.20000001043081284 * jax.random.uniform(streams_of[4], (MICRO, ROWS, TOP), jnp.float32) ** steps_of(streams_of[4], (MICRO, ROWS, TOP), ((1, 32),), -0.2, 0.2), 0.1, 0.3)
    gain_attention = jnp.clip(1.0 + 0.1 * jax.random.normal(streams_of[5], (D,), jnp.float32), 0.5, 1.5).astype(jnp.bfloat16)
    gain_experts = jnp.clip(1.0 + 0.1 * jax.random.normal(streams_of[6], (D,), jnp.float32), 0.5, 1.5).astype(jnp.bfloat16)
    query_proj = normal_values(streams_of[7], (D, D), D ** -0.5, 0.125, ((0, 4),))
    key_proj = normal_values(streams_of[8], (D, D), D ** -0.5, 0.125, ((0, 4),))
    value_proj = normal_values(streams_of[9], (D, D), D ** -0.5, 0.125, ((0, 4),))
    output_proj = normal_values(streams_of[10], (D, D), (D // 64) ** -0.5, 1.0, ((0, 4),))
    head_gains = jnp.clip(1.0 + 0.1 * jax.random.normal(streams_of[11], (2, HD), jnp.float32), 0.5, 1.5).astype(jnp.bfloat16)
    expert_gate = normal_values(streams_of[12], (EXPERTS, D, FFE), D ** -0.5, 0.125, ((0, 8), (1, 4)))
    expert_up = normal_values(streams_of[13], (EXPERTS, D, FFE), D ** -0.5, 0.125, ((0, 8), (1, 4)))
    expert_down = normal_values(streams_of[14], (EXPERTS, D, FFE), (FFE // 4) ** -0.5, 0.375, ((0, 8), (1, 4)))
    return dict(layer_input=layer_input, cotangent=cotangent, segments=segments, routes=routes, route_weights=route_weights, gain_attention=gain_attention, gain_experts=gain_experts, query_proj=query_proj, key_proj=key_proj, value_proj=value_proj, output_proj=output_proj, head_gains=head_gains, expert_gate=expert_gate, expert_up=expert_up, expert_down=expert_down)


eps = 1e-06
rope_base = 10000.0
masked_score = -1e+30
highest = lax.Precision.HIGHEST

@jax.custom_vjp
def low(v):
    return lax.optimization_barrier(v.astype(jnp.bfloat16)).astype(jnp.float32)

@jax.custom_vjp
def low_back(v):
    return v

def low_keep(v):
    return (low(v), None)

def low_pass(kept, grad):
    return (grad,)

def back_keep(v):
    return (v, None)

def back_low(kept, grad):
    return (low(grad),)
low.defvjp(low_keep, low_pass)
low_back.defvjp(back_keep, back_low)

def matmul(matrix_a, matrix_b):
    return jnp.dot(matrix_a, matrix_b, preferred_element_type=jnp.float32, precision=highest)

def rms_scale(values):
    return lax.rsqrt(lax.optimization_barrier(jnp.mean(values * values, axis=-1, keepdims=True)) + eps)

def rope_tables(length, width):
    middle = width // 2
    frequency = jnp.exp(-jnp.log(rope_base) * (2.0 * jnp.arange(middle, dtype=jnp.float32) / width))
    angles = jnp.arange(length, dtype=jnp.float32)[:, None] * frequency[None, :]
    return (jnp.cos(angles), jnp.sin(angles))

def rotate(values, cosine, sine_tab):
    middle = values.shape[-1] // 2
    first_half = values[..., :middle]
    second_half = values[..., middle:]
    cos_b = cosine[:, None, :]
    sin_b = sine_tab[:, None, :]
    return jnp.concatenate([first_half * cos_b - second_half * sin_b, second_half * cos_b + first_half * sin_b], axis=-1)

def attend_sequence(queries, key_rows, value_rows, segment, head_gains, cosine, sine_tab):
    scaling = 1.0 / math.sqrt(queries.shape[-1])
    queries = low(rotate(queries * rms_scale(queries) * head_gains[0], cosine, sine_tab))
    key_rows = low(rotate(key_rows * rms_scale(key_rows) * head_gains[1], cosine, sine_tab))
    scores = jnp.einsum('qhd,khd->hqk', queries, key_rows, precision=highest)
    scores = low_back(scores * scaling)
    allowed = (segment[:, None] == segment[None, :])[None, :, :]
    scores = jnp.where(allowed, scores, masked_score)
    probabilities = low(jax.nn.softmax(scores, axis=-1))
    return jnp.einsum('hqk,khd->qhd', probabilities, value_rows, precision=highest)

def dispatch_tables(group_routes, group_weights):
    flat_ids = group_routes.reshape(N_SEQ, TOK_DEV * TOP)
    onehot = (flat_ids[:, :, None] == jnp.arange(EXPERTS)[None, None, :]).astype(jnp.int32)
    rank_of = lax.optimization_barrier(jnp.sum((jnp.cumsum(onehot, axis=1) - onehot) * onehot, axis=2))
    column = jnp.arange(N_SEQ)[:, None] * CAPACITY + rank_of
    token_row = (jnp.arange(N_SEQ)[:, None] * TOK_DEV + jnp.arange(TOK_DEV * TOP)[None, :] // TOP).astype(jnp.int32)
    table_shape = (EXPERTS, N_SEQ * CAPACITY)
    rows_in = jnp.zeros(table_shape, jnp.int32).at[flat_ids, column].set(token_row)
    live_slot = jnp.zeros(table_shape, jnp.float32).at[flat_ids, column].set(1.0)
    weight_slot = jnp.zeros(table_shape, jnp.float32).at[flat_ids, column].set(group_weights.reshape(N_SEQ, TOK_DEV * TOP))
    return (rows_in, live_slot, weight_slot)

def group_forward(tokens, segment, group_routes, group_weights, params):
    gain_attention, gain_experts, query_proj, key_proj, value_proj, output_proj, head_gains, expert_gate, expert_up, expert_down = params
    token_count = tokens.shape[0]
    seqs_here = token_count // SEQ_LEN
    head_shape = (seqs_here, SEQ_LEN, H, HD)
    h_one = low(tokens * rms_scale(tokens) * gain_attention)
    queries = low_back(low(matmul(h_one, query_proj))).reshape(head_shape)
    key_rows = low_back(low(matmul(h_one, key_proj))).reshape(head_shape)
    value_rows = low_back(low(matmul(h_one, value_proj))).reshape(head_shape)
    cosine, sine_tab = rope_tables(SEQ_LEN, HD)

    def one_sequence(packed):
        return attend_sequence(packed[0], packed[1], packed[2], packed[3], head_gains, cosine, sine_tab)
    attended = lax.map(jax.checkpoint(one_sequence), (queries, key_rows, value_rows, segment.reshape(seqs_here, SEQ_LEN)))
    attended = low_back(low(attended.reshape(token_count, D)))
    middle = tokens + low_back(matmul(attended, output_proj))
    h_two = low(middle * rms_scale(middle) * gain_experts)
    rows_in, live_slot, weight_slot = dispatch_tables(group_routes, group_weights)

    def one_expert(packed):
        rows_idx, live_e, weight_e, w_gate, w_up, w_down = packed
        chosen = low_back(h_two[rows_idx] * live_e[:, None])
        gate_act = low_back(matmul(chosen, w_gate))
        up_act = low_back(matmul(chosen, w_up))
        hidden = low(jax.nn.silu(gate_act) * up_act)
        result = low_back(low(matmul(hidden, w_down.T)))
        return result * weight_e[:, None]
    expert_rows = lax.map(jax.checkpoint(one_expert), (rows_in, live_slot, weight_slot, expert_gate, expert_up, expert_down))
    mixture = jnp.zeros_like(middle).at[rows_in.reshape(-1)].add(expert_rows.reshape(-1, D))
    return middle + mixture

def reference(layer_input, cotangent, segments, routes, route_weights, gain_attention, gain_experts, query_proj, key_proj, value_proj, output_proj, head_gains, expert_gate, expert_up, expert_down):
    params = tuple((weight.astype(jnp.float32) for weight in (gain_attention, gain_experts, query_proj, key_proj, value_proj, output_proj, head_gains, expert_gate, expert_up, expert_down)))
    groups = MICRO * N_FSDP
    group_len = SEQS * SEQ_LEN
    tokens_all = layer_input.astype(jnp.float32).reshape(groups, group_len, D)
    seg_all = segments.reshape(groups, group_len)
    route_all = routes.reshape(groups, group_len, TOP)
    weight_all = route_weights.astype(jnp.float32).reshape(groups, group_len, TOP)

    def forward(tokens, *weights):

        def one_group(packed):
            return group_forward(packed[0], packed[1], packed[2], packed[3], weights)
        return lax.map(jax.checkpoint(one_group), (tokens, seg_all, route_all, weight_all))
    result, pullback = jax.vjp(forward, tokens_all, *params)
    gradients = pullback(cotangent.astype(jnp.float32).reshape(groups, group_len, D))
    layer_output = result.reshape(MICRO, ROWS, D).astype(jnp.bfloat16)
    input_grad = gradients[0].reshape(MICRO, ROWS, D)
    return (layer_output, input_grad, gradients[1], gradients[2], gradients[3], gradients[4], gradients[5], gradients[6], gradients[7], gradients[8], gradients[9], gradients[10])
```

```python
import math

import jax
import jax.numpy as jnp
from jax import lax
from jax.sharding import PartitionSpec as P

D = 2048
H = 16
HD = 128
FFE = 1024
TOP = 8
SEQ_LEN = 1024

eps = 1e-06
rope_base = 10000.0
masked_score = -1e30
f32 = jnp.float32
bf16 = jnp.bfloat16


def shift(value, axis, outer, inner, by_outer, by_inner):
    pairs = []
    for a in range(outer):
        for b in range(inner):
            there = ((a + by_outer) % outer) * inner + (b + by_inner) % inner
            pairs.append((a * inner + b, there))
    return lax.ppermute(value, axis, pairs)


def sizes(axis):
    count = lax.axis_size(axis)
    return (count // 2, 2) if axis == "fsdp" else (4, count // 4)


def ring_gather(value, axis):
    outer, inner = sizes(axis)
    blocks = []
    for a in range(outer):
        if a:
            value = shift(value, axis, outer, inner, 1, 0)
        moved = value
        blocks.append(moved)
        for b in range(1, inner):
            moved = shift(moved, axis, outer, inner, 0, 1)
            blocks.append(moved)
    return blocks


def ring_scatter(parts, axis):
    outer, inner = sizes(axis)
    reduced = [None] * outer
    for a in list(range(1, outer)) + [0]:
        total = parts[a * inner + 1 % inner]
        for b in range(2, inner + 1):
            moved = shift(total, axis, outer, inner, 0, 1)
            total = (moved.astype(f32) + parts[a * inner + b % inner].astype(f32)).astype(bf16)
        reduced[a] = total
    total = reduced[1 % outer]
    for a in range(2, outer + 1):
        moved = shift(total, axis, outer, inner, 1, 0)
        total = moved.astype(f32) + reduced[a % outer].astype(f32)
        if a < outer:
            total = total.astype(bf16)
    return total


def relative_order(axis):
    outer, inner = sizes(axis)
    me = lax.axis_index(axis)
    a, b = me // inner, me % inner
    k = jnp.arange(outer * inner)
    return ((a - k // inner) % outer) * inner + (b - k % inner) % inner


def rms_scale(values):
    return lax.rsqrt(jnp.mean(values * values, axis=-1, keepdims=True) + eps)


def rotate(values, cosine, sine_tab):
    middle = values.shape[-1] // 2
    first_half = values[..., :middle]
    second_half = values[..., middle:]
    cos_b = cosine[:, None, :]
    sin_b = sine_tab[:, None, :]
    return jnp.concatenate(
        [first_half * cos_b - second_half * sin_b, second_half * cos_b + first_half * sin_b],
        axis=-1,
    )


def norm_rotate(raw, gain, cosine, sine_tab):
    values = raw.astype(f32)
    inverse = rms_scale(values)
    normed = values * inverse
    turned = rotate(normed * gain, cosine, sine_tab)
    return (turned.astype(bf16), normed, inverse)


def norm_rotate_back(grad_turned, normed, inverse, gain, cosine, sine_tab):
    grad_scaled = rotate(grad_turned, cosine, -sine_tab)
    grad_gain = jnp.sum(grad_scaled * normed, axis=(0, 1, 2))
    grad_normed = grad_scaled * gain
    grad_raw = inverse * (
        grad_normed - normed * jnp.mean(grad_normed * normed, axis=-1, keepdims=True)
    )
    return (grad_raw, grad_gain)


def token_norm_back(grad_scaled, normed, inverse, gain):
    grad_gain = jnp.sum(grad_scaled * normed, axis=0)
    grad_normed = grad_scaled * gain
    grad_raw = inverse * (
        grad_normed - normed * jnp.mean(grad_normed * normed, axis=-1, keepdims=True)
    )
    return (grad_raw, grad_gain)


def masked_scores(queries, key_rows, segment):
    scaling = 1.0 / math.sqrt(queries.shape[-1])
    scores = jnp.einsum("mqhd,mkhd->mhqk", queries, key_rows, preferred_element_type=f32) * scaling
    allowed = (segment[:, :, None] == segment[:, None, :])[:, None, :, :]
    return jnp.where(allowed, scores, masked_score)


def attend(queries, key_rows, value_rows, segment):
    scores = masked_scores(queries, key_rows, segment)
    row_top = jnp.max(scores, axis=-1, keepdims=True)
    powered = jnp.exp(scores - row_top)
    totals = jnp.sum(powered, axis=-1, keepdims=True)
    probabilities = (powered / totals).astype(bf16)
    attended = jnp.einsum("mhqk,mkhd->mqhd", probabilities, value_rows, preferred_element_type=f32)
    return (attended, row_top + jnp.log(totals))


def attend_back(queries, key_rows, value_rows, segment, log_total, grad_out):
    scaling = 1.0 / math.sqrt(queries.shape[-1])
    scores = masked_scores(queries, key_rows, segment)
    probabilities = jnp.exp(scores - log_total)
    grad_probs = jnp.einsum("mqhd,mkhd->mhqk", grad_out, value_rows, preferred_element_type=f32)
    centre = jnp.sum(probabilities * grad_probs, axis=-1, keepdims=True)
    grad_scores = (probabilities * (grad_probs - centre)).astype(bf16)
    grad_query = (
        jnp.einsum("mhqk,mkhd->mqhd", grad_scores, key_rows, preferred_element_type=f32) * scaling
    )
    grad_key = (
        jnp.einsum("mhqk,mqhd->mkhd", grad_scores, queries, preferred_element_type=f32) * scaling
    )
    grad_value = jnp.einsum(
        "mhqk,mqhd->mkhd", probabilities.astype(bf16), grad_out, preferred_element_type=f32
    )
    return (grad_query, grad_key, grad_value)


def body(
    layer_input,
    cotangent,
    segments,
    routes,
    route_weights,
    gain_attention,
    gain_experts,
    query_proj,
    key_proj,
    value_proj,
    output_proj,
    head_gains,
    expert_gate,
    expert_up,
    expert_down,
):
    micro, rows, _ = layer_input.shape
    nf, ns = lax.axis_size("fsdp"), lax.axis_size("seq")
    seq_index = lax.axis_index("seq")
    fsdp_order = relative_order("fsdp")
    seq_order = relative_order("seq")
    tokens = micro * rows
    group = rows * ns
    heads_local = H // ns
    width = heads_local * HD
    local_experts = expert_gate.shape[0]
    experts = local_experts * ns
    capacity = ns * min(rows, 3 * rows * TOP // (2 * experts))
    head_gain = head_gains.astype(f32)

    def to_relative(value):
        cut = value.reshape(value.shape[:-1] + (nf, D // nf))
        return jnp.take(cut, fsdp_order, axis=-2).reshape(value.shape)

    inverse_order = jnp.argsort(fsdp_order)

    def from_relative(value):
        cut = value.reshape(value.shape[:-1] + (nf, D // nf))
        return jnp.take(cut, inverse_order, axis=-2).reshape(value.shape)

    def gather_tokens(value):
        return jnp.concatenate(ring_gather(value, "seq"), axis=1)

    def scatter_tokens(value):
        cut = value.reshape(micro, ns, rows, value.shape[-1])
        return ring_scatter([cut[:, k] for k in range(ns)], "seq")

    columns = [
        lax.dynamic_slice_in_dim(w, seq_index * width, width, axis=1)
        for w in (query_proj, key_proj, value_proj)
    ]
    w_qkv = jnp.concatenate(ring_gather(jnp.concatenate(columns, axis=1), "fsdp"), axis=0)
    gains = lax.all_gather(
        jnp.stack([gain_attention, gain_experts]), "fsdp", axis=1, tiled=True
    ).astype(f32)
    w_output = jnp.concatenate(ring_gather(output_proj, "fsdp"), axis=0)
    w_down = jnp.concatenate(ring_gather(expert_down, "fsdp"), axis=1)
    w_gate = jnp.concatenate(ring_gather(expert_gate, "fsdp"), axis=1)
    w_up = jnp.concatenate(ring_gather(expert_up, "fsdp"), axis=1)

    x_rows = layer_input.astype(f32)
    inv_one = rms_scale(x_rows)
    normed_one = x_rows * inv_one
    h_one = gather_tokens(to_relative((normed_one * gains[0]).astype(bf16)))
    qkv = jnp.einsum("mtd,de->mte", h_one, w_qkv, preferred_element_type=f32).astype(bf16)
    heads_shape = (micro, group, heads_local, HD)
    q_raw = qkv[..., :width].reshape(heads_shape)
    k_raw = qkv[..., width : 2 * width].reshape(heads_shape)
    v_heads = qkv[..., 2 * width :].reshape(heads_shape)

    places = (seq_order[:, None] * rows + jnp.arange(rows)[None, :]).reshape(-1)
    frequency = jnp.exp(
        -jnp.log(rope_base) * (2.0 * jnp.arange(HD // 2, dtype=f32) / HD)
    )
    angles = places.astype(f32)[:, None] * frequency[None, :]
    cosine, sine_tab = jnp.cos(angles), jnp.sin(angles)
    segment = jnp.take(segments.reshape(micro, ns, rows), seq_order, axis=1).reshape(micro, group)

    q_turn, q_normed, q_inverse = norm_rotate(q_raw, head_gain[0], cosine, sine_tab)
    k_turn, k_normed, k_inverse = norm_rotate(k_raw, head_gain[1], cosine, sine_tab)
    attended, log_total = attend(q_turn, k_turn, v_heads, segment)

    inverse_seq = jnp.argsort(seq_order)

    def to_blocks(value):
        cut = value.reshape(micro, ns, rows, value.shape[-1])
        return jnp.take(jnp.moveaxis(cut, 1, 0), inverse_seq, axis=0)

    o_heads = to_blocks(attended.astype(bf16).reshape(micro, group, width))
    o_back = lax.all_to_all(o_heads, "seq", split_axis=0, concat_axis=0, tiled=True)
    o_rows = jnp.moveaxis(o_back, 0, 2).reshape(tokens, D)
    o_all = lax.all_gather(o_heads.reshape(group * micro, width), "seq", axis=1, tiled=True)

    middle = x_rows.reshape(tokens, D) + jnp.dot(
        to_relative(o_rows), w_output, preferred_element_type=f32
    )
    inv_two = rms_scale(middle)
    normed_two = middle * inv_two
    h_two = gather_tokens(
        to_relative((normed_two * gains[1]).astype(bf16)).reshape(micro, rows, D)
    )

    packed = jnp.concatenate([routes.astype(f32), route_weights], axis=-1)
    packed = gather_tokens(packed)
    route_all, weight_all = packed[..., :TOP].astype(jnp.int32), packed[..., TOP:]
    mine = seq_index * local_experts + jnp.arange(local_experts)
    hit = route_all[:, :, None, :] == mine[None, None, :, None]
    chosen = jnp.any(hit, axis=-1)
    weight_of = jnp.sum(jnp.where(hit, weight_all[:, :, None, :], 0.0), axis=-1)
    block = 128
    counted = chosen.reshape(micro, group // block, block, local_experts).astype(f32)
    below = jnp.tril(jnp.ones((block, block), f32), -1)
    inside = jnp.einsum("ab,mkbe->mkae", below, counted)
    sums = jnp.sum(counted, axis=2)
    before = jnp.cumsum(sums, axis=1) - sums
    slot = (inside + before[:, :, None, :]).reshape(micro, group, local_experts).astype(jnp.int32)
    slot = jnp.where(chosen, slot, -1)
    slot_t = jnp.transpose(slot, (2, 0, 1))
    weight_t = jnp.transpose(weight_of, (2, 0, 1))
    onehot = slot_t[:, :, None, :] == jnp.arange(capacity)[None, None, :, None]
    weight_slot = jnp.sum(jnp.where(onehot, weight_t[:, :, None, :], 0.0), axis=-1)
    pick = onehot.astype(bf16)

    def dispatch(value):
        return jnp.einsum("emct,mtd->emcd", pick, value, preferred_element_type=f32)

    def combine(value):
        return jnp.einsum("emct,emcd->mtd", pick, value, preferred_element_type=f32).astype(bf16)

    grad_top = cotangent.astype(f32)
    g_all = gather_tokens(to_relative(cotangent))
    grad_rows = (dispatch(g_all) * weight_slot[..., None]).astype(bf16)
    grad_hidden = jnp.einsum("emcd,edf->emcf", grad_rows, w_down, preferred_element_type=f32)

    taken = dispatch(h_two).astype(bf16)
    gate_act = jnp.einsum("emcd,edf->emcf", taken, w_gate, preferred_element_type=f32)
    up_act = jnp.einsum("emcd,edf->emcf", taken, w_up, preferred_element_type=f32)
    gate_sig = jax.nn.sigmoid(gate_act)
    gate_silu = gate_act * gate_sig
    hidden = (gate_silu * up_act).astype(bf16)
    grad_gate_act = (grad_hidden * up_act * gate_sig * (1.0 + gate_act * (1.0 - gate_sig))).astype(
        bf16
    )
    grad_up_act = (grad_hidden * gate_silu).astype(bf16)
    grad_taken = jnp.einsum(
        "emcf,edf->emcd", grad_gate_act, w_gate, preferred_element_type=f32
    ) + jnp.einsum("emcf,edf->emcd", grad_up_act, w_up, preferred_element_type=f32)
    grad_h_two = from_relative(scatter_tokens(combine(grad_taken.astype(bf16))))

    def bank_grad(left, right):
        whole = jnp.einsum("emcd,emcf->edf", left, right, preferred_element_type=f32).astype(bf16)
        cut = whole.reshape(local_experts, nf, D // nf, FFE)
        return ring_scatter([cut[:, k] for k in range(nf)], "fsdp")

    grad_down = bank_grad(grad_rows, hidden)
    grad_gate = bank_grad(taken, grad_gate_act)
    grad_up = bank_grad(taken, grad_up_act)

    expert_out = jnp.einsum("emcf,edf->emcd", hidden, w_down, preferred_element_type=f32)
    mixed = from_relative(
        scatter_tokens(combine((expert_out * weight_slot[..., None]).astype(bf16)))
    )
    layer_output = (middle.reshape(micro, rows, D) + mixed).astype(bf16)

    grad_norm_two, grad_gain_two = token_norm_back(
        grad_h_two.reshape(tokens, D), normed_two, inv_two, gains[1]
    )
    grad_middle = grad_top.reshape(tokens, D) + grad_norm_two
    grad_attn = grad_middle.astype(bf16)
    grad_o = from_relative(
        jnp.einsum("te,de->td", grad_attn, w_output, preferred_element_type=f32).astype(bf16)
    )

    def to_heads(value):
        cut = value.reshape(micro, rows, ns, width)
        return lax.all_to_all(
            jnp.moveaxis(cut, 2, 0), "seq", split_axis=0, concat_axis=0, tiled=True
        )

    do_blocks = to_heads(grad_o)
    grad_attn_columns = to_heads(grad_attn).reshape(micro * group, width)
    do_heads = jnp.moveaxis(jnp.take(do_blocks, seq_order, axis=0), 0, 1).reshape(heads_shape)
    grad_q_turn, grad_k_turn, grad_v = attend_back(
        q_turn, k_turn, v_heads, segment, log_total, do_heads
    )
    grad_q, grad_q_gain = norm_rotate_back(
        grad_q_turn, q_normed, q_inverse, head_gain[0], cosine, sine_tab
    )
    grad_k, grad_k_gain = norm_rotate_back(
        grad_k_turn, k_normed, k_inverse, head_gain[1], cosine, sine_tab
    )
    grad_qkv = jnp.concatenate(
        [g.astype(bf16).reshape(micro, group, width) for g in (grad_q, grad_k, grad_v)], axis=-1
    )
    grad_h_one = from_relative(
        scatter_tokens(
            jnp.einsum("mte,de->mtd", grad_qkv, w_qkv, preferred_element_type=f32).astype(bf16)
        )
    )
    grad_norm_one, grad_gain_one = token_norm_back(
        grad_h_one.reshape(tokens, D), normed_one.reshape(tokens, D), inv_one.reshape(tokens, 1), gains[0]
    )
    input_grad = (grad_middle + grad_norm_one).reshape(micro, rows, D)

    from_qkv = jnp.einsum("mtd,mte->de", h_one, grad_qkv, preferred_element_type=f32)
    from_out = jnp.einsum("td,te->de", o_all, grad_attn_columns, preferred_element_type=f32)
    from_out = jnp.take(from_out.reshape(nf, D // nf, width), fsdp_order, axis=0).reshape(D, width)
    whole = jnp.concatenate([from_qkv, from_out], axis=1).astype(bf16)
    cut = whole.reshape(nf, D // nf, 4 * width)
    owned = ring_scatter([cut[k] for k in range(nf)], "fsdp").astype(bf16)
    owned = owned.reshape(ns, D // (nf * ns), 4 * width)
    owned = lax.all_to_all(owned, "seq", split_axis=0, concat_axis=0, tiled=True)
    owned = jnp.moveaxis(owned.reshape(ns, -1, 4, width), 0, 2).astype(f32)
    grad_query, grad_key, grad_value, grad_output = (
        owned[:, k].reshape(-1, D) for k in range(4)
    )

    vectors = lax.psum(
        jnp.concatenate([grad_gain_one, grad_gain_two, grad_q_gain, grad_k_gain]), ("fsdp", "seq")
    )
    share = D // (nf * ns)
    start = (lax.axis_index("fsdp") * ns + seq_index) * share
    grad_gain_attention = lax.dynamic_slice_in_dim(vectors, start, share)
    grad_gain_experts = lax.dynamic_slice_in_dim(vectors, D + start, share)
    grad_head_gains = vectors[2 * D :].reshape(2, HD)
    return (
        layer_output,
        input_grad,
        grad_gain_attention,
        grad_gain_experts,
        grad_query,
        grad_key,
        grad_value,
        grad_output,
        grad_head_gains,
        grad_gate,
        grad_up,
        grad_down,
    )


def solution(mesh):
    placed = (
        P(None, ("fsdp", "seq"), None),
        P(None, ("fsdp", "seq"), None),
        P(None, "fsdp"),
        P(None, ("fsdp", "seq"), None),
        P(None, ("fsdp", "seq"), None),
        P("fsdp"),
        P("fsdp"),
        P("fsdp", None),
        P("fsdp", None),
        P("fsdp", None),
        P("fsdp", None),
        P(),
        P("seq", "fsdp", None),
        P("seq", "fsdp", None),
        P("seq", "fsdp", None),
    )
    return jax.shard_map(
        body,
        mesh=mesh,
        in_specs=placed,
        out_specs=(
            P(None, ("fsdp", "seq"), None),
            P(None, ("fsdp", "seq"), None),
            P(("fsdp", "seq")),
            P(("fsdp", "seq")),
            P(("fsdp", "seq"), None),
            P(("fsdp", "seq"), None),
            P(("fsdp", "seq"), None),
            P(("fsdp", "seq"), None),
            P(),
            P("seq", "fsdp", None),
            P("seq", "fsdp", None),
            P("seq", "fsdp", None),
        ),
        check_vma=False,
    )
```

```python
import math

import jax
import jax.numpy as jnp
from jax import lax
from jax.experimental import pallas as pl
from jax.experimental.pallas import tpu as pltpu
from jax.sharding import PartitionSpec as P

D = 2048
H = 16
HD = 128
FFE = 1024
TOP = 8
SEQ_LEN = 1024

eps = 1e-06
rope_base = 10000.0
masked_score = -1e30
f32 = jnp.float32
little = pl.CostEstimate(flops=1, bytes_accessed=1, transcendentals=0)
bf16 = jnp.bfloat16


def shift(value, axis, outer, inner, by_outer, by_inner):
    pairs = []
    for a in range(outer):
        for b in range(inner):
            there = ((a + by_outer) % outer) * inner + (b + by_inner) % inner
            pairs.append((a * inner + b, there))
    return lax.ppermute(value, axis, pairs)


def sizes(axis):
    count = lax.axis_size(axis)
    return (count // 2, 2) if axis == "fsdp" else (4, count // 4)


def after(value, *others):
    others = [v for v in others if v is not None]
    if not others:
        return value
    anywhere = pl.BlockSpec(memory_space=pl.ANY)
    return pl.pallas_call(
        lambda *refs: None,
        in_specs=[anywhere] * (1 + len(others)),
        out_specs=anywhere,
        out_shape=jax.ShapeDtypeStruct(value.shape, value.dtype),
        input_output_aliases={0: 0},
        cost_estimate=little,
        name="after",
    )(value, *others)


def beside_step(moved, work):
    if work is None:
        return moved
    return [after(v, work) for v in moved]


def ring_gather(value, axis, work=(), then={}):
    outer, inner = sizes(axis)
    work = list(work) + [None] * (outer - len(work))
    blocks, arrived = [], []
    for a in range(outer):
        row = [value]
        for b in range(1, inner):
            row.append(shift(row[-1], axis, outer, inner, 0, 1))
        moved = row[1:]
        if a + 1 < outer:
            moved.append(shift(value, axis, outer, inner, 1, 0))
        moved = beside_step(moved, work[a] and work[a](arrived))
        if a in then:
            then[a](moved)
        blocks += [value] + moved[: inner - 1]
        value, arrived = moved[-1], moved
    return blocks


def ring_scatter(parts, axis, work=(), then={}):
    outer, inner = sizes(axis)
    work = list(work) + [None] * (outer - len(work))
    total, arrived = None, []
    for step in range(outer):
        a = (step + 1) % outer
        row = parts[a * inner + 1 % inner]
        for b in range(2, inner):
            row = shift(row, axis, outer, inner, 0, 1)
            row = (row.astype(f32) + parts[a * inner + b].astype(f32)).astype(bf16)
        moved = [shift(row, axis, outer, inner, 0, 1)] if inner > 1 else [row]
        if total is not None:
            moved.append(shift(total, axis, outer, inner, 1, 0))
        moved = beside_step(moved, work[step] and work[step](arrived))
        if step in then:
            then[step](moved)
        arrived = moved
        total = moved[0].astype(f32) + parts[a * inner].astype(f32)
        if step:
            total = total.astype(bf16).astype(f32) + moved[1].astype(f32)
        if step + 1 < outer:
            total = total.astype(bf16)
    return total


def relative_order(axis):
    outer, inner = sizes(axis)
    me = lax.axis_index(axis)
    a, b = me // inner, me % inner
    k = jnp.arange(outer * inner)
    return ((a - k // inner) % outer) * inner + (b - k % inner) % inner


def rms_scale(values):
    return lax.rsqrt(jnp.mean(values * values, axis=-1, keepdims=True) + eps)


def exchanges():
    steps = []
    for axis in ("fsdp", "seq"):
        count = lax.axis_size(axis)
        for k in range(count.bit_length() - 1):
            steps.append((axis, [(i, i ^ (1 << k)) for i in range(count)]))
    return steps


def turn(values, cosine, sine):
    return values * cosine + pltpu.roll(values, HD // 2, 1) * sine


def turn_back(values, cosine, sine):
    return values * cosine - pltpu.roll(values, HD // 2, 1) * sine


def dot(left, right, left_dim, right_dim):
    return lax.dot_general(
        left, right, (((left_dim,), (right_dim,)), ((), ())), preferred_element_type=f32
    )


def attend_kernel(tile, qkv_ref, cos_ref, sin_ref, seg_row_ref, seg_col_ref, gain_ref, o_ref):
    blocks, _, rows, _ = qkv_ref.shape
    group = blocks * rows
    cosine, sine = cos_ref[...], sin_ref[...]

    def turned(part, row):
        raw = qkv_ref[:, 0, :, part * HD : (part + 1) * HD].reshape(group, HD).astype(f32)
        return turn(raw * rms_scale(raw) * gain_ref[row : row + 1, :], cosine, sine).astype(bf16)

    queries, keys = turned(0, 0), turned(1, 1)
    values = qkv_ref[:, 0, :, 2 * HD : 3 * HD].reshape(group, HD)
    seg_row = seg_row_ref[0]
    for start in range(0, group, tile):
        scores = dot(queries[start : start + tile], keys, 1, 1) * (1.0 / math.sqrt(HD))
        allowed = seg_col_ref[0, start : start + tile, :] == seg_row
        scores = jnp.where(allowed, scores, masked_score)
        powered = jnp.exp(scores - jnp.max(scores, axis=-1, keepdims=True))
        scale = 1.0 / jnp.sum(powered, axis=-1, keepdims=True)
        attended = dot((powered * scale).astype(bf16), values, 1, 0).astype(bf16)
        o_ref[start // rows : (start + tile) // rows, 0, :, :] = attended.reshape(
            tile // rows, rows, HD
        )


def attend_back_kernel(
    tile,
    qkv_ref,
    do_ref,
    cos_ref,
    sin_ref,
    seg_row_ref,
    seg_col_ref,
    gain_ref,
    grad_ref,
    grad_gain_ref,
):
    blocks, _, rows, _ = qkv_ref.shape
    group = blocks * rows
    cosine, sine = cos_ref[...], sin_ref[...]
    scaling = 1.0 / math.sqrt(HD)

    def normed(part):
        raw = qkv_ref[:, 0, :, part * HD : (part + 1) * HD].reshape(group, HD).astype(f32)
        inverse = rms_scale(raw)
        return raw * inverse, inverse

    def turned(part):
        return turn(normed(part)[0] * gain_ref[part : part + 1, :], cosine, sine).astype(bf16)

    def finish(part, grad_turned):
        unit, inverse = normed(part)
        grad_scaled = turn_back(grad_turned, cosine, sine)
        grad_gain_ref[0, part : part + 1, :] = jnp.sum(grad_scaled * unit, axis=0, keepdims=True)
        grad_unit = grad_scaled * gain_ref[part : part + 1, :]
        grad_raw = inverse * (
            grad_unit - unit * jnp.mean(grad_unit * unit, axis=-1, keepdims=True)
        )
        return grad_raw

    def put(part, value):
        grad_ref[:, 0, :, part * HD : (part + 1) * HD] = value.astype(bf16).reshape(
            blocks, rows, HD
        )

    queries, keys = turned(0), turned(1)
    values = qkv_ref[:, 0, :, 2 * HD : 3 * HD].reshape(group, HD)
    grad_out = do_ref[:, 0, :, :].reshape(group, HD)
    seg_row = seg_row_ref[0]
    grad_query = []
    grad_key = jnp.zeros((group, HD), f32)
    grad_value = jnp.zeros((group, HD), f32)
    for start in range(0, group, tile):
        part = queries[start : start + tile]
        grad_part = grad_out[start : start + tile]
        scores = dot(part, keys, 1, 1) * scaling
        allowed = seg_col_ref[0, start : start + tile, :] == seg_row
        scores = jnp.where(allowed, scores, masked_score)
        powered = jnp.exp(scores - jnp.max(scores, axis=-1, keepdims=True))
        probabilities = powered * (1.0 / jnp.sum(powered, axis=-1, keepdims=True))
        grad_probs = dot(grad_part, values, 1, 1)
        centre = jnp.sum(probabilities * grad_probs, axis=-1, keepdims=True)
        grad_scores = (probabilities * (grad_probs - centre)).astype(bf16)
        grad_query.append(dot(grad_scores, keys, 1, 0) * scaling)
        grad_key = grad_key + dot(grad_scores, part, 0, 0)
        grad_value = grad_value + dot(probabilities.astype(bf16), grad_part, 0, 0)
    put(0, finish(0, jnp.concatenate(grad_query, axis=0)))
    put(1, finish(1, grad_key * scaling))
    put(2, grad_value)


def attention_specs(ns, micro, rows, heads):
    group = ns * rows
    tile = max(rows, 256)
    return (
        tile,
        pl.BlockSpec((ns, 1, rows, 3 * HD), lambda m, h: (0, m, 0, h)),
        pl.BlockSpec((ns, 1, rows, HD), lambda m, h: (0, m, 0, h)),
        [
            pl.BlockSpec((group, HD), lambda m, h: (0, 0)),
            pl.BlockSpec((group, HD), lambda m, h: (0, 0)),
            pl.BlockSpec((1, 1, group), lambda m, h: (m, 0, 0)),
            pl.BlockSpec((1, group, 1), lambda m, h: (m, 0, 0)),
            pl.BlockSpec((2, HD), lambda m, h: (0, 0)),
        ],
    )


def attend(qkv, tables):
    ns, micro, rows, width = qkv.shape
    heads = width // (3 * HD)
    tile, wide, narrow, shared = attention_specs(ns, micro, rows, heads)
    group = ns * rows
    return pl.pallas_call(
        lambda *refs: attend_kernel(tile, *refs),
        grid=(micro, heads),
        in_specs=[wide] + shared,
        out_specs=narrow,
        out_shape=jax.ShapeDtypeStruct((ns, micro, rows, heads * HD), bf16),
        compiler_params=pltpu.CompilerParams(vmem_limit_bytes=40 * 2**20),
        cost_estimate=little,
        name="attend",
    )(qkv, *tables)


def attend_back(qkv, grad_out, tables, ties=()):
    ns, micro, rows, width = qkv.shape
    heads = width // (3 * HD)
    tile, wide, narrow, shared = attention_specs(ns, micro, rows, heads)
    group = ns * rows
    return pl.pallas_call(
        lambda *refs: attend_back_kernel(tile, *refs[:7], *refs[-2:]),
        grid=(micro, heads),
        in_specs=[wide, narrow] + shared + [pl.BlockSpec(memory_space=pl.ANY)] * len(ties),
        out_specs=[wide, pl.BlockSpec((1, 2, HD), lambda m, h: (m * heads + h, 0, 0))],
        out_shape=[
            jax.ShapeDtypeStruct((ns, micro, rows, width), bf16),
            jax.ShapeDtypeStruct((micro * heads, 2, HD), f32),
        ],
        compiler_params=pltpu.CompilerParams(vmem_limit_bytes=40 * 2**20),
        cost_estimate=little,
        name="attend_back",
    )(qkv, grad_out, *tables, *ties)


part = 512


def spans(shape, *block):
    block = block or (1,)
    return pl.BlockSpec(
        tuple(block) + tuple(shape[len(block) :]), lambda e, *_: (e,) + (0,) * (len(shape) - 1)
    )


def whole_of(shape):
    return pl.BlockSpec(
        tuple(shape), lambda *_: (0,) * len(shape), pipeline_mode=pl.Buffered(buffer_count=1)
    )


def call(kernel, name, grid, ins, outs, flops, scratch=(), ties=()):
    ties = [t for t in ties if t is not None]
    count = len(ins)

    def run(*refs):
        kernel(*refs[:count], *refs[count + len(ties) :])

    return pl.pallas_call(
        run,
        grid=grid,
        in_specs=[spec for _, spec in ins] + [pl.BlockSpec(memory_space=pl.ANY)] * len(ties),
        out_specs=[spec for _, spec in outs],
        out_shape=[shape for shape, _ in outs],
        scratch_shapes=list(scratch),
        compiler_params=pltpu.CompilerParams(vmem_limit_bytes=56 * 2**20),
        cost_estimate=little,
        name=name,
    )(*[value for value, _ in ins], *ties)


def picked(slot_row, capacity):
    place = lax.broadcasted_iota(jnp.int32, (capacity, slot_row.shape[1]), 0)
    return place == slot_row


def slot_weights(slot_row, weight_row, capacity):
    chosen = jnp.where(picked(slot_row, capacity), weight_row, 0.0)
    return jnp.sum(chosen, axis=1, keepdims=True)


def dispatch_kernel(scaled, blocks, *refs):
    value_refs, (slot_ref, weight_ref, w_ref, rows_ref, act_ref) = refs[:blocks], refs[blocks:]
    capacity, each = rows_ref.shape[2], blocks // 2
    for h in range(2):
        slot_row = slot_ref[0, h : h + 1, :]
        pick = picked(slot_row, capacity).astype(f32).astype(bf16)
        if scaled:
            scale = slot_weights(slot_row, weight_ref[0, h : h + 1, :], capacity)
        for d in range(0, D, part):
            values = jnp.concatenate(
                [ref[:, d : d + part] for ref in value_refs[h * each : (h + 1) * each]], axis=0
            )
            taken = dot(pick, values, 1, 0)
            if scaled:
                taken = taken * scale
            rows_ref[0, h, :, d : d + part] = taken.astype(bf16)
        act_ref[0, h] = dot(rows_ref[0, h], w_ref[0], 1, 0)


def dispatch(values, slots, weights, bank, capacity, scaled, ties=()):
    count = bank.shape[0]
    values = [v.reshape(-1, v.shape[-1]) for v in values]
    rows_shape = (count, 2, capacity, D)
    act_shape = (count, 2, capacity, FFE)
    return call(
        lambda *refs: dispatch_kernel(scaled, len(values), *refs),
        "dispatch",
        (count,),
        [(v, whole_of(v.shape)) for v in values]
        + [(v, spans(v.shape)) for v in (slots, weights, bank)],
        [
            (jax.ShapeDtypeStruct(rows_shape, bf16), spans(rows_shape)),
            (jax.ShapeDtypeStruct(act_shape, f32), spans(act_shape)),
        ],
        4 * count * capacity * D * (FFE + len(values) * values[0].shape[0] // 2),
        ties=ties,
    )


def act_kernel(taken_ref, gate_ref, grad_ref, w_ref, hidden_ref, grad_gate_ref, grad_up_ref):
    up_act = dot(taken_ref[0, 0], w_ref[0], 1, 0)
    gate_act, grad_hidden = gate_ref[0, 0], grad_ref[0, 0]
    gate_sig = jax.nn.sigmoid(gate_act)
    gate_silu = gate_act * gate_sig
    hidden_ref[0, 0] = (gate_silu * up_act).astype(bf16)
    grad_gate = grad_hidden * up_act * gate_sig * (1.0 + gate_act * (1.0 - gate_sig))
    grad_gate_ref[0, 0] = grad_gate.astype(bf16)
    grad_up_ref[0, 0] = (grad_hidden * gate_silu).astype(bf16)


def activate(taken, gate_act, grad_hidden, w_up, ties=()):
    count, _, capacity, _ = taken.shape

    def of(width):
        return pl.BlockSpec((1, 1, capacity, width), lambda e, h: (e, h, 0, 0))

    result = jax.ShapeDtypeStruct((count, 2, capacity, FFE), bf16)
    return call(
        act_kernel,
        "activate",
        (count, 2),
        [
            (taken, of(D)),
            (gate_act, of(FFE)),
            (grad_hidden, of(FFE)),
            (w_up, spans(w_up.shape)),
        ],
        [(result, of(FFE))] * 3,
        4 * count * capacity * D * FFE,
        ties=ties,
    )


def bank_kernel(left_ref, right_ref, out_ref):
    rows = left_ref.shape[1] * left_ref.shape[2]
    left, right = left_ref[0].reshape(rows, -1), right_ref[0].reshape(rows, -1)
    out_ref[0] = dot(left, right, 0, 0).astype(bf16)


def bank_grad(left, right, ties=()):
    count, _, capacity, _ = left.shape
    result = jax.ShapeDtypeStruct((count, D, FFE), bf16)
    return call(
        bank_kernel,
        "bank_grad",
        (count, D // part),
        [
            (left, pl.BlockSpec((1, 2, capacity, part), lambda e, d: (e, 0, 0, d))),
            (right, pl.BlockSpec((1, 2, capacity, FFE), lambda e, d: (e, 0, 0, 0))),
        ],
        [(result, pl.BlockSpec((1, part, FFE), lambda e, d: (e, d, 0)))],
        4 * count * capacity * D * FFE,
        ties=ties,
    )[0]


def combine_kernel(scaled, acts, blocks, h, *refs):
    act_refs, w_refs = refs[:acts], refs[acts : 2 * acts]
    column_ref, slot_ref, weight_ref = refs[2 * acts : 2 * acts + 3]
    out_refs, total_ref = refs[2 * acts + 3 : -1], refs[-1]
    expert = pl.program_id(0)
    capacity = act_refs[0].shape[2]
    half = total_ref.shape[0]
    place = lax.broadcasted_iota(jnp.int32, (half, capacity), 1)
    pick = (place == column_ref[0, 0]).astype(f32).astype(bf16)
    if scaled:
        scale = slot_weights(slot_ref[0, h : h + 1, :], weight_ref[0, h : h + 1, :], capacity)

    @pl.when(expert == 0)
    def _():
        total_ref[...] = jnp.zeros_like(total_ref)

    for d in range(0, D, part):
        grads = [
            dot(a_ref[0, 0], w_ref[0, d : d + part, :], 1, 1)
            for a_ref, w_ref in zip(act_refs, w_refs)
        ]
        rows = sum(grads[1:], grads[0])
        if scaled:
            rows = rows * scale
        total_ref[:, d : d + part] += dot(pick, rows.astype(bf16), 1, 0)

    @pl.when(expert == pl.num_programs(0) - 1)
    def _():
        n = half // blocks
        for b, ref in enumerate(out_refs):
            ref[...] = total_ref[b * n : (b + 1) * n, :].astype(bf16)


def combine(acts, banks, columns, slots, weights, h, blocks, scaled, ties=()):
    count, _, capacity, _ = acts[0].shape
    half = columns.shape[2]
    result = jax.ShapeDtypeStruct((half // blocks, D), bf16)
    return call(
        lambda *refs: combine_kernel(scaled, len(acts), blocks, h, *refs),
        "combine",
        (count,),
        [(a, pl.BlockSpec((1, 1, capacity, FFE), lambda e: (e, h, 0, 0))) for a in acts]
        + [(w, spans(w.shape)) for w in banks]
        + [(columns, pl.BlockSpec((1, 1, half, 1), lambda e: (e, h, 0, 0)))]
        + [(v, spans(v.shape)) for v in (slots, weights)],
        [(result, whole_of(result.shape))] * blocks,
        2 * count * capacity * D * (FFE * len(acts) + half),
        scratch=[pltpu.VMEM((half, D), f32)],
        ties=ties,
    )


def body(
    layer_input,
    cotangent,
    segments,
    routes,
    route_weights,
    gain_attention,
    gain_experts,
    query_proj,
    key_proj,
    value_proj,
    output_proj,
    head_gains,
    expert_gate,
    expert_up,
    expert_down,
):
    micro, rows, _ = layer_input.shape
    nf, ns = lax.axis_size("fsdp"), lax.axis_size("seq")
    seq_index = lax.axis_index("seq")
    seq_order = relative_order("seq")
    tokens = micro * rows
    group = rows * ns
    half = group * micro // 2
    heads_local = H // ns
    width = heads_local * HD
    local_experts = expert_gate.shape[0]
    experts = local_experts * ns
    capacity = micro * ns // 2 * min(rows, 3 * rows * TOP // (2 * experts))
    share = D // (nf * ns)

    def spread(value, axis):
        return lax.all_gather(value, "fsdp", axis=axis, tiled=True)

    def gather_tokens(value):
        return jnp.stack(ring_gather(value, "seq"))

    def scatter_tokens(parts, work=(), then={}):
        parts = [v.reshape(micro, rows, D) for v in parts]
        return ring_scatter(parts, "seq", work, then).reshape(tokens, D)

    columns = [
        lax.dynamic_slice_in_dim(w, seq_index * width, width, axis=1).reshape(-1, heads_local, HD)
        for w in (query_proj, key_proj, value_proj)
    ]
    columns = jnp.stack(columns, axis=2).reshape(-1, 3 * width)
    extra = jnp.pad(jnp.stack([gain_attention, gain_experts], axis=1), ((0, 0), (0, HD - 2)))
    w_first = spread(jnp.concatenate([columns, extra], axis=1), 0)
    w_qkv = w_first[:, : 3 * width]
    gain_one = w_first[:, 3 * width].astype(f32)
    gain_two = w_first[:, 3 * width + 1].astype(f32)
    w_down = spread(expert_down, 1)
    w_output = spread(output_proj, 0)
    w_gate = spread(expert_gate, 1)
    w_up = spread(expert_up, 1)

    x_all = gather_tokens(layer_input)
    x_wide = x_all.astype(f32)
    inv_all = rms_scale(x_wide)
    h_one = (x_wide * inv_all * gain_one).astype(bf16)
    qkv = jnp.einsum("smtd,de->smte", h_one, w_qkv, preferred_element_type=f32).astype(bf16)

    places = (seq_order[:, None] * rows + jnp.arange(rows)[None, :]).reshape(-1)
    lane = jnp.arange(HD) % (HD // 2)
    frequency = jnp.exp(-jnp.log(rope_base) * (2.0 * lane.astype(f32) / HD))
    angles = places.astype(f32)[:, None] * frequency[None, :]
    sign = jnp.where(jnp.arange(HD) < HD // 2, -1.0, 1.0)
    segment = jnp.take(segments.reshape(micro, ns, rows), seq_order, axis=1).reshape(micro, group)
    tables = (
        jnp.cos(angles),
        jnp.sin(angles) * sign,
        segment[:, None, :],
        segment[:, :, None],
        head_gains.astype(f32),
    )
    o_heads = attend(qkv, tables)

    inverse_seq = jnp.argsort(seq_order)
    o_heads = jnp.take(o_heads, inverse_seq, axis=0)
    o_back = lax.all_to_all(o_heads, "seq", split_axis=0, concat_axis=0, tiled=True)
    o_rows = jnp.moveaxis(o_back, 0, 2).reshape(tokens, D)

    x_rows = layer_input.astype(f32).reshape(tokens, D)
    middle = x_rows + jnp.dot(o_rows, w_output, preferred_element_type=f32)
    inv_two = rms_scale(middle)
    normed_two = middle * inv_two
    h_two_own = (normed_two * gain_two).astype(bf16).reshape(micro, rows, D)
    weight_high = route_weights.astype(bf16)
    weight_low = (route_weights - weight_high.astype(f32)).astype(bf16)
    packed = jnp.concatenate([cotangent, routes.astype(bf16), weight_high, weight_low], axis=-1)
    packed = jnp.pad(packed, ((0, 0), (0, 0), (0, HD - 3 * TOP)))
    g_blocks = ring_gather(
        after(packed, x_all),
        "seq",
        (lambda _: qkv, lambda _: h_two_own),
    )

    packed = jnp.stack([v[..., D : D + 3 * TOP] for v in g_blocks]).astype(f32)
    packed = packed.reshape(2, half, 3 * TOP)
    route_all = packed[..., :TOP].astype(jnp.int32)
    weight_all = packed[..., TOP : 2 * TOP] + packed[..., 2 * TOP :]
    mine = seq_index * local_experts + jnp.arange(local_experts)
    hit = route_all[:, :, None, :] == mine[None, None, :, None]
    chosen = jnp.any(hit, axis=-1)
    weight_of = jnp.sum(jnp.where(hit, weight_all[:, :, None, :], 0.0), axis=-1)
    block = 128
    counted = chosen.reshape(2, half // block, block, local_experts).astype(f32)
    below = jnp.tril(jnp.ones((block, block), f32), -1)
    inside = jnp.einsum("ab,mkbe->mkae", below, counted)
    sums = jnp.sum(counted, axis=2)
    before = jnp.cumsum(sums, axis=1) - sums
    slot = (inside + before[:, :, None, :]).reshape(2, half, local_experts).astype(jnp.int32)
    slots = jnp.transpose(jnp.where(chosen, slot, -1), (2, 0, 1))
    weights = jnp.transpose(weight_of, (2, 0, 1))
    slot_columns = slots[..., None]

    grad_top = cotangent.astype(f32).reshape(tokens, D)
    done = {}

    def keep(**found):
        done.update(found)
        return next(iter(found.values()))

    def grad_work(ties):
        grad_rows, grad_hidden = dispatch(g_blocks, slots, weights, w_down, capacity, True, ties)
        return keep(grad_rows=grad_rows, grad_hidden=grad_hidden)

    h_blocks = ring_gather(h_two_own, "seq", (None, grad_work))
    grad_rows, grad_hidden = done["grad_rows"], done["grad_hidden"]

    def combined(acts, banks, h, scaled, ties=()):
        return combine(acts, banks, slot_columns, slots, weights, h, ns // 2, scaled, ties)

    def take_work(_):
        taken, gate_act = dispatch(h_blocks, slots, weights, w_gate, capacity, False)
        return keep(taken=taken, gate_act=gate_act)

    def act_work(ties):
        hidden, grad_gate_act, grad_up_act = activate(
            done["taken"], done["gate_act"], grad_hidden, w_up, ties
        )
        return keep(hidden=hidden, grad_gate_act=grad_gate_act, grad_up_act=grad_up_act)

    def down_work(ties):
        return keep(whole_down=bank_grad(grad_rows, done["hidden"], ties))

    def first_work(ties):
        acts = (done["grad_gate_act"], done["grad_up_act"])
        first = combined(acts, (w_gate, w_up), 0, False, tuple(ties) + (done["whole_down"],))
        return keep(tail=first[0], first=first)

    o_all = ring_gather(
        after(o_heads.reshape(group * micro, width), h_blocks[-1]),
        "seq",
        (take_work, act_work, down_work, first_work),
        {2: lambda moved: keep(sum_down=after(done["whole_down"], *moved))},
    )
    o_all = jnp.concatenate(o_all, axis=1)
    taken, hidden, first = done["taken"], done["hidden"], done["first"]
    grad_gate_act, grad_up_act = done["grad_gate_act"], done["grad_up_act"]
    second = combined((grad_gate_act, grad_up_act), (w_gate, w_up), 1, False, (first[0],))

    def gate_work(ties):
        return keep(whole_gate=bank_grad(taken, grad_gate_act, ties))

    def up_work(ties):
        return keep(whole_up=bank_grad(taken, grad_up_act, ties))

    def mixed_work(ties):
        mixed = combined((hidden,), (w_down,), 0, True, ties)
        return keep(tail=mixed[0], mixed_first=mixed)

    grad_h_two = scatter_tokens(
        list(first) + list(second),
        (lambda _: second[0], gate_work, up_work, mixed_work),
        {
            1: lambda moved: keep(sum_gate=after(done["whole_gate"], *moved)),
            2: lambda moved: keep(sum_up=after(done["whole_up"], *moved)),
        },
    )

    def bank_sum(whole):
        return lax.psum_scatter(whole, "fsdp", scatter_dimension=1, tiled=True).astype(f32)

    grad_down = bank_sum(done["sum_down"])
    grad_gate = bank_sum(done["sum_gate"])
    grad_up = bank_sum(done["sum_up"])

    grad_gain_two = jnp.sum(grad_h_two * normed_two, axis=0)
    grad_unit = grad_h_two * gain_two
    grad_middle = grad_top + inv_two * (
        grad_unit - normed_two * jnp.mean(grad_unit * normed_two, axis=-1, keepdims=True)
    )
    grad_attn = grad_middle.astype(bf16)
    grad_o = jnp.einsum("te,de->td", grad_attn, w_output, preferred_element_type=f32).astype(bf16)

    def to_heads(value):
        cut = value.reshape(micro, rows, ns, width)
        return lax.all_to_all(
            jnp.moveaxis(cut, 2, 0), "seq", split_axis=0, concat_axis=0, tiled=True
        )

    mixed_second = combined((hidden,), (w_down,), 1, True, (grad_o,))
    do_blocks = after(to_heads(grad_o), mixed_second[0])
    do_heads = jnp.take(do_blocks, seq_order, axis=0)

    def attend_work(ties):
        grad_qkv, grad_head = attend_back(qkv, do_heads, tables, ties)
        return keep(grad_qkv=grad_qkv, grad_head=grad_head)

    def attended_then(moved):
        columns = to_heads(after(grad_attn, *moved)).reshape(micro * group, width)
        keep(columns=columns, head=after(jnp.sum(done["grad_head"], axis=0), *moved), left=exchanges())

    def exchange(moved):
        if done["left"]:
            axis, pairs = done["left"].pop(0)
            keep(head=done["head"] + after(lax.ppermute(done["head"], axis, pairs), *moved))

    def qkv_work(_):
        grads = jnp.einsum(
            "smtd,smte->de", h_one, done["grad_qkv"], preferred_element_type=f32
        )
        return keep(from_qkv=grads)

    def part_work(_):
        wide = jnp.einsum("smte,de->smtd", done["grad_qkv"], w_qkv, preferred_element_type=f32)
        return keep(part=wide.astype(bf16), wide=wide)

    mixed = list(done["mixed_first"]) + list(mixed_second)
    mixed[ns // 4 + 1] = after(mixed[ns // 4 + 1], grad_h_two)
    mixed = scatter_tokens(
        mixed,
        (lambda _: do_heads, attend_work, part_work, qkv_work),
        {1: attended_then, 2: exchange, 3: exchange},
    )
    layer_output = (middle + mixed).astype(bf16).reshape(micro, rows, D)
    def out_work(ties):
        grads = jnp.einsum(
            "td,te->de", after(o_all, *ties), done["columns"], preferred_element_type=f32
        )
        return keep(from_out=grads)

    part_h_one = done["part"]
    grad_h_one = scatter_tokens(
        [part_h_one[k] for k in range(ns)],
        (lambda _: done["from_qkv"], out_work, lambda _: grad_down, lambda _: grad_gate),
        {step: exchange for step in range(4)},
    )
    while done["left"]:
        exchange(())
    grad_head_gains = done["head"]
    grad_gain_one = jnp.sum(done["wide"] * (x_wide * inv_all), axis=(0, 1, 2))
    inv_one = rms_scale(x_rows)
    normed_one = x_rows * inv_one
    grad_unit = grad_h_one * gain_one
    input_grad = grad_middle + inv_one * (
        grad_unit - normed_one * jnp.mean(grad_unit * normed_one, axis=-1, keepdims=True)
    )
    input_grad = input_grad.reshape(micro, rows, D)

    from_qkv, from_out = done["from_qkv"], done["from_out"]
    from_out = jnp.take(from_out.reshape(ns, width, width), inverse_seq, axis=0).reshape(D, width)
    from_gains = jnp.pad(jnp.stack([grad_gain_one, grad_gain_two], axis=1), ((0, 0), (0, HD - 2)))
    whole = jnp.concatenate([from_qkv, from_out, from_gains], axis=1).astype(bf16)
    order = relative_order("fsdp")
    whole = jnp.take(whole.reshape(nf, D // nf, -1), order, axis=0)
    owned = ring_scatter([whole[k] for k in range(nf)], "fsdp").astype(bf16)
    owned = lax.all_to_all(
        owned.reshape(ns, share, -1), "seq", split_axis=0, concat_axis=0, tiled=True
    ).astype(f32)
    of_qkv = owned[..., : 3 * width].reshape(ns, share, heads_local, 3, HD)
    grad_query, grad_key, grad_value = (
        jnp.moveaxis(of_qkv[..., k, :], 0, 1).reshape(share, D) for k in range(3)
    )
    grad_output = jnp.moveaxis(owned[..., 3 * width : 4 * width], 0, 1).reshape(share, D)
    of_gains = jnp.sum(owned[..., 4 * width : 4 * width + 2], axis=0)
    return (
        layer_output,
        input_grad,
        of_gains[:, 0],
        of_gains[:, 1],
        grad_query,
        grad_key,
        grad_value,
        grad_output,
        grad_head_gains,
        grad_gate,
        grad_up,
        grad_down,
    )


def solution(mesh):
    placed = (
        P(None, ("fsdp", "seq"), None),
        P(None, ("fsdp", "seq"), None),
        P(None, "fsdp"),
        P(None, ("fsdp", "seq"), None),
        P(None, ("fsdp", "seq"), None),
        P("fsdp"),
        P("fsdp"),
        P("fsdp", None),
        P("fsdp", None),
        P("fsdp", None),
        P("fsdp", None),
        P(),
        P("seq", "fsdp", None),
        P("seq", "fsdp", None),
        P("seq", "fsdp", None),
    )
    return jax.shard_map(
        body,
        mesh=mesh,
        in_specs=placed,
        out_specs=(
            P(None, ("fsdp", "seq"), None),
            P(None, ("fsdp", "seq"), None),
            P(("fsdp", "seq")),
            P(("fsdp", "seq")),
            P(("fsdp", "seq"), None),
            P(("fsdp", "seq"), None),
            P(("fsdp", "seq"), None),
            P(("fsdp", "seq"), None),
            P(),
            P("seq", "fsdp", None),
            P("seq", "fsdp", None),
            P("seq", "fsdp", None),
        ),
        check_vma=False,
    )
```

```python
import math

import jax
import jax.numpy as jnp
from jax import lax
from jax.experimental import pallas as pl
from jax.experimental.pallas import tpu as pltpu
from jax.sharding import PartitionSpec as P

D = 2048
H = 16
HD = 128
FFE = 1024
TOP = 8
SEQ_LEN = 1024

eps = 1e-06
rope_base = 10000.0
masked_score = -1e30
f32 = jnp.float32
little = pl.CostEstimate(flops=1, bytes_accessed=1, transcendentals=0)
bf16 = jnp.bfloat16


def shift(value, axis, outer, inner, by_outer, by_inner):
    pairs = []
    for a in range(outer):
        for b in range(inner):
            there = ((a + by_outer) % outer) * inner + (b + by_inner) % inner
            pairs.append((a * inner + b, there))
    return lax.ppermute(value, axis, pairs)


def sizes(axis):
    count = lax.axis_size(axis)
    return (count // 2, 2) if axis == "fsdp" else (4, count // 4)


def after(value, *others):
    others = [v for v in others if v is not None]
    if not others:
        return value
    anywhere = pl.BlockSpec(memory_space=pl.ANY)
    return pl.pallas_call(
        lambda *refs: None,
        in_specs=[anywhere] * (1 + len(others)),
        out_specs=anywhere,
        out_shape=jax.ShapeDtypeStruct(value.shape, value.dtype),
        input_output_aliases={0: 0},
        cost_estimate=little,
        name="after",
    )(value, *others)


def together(work, *moved):
    moved = list(moved)
    for k in range(len(moved)):
        moved[k] = after(moved[k], *work, *moved[:k], *moved[k + 1 :])
    return moved


def ring_gather(value, axis, work=None, then={}):
    outer, inner = sizes(axis)
    blocks, arrived = [], []
    for a in range(outer):
        row = [value]
        for b in range(1, inner):
            row.append(shift(row[-1], axis, outer, inner, 0, 1))
        moved = row[1:]
        if a + 1 < outer:
            moved.append(shift(value, axis, outer, inner, 1, 0))
        if work is not None:
            moved = together([f(arrived) for f in work[a : a + 1] if f], *moved)
        if a in then:
            then[a](moved)
        blocks += [value] + moved[: inner - 1]
        value, arrived = moved[-1], moved
    return blocks


def row_move(parts, a, axis):
    outer, inner = sizes(axis)
    row = parts[a * inner + 1 % inner]
    for b in range(2, inner):
        row = shift(row, axis, outer, inner, 0, 1)
        row = (row.astype(f32) + parts[a * inner + b].astype(f32)).astype(bf16)
    return shift(row, axis, outer, inner, 0, 1) if inner > 1 else row


def row_sum(moved, parts, a, axis):
    total = moved.astype(f32) + parts[a * sizes(axis)[1]].astype(f32)
    return total.astype(bf16)


def ahead(value, axis):
    return shift(value, axis, *sizes(axis), 1, 0)


def add(one, other):
    return one.astype(f32) + other.astype(f32)


def ring_scatter(parts, axis, work=(), then={}):
    outer, _ = sizes(axis)
    total, arrived = None, []
    for step in range(outer):
        a = (step + 1) % outer
        moved = [row_move(parts, a, axis)]
        if step:
            moved.append(ahead(total, axis))
        moved = together([f(arrived) for f in work[step : step + 1]], *moved)
        if step in then:
            then[step](moved)
        arrived = moved
        total = row_sum(moved[0], parts, a, axis)
        if step:
            total = add(total, moved[1])
        if step and step + 1 < outer:
            total = total.astype(bf16)
    return total


def relative_order(axis):
    outer, inner = sizes(axis)
    me = lax.axis_index(axis)
    a, b = me // inner, me % inner
    k = jnp.arange(outer * inner)
    return ((a - k // inner) % outer) * inner + (b - k % inner) % inner


def rms_scale(values):
    return lax.rsqrt(jnp.mean(values * values, axis=-1, keepdims=True) + eps)


def exchanges():
    steps = []
    for axis in ("fsdp", "seq"):
        count = lax.axis_size(axis)
        for k in range(count.bit_length() - 1):
            steps.append((axis, [(i, i ^ (1 << k)) for i in range(count)]))
    return steps


def turn(values, cosine, sine):
    return values * cosine + pltpu.roll(values, HD // 2, 1) * sine


def turn_back(values, cosine, sine):
    return values * cosine - pltpu.roll(values, HD // 2, 1) * sine


def dot(left, right, left_dim, right_dim):
    return lax.dot_general(
        left, right, (((left_dim,), (right_dim,)), ((), ())), preferred_element_type=f32
    )


def attend_kernel(tile, qkv_ref, cos_ref, sin_ref, seg_row_ref, seg_col_ref, gain_ref, o_ref):
    blocks, _, rows, _ = qkv_ref.shape
    group = blocks * rows
    cosine, sine = cos_ref[...], sin_ref[...]

    def turned(part, row):
        raw = qkv_ref[:, 0, :, part * HD : (part + 1) * HD].reshape(group, HD).astype(f32)
        return turn(raw * rms_scale(raw) * gain_ref[row : row + 1, :], cosine, sine).astype(bf16)

    queries, keys = turned(0, 0), turned(1, 1)
    values = qkv_ref[:, 0, :, 2 * HD : 3 * HD].reshape(group, HD)
    seg_row = seg_row_ref[0]
    for start in range(0, group, tile):
        scores = dot(queries[start : start + tile], keys, 1, 1) * (1.0 / math.sqrt(HD))
        allowed = seg_col_ref[0, start : start + tile, :] == seg_row
        scores = jnp.where(allowed, scores, masked_score)
        powered = jnp.exp(scores - jnp.max(scores, axis=-1, keepdims=True))
        scale = 1.0 / jnp.sum(powered, axis=-1, keepdims=True)
        attended = dot((powered * scale).astype(bf16), values, 1, 0).astype(bf16)
        o_ref[start // rows : (start + tile) // rows, 0, :, :] = attended.reshape(
            tile // rows, rows, HD
        )


def attend_back_kernel(
    tile,
    qkv_ref,
    do_ref,
    cos_ref,
    sin_ref,
    seg_row_ref,
    seg_col_ref,
    gain_ref,
    grad_ref,
    grad_gain_ref,
):
    blocks, _, rows, _ = qkv_ref.shape
    group = blocks * rows
    cosine, sine = cos_ref[...], sin_ref[...]
    scaling = 1.0 / math.sqrt(HD)

    def normed(part):
        raw = qkv_ref[:, 0, :, part * HD : (part + 1) * HD].reshape(group, HD).astype(f32)
        inverse = rms_scale(raw)
        return raw * inverse, inverse

    def turned(part):
        return turn(normed(part)[0] * gain_ref[part : part + 1, :], cosine, sine).astype(bf16)

    def finish(part, grad_turned):
        unit, inverse = normed(part)
        grad_scaled = turn_back(grad_turned, cosine, sine)
        grad_gain_ref[0, part : part + 1, :] = jnp.sum(grad_scaled * unit, axis=0, keepdims=True)
        grad_unit = grad_scaled * gain_ref[part : part + 1, :]
        grad_raw = inverse * (
            grad_unit - unit * jnp.mean(grad_unit * unit, axis=-1, keepdims=True)
        )
        return grad_raw

    def put(part, value):
        grad_ref[:, 0, :, part * HD : (part + 1) * HD] = value.astype(bf16).reshape(
            blocks, rows, HD
        )

    queries, keys = turned(0), turned(1)
    values = qkv_ref[:, 0, :, 2 * HD : 3 * HD].reshape(group, HD)
    grad_out = do_ref[:, 0, :, :].reshape(group, HD)
    seg_row = seg_row_ref[0]
    grad_query = []
    grad_key = jnp.zeros((group, HD), f32)
    grad_value = jnp.zeros((group, HD), f32)
    for start in range(0, group, tile):
        part = queries[start : start + tile]
        grad_part = grad_out[start : start + tile]
        scores = dot(part, keys, 1, 1) * scaling
        allowed = seg_col_ref[0, start : start + tile, :] == seg_row
        scores = jnp.where(allowed, scores, masked_score)
        powered = jnp.exp(scores - jnp.max(scores, axis=-1, keepdims=True))
        probabilities = powered * (1.0 / jnp.sum(powered, axis=-1, keepdims=True))
        grad_probs = dot(grad_part, values, 1, 1)
        centre = jnp.sum(probabilities * grad_probs, axis=-1, keepdims=True)
        grad_scores = (probabilities * (grad_probs - centre)).astype(bf16)
        grad_query.append(dot(grad_scores, keys, 1, 0) * scaling)
        grad_key = grad_key + dot(grad_scores, part, 0, 0)
        grad_value = grad_value + dot(probabilities.astype(bf16), grad_part, 0, 0)
    put(0, finish(0, jnp.concatenate(grad_query, axis=0)))
    put(1, finish(1, grad_key * scaling))
    put(2, grad_value)


def attention_specs(ns, micro, rows, heads):
    group = ns * rows
    tile = max(rows, 256)
    return (
        tile,
        pl.BlockSpec((ns, 1, rows, 3 * HD), lambda m, h: (0, m, 0, h)),
        pl.BlockSpec((ns, 1, rows, HD), lambda m, h: (0, m, 0, h)),
        [
            pl.BlockSpec((group, HD), lambda m, h: (0, 0)),
            pl.BlockSpec((group, HD), lambda m, h: (0, 0)),
            pl.BlockSpec((1, 1, group), lambda m, h: (m, 0, 0)),
            pl.BlockSpec((1, group, 1), lambda m, h: (m, 0, 0)),
            pl.BlockSpec((2, HD), lambda m, h: (0, 0)),
        ],
    )


def attend(qkv, tables):
    ns, micro, rows, width = qkv.shape
    heads = width // (3 * HD)
    tile, wide, narrow, shared = attention_specs(ns, micro, rows, heads)
    group = ns * rows
    return pl.pallas_call(
        lambda *refs: attend_kernel(tile, *refs),
        grid=(micro, heads),
        in_specs=[wide] + shared,
        out_specs=narrow,
        out_shape=jax.ShapeDtypeStruct((ns, micro, rows, heads * HD), bf16),
        compiler_params=pltpu.CompilerParams(vmem_limit_bytes=40 * 2**20),
        cost_estimate=little,
        name="attend",
    )(qkv, *tables)


def attend_back(qkv, grad_out, tables, ties=()):
    ns, micro, rows, width = qkv.shape
    heads = width // (3 * HD)
    tile, wide, narrow, shared = attention_specs(ns, micro, rows, heads)
    group = ns * rows
    return pl.pallas_call(
        lambda *refs: attend_back_kernel(tile, *refs[:7], *refs[-2:]),
        grid=(micro, heads),
        in_specs=[wide, narrow] + shared + [pl.BlockSpec(memory_space=pl.ANY)] * len(ties),
        out_specs=[wide, pl.BlockSpec((1, 2, HD), lambda m, h: (m * heads + h, 0, 0))],
        out_shape=[
            jax.ShapeDtypeStruct((ns, micro, rows, width), bf16),
            jax.ShapeDtypeStruct((micro * heads, 2, HD), f32),
        ],
        compiler_params=pltpu.CompilerParams(vmem_limit_bytes=40 * 2**20),
        cost_estimate=little,
        name="attend_back",
    )(qkv, grad_out, *tables, *ties)


part = 512


def spans(shape, *block):
    block = block or (1,)
    return pl.BlockSpec(
        tuple(block) + tuple(shape[len(block) :]), lambda e, *_: (e,) + (0,) * (len(shape) - 1)
    )


def whole_of(shape):
    return pl.BlockSpec(
        tuple(shape), lambda *_: (0,) * len(shape), pipeline_mode=pl.Buffered(buffer_count=1)
    )


def call(kernel, name, grid, ins, outs, flops, scratch=(), ties=(), aliases={}):
    ties = [t for t in ties if t is not None]
    count = len(ins)

    def run(*refs):
        kernel(*refs[:count], *refs[count + len(ties) :])

    return pl.pallas_call(
        run,
        grid=grid,
        in_specs=[spec for _, spec in ins] + [pl.BlockSpec(memory_space=pl.ANY)] * len(ties),
        out_specs=[spec for _, spec in outs],
        out_shape=[shape for shape, _ in outs],
        scratch_shapes=list(scratch),
        input_output_aliases=aliases,
        compiler_params=pltpu.CompilerParams(vmem_limit_bytes=56 * 2**20),
        cost_estimate=little,
        name=name,
    )(*[value for value, _ in ins], *ties)


def picked(slot_row, capacity):
    place = lax.broadcasted_iota(jnp.int32, (capacity, slot_row.shape[1]), 0)
    return place == slot_row


def slot_weights(slot_row, weight_row, capacity):
    chosen = jnp.where(picked(slot_row, capacity), weight_row, 0.0)
    return jnp.sum(chosen, axis=1, keepdims=True)


def dispatch_kernel(scaled, blocks, *refs):
    value_refs, (slot_ref, weight_ref, w_ref, rows_ref, act_ref) = refs[:blocks], refs[blocks:]
    capacity, each = rows_ref.shape[2], blocks // 2
    for h in range(2):
        slot_row = slot_ref[0, h : h + 1, :]
        pick = picked(slot_row, capacity).astype(f32).astype(bf16)
        if scaled:
            scale = slot_weights(slot_row, weight_ref[0, h : h + 1, :], capacity)
        for d in range(0, D, part):
            values = jnp.concatenate(
                [ref[:, d : d + part] for ref in value_refs[h * each : (h + 1) * each]], axis=0
            )
            taken = dot(pick, values, 1, 0)
            if scaled:
                taken = taken * scale
            rows_ref[0, h, :, d : d + part] = taken.astype(bf16)
        act_ref[0, h] = dot(rows_ref[0, h], w_ref[0], 1, 0)


def dispatch(values, slots, weights, bank, capacity, scaled, ties=()):
    count = bank.shape[0]
    values = [v.reshape(-1, v.shape[-1]) for v in values]
    rows_shape = (count, 2, capacity, D)
    act_shape = (count, 2, capacity, FFE)
    return call(
        lambda *refs: dispatch_kernel(scaled, len(values), *refs),
        "dispatch",
        (count,),
        [(v, whole_of(v.shape)) for v in values]
        + [(v, spans(v.shape)) for v in (slots, weights, bank)],
        [
            (jax.ShapeDtypeStruct(rows_shape, bf16), spans(rows_shape)),
            (jax.ShapeDtypeStruct(act_shape, f32), spans(act_shape)),
        ],
        4 * count * capacity * D * (FFE + len(values) * values[0].shape[0] // 2),
        ties=ties,
    )


def act_kernel(taken_ref, gate_ref, grad_ref, w_ref, hidden_ref, grad_gate_ref, grad_up_ref):
    up_act = dot(taken_ref[0, 0], w_ref[0], 1, 0)
    gate_act, grad_hidden = gate_ref[0, 0], grad_ref[0, 0]
    gate_sig = jax.nn.sigmoid(gate_act)
    gate_silu = gate_act * gate_sig
    hidden_ref[0, 0] = (gate_silu * up_act).astype(bf16)
    grad_gate = grad_hidden * up_act * gate_sig * (1.0 + gate_act * (1.0 - gate_sig))
    grad_gate_ref[0, 0] = grad_gate.astype(bf16)
    grad_up_ref[0, 0] = (grad_hidden * gate_silu).astype(bf16)


def activate(taken, gate_act, grad_hidden, w_up, first, count, before, ties=()):
    capacity = taken.shape[2]

    def of(width):
        return pl.BlockSpec((1, 1, capacity, width), lambda e, h: (first + e, h, 0, 0))

    result = jax.ShapeDtypeStruct(gate_act.shape, bf16)
    bank = pl.BlockSpec((1,) + w_up.shape[1:], lambda e, h: (first + e, 0, 0))
    return call(
        act_kernel,
        "activate",
        (count, 2),
        [(taken, of(D)), (gate_act, of(FFE)), (grad_hidden, of(FFE)), (w_up, bank)],
        [(result, of(FFE))] * 3,
        4 * count * capacity * D * FFE,
        ties=tuple(before) + tuple(ties),
        aliases={4 + k: k for k in range(len(before))},
    )


def bank_kernel(left_ref, right_ref, out_ref):
    rows = left_ref.shape[1] * left_ref.shape[2]
    left, right = left_ref[0].reshape(rows, -1), right_ref[0].reshape(rows, -1)
    out_ref[0] = dot(left, right, 0, 0).astype(bf16)


def bank_grad(left, right, ties=(), first=0, count=None):
    capacity = left.shape[2]
    count = count or left.shape[0]
    result = jax.ShapeDtypeStruct((count, D, FFE), bf16)
    return call(
        bank_kernel,
        "bank_grad",
        (count, D // part),
        [
            (left, pl.BlockSpec((1, 2, capacity, part), lambda e, d: (first + e, 0, 0, d))),
            (right, pl.BlockSpec((1, 2, capacity, FFE), lambda e, d: (first + e, 0, 0, 0))),
        ],
        [(result, pl.BlockSpec((1, part, FFE), lambda e, d: (e, d, 0)))],
        4 * count * capacity * D * FFE,
        ties=ties,
    )[0]


def combine_kernel(scaled, acts, blocks, h, *refs):
    act_refs, w_refs = refs[:acts], refs[acts : 2 * acts]
    column_ref, slot_ref, weight_ref = refs[2 * acts : 2 * acts + 3]
    out_refs, total_ref = refs[2 * acts + 3 : -1], refs[-1]
    expert = pl.program_id(0)
    capacity = act_refs[0].shape[2]
    half = total_ref.shape[0]
    place = lax.broadcasted_iota(jnp.int32, (half, capacity), 1)
    pick = (place == column_ref[0, 0]).astype(f32).astype(bf16)
    if scaled:
        scale = slot_weights(slot_ref[0, h : h + 1, :], weight_ref[0, h : h + 1, :], capacity)

    @pl.when(expert == 0)
    def _():
        total_ref[...] = jnp.zeros_like(total_ref)

    for d in range(0, D, part):
        grads = [
            dot(a_ref[0, 0], w_ref[0, d : d + part, :], 1, 1)
            for a_ref, w_ref in zip(act_refs, w_refs)
        ]
        rows = sum(grads[1:], grads[0])
        if scaled:
            rows = rows * scale
        total_ref[:, d : d + part] += dot(pick, rows.astype(bf16), 1, 0)

    @pl.when(expert == pl.num_programs(0) - 1)
    def _():
        n = half // blocks
        for b, ref in enumerate(out_refs):
            ref[...] = total_ref[b * n : (b + 1) * n, :].astype(bf16)


def combine(acts, banks, columns, slots, weights, h, blocks, scaled, ties=()):
    count, _, capacity, _ = acts[0].shape
    half = columns.shape[2]
    result = jax.ShapeDtypeStruct((half // blocks, D), bf16)
    return call(
        lambda *refs: combine_kernel(scaled, len(acts), blocks, h, *refs),
        "combine",
        (count,),
        [(a, pl.BlockSpec((1, 1, capacity, FFE), lambda e: (e, h, 0, 0))) for a in acts]
        + [(w, spans(w.shape)) for w in banks]
        + [(columns, pl.BlockSpec((1, 1, half, 1), lambda e: (e, h, 0, 0)))]
        + [(v, spans(v.shape)) for v in (slots, weights)],
        [(result, whole_of(result.shape))] * blocks,
        2 * count * capacity * D * (FFE * len(acts) + half),
        scratch=[pltpu.VMEM((half, D), f32)],
        ties=ties,
    )


def body(
    layer_input,
    cotangent,
    segments,
    routes,
    route_weights,
    gain_attention,
    gain_experts,
    query_proj,
    key_proj,
    value_proj,
    output_proj,
    head_gains,
    expert_gate,
    expert_up,
    expert_down,
):
    micro, rows, _ = layer_input.shape
    nf, ns = lax.axis_size("fsdp"), lax.axis_size("seq")
    seq_index = lax.axis_index("seq")
    seq_order = relative_order("seq")
    tokens = micro * rows
    group = rows * ns
    half = group * micro // 2
    heads_local = H // ns
    width = heads_local * HD
    local_experts = expert_gate.shape[0]
    experts = local_experts * ns
    capacity = micro * ns // 2 * min(rows, 3 * rows * TOP // (2 * experts))
    share = D // (nf * ns)

    def spread(value, axis):
        return lax.all_gather(value, "fsdp", axis=axis, tiled=True)

    def gather_tokens(value):
        return jnp.stack(ring_gather(value, "seq"))

    columns = [
        lax.dynamic_slice_in_dim(w, seq_index * width, width, axis=1).reshape(-1, heads_local, HD)
        for w in (query_proj, key_proj, value_proj)
    ]
    columns = jnp.stack(columns, axis=2).reshape(-1, 3 * width)
    extra = jnp.pad(jnp.stack([gain_attention, gain_experts], axis=1), ((0, 0), (0, HD - 2)))
    w_first = spread(jnp.concatenate([columns, extra], axis=1), 0)
    w_qkv = w_first[:, : 3 * width]
    gain_one = w_first[:, 3 * width].astype(f32)
    gain_two = w_first[:, 3 * width + 1].astype(f32)
    w_down = spread(expert_down, 1)
    w_output = spread(output_proj, 0)
    w_gate = spread(expert_gate, 1)
    w_up = spread(expert_up, 1)

    weight_high = route_weights.astype(bf16)
    weight_low = (route_weights - weight_high.astype(f32)).astype(bf16)
    packed = jnp.concatenate(
        [layer_input, routes.astype(bf16), weight_high, weight_low], axis=-1
    )
    packed = jnp.pad(packed, ((0, 0), (0, 0), (0, HD - 3 * TOP)))
    packed = gather_tokens(packed)
    x_wide = packed[..., :D].astype(f32)
    inv_all = rms_scale(x_wide)
    h_one = (x_wide * inv_all * gain_one).astype(bf16)
    qkv = jnp.einsum("smtd,de->smte", h_one, w_qkv, preferred_element_type=f32).astype(bf16)

    places = (seq_order[:, None] * rows + jnp.arange(rows)[None, :]).reshape(-1)
    lane = jnp.arange(HD) % (HD // 2)
    frequency = jnp.exp(-jnp.log(rope_base) * (2.0 * lane.astype(f32) / HD))
    angles = places.astype(f32)[:, None] * frequency[None, :]
    sign = jnp.where(jnp.arange(HD) < HD // 2, -1.0, 1.0)
    segment = jnp.take(segments.reshape(micro, ns, rows), seq_order, axis=1).reshape(micro, group)
    tables = (
        jnp.cos(angles),
        jnp.sin(angles) * sign,
        segment[:, None, :],
        segment[:, :, None],
        head_gains.astype(f32),
    )
    o_heads = attend(qkv, tables)

    inverse_seq = jnp.argsort(seq_order)
    o_heads = jnp.take(o_heads, inverse_seq, axis=0)
    o_back = lax.all_to_all(o_heads, "seq", split_axis=0, concat_axis=0, tiled=True)
    o_rows = jnp.moveaxis(o_back, 0, 2).reshape(tokens, D)

    x_rows = layer_input.astype(f32).reshape(tokens, D)
    middle = x_rows + jnp.dot(o_rows, w_output, preferred_element_type=f32)
    inv_two = rms_scale(middle)
    normed_two = middle * inv_two
    h_two_own = (normed_two * gain_two).astype(bf16).reshape(micro, rows, D)
    h_blocks = ring_gather(h_two_own, "seq", ())

    packed = packed[..., D : D + 3 * TOP].astype(f32)
    packed = packed.reshape(2, half, 3 * TOP)
    route_all = packed[..., :TOP].astype(jnp.int32)
    weight_all = packed[..., TOP : 2 * TOP] + packed[..., 2 * TOP :]
    mine = seq_index * local_experts + jnp.arange(local_experts)
    hit = route_all[:, :, None, :] == mine[None, None, :, None]
    chosen = jnp.any(hit, axis=-1)
    weight_of = jnp.sum(jnp.where(hit, weight_all[:, :, None, :], 0.0), axis=-1)
    block = 128
    counted = chosen.reshape(2, half // block, block, local_experts).astype(f32)
    below = jnp.tril(jnp.ones((block, block), f32), -1)
    inside = jnp.einsum("ab,mkbe->mkae", below, counted)
    sums = jnp.sum(counted, axis=2)
    before = jnp.cumsum(sums, axis=1) - sums
    slot = (inside + before[:, :, None, :]).reshape(2, half, local_experts).astype(jnp.int32)
    slots = jnp.transpose(jnp.where(chosen, slot, -1), (2, 0, 1))
    weights = jnp.transpose(weight_of, (2, 0, 1))
    slot_columns = slots[..., None]

    grad_top = cotangent.astype(f32).reshape(tokens, D)
    done = {}

    def keep(**found):
        done.update(found)
        return next(iter(found.values()))

    def combined(acts, banks, h, scaled, ties=()):
        return combine(acts, banks, slot_columns, slots, weights, h, ns // 2, scaled, ties)

    def take_work(ties):
        taken, gate_act = dispatch(h_blocks, slots, weights, w_gate, capacity, False, ties)
        return keep(taken=taken, gate_act=gate_act)

    g_blocks = ring_gather(after(cotangent, h_blocks[-1]), "seq", (None, take_work))

    def grad_work(_):
        grad_rows, grad_hidden = dispatch(g_blocks, slots, weights, w_down, capacity, True)
        return keep(grad_rows=grad_rows, grad_hidden=grad_hidden)

    pair = local_experts // 2

    def act_work(first):
        def work(ties):
            before = done.get("acts", ())
            acts = activate(
                done["taken"], done["gate_act"], done["grad_hidden"], w_up, first, pair, before, ties
            )
            whole = bank_grad(done["grad_rows"], acts[0], (), first, pair)
            done.setdefault("whole_down", []).append(whole)
            done["acts"] = acts
            return whole

        return work

    def down_then(moved):
        done.setdefault("sum_down", []).append(after(done["whole_down"][-1], *moved))

    def first_work(ties):
        first = combined(done["acts"][1:], (w_gate, w_up), 0, False, ties)
        return keep(tail=first[0], first=first)

    o_all = ring_gather(
        after(o_heads.reshape(group * micro, width), g_blocks[-1]),
        "seq",
        (grad_work, act_work(0), act_work(pair), first_work),
        {1: down_then, 2: down_then},
    )
    o_last = o_all[-1]
    o_all = jnp.concatenate(o_all, axis=1)
    taken, first = done["taken"], done["first"]
    hidden, grad_gate_act, grad_up_act = done["acts"]
    second = combined(
        (grad_gate_act, grad_up_act), (w_gate, w_up), 1, False, (first[0], o_last)
    )

    def gate_work(ties):
        return keep(whole_gate=bank_grad(taken, grad_gate_act, ties))

    def up_work(ties):
        return keep(whole_up=bank_grad(taken, grad_up_act, ties))

    def mixed_work(ties):
        mixed = combined((hidden,), (w_down,), 0, True, ties)
        return keep(tail=mixed[0], mixed_first=mixed)

    parts = [v.reshape(micro, rows, D) for v in list(first) + list(second)]
    grad_h_two = ring_scatter(
        parts,
        "seq",
        (lambda _: second[0], gate_work, up_work, mixed_work),
        {
            1: lambda moved: keep(sum_gate=after(done["whole_gate"], *moved)),
            2: lambda moved: keep(sum_up=after(done["whole_up"], *moved)),
            3: lambda moved: keep(last=moved),
        },
    ).reshape(tokens, D)

    def bank_sum(whole):
        return lax.psum_scatter(whole, "fsdp", scatter_dimension=1, tiled=True).astype(f32)

    grad_down = jnp.concatenate([bank_sum(v) for v in done["sum_down"]], axis=0)
    grad_gate = bank_sum(done["sum_gate"])
    grad_up = bank_sum(done["sum_up"])

    grad_gain_two = jnp.sum(grad_h_two * normed_two, axis=0)
    grad_unit = grad_h_two * gain_two
    grad_middle = grad_top + inv_two * (
        grad_unit - normed_two * jnp.mean(grad_unit * normed_two, axis=-1, keepdims=True)
    )
    grad_attn = grad_middle.astype(bf16)
    grad_o = jnp.einsum("te,de->td", grad_attn, w_output, preferred_element_type=f32).astype(bf16)

    def to_heads(value):
        cut = value.reshape(micro, rows, ns, width)
        return lax.all_to_all(
            jnp.moveaxis(cut, 2, 0), "seq", split_axis=0, concat_axis=0, tiled=True
        )

    mixed_second = combined((hidden,), (w_down,), 1, True, (grad_o,))
    mixed = [v.reshape(micro, rows, D) for v in list(done["mixed_first"]) + list(mixed_second)]
    inner = sizes("seq")[1]
    for a in (0, 1):
        k = a * inner + 1 % inner
        mixed[k] = after(mixed[k], *done["last"])
    one, zero, do_blocks = together(
        (mixed_second[0],), row_move(mixed, 1, "seq"), row_move(mixed, 0, "seq"), to_heads(grad_o)
    )
    do_heads = jnp.take(do_blocks, seq_order, axis=0)

    total = ahead(row_sum(one, mixed, 1, "seq"), "seq")
    grad_qkv, grad_head = attend_back(qkv, do_heads, tables)
    wide = jnp.einsum("smte,de->smtd", grad_qkv, w_qkv, preferred_element_type=f32)
    part_h_one = wide.astype(bf16)
    total, two, columns = together(
        (part_h_one,), total, row_move(mixed, 2, "seq"), to_heads(after(grad_attn, do_blocks))
    )

    part_h_one = after(part_h_one, total)
    part_h_one = [part_h_one[k] for k in range(ns)]
    from_qkv = jnp.einsum(
        "smtd,smte->de", after(h_one, total), grad_qkv, preferred_element_type=f32
    )
    from_out = jnp.einsum(
        "td,te->de",
        after(o_all, total),
        columns.reshape(micro * group, width),
        preferred_element_type=f32,
    )
    left = exchanges()
    head = jnp.sum(after(grad_head, total), axis=0)

    def exchange(head):
        axis, pairs = left.pop(0)
        return lax.ppermute(head, axis, pairs)

    total = ahead(add(row_sum(two, mixed, 2, "seq"), total).astype(bf16), "seq")
    head = head + exchange(head)
    total, three, one, moved = together(
        (from_qkv, from_out),
        total,
        row_move(mixed, 3, "seq"),
        row_move(part_h_one, 1, "seq"),
        exchange(head),
    )
    head = head + moved

    from_out = jnp.take(from_out.reshape(ns, width, width), inverse_seq, axis=0).reshape(D, width)
    grad_gain_one = jnp.sum(wide * (x_wide * inv_all), axis=(0, 1, 2))
    from_gains = jnp.pad(jnp.stack([grad_gain_one, grad_gain_two], axis=1), ((0, 0), (0, HD - 2)))
    whole = jnp.concatenate([from_qkv, from_out, from_gains], axis=1).astype(bf16)
    whole = after(whole, total)
    whole = jnp.take(whole.reshape(nf, D // nf, -1), relative_order("fsdp"), axis=0)
    owned = ring_scatter([whole[k] for k in range(nf)], "fsdp").astype(bf16)

    total = ahead(add(row_sum(three, mixed, 3, "seq"), total).astype(bf16), "seq")
    grad_total = ahead(row_sum(one, part_h_one, 1, "seq"), "seq")
    total, grad_total, two, moved = together(
        (), total, grad_total, row_move(part_h_one, 2, "seq"), exchange(head)
    )
    head = head + moved
    mixed = add(row_sum(zero, mixed, 0, "seq"), total).reshape(tokens, D)
    layer_output = (middle + mixed).astype(bf16).reshape(micro, rows, D)

    grad_total = add(row_sum(two, part_h_one, 2, "seq"), grad_total).astype(bf16)
    grad_total, three, moved, owned = together(
        (grad_down,),
        ahead(grad_total, "seq"),
        row_move(part_h_one, 3, "seq"),
        exchange(head),
        owned,
    )
    head = head + moved
    owned = lax.all_to_all(
        owned.reshape(ns, share, -1), "seq", split_axis=0, concat_axis=0, tiled=True
    )

    grad_total = add(row_sum(three, part_h_one, 3, "seq"), grad_total).astype(bf16)
    grad_total, zero, moved, owned = together(
        (grad_gate,),
        ahead(grad_total, "seq"),
        row_move(part_h_one, 0, "seq"),
        exchange(head),
        owned,
    )
    head = head + moved
    while left:
        head = head + exchange(head)
    grad_head_gains = head
    grad_h_one = add(row_sum(zero, part_h_one, 0, "seq"), grad_total).reshape(tokens, D)
    inv_one = rms_scale(x_rows)
    normed_one = x_rows * inv_one
    grad_unit = grad_h_one * gain_one
    input_grad = grad_middle + inv_one * (
        grad_unit - normed_one * jnp.mean(grad_unit * normed_one, axis=-1, keepdims=True)
    )
    input_grad = input_grad.reshape(micro, rows, D)
    owned = owned.astype(f32)
    of_qkv = owned[..., : 3 * width].reshape(ns, share, heads_local, 3, HD)
    grad_query, grad_key, grad_value = (
        jnp.moveaxis(of_qkv[..., k, :], 0, 1).reshape(share, D) for k in range(3)
    )
    grad_output = jnp.moveaxis(owned[..., 3 * width : 4 * width], 0, 1).reshape(share, D)
    of_gains = jnp.sum(owned[..., 4 * width : 4 * width + 2], axis=0)
    return (
        layer_output,
        input_grad,
        of_gains[:, 0],
        of_gains[:, 1],
        grad_query,
        grad_key,
        grad_value,
        grad_output,
        grad_head_gains,
        grad_gate,
        grad_up,
        grad_down,
    )


def solution(mesh):
    placed = (
        P(None, ("fsdp", "seq"), None),
        P(None, ("fsdp", "seq"), None),
        P(None, "fsdp"),
        P(None, ("fsdp", "seq"), None),
        P(None, ("fsdp", "seq"), None),
        P("fsdp"),
        P("fsdp"),
        P("fsdp", None),
        P("fsdp", None),
        P("fsdp", None),
        P("fsdp", None),
        P(),
        P("seq", "fsdp", None),
        P("seq", "fsdp", None),
        P("seq", "fsdp", None),
    )
    return jax.shard_map(
        body,
        mesh=mesh,
        in_specs=placed,
        out_specs=(
            P(None, ("fsdp", "seq"), None),
            P(None, ("fsdp", "seq"), None),
            P(("fsdp", "seq")),
            P(("fsdp", "seq")),
            P(("fsdp", "seq"), None),
            P(("fsdp", "seq"), None),
            P(("fsdp", "seq"), None),
            P(("fsdp", "seq"), None),
            P(),
            P("seq", "fsdp", None),
            P("seq", "fsdp", None),
            P("seq", "fsdp", None),
        ),
        check_vma=False,
    )
```

```python
import math

import jax
import jax.numpy as jnp
from jax import lax
from jax.experimental import pallas as pl
from jax.experimental.pallas import tpu as pltpu
from jax.sharding import PartitionSpec as P

D = 2048
H = 16
HD = 128
FFE = 1024
TOP = 8
SEQ_LEN = 1024

eps = 1e-06
rope_base = 10000.0
masked_score = -1e30
f32 = jnp.float32
little = pl.CostEstimate(flops=1, bytes_accessed=1, transcendentals=0)
bf16 = jnp.bfloat16


def shift(value, axis, outer, inner, by_outer, by_inner):
    pairs = []
    for a in range(outer):
        for b in range(inner):
            there = ((a + by_outer) % outer) * inner + (b + by_inner) % inner
            pairs.append((a * inner + b, there))
    return lax.ppermute(value, axis, pairs)


def sizes(axis):
    count = lax.axis_size(axis)
    return (count // 2, 2) if axis == "fsdp" else (4, count // 4)


def after(value, *others):
    others = [v for v in others if v is not None]
    if not others:
        return value
    anywhere = pl.BlockSpec(memory_space=pl.ANY)
    return pl.pallas_call(
        lambda *refs: None,
        in_specs=[anywhere] * (1 + len(others)),
        out_specs=anywhere,
        out_shape=jax.ShapeDtypeStruct(value.shape, value.dtype),
        input_output_aliases={0: 0},
        cost_estimate=little,
        name="after",
    )(value, *others)


def together(work, *moved):
    moved = list(moved)
    for k in range(len(moved)):
        moved[k] = after(moved[k], *work, *moved[:k], *moved[k + 1 :])
    return moved


def ring_gather(value, axis, work=None, then={}):
    outer, inner = sizes(axis)
    blocks, arrived = [], []
    for a in range(outer):
        row = [value]
        for b in range(1, inner):
            row.append(shift(row[-1], axis, outer, inner, 0, 1))
        moved = row[1:]
        if a + 1 < outer:
            moved.append(shift(value, axis, outer, inner, 1, 0))
        if work is not None:
            moved = together([f(arrived) for f in work[a : a + 1] if f], *moved)
        if a in then:
            then[a](moved)
        blocks += [value] + moved[: inner - 1]
        value, arrived = moved[-1], moved
    return blocks


def row_move(parts, a, axis):
    outer, inner = sizes(axis)
    row = parts[a * inner + 1 % inner]
    for b in range(2, inner):
        row = shift(row, axis, outer, inner, 0, 1)
        row = (row.astype(f32) + parts[a * inner + b].astype(f32)).astype(bf16)
    return shift(row, axis, outer, inner, 0, 1) if inner > 1 else row


def row_sum(moved, parts, a, axis):
    total = moved.astype(f32) + parts[a * sizes(axis)[1]].astype(f32)
    return total.astype(bf16)


def ahead(value, axis):
    return shift(value, axis, *sizes(axis), 1, 0)


def add(one, other):
    return one.astype(f32) + other.astype(f32)


def ring_scatter(parts, axis, work=(), then={}):
    outer, _ = sizes(axis)
    total, arrived = None, []
    for step in range(outer):
        a = (step + 1) % outer
        moved = [row_move(parts, a, axis)]
        if step:
            moved.append(ahead(total, axis))
        moved = together([f(arrived) for f in work[step : step + 1]], *moved)
        if step in then:
            then[step](moved)
        arrived = moved
        total = row_sum(moved[0], parts, a, axis)
        if step:
            total = add(total, moved[1])
        if step and step + 1 < outer:
            total = total.astype(bf16)
    return total


def relative_order(axis):
    outer, inner = sizes(axis)
    me = lax.axis_index(axis)
    a, b = me // inner, me % inner
    k = jnp.arange(outer * inner)
    return ((a - k // inner) % outer) * inner + (b - k % inner) % inner


def reorder(value, order, axis=0):
    value = jnp.moveaxis(value, axis, 0)
    value = value.at[order].get(mode="promise_in_bounds", unique_indices=True)
    return jnp.moveaxis(value, 0, axis)


def rms_scale(values):
    return lax.rsqrt(jnp.mean(values * values, axis=-1, keepdims=True) + eps)


def exchanges():
    steps = []
    for axis in ("fsdp", "seq"):
        count = lax.axis_size(axis)
        for k in range(count.bit_length() - 1):
            steps.append((axis, [(i, i ^ (1 << k)) for i in range(count)]))
    return steps


def turn(values, cosine, sine):
    return values * cosine + pltpu.roll(values, HD // 2, 1) * sine


def turn_back(values, cosine, sine):
    return values * cosine - pltpu.roll(values, HD // 2, 1) * sine


def dot(left, right, left_dim, right_dim):
    return lax.dot_general(
        left, right, (((left_dim,), (right_dim,)), ((), ())), preferred_element_type=f32
    )


def attend_kernel(tile, qkv_ref, cos_ref, sin_ref, seg_row_ref, seg_col_ref, gain_ref, o_ref):
    blocks, _, rows, _ = qkv_ref.shape
    group = blocks * rows
    cosine, sine = cos_ref[...], sin_ref[...]

    def turned(part, row):
        raw = qkv_ref[:, 0, :, part * HD : (part + 1) * HD].reshape(group, HD).astype(f32)
        return turn(raw * rms_scale(raw) * gain_ref[row : row + 1, :], cosine, sine).astype(bf16)

    queries, keys = turned(0, 0), turned(1, 1)
    values = qkv_ref[:, 0, :, 2 * HD : 3 * HD].reshape(group, HD)
    seg_row = seg_row_ref[0]
    for start in range(0, group, tile):
        scores = dot(queries[start : start + tile], keys, 1, 1) * (1.0 / math.sqrt(HD))
        allowed = seg_col_ref[0, start : start + tile, :] == seg_row
        scores = jnp.where(allowed, scores, masked_score)
        powered = jnp.exp(scores - jnp.max(scores, axis=-1, keepdims=True))
        scale = 1.0 / jnp.sum(powered, axis=-1, keepdims=True)
        attended = dot((powered * scale).astype(bf16), values, 1, 0).astype(bf16)
        o_ref[start // rows : (start + tile) // rows, 0, :, :] = attended.reshape(
            tile // rows, rows, HD
        )


def attend_back_kernel(
    tile,
    qkv_ref,
    do_ref,
    cos_ref,
    sin_ref,
    seg_row_ref,
    seg_col_ref,
    gain_ref,
    grad_ref,
    grad_gain_ref,
):
    blocks, _, rows, _ = qkv_ref.shape
    group = blocks * rows
    cosine, sine = cos_ref[...], sin_ref[...]
    scaling = 1.0 / math.sqrt(HD)

    def normed(part):
        raw = qkv_ref[:, 0, :, part * HD : (part + 1) * HD].reshape(group, HD).astype(f32)
        inverse = rms_scale(raw)
        return raw * inverse, inverse

    def turned(part):
        return turn(normed(part)[0] * gain_ref[part : part + 1, :], cosine, sine).astype(bf16)

    def finish(part, grad_turned):
        unit, inverse = normed(part)
        grad_scaled = turn_back(grad_turned, cosine, sine)
        grad_gain_ref[0, part : part + 1, :] = jnp.sum(grad_scaled * unit, axis=0, keepdims=True)
        grad_unit = grad_scaled * gain_ref[part : part + 1, :]
        grad_raw = inverse * (
            grad_unit - unit * jnp.mean(grad_unit * unit, axis=-1, keepdims=True)
        )
        return grad_raw

    def put(part, value):
        grad_ref[:, 0, :, part * HD : (part + 1) * HD] = value.astype(bf16).reshape(
            blocks, rows, HD
        )

    queries, keys = turned(0), turned(1)
    values = qkv_ref[:, 0, :, 2 * HD : 3 * HD].reshape(group, HD)
    grad_out = do_ref[:, 0, :, :].reshape(group, HD)
    seg_row = seg_row_ref[0]
    grad_query = []
    grad_key = jnp.zeros((group, HD), f32)
    grad_value = jnp.zeros((group, HD), f32)
    for start in range(0, group, tile):
        part = queries[start : start + tile]
        grad_part = grad_out[start : start + tile]
        scores = dot(part, keys, 1, 1) * scaling
        allowed = seg_col_ref[0, start : start + tile, :] == seg_row
        scores = jnp.where(allowed, scores, masked_score)
        powered = jnp.exp(scores - jnp.max(scores, axis=-1, keepdims=True))
        probabilities = powered * (1.0 / jnp.sum(powered, axis=-1, keepdims=True))
        grad_probs = dot(grad_part, values, 1, 1)
        centre = jnp.sum(probabilities * grad_probs, axis=-1, keepdims=True)
        grad_scores = (probabilities * (grad_probs - centre)).astype(bf16)
        grad_query.append(dot(grad_scores, keys, 1, 0) * scaling)
        grad_key = grad_key + dot(grad_scores, part, 0, 0)
        grad_value = grad_value + dot(probabilities.astype(bf16), grad_part, 0, 0)
    put(0, finish(0, jnp.concatenate(grad_query, axis=0)))
    put(1, finish(1, grad_key * scaling))
    put(2, grad_value)


def attention_specs(ns, micro, rows, heads):
    group = ns * rows
    tile = max(rows, 256)
    return (
        tile,
        pl.BlockSpec((ns, 1, rows, 3 * HD), lambda m, h: (0, m, 0, h)),
        pl.BlockSpec((ns, 1, rows, HD), lambda m, h: (0, m, 0, h)),
        [
            pl.BlockSpec((group, HD), lambda m, h: (0, 0)),
            pl.BlockSpec((group, HD), lambda m, h: (0, 0)),
            pl.BlockSpec((1, 1, group), lambda m, h: (m, 0, 0)),
            pl.BlockSpec((1, group, 1), lambda m, h: (m, 0, 0)),
            pl.BlockSpec((2, HD), lambda m, h: (0, 0)),
        ],
    )


def attend(qkv, tables):
    ns, micro, rows, width = qkv.shape
    heads = width // (3 * HD)
    tile, wide, narrow, shared = attention_specs(ns, micro, rows, heads)
    group = ns * rows
    return pl.pallas_call(
        lambda *refs: attend_kernel(tile, *refs),
        grid=(micro, heads),
        in_specs=[wide] + shared,
        out_specs=narrow,
        out_shape=jax.ShapeDtypeStruct((ns, micro, rows, heads * HD), bf16),
        compiler_params=pltpu.CompilerParams(vmem_limit_bytes=40 * 2**20),
        cost_estimate=little,
        name="attend",
    )(qkv, *tables)


def attend_back(qkv, grad_out, tables, ties=()):
    ns, micro, rows, width = qkv.shape
    heads = width // (3 * HD)
    tile, wide, narrow, shared = attention_specs(ns, micro, rows, heads)
    group = ns * rows
    return pl.pallas_call(
        lambda *refs: attend_back_kernel(tile, *refs[:7], *refs[-2:]),
        grid=(micro, heads),
        in_specs=[wide, narrow] + shared + [pl.BlockSpec(memory_space=pl.ANY)] * len(ties),
        out_specs=[wide, pl.BlockSpec((1, 2, HD), lambda m, h: (m * heads + h, 0, 0))],
        out_shape=[
            jax.ShapeDtypeStruct((ns, micro, rows, width), bf16),
            jax.ShapeDtypeStruct((micro * heads, 2, HD), f32),
        ],
        compiler_params=pltpu.CompilerParams(vmem_limit_bytes=40 * 2**20),
        cost_estimate=little,
        name="attend_back",
    )(qkv, grad_out, *tables, *ties)


def part_kernel(grad_ref, w_ref, x_ref, inv_ref, *out_refs):
    out_refs, gain_ref = out_refs[:-1], out_refs[-1]
    rows = out_refs[0].shape[0]
    gain = jnp.zeros(gain_ref.shape, f32)
    for b, ref in enumerate(out_refs):
        span = slice(b * rows, (b + 1) * rows)
        wide = dot(grad_ref[span, :], w_ref[...], 1, 1)
        ref[...] = wide.astype(bf16)
        normed = x_ref[span, :].astype(f32) * inv_ref[span, :]
        gain = gain + jnp.sum(wide * normed, axis=0, keepdims=True)
    gain_ref[...] = gain


def part_grads(grad_qkv, w_qkv, x_all, inv_all, ties=()):
    blocks = grad_qkv.shape[0]
    width = grad_qkv.shape[-1]
    count = grad_qkv.size // width
    block = jax.ShapeDtypeStruct((count // blocks, D), bf16)
    found = call(
        part_kernel,
        "part_grads",
        (D // part,),
        [
            (grad_qkv.reshape(count, width), whole_of((count, width))),
            (w_qkv, pl.BlockSpec((part, width), lambda d: (d, 0))),
            (x_all.reshape(count, x_all.shape[-1]), pl.BlockSpec((count, part), lambda d: (0, d))),
            (inv_all.reshape(count, 1), whole_of((count, 1))),
        ],
        [(block, pl.BlockSpec((block.shape[0], part), lambda d: (0, d)))] * blocks
        + [(jax.ShapeDtypeStruct((1, D), f32), pl.BlockSpec((1, part), lambda d: (0, d)))],
        2 * count * width * D,
        ties=ties,
    )
    return found[:-1], found[-1][0]


part = 512


def spans(shape, *block):
    block = block or (1,)
    return pl.BlockSpec(
        tuple(block) + tuple(shape[len(block) :]), lambda e, *_: (e,) + (0,) * (len(shape) - 1)
    )


def whole_of(shape):
    return pl.BlockSpec(
        tuple(shape), lambda *_: (0,) * len(shape), pipeline_mode=pl.Buffered(buffer_count=1)
    )


def call(kernel, name, grid, ins, outs, flops, scratch=(), ties=(), aliases={}):
    ties = [t for t in ties if t is not None]
    count = len(ins)

    def run(*refs):
        kernel(*refs[:count], *refs[count + len(ties) :])

    return pl.pallas_call(
        run,
        grid=grid,
        in_specs=[spec for _, spec in ins] + [pl.BlockSpec(memory_space=pl.ANY)] * len(ties),
        out_specs=[spec for _, spec in outs],
        out_shape=[shape for shape, _ in outs],
        scratch_shapes=list(scratch),
        input_output_aliases=aliases,
        compiler_params=pltpu.CompilerParams(vmem_limit_bytes=56 * 2**20),
        cost_estimate=little,
        name=name,
    )(*[value for value, _ in ins], *ties)


def picked(slot_row, capacity):
    place = lax.broadcasted_iota(jnp.int32, (capacity, slot_row.shape[1]), 0)
    return place == slot_row


def slot_weights(slot_row, weight_row, capacity):
    chosen = jnp.where(picked(slot_row, capacity), weight_row, 0.0)
    return jnp.sum(chosen, axis=1, keepdims=True)


def dispatch_kernel(scaled, blocks, *refs):
    value_refs, (slot_ref, weight_ref, w_ref, rows_ref, act_ref) = refs[:blocks], refs[blocks:]
    capacity, each = rows_ref.shape[2], blocks // 2
    for h in range(2):
        slot_row = slot_ref[0, h : h + 1, :]
        pick = picked(slot_row, capacity).astype(f32).astype(bf16)
        if scaled:
            scale = slot_weights(slot_row, weight_ref[0, h : h + 1, :], capacity)
        for d in range(0, D, part):
            values = jnp.concatenate(
                [ref[:, d : d + part] for ref in value_refs[h * each : (h + 1) * each]], axis=0
            )
            taken = dot(pick, values, 1, 0)
            if scaled:
                taken = taken * scale
            rows_ref[0, h, :, d : d + part] = taken.astype(bf16)
        act_ref[0, h] = dot(rows_ref[0, h], w_ref[0], 1, 0)


def dispatch(
    values, slots, weights, bank, capacity, scaled, ties=(), first=0, count=None, before=()
):
    experts = bank.shape[0]
    count = count or experts
    values = [v.reshape(-1, v.shape[-1]) for v in values]
    rows_shape = (experts, 2, capacity, D)
    act_shape = (experts, 2, capacity, FFE)

    def of(shape):
        return pl.BlockSpec((1,) + shape[1:], lambda e: (first + e,) + (0,) * (len(shape) - 1))

    return call(
        lambda *refs: dispatch_kernel(scaled, len(values), *refs),
        "dispatch",
        (count,),
        [(v, whole_of(v.shape)) for v in values]
        + [(v, of(v.shape)) for v in (slots, weights, bank)],
        [
            (jax.ShapeDtypeStruct(rows_shape, bf16), of(rows_shape)),
            (jax.ShapeDtypeStruct(act_shape, f32), of(act_shape)),
        ],
        4 * count * capacity * D * (FFE + len(values) * values[0].shape[0] // 2),
        ties=tuple(before) + tuple(ties),
        aliases={len(values) + 3 + k: k for k in range(len(before))},
    )


def act_kernel(taken_ref, gate_ref, grad_ref, w_ref, hidden_ref, grad_gate_ref, grad_up_ref):
    up_act = dot(taken_ref[0, 0], w_ref[0], 1, 0)
    gate_act, grad_hidden = gate_ref[0, 0], grad_ref[0, 0]
    gate_sig = jax.nn.sigmoid(gate_act)
    gate_silu = gate_act * gate_sig
    hidden_ref[0, 0] = (gate_silu * up_act).astype(bf16)
    grad_gate = grad_hidden * up_act * gate_sig * (1.0 + gate_act * (1.0 - gate_sig))
    grad_gate_ref[0, 0] = grad_gate.astype(bf16)
    grad_up_ref[0, 0] = (grad_hidden * gate_silu).astype(bf16)


def activate(taken, gate_act, grad_hidden, w_up, ties=()):
    count, _, capacity, _ = taken.shape

    def of(width):
        return pl.BlockSpec((1, 1, capacity, width), lambda e, h: (e, h, 0, 0))

    result = jax.ShapeDtypeStruct(gate_act.shape, bf16)
    return call(
        act_kernel,
        "activate",
        (count, 2),
        [
            (taken, of(D)),
            (gate_act, of(FFE)),
            (grad_hidden, of(FFE)),
            (w_up, spans(w_up.shape)),
        ],
        [(result, of(FFE))] * 3,
        4 * count * capacity * D * FFE,
        ties=ties,
    )


def bank_kernel(left_ref, right_ref, out_ref):
    rows = left_ref.shape[1] * left_ref.shape[2]
    left, right = left_ref[0].reshape(rows, -1), right_ref[0].reshape(rows, -1)
    out_ref[0] = dot(left, right, 0, 0).astype(bf16)


def bank_grad(left, right, ties=()):
    count, _, capacity, _ = left.shape
    result = jax.ShapeDtypeStruct((count, D, FFE), bf16)
    return call(
        bank_kernel,
        "bank_grad",
        (count, D // part),
        [
            (left, pl.BlockSpec((1, 2, capacity, part), lambda e, d: (e, 0, 0, d))),
            (right, pl.BlockSpec((1, 2, capacity, FFE), lambda e, d: (e, 0, 0, 0))),
        ],
        [(result, pl.BlockSpec((1, part, FFE), lambda e, d: (e, d, 0)))],
        4 * count * capacity * D * FFE,
        ties=ties,
    )[0]


def combine_kernel(scaled, acts, blocks, h, *refs):
    act_refs, w_refs = refs[:acts], refs[acts : 2 * acts]
    column_ref, slot_ref, weight_ref = refs[2 * acts : 2 * acts + 3]
    out_refs, total_ref = refs[2 * acts + 3 : -1], refs[-1]
    expert = pl.program_id(0)
    capacity = act_refs[0].shape[2]
    half = total_ref.shape[0]
    place = lax.broadcasted_iota(jnp.int32, (half, capacity), 1)
    pick = (place == column_ref[0, 0]).astype(f32).astype(bf16)
    if scaled:
        scale = slot_weights(slot_ref[0, h : h + 1, :], weight_ref[0, h : h + 1, :], capacity)

    @pl.when(expert == 0)
    def _():
        total_ref[...] = jnp.zeros_like(total_ref)

    for d in range(0, D, part):
        grads = [
            dot(a_ref[0, 0], w_ref[0, d : d + part, :], 1, 1)
            for a_ref, w_ref in zip(act_refs, w_refs)
        ]
        rows = sum(grads[1:], grads[0])
        if scaled:
            rows = rows * scale
        total_ref[:, d : d + part] += dot(pick, rows.astype(bf16), 1, 0)

    @pl.when(expert == pl.num_programs(0) - 1)
    def _():
        n = half // blocks
        for b, ref in enumerate(out_refs):
            ref[...] = total_ref[b * n : (b + 1) * n, :].astype(bf16)


def combine(acts, banks, columns, slots, weights, h, blocks, scaled, ties=()):
    count, _, capacity, _ = acts[0].shape
    half = columns.shape[2]
    result = jax.ShapeDtypeStruct((half // blocks, D), bf16)
    return call(
        lambda *refs: combine_kernel(scaled, len(acts), blocks, h, *refs),
        "combine",
        (count,),
        [(a, pl.BlockSpec((1, 1, capacity, FFE), lambda e: (e, h, 0, 0))) for a in acts]
        + [(w, spans(w.shape)) for w in banks]
        + [(columns, pl.BlockSpec((1, 1, half, 1), lambda e: (e, h, 0, 0)))]
        + [(v, spans(v.shape)) for v in (slots, weights)],
        [(result, whole_of(result.shape))] * blocks,
        2 * count * capacity * D * (FFE * len(acts) + half),
        scratch=[pltpu.VMEM((half, D), f32)],
        ties=ties,
    )


def body(
    layer_input,
    cotangent,
    segments,
    routes,
    route_weights,
    gain_attention,
    gain_experts,
    query_proj,
    key_proj,
    value_proj,
    output_proj,
    head_gains,
    expert_gate,
    expert_up,
    expert_down,
):
    micro, rows, _ = layer_input.shape
    nf, ns = lax.axis_size("fsdp"), lax.axis_size("seq")
    seq_index = lax.axis_index("seq")
    seq_order = relative_order("seq")
    tokens = micro * rows
    group = rows * ns
    half = group * micro // 2
    heads_local = H // ns
    width = heads_local * HD
    local_experts = expert_gate.shape[0]
    experts = local_experts * ns
    capacity = micro * ns // 2 * min(rows, 3 * rows * TOP // (2 * experts))
    share = D // (nf * ns)

    def spread(value, axis):
        return lax.all_gather(value, "fsdp", axis=axis, tiled=True)

    def gather_tokens(value):
        return jnp.stack(ring_gather(value, "seq"))

    columns = [
        lax.dynamic_slice_in_dim(w, seq_index * width, width, axis=1).reshape(-1, heads_local, HD)
        for w in (query_proj, key_proj, value_proj)
    ]
    columns = jnp.stack(columns, axis=2).reshape(-1, 3 * width)
    extra = jnp.pad(jnp.stack([gain_attention, gain_experts], axis=1), ((0, 0), (0, HD - 2)))
    w_first = spread(jnp.concatenate([columns, extra], axis=1), 0)
    w_qkv = w_first[:, : 3 * width]
    gain_one = w_first[:, 3 * width].astype(f32)
    gain_two = w_first[:, 3 * width + 1].astype(f32)
    w_down = spread(expert_down, 1)
    w_output = spread(output_proj, 0)
    w_gate = spread(expert_gate, 1)
    w_up = spread(expert_up, 1)

    weight_high = route_weights.astype(bf16)
    weight_low = (route_weights - weight_high.astype(f32)).astype(bf16)
    packed = jnp.concatenate(
        [layer_input, routes.astype(bf16), weight_high, weight_low], axis=-1
    )
    packed = jnp.pad(packed, ((0, 0), (0, 0), (0, HD - 3 * TOP)))
    packed = x_all = gather_tokens(packed)
    x_wide = packed[..., :D].astype(f32)
    inv_all = rms_scale(x_wide)
    h_one = (x_wide * inv_all * gain_one).astype(bf16)
    qkv = jnp.einsum("smtd,de->smte", h_one, w_qkv, preferred_element_type=f32).astype(bf16)

    places = (seq_order[:, None] * rows + jnp.arange(rows)[None, :]).reshape(-1)
    lane = jnp.arange(HD) % (HD // 2)
    frequency = jnp.exp(-jnp.log(rope_base) * (2.0 * lane.astype(f32) / HD))
    angles = places.astype(f32)[:, None] * frequency[None, :]
    sign = jnp.where(jnp.arange(HD) < HD // 2, -1.0, 1.0)
    segment = reorder(segments.reshape(micro, ns, rows), seq_order, axis=1).reshape(micro, group)
    tables = (
        jnp.cos(angles),
        jnp.sin(angles) * sign,
        segment[:, None, :],
        segment[:, :, None],
        head_gains.astype(f32),
    )
    o_heads = attend(qkv, tables)

    inverse_seq = jnp.argsort(seq_order)
    o_heads = reorder(o_heads, inverse_seq, axis=0)
    o_back = lax.all_to_all(o_heads, "seq", split_axis=0, concat_axis=0, tiled=True)
    o_rows = jnp.moveaxis(o_back, 0, 2).reshape(tokens, D)

    x_rows = layer_input.astype(f32).reshape(tokens, D)
    middle = x_rows + jnp.dot(o_rows, w_output, preferred_element_type=f32)
    inv_two = rms_scale(middle)
    normed_two = middle * inv_two
    h_two_own = (normed_two * gain_two).astype(bf16).reshape(micro, rows, D)
    h_blocks = ring_gather(h_two_own, "seq", ())

    packed = packed[..., D : D + 3 * TOP].astype(f32)
    packed = packed.reshape(2, half, 3 * TOP)
    route_all = packed[..., :TOP].astype(jnp.int32)
    weight_all = packed[..., TOP : 2 * TOP] + packed[..., 2 * TOP :]
    mine = seq_index * local_experts + jnp.arange(local_experts)
    hit = route_all[:, :, None, :] == mine[None, None, :, None]
    chosen = jnp.any(hit, axis=-1)
    weight_of = jnp.sum(jnp.where(hit, weight_all[:, :, None, :], 0.0), axis=-1)
    block = 128
    counted = chosen.reshape(2, half // block, block, local_experts).astype(f32)
    below = jnp.tril(jnp.ones((block, block), f32), -1)
    inside = jnp.einsum("ab,mkbe->mkae", below, counted)
    sums = jnp.sum(counted, axis=2)
    before = jnp.cumsum(sums, axis=1) - sums
    slot = (inside + before[:, :, None, :]).reshape(2, half, local_experts).astype(jnp.int32)
    slots = jnp.transpose(jnp.where(chosen, slot, -1), (2, 0, 1))
    weights = jnp.transpose(weight_of, (2, 0, 1))
    slot_columns = slots[..., None]

    grad_top = cotangent.astype(f32).reshape(tokens, D)
    done = {}

    def keep(**found):
        done.update(found)
        return next(iter(found.values()))

    def combined(acts, banks, h, scaled, ties=()):
        return combine(acts, banks, slot_columns, slots, weights, h, ns // 2, scaled, ties)

    pair = local_experts // 2

    def take_work(first):
        def work(ties):
            before = done.get("takes", ())
            done["takes"] = dispatch(
                h_blocks, slots, weights, w_gate, capacity, False, ties, first, pair, before
            )
            return done["takes"][0]

        return work

    g_blocks = ring_gather(
        after(cotangent, h_blocks[-1]), "seq", (None, take_work(0), take_work(pair))
    )
    taken, gate_act = done["takes"]

    def grad_work(_):
        grad_rows, grad_hidden = dispatch(g_blocks, slots, weights, w_down, capacity, True)
        return keep(grad_rows=grad_rows, grad_hidden=grad_hidden)

    def act_work(ties):
        acts = activate(taken, gate_act, done["grad_hidden"], w_up, ties)
        return keep(tail=acts[0], acts=acts)

    def first_work(ties):
        first = combined(done["acts"][1:], (w_gate, w_up), 0, False, ties)
        return keep(tail=first[0], first=first)

    o_all = ring_gather(
        after(o_heads.reshape(group * micro, width), g_blocks[-1]),
        "seq",
        (grad_work, act_work, first_work),
    )
    o_last = o_all[-1]
    o_all = jnp.concatenate(o_all, axis=1)
    first = done["first"]
    grad_rows = done["grad_rows"]
    hidden, grad_gate_act, grad_up_act = done["acts"]
    second = combined((grad_gate_act, grad_up_act), (w_gate, w_up), 1, False, (first[0],))

    def down_work(ties):
        return keep(whole_down=bank_grad(grad_rows, hidden, tuple(ties) + (o_last,)))

    def mixed_work(h):
        def work(ties):
            mixed = combined((hidden,), (w_down,), h, True, ties)
            done.setdefault("mixed", []).extend(mixed)
            return mixed[0]

        return work

    parts = [v.reshape(micro, rows, D) for v in list(first) + list(second)]
    grad_h_two = ring_scatter(
        parts,
        "seq",
        (lambda _: second[0], down_work, mixed_work(0), mixed_work(1)),
        {
            1: lambda moved: keep(sum_down=after(done["whole_down"], *moved)),
            3: lambda moved: keep(last=moved),
        },
    ).reshape(tokens, D)

    def bank_sum(whole):
        return lax.psum_scatter(whole, "fsdp", scatter_dimension=1, tiled=True).astype(f32)

    grad_down = bank_sum(done["sum_down"])

    grad_gain_two = jnp.sum(grad_h_two * normed_two, axis=0)
    grad_unit = grad_h_two * gain_two
    grad_middle = grad_top + inv_two * (
        grad_unit - normed_two * jnp.mean(grad_unit * normed_two, axis=-1, keepdims=True)
    )
    grad_attn = grad_middle.astype(bf16)
    grad_o = jnp.einsum("te,de->td", grad_attn, w_output, preferred_element_type=f32).astype(bf16)

    def to_heads(value):
        cut = value.reshape(micro, rows, ns, width)
        return lax.all_to_all(
            jnp.moveaxis(cut, 2, 0), "seq", split_axis=0, concat_axis=0, tiled=True
        )

    whole_gate = bank_grad(taken, grad_gate_act, (grad_o,))
    (do_blocks,) = together((whole_gate,), to_heads(grad_o))
    grad_gate = bank_sum(after(whole_gate, do_blocks))
    do_heads = reorder(do_blocks, seq_order)

    mixed = [v.reshape(micro, rows, D) for v in done["mixed"]]
    k = sizes("seq")[1] + 1 % sizes("seq")[1]
    mixed[k] = after(mixed[k], do_blocks)
    grad_qkv, grad_head = attend_back(qkv, do_heads, tables)
    part_h_one, grad_gain_one = part_grads(grad_qkv, w_qkv, x_all, inv_all)
    one, columns = together(
        (grad_gain_one,), row_move(mixed, 1, "seq"), to_heads(after(grad_attn, do_blocks))
    )

    total = one
    part_h_one = [v.reshape(micro, rows, D) for v in part_h_one]
    part_h_one[k] = after(part_h_one[k], total)
    from_qkv = jnp.einsum(
        "smtd,smte->de", after(h_one, total), grad_qkv, preferred_element_type=f32
    )
    from_out = jnp.einsum(
        "td,te->de",
        after(o_all, total),
        columns.reshape(micro * group, width),
        preferred_element_type=f32,
    )
    left = exchanges()
    head = jnp.sum(after(grad_head, total), axis=0)

    def exchange(head):
        axis, pairs = left.pop(0)
        return lax.ppermute(head, axis, pairs)

    total = ahead(row_sum(total, mixed, 1, "seq"), "seq")
    head = head + exchange(head)
    total, two, one, moved = together(
        (from_qkv, from_out),
        total,
        row_move(mixed, 2, "seq"),
        row_move(part_h_one, 1, "seq"),
        exchange(head),
    )
    head = head + moved

    from_out = reorder(from_out.reshape(ns, width, width), inverse_seq, axis=0).reshape(D, width)
    from_gains = jnp.pad(jnp.stack([grad_gain_one, grad_gain_two], axis=1), ((0, 0), (0, HD - 2)))
    whole = jnp.concatenate([from_qkv, from_out, from_gains], axis=1).astype(bf16)
    whole = after(whole, total)
    whole = reorder(whole.reshape(nf, D // nf, -1), relative_order("fsdp"), axis=0)
    owned = ring_scatter([whole[k] for k in range(nf)], "fsdp").astype(bf16)

    whole_up = bank_grad(taken, grad_up_act, (one,))
    total = ahead(add(row_sum(two, mixed, 2, "seq"), total).astype(bf16), "seq")
    grad_total = ahead(row_sum(one, part_h_one, 1, "seq"), "seq")
    total, grad_total, three, two, owned = together(
        (whole_up,),
        total,
        grad_total,
        row_move(mixed, 3, "seq"),
        row_move(part_h_one, 2, "seq"),
        owned,
    )
    grad_up = bank_sum(after(whole_up, owned))
    owned = lax.all_to_all(
        owned.reshape(ns, share, -1), "seq", split_axis=0, concat_axis=0, tiled=True
    )

    total = ahead(add(row_sum(three, mixed, 3, "seq"), total).astype(bf16), "seq")
    grad_total = add(row_sum(two, part_h_one, 2, "seq"), grad_total).astype(bf16)
    total, grad_total, three, moved, owned = together(
        (grad_down,),
        total,
        ahead(grad_total, "seq"),
        row_move(part_h_one, 3, "seq"),
        exchange(head),
        owned,
    )
    head = head + moved

    grad_total = add(row_sum(three, part_h_one, 3, "seq"), grad_total).astype(bf16)
    grad_total, zero, moved, last = together(
        (grad_gate,),
        ahead(grad_total, "seq"),
        row_move(part_h_one, 0, "seq"),
        exchange(head),
        row_move(mixed, 0, "seq"),
    )
    head = head + moved
    mixed = add(row_sum(last, mixed, 0, "seq"), total).reshape(tokens, D)
    layer_output = (middle + mixed).astype(bf16).reshape(micro, rows, D)
    while left:
        head = head + exchange(head)
    grad_head_gains = head
    grad_h_one = add(row_sum(zero, part_h_one, 0, "seq"), grad_total).reshape(tokens, D)
    inv_one = rms_scale(x_rows)
    normed_one = x_rows * inv_one
    grad_unit = grad_h_one * gain_one
    input_grad = grad_middle + inv_one * (
        grad_unit - normed_one * jnp.mean(grad_unit * normed_one, axis=-1, keepdims=True)
    )
    input_grad = input_grad.reshape(micro, rows, D)
    owned = owned.astype(f32)
    of_qkv = owned[..., : 3 * width].reshape(ns, share, heads_local, 3, HD)
    grad_query, grad_key, grad_value = (
        jnp.moveaxis(of_qkv[..., k, :], 0, 1).reshape(share, D) for k in range(3)
    )
    grad_output = jnp.moveaxis(owned[..., 3 * width : 4 * width], 0, 1).reshape(share, D)
    of_gains = jnp.sum(owned[..., 4 * width : 4 * width + 2], axis=0)
    return (
        layer_output,
        input_grad,
        of_gains[:, 0],
        of_gains[:, 1],
        grad_query,
        grad_key,
        grad_value,
        grad_output,
        grad_head_gains,
        grad_gate,
        grad_up,
        grad_down,
    )


def solution(mesh):
    placed = (
        P(None, ("fsdp", "seq"), None),
        P(None, ("fsdp", "seq"), None),
        P(None, "fsdp"),
        P(None, ("fsdp", "seq"), None),
        P(None, ("fsdp", "seq"), None),
        P("fsdp"),
        P("fsdp"),
        P("fsdp", None),
        P("fsdp", None),
        P("fsdp", None),
        P("fsdp", None),
        P(),
        P("seq", "fsdp", None),
        P("seq", "fsdp", None),
        P("seq", "fsdp", None),
    )
    return jax.shard_map(
        body,
        mesh=mesh,
        in_specs=placed,
        out_specs=(
            P(None, ("fsdp", "seq"), None),
            P(None, ("fsdp", "seq"), None),
            P(("fsdp", "seq")),
            P(("fsdp", "seq")),
            P(("fsdp", "seq"), None),
            P(("fsdp", "seq"), None),
            P(("fsdp", "seq"), None),
            P(("fsdp", "seq"), None),
            P(),
            P("seq", "fsdp", None),
            P("seq", "fsdp", None),
            P("seq", "fsdp", None),
        ),
        check_vma=False,
    )
```

```python
import math

import jax
import jax.numpy as jnp
from jax import lax
from jax.experimental import pallas as pl
from jax.experimental.pallas import tpu as pltpu
from jax.sharding import PartitionSpec as P

D = 2048
H = 16
HD = 128
FFE = 1024
TOP = 8
SEQ_LEN = 1024

eps = 1e-06
rope_base = 10000.0
masked_score = -1e30
f32 = jnp.float32
little = pl.CostEstimate(flops=1, bytes_accessed=1, transcendentals=0)
bf16 = jnp.bfloat16


def shift(value, axis, outer, inner, by_outer, by_inner):
    pairs = []
    for a in range(outer):
        for b in range(inner):
            there = ((a + by_outer) % outer) * inner + (b + by_inner) % inner
            pairs.append((a * inner + b, there))
    return lax.ppermute(value, axis, pairs)


def sizes(axis):
    count = lax.axis_size(axis)
    return (count // 2, 2) if axis == "fsdp" else (4, count // 4)


def after(value, *others):
    others = [v for v in others if v is not None]
    if not others:
        return value
    anywhere = pl.BlockSpec(memory_space=pl.ANY)
    return pl.pallas_call(
        lambda *refs: None,
        in_specs=[anywhere] * (1 + len(others)),
        out_specs=anywhere,
        out_shape=jax.ShapeDtypeStruct(value.shape, value.dtype),
        input_output_aliases={0: 0},
        cost_estimate=little,
        name="after",
    )(value, *others)


def together(work, *moved):
    moved = list(moved)
    for k in range(len(moved)):
        moved[k] = after(moved[k], *work, *moved[:k], *moved[k + 1 :])
    return moved


def ring_gather(value, axis, work=None, then={}, tie_last=True):
    outer, inner = sizes(axis)
    blocks, arrived = [], []
    for a in range(outer):
        row = [value]
        for b in range(1, inner):
            row.append(shift(row[-1], axis, outer, inner, 0, 1))
        moved = row[1:]
        if a + 1 < outer:
            moved.append(shift(value, axis, outer, inner, 1, 0))
        if work is not None and (tie_last or a + 1 < outer):
            moved = together([f(arrived) for f in work[a : a + 1] if f], *moved)
        if a in then:
            then[a](moved)
        blocks += [value] + moved[: inner - 1]
        value, arrived = moved[-1], moved
    return blocks


def row_move(parts, a, axis):
    outer, inner = sizes(axis)
    row = parts[a * inner + 1 % inner]
    for b in range(2, inner):
        row = shift(row, axis, outer, inner, 0, 1)
        row = (row.astype(f32) + parts[a * inner + b].astype(f32)).astype(bf16)
    return shift(row, axis, outer, inner, 0, 1) if inner > 1 else row


def row_sum(moved, parts, a, axis):
    total = moved.astype(f32) + parts[a * sizes(axis)[1]].astype(f32)
    return total.astype(bf16)


def ahead(value, axis):
    return shift(value, axis, *sizes(axis), 1, 0)


def add(one, other):
    return one.astype(f32) + other.astype(f32)


def ring_scatter(parts, axis, work=(), then={}):
    outer, _ = sizes(axis)
    total, arrived = None, []
    for step in range(outer):
        a = (step + 1) % outer
        moved = [row_move(parts, a, axis)]
        if step:
            moved.append(ahead(total, axis))
        moved = together([f(arrived) for f in work[step : step + 1] if f], *moved)
        if step in then:
            then[step](moved)
        arrived = moved
        total = row_sum(moved[0], parts, a, axis)
        if step:
            total = add(total, moved[1])
        if step and step + 1 < outer:
            total = total.astype(bf16)
    return total


def relative_order(axis):
    outer, inner = sizes(axis)
    me = lax.axis_index(axis)
    a, b = me // inner, me % inner
    k = jnp.arange(outer * inner)
    return ((a - k // inner) % outer) * inner + (b - k % inner) % inner


def reorder(value, order, axis=0):
    value = jnp.moveaxis(value, axis, 0)
    value = value.at[order].get(mode="promise_in_bounds", unique_indices=True)
    return jnp.moveaxis(value, 0, axis)


def rms_scale(values):
    return lax.rsqrt(jnp.mean(values * values, axis=-1, keepdims=True) + eps)


def exchanges():
    steps = []
    for axis in ("fsdp", "seq"):
        count = lax.axis_size(axis)
        for k in range(count.bit_length() - 1):
            steps.append((axis, [(i, i ^ (1 << k)) for i in range(count)]))
    return steps


def turn(values, cosine, sine):
    return values * cosine + pltpu.roll(values, HD // 2, 1) * sine


def turn_back(values, cosine, sine):
    return values * cosine - pltpu.roll(values, HD // 2, 1) * sine


def dot(left, right, left_dim, right_dim):
    return lax.dot_general(
        left, right, (((left_dim,), (right_dim,)), ((), ())), preferred_element_type=f32
    )


def attend_kernel(tile, qkv_ref, cos_ref, sin_ref, seg_row_ref, seg_col_ref, gain_ref, o_ref):
    blocks, _, rows, _ = qkv_ref.shape
    group = blocks * rows
    cosine, sine = cos_ref[...], sin_ref[...]

    def turned(part, row):
        raw = qkv_ref[:, 0, :, part * HD : (part + 1) * HD].reshape(group, HD).astype(f32)
        return turn(raw * rms_scale(raw) * gain_ref[row : row + 1, :], cosine, sine).astype(bf16)

    queries, keys = turned(0, 0), turned(1, 1)
    values = qkv_ref[:, 0, :, 2 * HD : 3 * HD].reshape(group, HD)
    seg_row = seg_row_ref[0]
    for start in range(0, group, tile):
        scores = dot(queries[start : start + tile], keys, 1, 1) * (1.0 / math.sqrt(HD))
        allowed = seg_col_ref[0, start : start + tile, :] == seg_row
        scores = jnp.where(allowed, scores, masked_score)
        powered = jnp.exp(scores - jnp.max(scores, axis=-1, keepdims=True))
        scale = 1.0 / jnp.sum(powered, axis=-1, keepdims=True)
        attended = dot((powered * scale).astype(bf16), values, 1, 0).astype(bf16)
        o_ref[start // rows : (start + tile) // rows, 0, :, :] = attended.reshape(
            tile // rows, rows, HD
        )


def attend_back_kernel(
    tile,
    qkv_ref,
    do_ref,
    cos_ref,
    sin_ref,
    seg_row_ref,
    seg_col_ref,
    gain_ref,
    grad_ref,
    grad_gain_ref,
):
    blocks, _, rows, _ = qkv_ref.shape
    group = blocks * rows
    cosine, sine = cos_ref[...], sin_ref[...]
    scaling = 1.0 / math.sqrt(HD)

    def normed(part):
        raw = qkv_ref[:, 0, :, part * HD : (part + 1) * HD].reshape(group, HD).astype(f32)
        inverse = rms_scale(raw)
        return raw * inverse, inverse

    def turned(part):
        return turn(normed(part)[0] * gain_ref[part : part + 1, :], cosine, sine).astype(bf16)

    def finish(part, grad_turned):
        unit, inverse = normed(part)
        grad_scaled = turn_back(grad_turned, cosine, sine)
        grad_gain_ref[0, part : part + 1, :] = jnp.sum(grad_scaled * unit, axis=0, keepdims=True)
        grad_unit = grad_scaled * gain_ref[part : part + 1, :]
        grad_raw = inverse * (
            grad_unit - unit * jnp.mean(grad_unit * unit, axis=-1, keepdims=True)
        )
        return grad_raw

    def put(part, value):
        grad_ref[:, 0, :, part * HD : (part + 1) * HD] = value.astype(bf16).reshape(
            blocks, rows, HD
        )

    queries, keys = turned(0), turned(1)
    values = qkv_ref[:, 0, :, 2 * HD : 3 * HD].reshape(group, HD)
    grad_out = do_ref[:, 0, :, :].reshape(group, HD)
    seg_row = seg_row_ref[0]
    grad_query = []
    grad_key = jnp.zeros((group, HD), f32)
    grad_value = jnp.zeros((group, HD), f32)
    for start in range(0, group, tile):
        part = queries[start : start + tile]
        grad_part = grad_out[start : start + tile]
        scores = dot(part, keys, 1, 1) * scaling
        allowed = seg_col_ref[0, start : start + tile, :] == seg_row
        scores = jnp.where(allowed, scores, masked_score)
        powered = jnp.exp(scores - jnp.max(scores, axis=-1, keepdims=True))
        probabilities = powered * (1.0 / jnp.sum(powered, axis=-1, keepdims=True))
        grad_probs = dot(grad_part, values, 1, 1)
        centre = jnp.sum(probabilities * grad_probs, axis=-1, keepdims=True)
        grad_scores = (probabilities * (grad_probs - centre)).astype(bf16)
        grad_query.append(dot(grad_scores, keys, 1, 0) * scaling)
        grad_key = grad_key + dot(grad_scores, part, 0, 0)
        grad_value = grad_value + dot(probabilities.astype(bf16), grad_part, 0, 0)
    put(0, finish(0, jnp.concatenate(grad_query, axis=0)))
    put(1, finish(1, grad_key * scaling))
    put(2, grad_value)


def attention_specs(ns, micro, rows, heads):
    group = ns * rows
    tile = max(rows, 256)
    return (
        tile,
        pl.BlockSpec((ns, 1, rows, 3 * HD), lambda m, h: (0, m, 0, h)),
        pl.BlockSpec((ns, 1, rows, HD), lambda m, h: (0, m, 0, h)),
        [
            pl.BlockSpec((group, HD), lambda m, h: (0, 0)),
            pl.BlockSpec((group, HD), lambda m, h: (0, 0)),
            pl.BlockSpec((1, 1, group), lambda m, h: (m, 0, 0)),
            pl.BlockSpec((1, group, 1), lambda m, h: (m, 0, 0)),
            pl.BlockSpec((2, HD), lambda m, h: (0, 0)),
        ],
    )


def attend(qkv, tables):
    ns, micro, rows, width = qkv.shape
    heads = width // (3 * HD)
    tile, wide, narrow, shared = attention_specs(ns, micro, rows, heads)
    group = ns * rows
    return pl.pallas_call(
        lambda *refs: attend_kernel(tile, *refs),
        grid=(micro, heads),
        in_specs=[wide] + shared,
        out_specs=narrow,
        out_shape=jax.ShapeDtypeStruct((ns, micro, rows, heads * HD), bf16),
        compiler_params=pltpu.CompilerParams(vmem_limit_bytes=40 * 2**20),
        cost_estimate=little,
        name="attend",
    )(qkv, *tables)


def attend_back(qkv, grad_out, tables, ties=()):
    ns, micro, rows, width = qkv.shape
    heads = width // (3 * HD)
    tile, wide, narrow, shared = attention_specs(ns, micro, rows, heads)
    group = ns * rows
    return pl.pallas_call(
        lambda *refs: attend_back_kernel(tile, *refs[:7], *refs[-2:]),
        grid=(micro, heads),
        in_specs=[wide, narrow] + shared + [pl.BlockSpec(memory_space=pl.ANY)] * len(ties),
        out_specs=[wide, pl.BlockSpec((1, 2, HD), lambda m, h: (m * heads + h, 0, 0))],
        out_shape=[
            jax.ShapeDtypeStruct((ns, micro, rows, width), bf16),
            jax.ShapeDtypeStruct((micro * heads, 2, HD), f32),
        ],
        compiler_params=pltpu.CompilerParams(vmem_limit_bytes=40 * 2**20),
        cost_estimate=little,
        name="attend_back",
    )(qkv, grad_out, *tables, *ties)


def part_kernel(grad_ref, w_ref, x_ref, inv_ref, *out_refs):
    out_refs, gain_ref = out_refs[:-1], out_refs[-1]
    rows = out_refs[0].shape[0]
    gain = jnp.zeros(gain_ref.shape, f32)
    for b, ref in enumerate(out_refs):
        span = slice(b * rows, (b + 1) * rows)
        wide = dot(grad_ref[span, :], w_ref[...], 1, 1)
        ref[...] = wide.astype(bf16)
        normed = x_ref[span, :].astype(f32) * inv_ref[span, :]
        gain = gain + jnp.sum(wide * normed, axis=0, keepdims=True)
    gain_ref[...] = gain


def part_grads(grad_qkv, w_first, x_all, inv_all, ties=()):
    blocks = grad_qkv.shape[0]
    width = grad_qkv.shape[-1]
    count = grad_qkv.size // width
    block = jax.ShapeDtypeStruct((count // blocks, D), bf16)
    found = call(
        part_kernel,
        "part_grads",
        (D // part,),
        [
            (grad_qkv.reshape(count, width), whole_of((count, width))),
            (w_first, pl.BlockSpec((part, width), lambda d: (d, 0))),
            (x_all.reshape(count, x_all.shape[-1]), pl.BlockSpec((count, part), lambda d: (0, d))),
            (inv_all.reshape(count, 1), whole_of((count, 1))),
        ],
        [(block, pl.BlockSpec((block.shape[0], part), lambda d: (0, d)))] * blocks
        + [(jax.ShapeDtypeStruct((1, D), f32), pl.BlockSpec((1, part), lambda d: (0, d)))],
        2 * count * width * D,
        ties=ties,
    )
    return found[:-1], found[-1][0]


def proj_kernel(blocks, order_ref, place_ref, h_ref, grad_ref, column_ref, gain_ref, *refs):
    o_refs, out_refs, found_ref = refs[:blocks], refs[blocks:-1], refs[-1]
    k = pl.program_id(0)
    inputs, width = grad_ref.shape[1], column_ref.shape[1]
    owners = found_ref.shape[0] // width
    found_ref[:, :inputs] = dot(h_ref[...], grad_ref[...], 0, 0)
    for j in range(owners):
        place = place_ref[order_ref[k] * owners + j]
        for b in range(blocks):

            @pl.when(place == b)
            def _(b=b, j=j):
                found_ref[j * width : (j + 1) * width, inputs : inputs + width] = dot(
                    o_refs[b][...], column_ref[...], 0, 0
                )

    found_ref[:, inputs + width :] = gain_ref[...]
    for b, ref in enumerate(out_refs):

        @pl.when(k == b)
        def _(ref=ref):
            ref[...] = found_ref[...].astype(bf16)


def proj_grads(h_one, grad_qkv, o_blocks, columns, gains, order, places, ties=()):
    count, inputs = h_one.size // D, grad_qkv.shape[-1]
    width, nf = columns.shape[1], order.shape[0]
    rows, across = D // nf, inputs + width + gains.shape[1]
    result = jax.ShapeDtypeStruct((rows, across), bf16)
    ins = [
        (h_one.reshape(count, D), pl.BlockSpec((count, rows), lambda k, order, _: (0, order[k]))),
        (grad_qkv.reshape(count, inputs), whole_of((count, inputs))),
        (columns, whole_of(columns.shape)),
        (gains, pl.BlockSpec((rows, gains.shape[1]), lambda k, order, _: (order[k], 0))),
    ] + [(v, whole_of(v.shape)) for v in o_blocks]

    def run(*refs):
        lead = 2 + len(ins)
        proj_kernel(len(o_blocks), *refs[:lead], *refs[lead + len(ties) :])

    return pl.pallas_call(
        run,
        grid_spec=pltpu.PrefetchScalarGridSpec(
            num_scalar_prefetch=2,
            grid=(nf,),
            in_specs=[spec for _, spec in ins] + [pl.BlockSpec(memory_space=pl.ANY)] * len(ties),
            out_specs=[whole_of(result.shape)] * nf,
            scratch_shapes=[pltpu.VMEM((rows, across), f32)],
        ),
        out_shape=[result] * nf,
        compiler_params=pltpu.CompilerParams(vmem_limit_bytes=56 * 2**20),
        cost_estimate=little,
        name="proj_grads",
    )(order, places, *[value for value, _ in ins], *ties)


part = 512


def spans(shape, *block):
    block = block or (1,)
    return pl.BlockSpec(
        tuple(block) + tuple(shape[len(block) :]), lambda e, *_: (e,) + (0,) * (len(shape) - 1)
    )


def whole_of(shape):
    return pl.BlockSpec(
        tuple(shape), lambda *_: (0,) * len(shape), pipeline_mode=pl.Buffered(buffer_count=1)
    )


def call(kernel, name, grid, ins, outs, flops, scratch=(), ties=(), aliases={}):
    ties = [t for t in ties if t is not None]
    count = len(ins)

    def run(*refs):
        kernel(*refs[:count], *refs[count + len(ties) :])

    return pl.pallas_call(
        run,
        grid=grid,
        in_specs=[spec for _, spec in ins] + [pl.BlockSpec(memory_space=pl.ANY)] * len(ties),
        out_specs=[spec for _, spec in outs],
        out_shape=[shape for shape, _ in outs],
        scratch_shapes=list(scratch),
        input_output_aliases=aliases,
        compiler_params=pltpu.CompilerParams(vmem_limit_bytes=56 * 2**20),
        cost_estimate=little,
        name=name,
    )(*[value for value, _ in ins], *ties)


def picked(slot_row, capacity):
    place = lax.broadcasted_iota(jnp.int32, (capacity, slot_row.shape[1]), 0)
    return place == slot_row


def slot_weights(slot_row, weight_row, capacity):
    chosen = jnp.where(picked(slot_row, capacity), weight_row, 0.0)
    return jnp.sum(chosen, axis=1, keepdims=True)


def dispatch_kernel(scaled, blocks, *refs):
    value_refs, (slot_ref, weight_ref, w_ref, rows_ref, act_ref) = refs[:blocks], refs[blocks:]
    capacity, each = rows_ref.shape[2], blocks // 2
    for h in range(2):
        slot_row = slot_ref[0, h : h + 1, :]
        pick = picked(slot_row, capacity).astype(f32).astype(bf16)
        if scaled:
            scale = slot_weights(slot_row, weight_ref[0, h : h + 1, :], capacity)
        for d in range(0, D, part):
            values = jnp.concatenate(
                [ref[:, d : d + part] for ref in value_refs[h * each : (h + 1) * each]], axis=0
            )
            taken = dot(pick, values, 1, 0)
            if scaled:
                taken = taken * scale
            rows_ref[0, h, :, d : d + part] = taken.astype(bf16)
        act_ref[0, h] = dot(rows_ref[0, h], w_ref[0], 1, 0)


def dispatch(
    values, slots, weights, bank, capacity, scaled, ties=(), first=0, count=None, before=()
):
    experts = bank.shape[0]
    count = count or experts
    values = [v.reshape(-1, v.shape[-1]) for v in values]
    rows_shape = (experts, 2, capacity, D)
    act_shape = (experts, 2, capacity, FFE)

    def of(shape):
        return pl.BlockSpec((1,) + shape[1:], lambda e: (first + e,) + (0,) * (len(shape) - 1))

    return call(
        lambda *refs: dispatch_kernel(scaled, len(values), *refs),
        "dispatch",
        (count,),
        [(v, whole_of(v.shape)) for v in values]
        + [(v, of(v.shape)) for v in (slots, weights, bank)],
        [
            (jax.ShapeDtypeStruct(rows_shape, bf16), of(rows_shape)),
            (jax.ShapeDtypeStruct(act_shape, f32), of(act_shape)),
        ],
        4 * count * capacity * D * (FFE + len(values) * values[0].shape[0] // 2),
        ties=tuple(before) + tuple(ties),
        aliases={len(values) + 3 + k: k for k in range(len(before))},
    )


def act_kernel(taken_ref, gate_ref, grad_ref, w_ref, hidden_ref, grad_gate_ref, grad_up_ref):
    up_act = dot(taken_ref[0, 0], w_ref[0], 1, 0)
    gate_act, grad_hidden = gate_ref[0, 0], grad_ref[0, 0]
    gate_sig = jax.nn.sigmoid(gate_act)
    gate_silu = gate_act * gate_sig
    hidden_ref[0, 0] = (gate_silu * up_act).astype(bf16)
    grad_gate = grad_hidden * up_act * gate_sig * (1.0 + gate_act * (1.0 - gate_sig))
    grad_gate_ref[0, 0] = grad_gate.astype(bf16)
    grad_up_ref[0, 0] = (grad_hidden * gate_silu).astype(bf16)


def activate(taken, gate_act, grad_hidden, w_up, ties=()):
    count, _, capacity, _ = taken.shape

    def of(width):
        return pl.BlockSpec((1, 1, capacity, width), lambda e, h: (e, h, 0, 0))

    result = jax.ShapeDtypeStruct(gate_act.shape, bf16)
    return call(
        act_kernel,
        "activate",
        (count, 2),
        [
            (taken, of(D)),
            (gate_act, of(FFE)),
            (grad_hidden, of(FFE)),
            (w_up, spans(w_up.shape)),
        ],
        [(result, of(FFE))] * 3,
        4 * count * capacity * D * FFE,
        ties=ties,
    )


def bank_kernel(left_ref, right_ref, out_ref):
    rows = left_ref.shape[1] * left_ref.shape[2]
    left, right = left_ref[0].reshape(rows, -1), right_ref[0].reshape(rows, -1)
    out_ref[0] = dot(left, right, 0, 0).astype(bf16)


def bank_grad(left, right, ties=()):
    count, _, capacity, _ = left.shape
    result = jax.ShapeDtypeStruct((count, D, FFE), bf16)
    return call(
        bank_kernel,
        "bank_grad",
        (count, D // part),
        [
            (left, pl.BlockSpec((1, 2, capacity, part), lambda e, d: (e, 0, 0, d))),
            (right, pl.BlockSpec((1, 2, capacity, FFE), lambda e, d: (e, 0, 0, 0))),
        ],
        [(result, pl.BlockSpec((1, part, FFE), lambda e, d: (e, d, 0)))],
        4 * count * capacity * D * FFE,
        ties=ties,
    )[0]


def combine_kernel(scaled, acts, blocks, h, *refs):
    act_refs, w_refs = refs[:acts], refs[acts : 2 * acts]
    column_ref, slot_ref, weight_ref = refs[2 * acts : 2 * acts + 3]
    out_refs, total_ref = refs[2 * acts + 3 : -1], refs[-1]
    expert = pl.program_id(0)
    capacity = act_refs[0].shape[2]
    half = total_ref.shape[0]
    place = lax.broadcasted_iota(jnp.int32, (half, capacity), 1)
    pick = (place == column_ref[0, 0]).astype(f32).astype(bf16)
    if scaled:
        scale = slot_weights(slot_ref[0, h : h + 1, :], weight_ref[0, h : h + 1, :], capacity)

    @pl.when(expert == 0)
    def _():
        total_ref[...] = jnp.zeros_like(total_ref)

    for d in range(0, D, part):
        grads = [
            dot(a_ref[0, 0], w_ref[0, d : d + part, :], 1, 1)
            for a_ref, w_ref in zip(act_refs, w_refs)
        ]
        rows = sum(grads[1:], grads[0])
        if scaled:
            rows = rows * scale
        total_ref[:, d : d + part] += dot(pick, rows.astype(bf16), 1, 0)

    @pl.when(expert == pl.num_programs(0) - 1)
    def _():
        n = half // blocks
        for b, ref in enumerate(out_refs):
            ref[...] = total_ref[b * n : (b + 1) * n, :].astype(bf16)


def combine(acts, banks, columns, slots, weights, h, blocks, scaled, ties=()):
    count, _, capacity, _ = acts[0].shape
    half = columns.shape[2]
    result = jax.ShapeDtypeStruct((half // blocks, D), bf16)
    return call(
        lambda *refs: combine_kernel(scaled, len(acts), blocks, h, *refs),
        "combine",
        (count,),
        [(a, pl.BlockSpec((1, 1, capacity, FFE), lambda e: (e, h, 0, 0))) for a in acts]
        + [(w, spans(w.shape)) for w in banks]
        + [(columns, pl.BlockSpec((1, 1, half, 1), lambda e: (e, h, 0, 0)))]
        + [(v, spans(v.shape)) for v in (slots, weights)],
        [(result, whole_of(result.shape))] * blocks,
        2 * count * capacity * D * (FFE * len(acts) + half),
        scratch=[pltpu.VMEM((half, D), f32)],
        ties=ties,
    )


def body(
    layer_input,
    cotangent,
    segments,
    routes,
    route_weights,
    gain_attention,
    gain_experts,
    query_proj,
    key_proj,
    value_proj,
    output_proj,
    head_gains,
    expert_gate,
    expert_up,
    expert_down,
):
    micro, rows, _ = layer_input.shape
    nf, ns = lax.axis_size("fsdp"), lax.axis_size("seq")
    seq_index = lax.axis_index("seq")
    seq_order = relative_order("seq")
    tokens = micro * rows
    group = rows * ns
    half = group * micro // 2
    heads_local = H // ns
    width = heads_local * HD
    local_experts = expert_gate.shape[0]
    experts = local_experts * ns
    capacity = micro * ns // 2 * min(rows, 3 * rows * TOP // (2 * experts))
    share = D // (nf * ns)

    def spread(value, axis):
        return lax.all_gather(value, "fsdp", axis=axis, tiled=True)

    def gather_tokens(value):
        return jnp.stack(ring_gather(value, "seq"))

    columns = [
        lax.dynamic_slice_in_dim(w, seq_index * width, width, axis=1).reshape(-1, heads_local, HD)
        for w in (query_proj, key_proj, value_proj)
    ]
    columns = jnp.stack(columns, axis=2).reshape(-1, 3 * width)
    extra = jnp.pad(jnp.stack([gain_attention, gain_experts], axis=1), ((0, 0), (0, HD - 2)))
    w_first = spread(jnp.concatenate([columns, extra], axis=1), 0)
    w_qkv = w_first[:, : 3 * width]
    gain_one = w_first[:, 3 * width].astype(f32)
    gain_two = w_first[:, 3 * width + 1].astype(f32)
    w_down = spread(expert_down, 1)
    w_output = spread(output_proj, 0)
    w_gate = spread(expert_gate, 1)
    w_up = spread(expert_up, 1)

    weight_high = route_weights.astype(bf16)
    weight_low = (route_weights - weight_high.astype(f32)).astype(bf16)
    packed = jnp.concatenate(
        [layer_input, routes.astype(bf16), weight_high, weight_low], axis=-1
    )
    packed = jnp.pad(packed, ((0, 0), (0, 0), (0, HD - 3 * TOP)))
    packed = x_all = gather_tokens(packed)
    x_wide = packed[..., :D].astype(f32)
    inv_all = rms_scale(x_wide)
    h_one = (x_wide * inv_all * gain_one).astype(bf16)
    qkv = jnp.einsum("smtd,de->smte", h_one, w_qkv, preferred_element_type=f32).astype(bf16)

    places = (seq_order[:, None] * rows + jnp.arange(rows)[None, :]).reshape(-1)
    lane = jnp.arange(HD) % (HD // 2)
    frequency = jnp.exp(-jnp.log(rope_base) * (2.0 * lane.astype(f32) / HD))
    angles = places.astype(f32)[:, None] * frequency[None, :]
    sign = jnp.where(jnp.arange(HD) < HD // 2, -1.0, 1.0)
    segment = reorder(segments.reshape(micro, ns, rows), seq_order, axis=1).reshape(micro, group)
    tables = (
        jnp.cos(angles),
        jnp.sin(angles) * sign,
        segment[:, None, :],
        segment[:, :, None],
        head_gains.astype(f32),
    )
    o_heads = attend(qkv, tables)

    inverse_seq = jnp.argsort(seq_order)
    o_heads = reorder(o_heads, inverse_seq, axis=0)
    o_back = lax.all_to_all(o_heads, "seq", split_axis=0, concat_axis=0, tiled=True)
    o_rows = jnp.moveaxis(o_back, 0, 2).reshape(tokens, D)

    x_rows = layer_input.astype(f32).reshape(tokens, D)
    middle = x_rows + jnp.dot(o_rows, w_output, preferred_element_type=f32)
    inv_two = rms_scale(middle)
    normed_two = middle * inv_two
    h_two_own = (normed_two * gain_two).astype(bf16).reshape(micro, rows, D)
    h_blocks = ring_gather(h_two_own, "seq", ())

    packed = packed[..., D : D + 3 * TOP].astype(f32)
    packed = packed.reshape(2, half, 3 * TOP)
    route_all = packed[..., :TOP].astype(jnp.int32)
    weight_all = packed[..., TOP : 2 * TOP] + packed[..., 2 * TOP :]
    mine = seq_index * local_experts + jnp.arange(local_experts)
    hit = route_all[:, :, None, :] == mine[None, None, :, None]
    chosen = jnp.any(hit, axis=-1)
    weight_of = jnp.sum(jnp.where(hit, weight_all[:, :, None, :], 0.0), axis=-1)
    block = 128
    counted = chosen.reshape(2, half // block, block, local_experts).astype(f32)
    below = jnp.tril(jnp.ones((block, block), f32), -1)
    inside = jnp.einsum("ab,mkbe->mkae", below, counted)
    sums = jnp.sum(counted, axis=2)
    before = jnp.cumsum(sums, axis=1) - sums
    slot = (inside + before[:, :, None, :]).reshape(2, half, local_experts).astype(jnp.int32)
    slots = jnp.transpose(jnp.where(chosen, slot, -1), (2, 0, 1))
    weights = jnp.transpose(weight_of, (2, 0, 1))
    slot_columns = slots[..., None]

    grad_top = cotangent.astype(f32).reshape(tokens, D)
    done = {}

    def keep(**found):
        done.update(found)
        return next(iter(found.values()))

    def combined(acts, banks, h, scaled, ties=()):
        return combine(acts, banks, slot_columns, slots, weights, h, ns // 2, scaled, ties)

    pair = local_experts // 2

    def take_work(first):
        def work(ties):
            before = done.get("takes", ())
            done["takes"] = dispatch(
                h_blocks, slots, weights, w_gate, capacity, False, ties, first, pair, before
            )
            return done["takes"][0]

        return work

    g_blocks = ring_gather(
        after(cotangent, h_blocks[-1]), "seq", (None, take_work(0), take_work(pair))
    )
    taken, gate_act = done["takes"]

    def grad_work(_):
        grad_rows, grad_hidden = dispatch(g_blocks, slots, weights, w_down, capacity, True)
        return keep(grad_rows=grad_rows, grad_hidden=grad_hidden)

    def act_work(ties):
        acts = activate(taken, gate_act, done["grad_hidden"], w_up, ties)
        return keep(tail=acts[0], acts=acts)

    def first_work(ties):
        first = combined(done["acts"][1:], (w_gate, w_up), 0, False, ties)
        return keep(tail=first[0], first=first)

    o_all = ring_gather(
        after(o_heads.reshape(group * micro, width), g_blocks[-1]),
        "seq",
        (grad_work, act_work, first_work),
        {2: lambda moved: keep(o_moved=moved)},
        tie_last=False,
    )
    across = sizes("seq")[1] - 1
    o_all, o_last = o_all[:-across], o_all[-across:]
    first = done["first"]
    grad_rows = done["grad_rows"]
    hidden, grad_gate_act, grad_up_act = done["acts"]
    second = combined(
        (grad_gate_act, grad_up_act), (w_gate, w_up), 1, False, (first[0], *done["o_moved"])
    )

    def down_work(ties):
        return keep(whole_down=bank_grad(grad_rows, hidden, ties))

    def down_then(moved):
        o_all.extend(together((done["whole_down"], *moved), *o_last))
        keep(sum_down=after(done["whole_down"], o_all[-1]))

    def mixed_work(h):
        def work(ties):
            mixed = combined((hidden,), (w_down,), h, True, tuple(ties) + tuple(o_all[-across:]))
            done.setdefault("mixed", []).extend(mixed)
            return mixed[0]

        return work

    parts = [v.reshape(micro, rows, D) for v in list(first) + list(second)]
    grad_h_two = ring_scatter(
        parts,
        "seq",
        (lambda _: second[0], down_work, mixed_work(0), mixed_work(1)),
        {
            1: down_then,
            3: lambda moved: keep(last=moved),
        },
    ).reshape(tokens, D)

    def bank_sum(whole):
        return lax.psum_scatter(whole, "fsdp", scatter_dimension=1, tiled=True).astype(f32)

    grad_down = bank_sum(done["sum_down"])

    grad_gain_two = jnp.sum(grad_h_two * normed_two, axis=0)
    grad_unit = grad_h_two * gain_two
    grad_middle = grad_top + inv_two * (
        grad_unit - normed_two * jnp.mean(grad_unit * normed_two, axis=-1, keepdims=True)
    )
    grad_attn = grad_middle.astype(bf16)
    grad_o = jnp.einsum("te,de->td", grad_attn, w_output, preferred_element_type=f32).astype(bf16)

    def to_heads(value):
        cut = value.reshape(micro, rows, ns, width)
        return lax.all_to_all(
            jnp.moveaxis(cut, 2, 0), "seq", split_axis=0, concat_axis=0, tiled=True
        )

    whole_gate = bank_grad(taken, grad_gate_act, (grad_o,))
    (do_blocks,) = together((whole_gate,), to_heads(grad_o))
    grad_gate = bank_sum(after(whole_gate, do_blocks))
    do_heads = reorder(do_blocks, seq_order)

    mixed = [v.reshape(micro, rows, D) for v in done["mixed"]]
    k = sizes("seq")[1] + 1 % sizes("seq")[1]
    mixed[k] = after(mixed[k], do_blocks)
    grad_qkv, grad_head = attend_back(qkv, do_heads, tables)
    part_h_one, grad_gain_one = part_grads(grad_qkv, w_first, x_all, inv_all)
    one, columns = together(
        (grad_gain_one,), row_move(mixed, 1, "seq"), to_heads(after(grad_attn, do_blocks))
    )

    total = one
    part_h_one = [v.reshape(micro, rows, D) for v in part_h_one]
    part_h_one[k] = after(part_h_one[k], total)
    gains = jnp.pad(jnp.stack([grad_gain_one, grad_gain_two], axis=1), ((0, 0), (0, HD - 2)))
    whole = proj_grads(
        h_one,
        grad_qkv,
        o_all,
        columns.reshape(micro * group, width),
        gains,
        relative_order("fsdp"),
        inverse_seq,
        (total,),
    )
    left = exchanges()
    head = jnp.sum(after(grad_head, total), axis=0)

    def exchange(head):
        axis, pairs = left.pop(0)
        return lax.ppermute(head, axis, pairs)

    total = ahead(row_sum(total, mixed, 1, "seq"), "seq")
    head = head + exchange(head)
    total, two, one, moved = together(
        (whole[0],),
        total,
        row_move(mixed, 2, "seq"),
        row_move(part_h_one, 1, "seq"),
        exchange(head),
    )
    head = head + moved

    whole_up = bank_grad(taken, grad_up_act, (one,))
    whole = [after(v, one) for v in whole]
    owned = ring_scatter(whole, "fsdp", (None, lambda _: whole_up)).astype(bf16)

    total = ahead(add(row_sum(two, mixed, 2, "seq"), total).astype(bf16), "seq")
    grad_total = ahead(row_sum(one, part_h_one, 1, "seq"), "seq")
    total, grad_total, three, two, owned = together(
        (whole_up,),
        total,
        grad_total,
        row_move(mixed, 3, "seq"),
        row_move(part_h_one, 2, "seq"),
        owned,
    )
    grad_up = bank_sum(after(whole_up, owned))
    owned = lax.all_to_all(
        owned.reshape(ns, share, -1), "seq", split_axis=0, concat_axis=0, tiled=True
    )

    grad_total = add(row_sum(two, part_h_one, 2, "seq"), grad_total).astype(bf16)
    grad_total, zero, moved, owned = together(
        (grad_down,),
        ahead(grad_total, "seq"),
        row_move(part_h_one, 3, "seq"),
        exchange(head),
        owned,
    )
    head = head + moved

    k = 1 % sizes("seq")[1]
    mixed[k], part_h_one[k] = after(mixed[k], owned), after(part_h_one[k], owned)
    total = ahead(add(row_sum(three, mixed, 3, "seq"), total).astype(bf16), "seq")
    grad_total = add(row_sum(zero, part_h_one, 3, "seq"), grad_total).astype(bf16)
    grad_total, zero, moved, last, total = together(
        (grad_gate,),
        ahead(grad_total, "seq"),
        row_move(part_h_one, 0, "seq"),
        exchange(head),
        row_move(mixed, 0, "seq"),
        total,
    )
    head = head + moved
    mixed = add(row_sum(last, mixed, 0, "seq"), total).reshape(tokens, D)
    layer_output = (middle + mixed).astype(bf16).reshape(micro, rows, D)
    while left:
        head = head + exchange(head)
    grad_head_gains = head
    grad_h_one = add(row_sum(zero, part_h_one, 0, "seq"), grad_total).reshape(tokens, D)
    inv_one = rms_scale(x_rows)
    normed_one = x_rows * inv_one
    grad_unit = grad_h_one * gain_one
    input_grad = grad_middle + inv_one * (
        grad_unit - normed_one * jnp.mean(grad_unit * normed_one, axis=-1, keepdims=True)
    )
    input_grad = input_grad.reshape(micro, rows, D)
    owned = owned.astype(f32)
    of_qkv = owned[..., : 3 * width].reshape(ns, share, heads_local, 3, HD)
    grad_query, grad_key, grad_value = (
        jnp.moveaxis(of_qkv[..., k, :], 0, 1).reshape(share, D) for k in range(3)
    )
    grad_output = jnp.moveaxis(owned[..., 3 * width : 4 * width], 0, 1).reshape(share, D)
    of_gains = jnp.sum(owned[..., 4 * width : 4 * width + 2], axis=0)
    return (
        layer_output,
        input_grad,
        of_gains[:, 0],
        of_gains[:, 1],
        grad_query,
        grad_key,
        grad_value,
        grad_output,
        grad_head_gains,
        grad_gate,
        grad_up,
        grad_down,
    )


def solution(mesh):
    placed = (
        P(None, ("fsdp", "seq"), None),
        P(None, ("fsdp", "seq"), None),
        P(None, "fsdp"),
        P(None, ("fsdp", "seq"), None),
        P(None, ("fsdp", "seq"), None),
        P("fsdp"),
        P("fsdp"),
        P("fsdp", None),
        P("fsdp", None),
        P("fsdp", None),
        P("fsdp", None),
        P(),
        P("seq", "fsdp", None),
        P("seq", "fsdp", None),
        P("seq", "fsdp", None),
    )
    return jax.shard_map(
        body,
        mesh=mesh,
        in_specs=placed,
        out_specs=(
            P(None, ("fsdp", "seq"), None),
            P(None, ("fsdp", "seq"), None),
            P(("fsdp", "seq")),
            P(("fsdp", "seq")),
            P(("fsdp", "seq"), None),
            P(("fsdp", "seq"), None),
            P(("fsdp", "seq"), None),
            P(("fsdp", "seq"), None),
            P(),
            P("seq", "fsdp", None),
            P("seq", "fsdp", None),
            P("seq", "fsdp", None),
        ),
        check_vma=False,
    )
```

```python
import math

import jax
import jax.numpy as jnp
from jax import lax
from jax.experimental import pallas as pl
from jax.experimental.pallas import tpu as pltpu
from jax.sharding import PartitionSpec as P

D = 2048
H = 16
HD = 128
FFE = 1024
TOP = 8
SEQ_LEN = 1024

eps = 1e-06
rope_base = 10000.0
masked_score = -1e30
f32 = jnp.float32
little = pl.CostEstimate(flops=1, bytes_accessed=1, transcendentals=0)
bf16 = jnp.bfloat16


def shift(value, axis, outer, inner, by_outer, by_inner):
    pairs = []
    for a in range(outer):
        for b in range(inner):
            there = ((a + by_outer) % outer) * inner + (b + by_inner) % inner
            pairs.append((a * inner + b, there))
    return lax.ppermute(value, axis, pairs)


def sizes(axis):
    count = lax.axis_size(axis)
    return (count // 2, 2) if axis == "fsdp" else (4, count // 4)


def after(value, *others):
    others = [v for v in others if v is not None]
    if not others:
        return value
    anywhere = pl.BlockSpec(memory_space=pl.ANY)
    return pl.pallas_call(
        lambda *refs: None,
        in_specs=[anywhere] * (1 + len(others)),
        out_specs=anywhere,
        out_shape=jax.ShapeDtypeStruct(value.shape, value.dtype),
        input_output_aliases={0: 0},
        cost_estimate=little,
        name="after",
    )(value, *others)


def together(work, *moved):
    moved = list(moved)
    for k in range(len(moved)):
        moved[k] = after(moved[k], *work, *moved[:k], *moved[k + 1 :])
    return moved


def ring_gather(value, axis, work=None, split=False):
    outer, inner = sizes(axis)
    blocks, arrived = [], []
    for a in range(outer):
        row = [value]
        for b in range(1, inner):
            row.append(shift(row[-1], axis, outer, inner, 0, 1))
        moved = row[1:]
        if a + 1 < outer:
            moved.append(shift(value, axis, outer, inner, 1, 0))
        last = split and inner == 2 and a + 1 == outer
        if last:
            cut = value.shape[0] // 2
            moved = [
                shift(value[:cut], axis, outer, inner, 0, 1),
                shift(blocks[-1][cut:], axis, outer, inner, 1, 0),
            ]
        if work is not None:
            moved = together([f(arrived) for f in work[a : a + 1] if f], *moved)
        blocks += [value] + (moved if last else moved[: inner - 1])
        value, arrived = moved[-1], moved
    return blocks


def row_move(parts, a, axis):
    outer, inner = sizes(axis)
    row = parts[a * inner + 1 % inner]
    for b in range(2, inner):
        row = shift(row, axis, outer, inner, 0, 1)
        row = (row.astype(f32) + parts[a * inner + b].astype(f32)).astype(bf16)
    return shift(row, axis, outer, inner, 0, 1) if inner > 1 else row


def row_sum(moved, parts, a, axis):
    total = moved.astype(f32) + parts[a * sizes(axis)[1]].astype(f32)
    return total.astype(bf16)


def ahead(value, axis):
    return shift(value, axis, *sizes(axis), 1, 0)


def add(one, other):
    return one.astype(f32) + other.astype(f32)


def ring_scatter(parts, axis, work=(), then={}):
    outer, _ = sizes(axis)
    total, arrived = None, []
    for step in range(outer):
        a = (step + 1) % outer
        moved = [row_move(parts, a, axis)]
        if step:
            moved.append(ahead(total, axis))
        moved = together([f(arrived) for f in work[step : step + 1] if f], *moved)
        if step in then:
            then[step](moved)
        arrived = moved
        total = row_sum(moved[0], parts, a, axis)
        if step:
            total = add(total, moved[1])
        if step and step + 1 < outer:
            total = total.astype(bf16)
    return total


def relative_order(axis):
    outer, inner = sizes(axis)
    me = lax.axis_index(axis)
    a, b = me // inner, me % inner
    k = jnp.arange(outer * inner)
    return ((a - k // inner) % outer) * inner + (b - k % inner) % inner


def reorder(value, order, axis=0):
    value = jnp.moveaxis(value, axis, 0)
    value = value.at[order].get(mode="promise_in_bounds", unique_indices=True)
    return jnp.moveaxis(value, 0, axis)


def rms_scale(values):
    return lax.rsqrt(jnp.mean(values * values, axis=-1, keepdims=True) + eps)


def exchanges():
    steps = []
    for axis in ("fsdp", "seq"):
        count = lax.axis_size(axis)
        for k in range(count.bit_length() - 1):
            steps.append((axis, [(i, i ^ (1 << k)) for i in range(count)]))
    return steps


def turn(values, cosine, sine):
    return values * cosine + pltpu.roll(values, HD // 2, 1) * sine


def turn_back(values, cosine, sine):
    return values * cosine - pltpu.roll(values, HD // 2, 1) * sine


def dot(left, right, left_dim, right_dim):
    return lax.dot_general(
        left, right, (((left_dim,), (right_dim,)), ((), ())), preferred_element_type=f32
    )


def attend_kernel(tile, qkv_ref, cos_ref, sin_ref, seg_row_ref, seg_col_ref, gain_ref, o_ref):
    blocks, _, rows, _ = qkv_ref.shape
    group = blocks * rows
    cosine, sine = cos_ref[...], sin_ref[...]

    def turned(part, row):
        raw = qkv_ref[:, 0, :, part * HD : (part + 1) * HD].reshape(group, HD).astype(f32)
        return turn(raw * rms_scale(raw) * gain_ref[row : row + 1, :], cosine, sine).astype(bf16)

    queries, keys = turned(0, 0), turned(1, 1)
    values = qkv_ref[:, 0, :, 2 * HD : 3 * HD].reshape(group, HD)
    seg_row = seg_row_ref[0]
    for start in range(0, group, tile):
        scores = dot(queries[start : start + tile], keys, 1, 1) * (1.0 / math.sqrt(HD))
        allowed = seg_col_ref[0, start : start + tile, :] == seg_row
        scores = jnp.where(allowed, scores, masked_score)
        powered = jnp.exp(scores - jnp.max(scores, axis=-1, keepdims=True))
        scale = 1.0 / jnp.sum(powered, axis=-1, keepdims=True)
        attended = dot((powered * scale).astype(bf16), values, 1, 0).astype(bf16)
        o_ref[start // rows : (start + tile) // rows, 0, :, :] = attended.reshape(
            tile // rows, rows, HD
        )


def attend_back_kernel(
    tile,
    qkv_ref,
    do_ref,
    cos_ref,
    sin_ref,
    seg_row_ref,
    seg_col_ref,
    gain_ref,
    grad_ref,
    grad_gain_ref,
):
    blocks, _, rows, _ = qkv_ref.shape
    group = blocks * rows
    cosine, sine = cos_ref[...], sin_ref[...]
    scaling = 1.0 / math.sqrt(HD)

    def normed(part):
        raw = qkv_ref[:, 0, :, part * HD : (part + 1) * HD].reshape(group, HD).astype(f32)
        inverse = rms_scale(raw)
        return raw * inverse, inverse

    def turned(part):
        return turn(normed(part)[0] * gain_ref[part : part + 1, :], cosine, sine).astype(bf16)

    def finish(part, grad_turned):
        unit, inverse = normed(part)
        grad_scaled = turn_back(grad_turned, cosine, sine)
        grad_gain_ref[0, part : part + 1, :] = jnp.sum(grad_scaled * unit, axis=0, keepdims=True)
        grad_unit = grad_scaled * gain_ref[part : part + 1, :]
        grad_raw = inverse * (
            grad_unit - unit * jnp.mean(grad_unit * unit, axis=-1, keepdims=True)
        )
        return grad_raw

    def put(part, value):
        grad_ref[:, 0, :, part * HD : (part + 1) * HD] = value.astype(bf16).reshape(
            blocks, rows, HD
        )

    queries, keys = turned(0), turned(1)
    values = qkv_ref[:, 0, :, 2 * HD : 3 * HD].reshape(group, HD)
    grad_out = do_ref[:, 0, :, :].reshape(group, HD)
    seg_row = seg_row_ref[0]
    grad_query = []
    grad_key = jnp.zeros((group, HD), f32)
    grad_value = jnp.zeros((group, HD), f32)
    for start in range(0, group, tile):
        part = queries[start : start + tile]
        grad_part = grad_out[start : start + tile]
        scores = dot(part, keys, 1, 1) * scaling
        allowed = seg_col_ref[0, start : start + tile, :] == seg_row
        scores = jnp.where(allowed, scores, masked_score)
        powered = jnp.exp(scores - jnp.max(scores, axis=-1, keepdims=True))
        probabilities = powered * (1.0 / jnp.sum(powered, axis=-1, keepdims=True))
        grad_probs = dot(grad_part, values, 1, 1)
        centre = jnp.sum(probabilities * grad_probs, axis=-1, keepdims=True)
        grad_scores = (probabilities * (grad_probs - centre)).astype(bf16)
        grad_query.append(dot(grad_scores, keys, 1, 0) * scaling)
        grad_key = grad_key + dot(grad_scores, part, 0, 0)
        grad_value = grad_value + dot(probabilities.astype(bf16), grad_part, 0, 0)
    put(0, finish(0, jnp.concatenate(grad_query, axis=0)))
    put(1, finish(1, grad_key * scaling))
    put(2, grad_value)


def attention_specs(ns, micro, rows, heads):
    group = ns * rows
    tile = max(rows, 256)
    return (
        tile,
        pl.BlockSpec((ns, 1, rows, 3 * HD), lambda m, h: (0, m, 0, h)),
        pl.BlockSpec((ns, 1, rows, HD), lambda m, h: (0, m, 0, h)),
        [
            pl.BlockSpec((group, HD), lambda m, h: (0, 0)),
            pl.BlockSpec((group, HD), lambda m, h: (0, 0)),
            pl.BlockSpec((1, 1, group), lambda m, h: (m, 0, 0)),
            pl.BlockSpec((1, group, 1), lambda m, h: (m, 0, 0)),
            pl.BlockSpec((2, HD), lambda m, h: (0, 0)),
        ],
    )


def attend(qkv, tables):
    ns, micro, rows, width = qkv.shape
    heads = width // (3 * HD)
    tile, wide, narrow, shared = attention_specs(ns, micro, rows, heads)
    group = ns * rows
    return pl.pallas_call(
        lambda *refs: attend_kernel(tile, *refs),
        grid=(micro, heads),
        in_specs=[wide] + shared,
        out_specs=narrow,
        out_shape=jax.ShapeDtypeStruct((ns, micro, rows, heads * HD), bf16),
        compiler_params=pltpu.CompilerParams(vmem_limit_bytes=40 * 2**20),
        cost_estimate=little,
        name="attend",
    )(qkv, *tables)


def attend_back(qkv, grad_out, tables, ties=()):
    ns, micro, rows, width = qkv.shape
    heads = width // (3 * HD)
    tile, wide, narrow, shared = attention_specs(ns, micro, rows, heads)
    group = ns * rows
    return pl.pallas_call(
        lambda *refs: attend_back_kernel(tile, *refs[:7], *refs[-2:]),
        grid=(micro, heads),
        in_specs=[wide, narrow] + shared + [pl.BlockSpec(memory_space=pl.ANY)] * len(ties),
        out_specs=[wide, pl.BlockSpec((1, 2, HD), lambda m, h: (m * heads + h, 0, 0))],
        out_shape=[
            jax.ShapeDtypeStruct((ns, micro, rows, width), bf16),
            jax.ShapeDtypeStruct((micro * heads, 2, HD), f32),
        ],
        compiler_params=pltpu.CompilerParams(vmem_limit_bytes=40 * 2**20),
        cost_estimate=little,
        name="attend_back",
    )(qkv, grad_out, *tables, *ties)


def part_kernel(grad_ref, w_ref, x_ref, inv_ref, *out_refs):
    out_refs, gain_ref = out_refs[:-1], out_refs[-1]
    rows = out_refs[0].shape[0]
    gain = jnp.zeros(gain_ref.shape, f32)
    for b, ref in enumerate(out_refs):
        span = slice(b * rows, (b + 1) * rows)
        wide = dot(grad_ref[span, :], w_ref[...], 1, 1)
        ref[...] = wide.astype(bf16)
        normed = x_ref[span, :].astype(f32) * inv_ref[span, :]
        gain = gain + jnp.sum(wide * normed, axis=0, keepdims=True)
    gain_ref[...] = gain


def part_grads(grad_qkv, w_first, x_all, inv_all, ties=()):
    blocks = grad_qkv.shape[0]
    width = grad_qkv.shape[-1]
    count = grad_qkv.size // width
    block = jax.ShapeDtypeStruct((count // blocks, D), bf16)
    found = call(
        part_kernel,
        "part_grads",
        (D // part,),
        [
            (grad_qkv.reshape(count, width), whole_of((count, width))),
            (w_first, pl.BlockSpec((part, width), lambda d: (d, 0))),
            (x_all.reshape(count, x_all.shape[-1]), pl.BlockSpec((count, part), lambda d: (0, d))),
            (inv_all.reshape(count, 1), whole_of((count, 1))),
        ],
        [(block, pl.BlockSpec((block.shape[0], part), lambda d: (0, d)))] * blocks
        + [(jax.ShapeDtypeStruct((1, D), f32), pl.BlockSpec((1, part), lambda d: (0, d)))],
        ties=ties,
    )
    return found[:-1], found[-1][0]


def proj_kernel(blocks, order_ref, place_ref, h_ref, grad_ref, column_ref, gain_ref, *refs):
    o_refs, out_refs, found_ref = refs[:blocks], refs[blocks:-1], refs[-1]
    k = pl.program_id(0)
    inputs, width = grad_ref.shape[1], column_ref.shape[1]
    owners = found_ref.shape[0] // width
    found_ref[:, :inputs] = dot(h_ref[...], grad_ref[...], 0, 0)
    for j in range(owners):
        place = place_ref[order_ref[k] * owners + j]
        for b in range(blocks):

            @pl.when(place == b)
            def _(b=b, j=j):
                found_ref[j * width : (j + 1) * width, inputs : inputs + width] = dot(
                    o_refs[b][...], column_ref[...], 0, 0
                )

    found_ref[:, inputs + width :] = gain_ref[...]
    for b, ref in enumerate(out_refs):

        @pl.when(k == b)
        def _(ref=ref):
            ref[...] = found_ref[...].astype(bf16)


def proj_grads(h_one, grad_qkv, o_blocks, columns, gains, order, places, ties=()):
    count, inputs = h_one.size // D, grad_qkv.shape[-1]
    width, nf = columns.shape[1], order.shape[0]
    rows, across = D // nf, inputs + width + gains.shape[1]
    result = jax.ShapeDtypeStruct((rows, across), bf16)
    ins = [
        (h_one.reshape(count, D), pl.BlockSpec((count, rows), lambda k, order, _: (0, order[k]))),
        (grad_qkv.reshape(count, inputs), whole_of((count, inputs))),
        (columns, whole_of(columns.shape)),
        (gains, pl.BlockSpec((rows, gains.shape[1]), lambda k, order, _: (order[k], 0))),
    ] + [(v, whole_of(v.shape)) for v in o_blocks]

    def run(*refs):
        lead = 2 + len(ins)
        proj_kernel(len(o_blocks), *refs[:lead], *refs[lead + len(ties) :])

    return pl.pallas_call(
        run,
        grid_spec=pltpu.PrefetchScalarGridSpec(
            num_scalar_prefetch=2,
            grid=(nf,),
            in_specs=[spec for _, spec in ins] + [pl.BlockSpec(memory_space=pl.ANY)] * len(ties),
            out_specs=[whole_of(result.shape)] * nf,
            scratch_shapes=[pltpu.VMEM((rows, across), f32)],
        ),
        out_shape=[result] * nf,
        compiler_params=pltpu.CompilerParams(vmem_limit_bytes=56 * 2**20),
        cost_estimate=little,
        name="proj_grads",
    )(order, places, *[value for value, _ in ins], *ties)


part = 512


def spans(shape, *block):
    block = block or (1,)
    return pl.BlockSpec(
        tuple(block) + tuple(shape[len(block) :]), lambda e, *_: (e,) + (0,) * (len(shape) - 1)
    )


def whole_of(shape):
    return pl.BlockSpec(
        tuple(shape), lambda *_: (0,) * len(shape), pipeline_mode=pl.Buffered(buffer_count=1)
    )


def call(kernel, name, grid, ins, outs, scratch=(), ties=(), aliases={}):
    ties = [t for t in ties if t is not None]
    count = len(ins)

    def run(*refs):
        kernel(*refs[:count], *refs[count + len(ties) :])

    return pl.pallas_call(
        run,
        grid=grid,
        in_specs=[spec for _, spec in ins] + [pl.BlockSpec(memory_space=pl.ANY)] * len(ties),
        out_specs=[spec for _, spec in outs],
        out_shape=[shape for shape, _ in outs],
        scratch_shapes=list(scratch),
        input_output_aliases=aliases,
        compiler_params=pltpu.CompilerParams(vmem_limit_bytes=56 * 2**20),
        cost_estimate=little,
        name=name,
    )(*[value for value, _ in ins], *ties)


def picked(slot_row, capacity):
    place = lax.broadcasted_iota(jnp.int32, (capacity, slot_row.shape[1]), 0)
    return place == slot_row


def slot_weights(slot_row, weight_row, capacity):
    chosen = jnp.where(picked(slot_row, capacity), weight_row, 0.0)
    return jnp.sum(chosen, axis=1, keepdims=True)


def dispatch_kernel(scaled, blocks, *refs):
    value_refs, (slot_ref, weight_ref, w_ref, rows_ref, act_ref) = refs[:blocks], refs[blocks:]
    capacity, half = rows_ref.shape[2], slot_ref.shape[2]
    halves, seen = ([], []), 0
    for ref in value_refs:
        halves[seen // half].append(ref)
        seen += ref.shape[0]
    for h in range(2):
        slot_row = slot_ref[0, h : h + 1, :]
        pick = picked(slot_row, capacity).astype(f32).astype(bf16)
        if scaled:
            scale = slot_weights(slot_row, weight_ref[0, h : h + 1, :], capacity)
        for d in range(0, D, part):
            values = jnp.concatenate(
                [ref[:, d : d + part] for ref in halves[h]], axis=0
            )
            taken = dot(pick, values, 1, 0)
            if scaled:
                taken = taken * scale
            rows_ref[0, h, :, d : d + part] = taken.astype(bf16)
        act_ref[0, h] = dot(rows_ref[0, h], w_ref[0], 1, 0)


def dispatch(
    values, slots, weights, bank, capacity, scaled, ties=(), first=0, count=None, before=()
):
    experts = bank.shape[0]
    count = count or experts
    values = [v.reshape(-1, v.shape[-1]) for v in values]
    rows_shape = (experts, 2, capacity, D)
    act_shape = (experts, 2, capacity, FFE)

    def of(shape):
        return pl.BlockSpec((1,) + shape[1:], lambda e: (first + e,) + (0,) * (len(shape) - 1))

    return call(
        lambda *refs: dispatch_kernel(scaled, len(values), *refs),
        "dispatch",
        (count,),
        [(v, whole_of(v.shape)) for v in values]
        + [(v, of(v.shape)) for v in (slots, weights, bank)],
        [
            (jax.ShapeDtypeStruct(rows_shape, bf16), of(rows_shape)),
            (jax.ShapeDtypeStruct(act_shape, f32), of(act_shape)),
        ],
        ties=tuple(before) + tuple(ties),
        aliases={len(values) + 3 + k: k for k in range(len(before))},
    )


def act_kernel(taken_ref, gate_ref, grad_ref, w_ref, hidden_ref, grad_gate_ref, grad_up_ref):
    for f in range(0, FFE, 256):
        span = slice(f, f + 256)
        up_act = dot(taken_ref[0, 0], w_ref[0, :, span], 1, 0)
        gate_act, grad_hidden = gate_ref[0, 0, :, span], grad_ref[0, 0, :, span]
        gate_sig = jax.nn.sigmoid(gate_act)
        gate_silu = gate_act * gate_sig
        hidden_ref[0, 0, :, span] = (gate_silu * up_act).astype(bf16)
        grad_gate = grad_hidden * up_act * gate_sig * (1.0 + gate_act * (1.0 - gate_sig))
        grad_gate_ref[0, 0, :, span] = grad_gate.astype(bf16)
        grad_up_ref[0, 0, :, span] = (grad_hidden * gate_silu).astype(bf16)


def activate(taken, gate_act, grad_hidden, w_up, ties=()):
    count, _, capacity, _ = taken.shape

    def of(width):
        return pl.BlockSpec((1, 1, capacity, width), lambda e, h: (e, h, 0, 0))

    result = jax.ShapeDtypeStruct(gate_act.shape, bf16)
    return call(
        act_kernel,
        "activate",
        (count, 2),
        [
            (taken, of(D)),
            (gate_act, of(FFE)),
            (grad_hidden, of(FFE)),
            (w_up, spans(w_up.shape)),
        ],
        [(result, of(FFE))] * 3,
        ties=ties,
    )


def bank_kernel(left_ref, right_ref, out_ref):
    rows = left_ref.shape[1] * left_ref.shape[2]
    left, right = left_ref[0].reshape(rows, -1), right_ref[0].reshape(rows, -1)
    out_ref[0] = dot(left, right, 0, 0).astype(bf16)


def bank_grad(left, right, ties=()):
    count, _, capacity, _ = left.shape
    result = jax.ShapeDtypeStruct((count, D, FFE), bf16)
    return call(
        bank_kernel,
        "bank_grad",
        (count, D // part),
        [
            (left, pl.BlockSpec((1, 2, capacity, part), lambda e, d: (e, 0, 0, d))),
            (right, pl.BlockSpec((1, 2, capacity, FFE), lambda e, d: (e, 0, 0, 0))),
        ],
        [(result, pl.BlockSpec((1, part, FFE), lambda e, d: (e, d, 0)))],
        ties=ties,
    )[0]


def combine_kernel(scaled, acts, h, *refs):
    act_refs, w_refs = refs[:acts], refs[acts : 2 * acts]
    column_ref, slot_ref, weight_ref = refs[2 * acts : 2 * acts + 3]
    out_refs, (pick_ref, rows_ref, scale_ref) = refs[2 * acts + 3 : -3], refs[-3:]
    count, _, capacity, _ = act_refs[0].shape
    half, stride = pick_ref.shape[0], rows_ref.shape[0] // count

    @pl.when(pl.program_id(0) == 0)
    def _():
        rows_ref[...] = jnp.zeros_like(rows_ref)
        place = lax.broadcasted_iota(jnp.int32, (half, stride), 1)
        for e in range(count):
            pick = (place == column_ref[e, 0]).astype(f32).astype(bf16)
            pick_ref[:, e * stride : (e + 1) * stride] = pick
            if scaled:
                scale_ref[e] = slot_weights(
                    slot_ref[e, h : h + 1, :], weight_ref[e, h : h + 1, :], capacity
                )

    for e in range(count):
        grads = [dot(a_ref[e, 0], w_ref[e], 1, 1) for a_ref, w_ref in zip(act_refs, w_refs)]
        rows = sum(grads[1:], grads[0])
        if scaled:
            rows = rows * scale_ref[e]
        rows_ref[e * stride : e * stride + capacity, :] = rows.astype(bf16)
    n = out_refs[0].shape[0]
    for b, ref in enumerate(out_refs):
        ref[...] = dot(pick_ref[b * n : (b + 1) * n, :], rows_ref[...], 1, 0).astype(bf16)


def combine(acts, banks, columns, slots, weights, h, blocks, scaled, ties=()):
    count, _, capacity, _ = acts[0].shape
    half = columns.shape[2]
    stride = -(-capacity // 128) * 128
    result = jax.ShapeDtypeStruct((half // blocks, D), bf16)
    once = pl.Buffered(buffer_count=1)
    act = pl.BlockSpec((count, 1, capacity, FFE), lambda d: (0, h, 0, 0), pipeline_mode=once)
    column = pl.BlockSpec((count, 1, half, 1), lambda d: (0, h, 0, 0), pipeline_mode=once)
    return call(
        lambda *refs: combine_kernel(scaled, len(acts), h, *refs),
        "combine",
        (D // part,),
        [(a, act) for a in acts]
        + [(w, pl.BlockSpec((count, part, FFE), lambda d: (0, d, 0))) for w in banks]
        + [(columns, column)]
        + [(v, whole_of(v.shape)) for v in (slots, weights)],
        [(result, pl.BlockSpec((half // blocks, part), lambda d: (0, d)))] * blocks,
        scratch=[
            pltpu.VMEM((half, count * stride), bf16),
            pltpu.VMEM((count * stride, part), bf16),
            pltpu.VMEM((count, capacity, 1), f32),
        ],
        ties=ties,
    )


def body(
    layer_input,
    cotangent,
    segments,
    routes,
    route_weights,
    gain_attention,
    gain_experts,
    query_proj,
    key_proj,
    value_proj,
    output_proj,
    head_gains,
    expert_gate,
    expert_up,
    expert_down,
):
    micro, rows, _ = layer_input.shape
    nf, ns = lax.axis_size("fsdp"), lax.axis_size("seq")
    seq_index = lax.axis_index("seq")
    seq_order = relative_order("seq")
    tokens = micro * rows
    group = rows * ns
    half = group * micro // 2
    heads_local = H // ns
    width = heads_local * HD
    local_experts = expert_gate.shape[0]
    experts = local_experts * ns
    capacity = micro * ns // 2 * min(rows, 3 * rows * TOP // (2 * experts))
    share = D // (nf * ns)

    def spread(value, axis):
        return lax.all_gather(value, "fsdp", axis=axis, tiled=True)

    def gather_tokens(value):
        blocks = jnp.concatenate(ring_gather(value, "seq", split=True), axis=0)
        return blocks.reshape((ns,) + value.shape)

    columns = [
        lax.dynamic_slice_in_dim(w, seq_index * width, width, axis=1).reshape(-1, heads_local, HD)
        for w in (query_proj, key_proj, value_proj)
    ]
    columns = jnp.stack(columns, axis=2).reshape(-1, 3 * width)
    extra = jnp.pad(jnp.stack([gain_attention, gain_experts], axis=1), ((0, 0), (0, HD - 2)))
    w_first = spread(jnp.concatenate([columns, extra], axis=1), 0)
    w_qkv = w_first[:, : 3 * width]
    gain_one = w_first[:, 3 * width].astype(f32)
    gain_two = w_first[:, 3 * width + 1].astype(f32)
    w_down = spread(expert_down, 1)
    w_output = spread(output_proj, 0)
    w_gate = spread(expert_gate, 1)
    w_up = spread(expert_up, 1)

    weight_high = route_weights.astype(bf16)
    weight_low = (route_weights - weight_high.astype(f32)).astype(bf16)
    packed = jnp.concatenate(
        [layer_input, routes.astype(bf16), weight_high, weight_low], axis=-1
    )
    packed = jnp.pad(packed, ((0, 0), (0, 0), (0, HD - 3 * TOP)))
    packed = x_all = gather_tokens(packed)
    x_wide = packed[..., :D].astype(f32)
    inv_all = rms_scale(x_wide)
    h_one = (x_wide * inv_all * gain_one).astype(bf16)
    qkv = jnp.einsum("smtd,de->smte", h_one, w_qkv, preferred_element_type=f32).astype(bf16)

    places = (seq_order[:, None] * rows + jnp.arange(rows)[None, :]).reshape(-1)
    lane = jnp.arange(HD) % (HD // 2)
    frequency = jnp.exp(-jnp.log(rope_base) * (2.0 * lane.astype(f32) / HD))
    angles = places.astype(f32)[:, None] * frequency[None, :]
    sign = jnp.where(jnp.arange(HD) < HD // 2, -1.0, 1.0)
    segment = reorder(segments.reshape(micro, ns, rows), seq_order, axis=1).reshape(micro, group)
    tables = (
        jnp.cos(angles),
        jnp.sin(angles) * sign,
        segment[:, None, :],
        segment[:, :, None],
        head_gains.astype(f32),
    )
    o_heads = attend(qkv, tables)

    inverse_seq = jnp.argsort(seq_order)
    o_heads = reorder(o_heads, inverse_seq, axis=0)
    o_back = lax.all_to_all(o_heads, "seq", split_axis=0, concat_axis=0, tiled=True)
    o_rows = jnp.moveaxis(o_back, 0, 2).reshape(tokens, D)

    x_rows = layer_input.astype(f32).reshape(tokens, D)
    middle = x_rows + jnp.dot(o_rows, w_output, preferred_element_type=f32)
    inv_two = rms_scale(middle)
    normed_two = middle * inv_two
    h_two_own = (normed_two * gain_two).astype(bf16).reshape(micro, rows, D)
    h_blocks = ring_gather(h_two_own, "seq", (), True)

    packed = packed[..., D : D + 3 * TOP].astype(f32)
    packed = packed.reshape(2, half, 3 * TOP)
    route_all = packed[..., :TOP].astype(jnp.int32)
    weight_all = packed[..., TOP : 2 * TOP] + packed[..., 2 * TOP :]
    mine = seq_index * local_experts + jnp.arange(local_experts)
    hit = route_all[:, :, None, :] == mine[None, None, :, None]
    chosen = jnp.any(hit, axis=-1)
    weight_of = jnp.sum(jnp.where(hit, weight_all[:, :, None, :], 0.0), axis=-1)
    block = 128
    counted = chosen.reshape(2, half // block, block, local_experts).astype(f32)
    below = jnp.tril(jnp.ones((block, block), f32), -1)
    inside = jnp.einsum("ab,mkbe->mkae", below, counted)
    sums = jnp.sum(counted, axis=2)
    before = jnp.cumsum(sums, axis=1) - sums
    slot = (inside + before[:, :, None, :]).reshape(2, half, local_experts).astype(jnp.int32)
    slots = jnp.transpose(jnp.where(chosen, slot, -1), (2, 0, 1))
    weights = jnp.transpose(weight_of, (2, 0, 1))
    slot_columns = slots[..., None]

    grad_top = cotangent.astype(f32).reshape(tokens, D)
    done = {}

    def keep(**found):
        done.update(found)
        return next(iter(found.values()))

    def combined(acts, banks, h, scaled, ties=()):
        return combine(acts, banks, slot_columns, slots, weights, h, ns // 2, scaled, ties)

    pair = local_experts // 2

    def take_work(first):
        def work(ties):
            before = done.get("takes", ())
            done["takes"] = dispatch(
                h_blocks, slots, weights, w_gate, capacity, False, ties, first, pair, before
            )
            return done["takes"][0]

        return work

    g_blocks = ring_gather(
        after(cotangent, h_blocks[-1]), "seq", (None, None, take_work(0), take_work(pair)), True
    )
    taken, gate_act = done["takes"]

    def grad_work(_):
        grad_rows, grad_hidden = dispatch(g_blocks, slots, weights, w_down, capacity, True)
        return keep(grad_rows=grad_rows, grad_hidden=grad_hidden)

    def act_work(ties):
        acts = activate(taken, gate_act, done["grad_hidden"], w_up, ties)
        return keep(tail=acts[0], acts=acts)

    def first_work(ties):
        first = combined(done["acts"][1:], (w_gate, w_up), 0, False, ties)
        return keep(tail=first[0], first=first)

    o_all = ring_gather(
        after(o_heads.reshape(group * micro, width), g_blocks[-1]),
        "seq",
        (grad_work, None, act_work, first_work),
    )
    first = done["first"]
    grad_rows = done["grad_rows"]
    hidden, grad_gate_act, grad_up_act = done["acts"]
    second = combined((grad_gate_act, grad_up_act), (w_gate, w_up), 1, False, (first[0], o_all[-1]))

    def down_work(ties):
        return keep(whole_down=bank_grad(grad_rows, hidden, ties))

    def down_then(moved):
        keep(sum_down=after(done["whole_down"], *moved))

    def mixed_work(h):
        def work(ties):
            mixed = combined((hidden,), (w_down,), h, True, ties)
            done.setdefault("mixed", []).extend(mixed)
            return mixed[0]

        return work

    parts = [v.reshape(micro, rows, D) for v in list(first) + list(second)]
    grad_h_two = ring_scatter(
        parts,
        "seq",
        (lambda _: second[0], down_work, mixed_work(0), mixed_work(1)),
        {
            1: down_then,
            3: lambda moved: keep(last=moved),
        },
    ).reshape(tokens, D)

    def bank_sum(whole):
        return lax.psum_scatter(whole, "fsdp", scatter_dimension=1, tiled=True).astype(f32)

    grad_down = bank_sum(done["sum_down"])

    grad_gain_two = jnp.sum(grad_h_two * normed_two, axis=0)
    grad_unit = grad_h_two * gain_two
    grad_middle = grad_top + inv_two * (
        grad_unit - normed_two * jnp.mean(grad_unit * normed_two, axis=-1, keepdims=True)
    )
    grad_attn = grad_middle.astype(bf16)
    grad_o = jnp.einsum("te,de->td", grad_attn, w_output, preferred_element_type=f32).astype(bf16)

    def to_heads(value):
        cut = value.reshape(micro, rows, ns, width)
        return lax.all_to_all(
            jnp.moveaxis(cut, 2, 0), "seq", split_axis=0, concat_axis=0, tiled=True
        )

    whole_gate = bank_grad(taken, grad_gate_act, (grad_o,))
    (do_blocks,) = together((whole_gate,), to_heads(grad_o))
    grad_gate = bank_sum(after(whole_gate, do_blocks))
    do_heads = reorder(do_blocks, seq_order)

    mixed = [v.reshape(micro, rows, D) for v in done["mixed"]]
    k = sizes("seq")[1] + 1 % sizes("seq")[1]
    mixed[k] = after(mixed[k], do_blocks)
    grad_qkv, grad_head = attend_back(qkv, do_heads, tables)
    part_h_one, grad_gain_one = part_grads(grad_qkv, w_first, x_all, inv_all)
    one, columns = together(
        (grad_gain_one,), row_move(mixed, 1, "seq"), to_heads(after(grad_attn, do_blocks))
    )

    total = one
    part_h_one = [v.reshape(micro, rows, D) for v in part_h_one]
    part_h_one[k] = after(part_h_one[k], total)
    gains = jnp.pad(jnp.stack([grad_gain_one, grad_gain_two], axis=1), ((0, 0), (0, HD - 2)))
    whole = proj_grads(
        h_one,
        grad_qkv,
        o_all,
        columns.reshape(micro * group, width),
        gains,
        relative_order("fsdp"),
        inverse_seq,
        (total,),
    )
    left = exchanges()
    head = jnp.sum(after(grad_head, total), axis=0)

    def exchange(head):
        axis, pairs = left.pop(0)
        return lax.ppermute(head, axis, pairs)

    total = ahead(row_sum(total, mixed, 1, "seq"), "seq")
    head = head + exchange(head)
    total, two, one, moved = together(
        (whole[0],),
        total,
        row_move(mixed, 2, "seq"),
        row_move(part_h_one, 1, "seq"),
        exchange(head),
    )
    head = head + moved

    whole_up = bank_grad(taken, grad_up_act, (one,))
    whole = [after(v, one) for v in whole]
    owned = ring_scatter(whole, "fsdp", (None, lambda _: whole_up)).astype(bf16)

    total = ahead(add(row_sum(two, mixed, 2, "seq"), total).astype(bf16), "seq")
    grad_total = ahead(row_sum(one, part_h_one, 1, "seq"), "seq")
    total, grad_total, three, two, owned = together(
        (whole_up,),
        total,
        grad_total,
        row_move(mixed, 3, "seq"),
        row_move(part_h_one, 2, "seq"),
        owned,
    )
    grad_up = bank_sum(after(whole_up, owned))
    owned = lax.all_to_all(
        owned.reshape(ns, share, -1), "seq", split_axis=0, concat_axis=0, tiled=True
    )

    grad_total = add(row_sum(two, part_h_one, 2, "seq"), grad_total).astype(bf16)
    grad_total, zero, moved, owned = together(
        (grad_down,),
        ahead(grad_total, "seq"),
        row_move(part_h_one, 3, "seq"),
        exchange(head),
        owned,
    )
    head = head + moved

    k = 1 % sizes("seq")[1]
    mixed[k], part_h_one[k] = after(mixed[k], owned), after(part_h_one[k], owned)
    total = ahead(add(row_sum(three, mixed, 3, "seq"), total).astype(bf16), "seq")
    grad_total = add(row_sum(zero, part_h_one, 3, "seq"), grad_total).astype(bf16)
    grad_total, zero, moved, last, total = together(
        (grad_gate,),
        ahead(grad_total, "seq"),
        row_move(part_h_one, 0, "seq"),
        exchange(head),
        row_move(mixed, 0, "seq"),
        total,
    )
    head = head + moved
    mixed = add(row_sum(last, mixed, 0, "seq"), total).reshape(tokens, D)
    layer_output = (middle + mixed).astype(bf16).reshape(micro, rows, D)
    while left:
        head = head + exchange(head)
    grad_head_gains = head
    grad_h_one = add(row_sum(zero, part_h_one, 0, "seq"), grad_total).reshape(tokens, D)
    inv_one = rms_scale(x_rows)
    normed_one = x_rows * inv_one
    grad_unit = grad_h_one * gain_one
    input_grad = grad_middle + inv_one * (
        grad_unit - normed_one * jnp.mean(grad_unit * normed_one, axis=-1, keepdims=True)
    )
    input_grad = input_grad.reshape(micro, rows, D)
    owned = owned.astype(f32)
    of_qkv = owned[..., : 3 * width].reshape(ns, share, heads_local, 3, HD)
    grad_query, grad_key, grad_value = (
        jnp.moveaxis(of_qkv[..., k, :], 0, 1).reshape(share, D) for k in range(3)
    )
    grad_output = jnp.moveaxis(owned[..., 3 * width : 4 * width], 0, 1).reshape(share, D)
    of_gains = jnp.sum(owned[..., 4 * width : 4 * width + 2], axis=0)
    return (
        layer_output,
        input_grad,
        of_gains[:, 0],
        of_gains[:, 1],
        grad_query,
        grad_key,
        grad_value,
        grad_output,
        grad_head_gains,
        grad_gate,
        grad_up,
        grad_down,
    )


def solution(mesh):
    placed = (
        P(None, ("fsdp", "seq"), None),
        P(None, ("fsdp", "seq"), None),
        P(None, "fsdp"),
        P(None, ("fsdp", "seq"), None),
        P(None, ("fsdp", "seq"), None),
        P("fsdp"),
        P("fsdp"),
        P("fsdp", None),
        P("fsdp", None),
        P("fsdp", None),
        P("fsdp", None),
        P(),
        P("seq", "fsdp", None),
        P("seq", "fsdp", None),
        P("seq", "fsdp", None),
    )
    return jax.shard_map(
        body,
        mesh=mesh,
        in_specs=placed,
        out_specs=(
            P(None, ("fsdp", "seq"), None),
            P(None, ("fsdp", "seq"), None),
            P(("fsdp", "seq")),
            P(("fsdp", "seq")),
            P(("fsdp", "seq"), None),
            P(("fsdp", "seq"), None),
            P(("fsdp", "seq"), None),
            P(("fsdp", "seq"), None),
            P(),
            P("seq", "fsdp", None),
            P("seq", "fsdp", None),
            P("seq", "fsdp", None),
        ),
        check_vma=False,
    )
```

```python
import math

import jax
import jax.numpy as jnp
from jax import lax
from jax.experimental import pallas as pl
from jax.experimental.pallas import tpu as pltpu
from jax.sharding import PartitionSpec as P

D = 2048
H = 16
HD = 128
FFE = 1024
TOP = 8
SEQ_LEN = 1024

eps = 1e-06
rope_base = 10000.0
masked_score = -1e30
f32 = jnp.float32
little = pl.CostEstimate(flops=1, bytes_accessed=1, transcendentals=0)
bf16 = jnp.bfloat16


def shift(value, axis, outer, inner, by_outer, by_inner):
    pairs = []
    for a in range(outer):
        for b in range(inner):
            there = ((a + by_outer) % outer) * inner + (b + by_inner) % inner
            pairs.append((a * inner + b, there))
    return lax.ppermute(value, axis, pairs)


def sizes(axis):
    count = lax.axis_size(axis)
    return (count // 2, 2) if axis == "fsdp" else (4, count // 4)


def after(value, *others):
    others = [v for v in others if v is not None]
    if not others:
        return value
    anywhere = pl.BlockSpec(memory_space=pl.ANY)
    return pl.pallas_call(
        lambda *refs: None,
        in_specs=[anywhere] * (1 + len(others)),
        out_specs=anywhere,
        out_shape=jax.ShapeDtypeStruct(value.shape, value.dtype),
        input_output_aliases={0: 0},
        cost_estimate=little,
        name="after",
    )(value, *others)


def together(work, *moved):
    moved = list(moved)
    for k in range(len(moved)):
        moved[k] = after(moved[k], *work, *moved[:k], *moved[k + 1 :])
    return moved


def ring_gather(value, axis, work=None, split=False, blocks=(), stop=None):
    outer, inner = sizes(axis)
    blocks, arrived = list(blocks), []
    for a in range(len(blocks) // inner, outer if stop is None else stop):
        row = [value]
        for b in range(1, inner):
            row.append(shift(row[-1], axis, outer, inner, 0, 1))
        moved = row[1:]
        if a + 1 < outer:
            moved.append(shift(value, axis, outer, inner, 1, 0))
        last = split and inner == 2 and a + 1 == outer
        if last:
            cut = value.shape[0] // 2
            moved = [
                shift(value[:cut], axis, outer, inner, 0, 1),
                shift(blocks[-1][cut:], axis, outer, inner, 1, 0),
            ]
        if work is not None:
            moved = together([f(arrived) for f in work[a : a + 1] if f], *moved)
        blocks += [value] + (moved if last else moved[: inner - 1])
        value, arrived = moved[-1], moved
    return blocks if stop is None else (blocks, value)


def row_move(parts, a, axis):
    outer, inner = sizes(axis)
    row = parts[a * inner + 1 % inner]
    for b in range(2, inner):
        row = shift(row, axis, outer, inner, 0, 1)
        row = (row.astype(f32) + parts[a * inner + b].astype(f32)).astype(bf16)
    return shift(row, axis, outer, inner, 0, 1) if inner > 1 else row


def row_sum(moved, parts, a, axis):
    total = moved.astype(f32) + parts[a * sizes(axis)[1]].astype(f32)
    return total.astype(bf16)


def ahead(value, axis):
    return shift(value, axis, *sizes(axis), 1, 0)


def add(one, other):
    return one.astype(f32) + other.astype(f32)


def ring_scatter(parts, axis, work=(), then={}):
    outer, _ = sizes(axis)
    total, arrived = None, []
    for step in range(outer):
        a = (step + 1) % outer
        moved = [row_move(parts, a, axis)]
        if step:
            moved.append(ahead(total, axis))
        moved = together([f(arrived) for f in work[step : step + 1] if f], *moved)
        if step in then:
            then[step](moved)
        arrived = moved
        total = row_sum(moved[0], parts, a, axis)
        if step:
            total = add(total, moved[1])
        if step and step + 1 < outer:
            total = total.astype(bf16)
    return total


def relative_order(axis):
    outer, inner = sizes(axis)
    me = lax.axis_index(axis)
    a, b = me // inner, me % inner
    k = jnp.arange(outer * inner)
    return ((a - k // inner) % outer) * inner + (b - k % inner) % inner


def reorder(value, order, axis=0):
    value = jnp.moveaxis(value, axis, 0)
    value = value.at[order].get(mode="promise_in_bounds", unique_indices=True)
    return jnp.moveaxis(value, 0, axis)


def rms_scale(values):
    return lax.rsqrt(jnp.mean(values * values, axis=-1, keepdims=True) + eps)


def exchanges():
    steps = []
    for axis in ("fsdp", "seq"):
        count = lax.axis_size(axis)
        for k in range(count.bit_length() - 1):
            steps.append((axis, [(i, i ^ (1 << k)) for i in range(count)]))
    return steps


def turn(values, cosine, sine):
    return values * cosine + pltpu.roll(values, HD // 2, 1) * sine


def turn_back(values, cosine, sine):
    return values * cosine - pltpu.roll(values, HD // 2, 1) * sine


def dot(left, right, left_dim, right_dim):
    return lax.dot_general(
        left, right, (((left_dim,), (right_dim,)), ((), ())), preferred_element_type=f32
    )


def attend_kernel(tile, qkv_ref, cos_ref, sin_ref, seg_row_ref, seg_col_ref, gain_ref, o_ref):
    blocks, _, rows, _ = qkv_ref.shape
    group = blocks * rows
    cosine, sine = cos_ref[...], sin_ref[...]

    def turned(part, row):
        raw = qkv_ref[:, 0, :, part * HD : (part + 1) * HD].reshape(group, HD).astype(f32)
        return turn(raw * rms_scale(raw) * gain_ref[row : row + 1, :], cosine, sine).astype(bf16)

    queries, keys = turned(0, 0), turned(1, 1)
    values = qkv_ref[:, 0, :, 2 * HD : 3 * HD].reshape(group, HD)
    seg_row = seg_row_ref[0]
    for start in range(0, group, tile):
        scores = dot(queries[start : start + tile], keys, 1, 1) * (1.0 / math.sqrt(HD))
        allowed = seg_col_ref[0, start : start + tile, :] == seg_row
        scores = jnp.where(allowed, scores, masked_score)
        powered = jnp.exp(scores - jnp.max(scores, axis=-1, keepdims=True))
        scale = 1.0 / jnp.sum(powered, axis=-1, keepdims=True)
        attended = dot((powered * scale).astype(bf16), values, 1, 0).astype(bf16)
        o_ref[start // rows : (start + tile) // rows, 0, :, :] = attended.reshape(
            tile // rows, rows, HD
        )


def attend_back_kernel(
    tile,
    qkv_ref,
    do_ref,
    cos_ref,
    sin_ref,
    seg_row_ref,
    seg_col_ref,
    gain_ref,
    grad_ref,
    grad_gain_ref,
):
    blocks, _, rows, _ = qkv_ref.shape
    group = blocks * rows
    cosine, sine = cos_ref[...], sin_ref[...]
    scaling = 1.0 / math.sqrt(HD)

    def normed(part):
        raw = qkv_ref[:, 0, :, part * HD : (part + 1) * HD].reshape(group, HD).astype(f32)
        inverse = rms_scale(raw)
        return raw * inverse, inverse

    def turned(part):
        return turn(normed(part)[0] * gain_ref[part : part + 1, :], cosine, sine).astype(bf16)

    def finish(part, grad_turned):
        unit, inverse = normed(part)
        grad_scaled = turn_back(grad_turned, cosine, sine)
        grad_gain_ref[0, part : part + 1, :] = jnp.sum(grad_scaled * unit, axis=0, keepdims=True)
        grad_unit = grad_scaled * gain_ref[part : part + 1, :]
        grad_raw = inverse * (
            grad_unit - unit * jnp.mean(grad_unit * unit, axis=-1, keepdims=True)
        )
        return grad_raw

    def put(part, value):
        grad_ref[:, 0, :, part * HD : (part + 1) * HD] = value.astype(bf16).reshape(
            blocks, rows, HD
        )

    queries, keys = turned(0), turned(1)
    values = qkv_ref[:, 0, :, 2 * HD : 3 * HD].reshape(group, HD)
    grad_out = do_ref[:, 0, :, :].reshape(group, HD)
    seg_row = seg_row_ref[0]
    grad_query = []
    grad_key = jnp.zeros((group, HD), f32)
    grad_value = jnp.zeros((group, HD), f32)
    for start in range(0, group, tile):
        part = queries[start : start + tile]
        grad_part = grad_out[start : start + tile]
        scores = dot(part, keys, 1, 1) * scaling
        allowed = seg_col_ref[0, start : start + tile, :] == seg_row
        scores = jnp.where(allowed, scores, masked_score)
        powered = jnp.exp(scores - jnp.max(scores, axis=-1, keepdims=True))
        probabilities = powered * (1.0 / jnp.sum(powered, axis=-1, keepdims=True))
        grad_probs = dot(grad_part, values, 1, 1)
        centre = jnp.sum(probabilities * grad_probs, axis=-1, keepdims=True)
        grad_scores = (probabilities * (grad_probs - centre)).astype(bf16)
        grad_query.append(dot(grad_scores, keys, 1, 0) * scaling)
        grad_key = grad_key + dot(grad_scores, part, 0, 0)
        grad_value = grad_value + dot(probabilities.astype(bf16), grad_part, 0, 0)
    put(0, finish(0, jnp.concatenate(grad_query, axis=0)))
    put(1, finish(1, grad_key * scaling))
    put(2, grad_value)


def attention_specs(ns, micro, rows, heads):
    group = ns * rows
    tile = max(rows, 256)
    return (
        tile,
        pl.BlockSpec((ns, 1, rows, 3 * HD), lambda m, h: (0, m, 0, h)),
        pl.BlockSpec((ns, 1, rows, HD), lambda m, h: (0, m, 0, h)),
        [
            pl.BlockSpec((group, HD), lambda m, h: (0, 0)),
            pl.BlockSpec((group, HD), lambda m, h: (0, 0)),
            pl.BlockSpec((1, 1, group), lambda m, h: (m, 0, 0)),
            pl.BlockSpec((1, group, 1), lambda m, h: (m, 0, 0)),
            pl.BlockSpec((2, HD), lambda m, h: (0, 0)),
        ],
    )


def attend(qkv, tables):
    ns, micro, rows, width = qkv.shape
    heads = width // (3 * HD)
    tile, wide, narrow, shared = attention_specs(ns, micro, rows, heads)
    group = ns * rows
    return pl.pallas_call(
        lambda *refs: attend_kernel(tile, *refs),
        grid=(micro, heads),
        in_specs=[wide] + shared,
        out_specs=narrow,
        out_shape=jax.ShapeDtypeStruct((ns, micro, rows, heads * HD), bf16),
        compiler_params=pltpu.CompilerParams(vmem_limit_bytes=40 * 2**20),
        cost_estimate=little,
        name="attend",
    )(qkv, *tables)


def attend_back(qkv, grad_out, tables, ties=()):
    ns, micro, rows, width = qkv.shape
    heads = width // (3 * HD)
    tile, wide, narrow, shared = attention_specs(ns, micro, rows, heads)
    group = ns * rows
    return pl.pallas_call(
        lambda *refs: attend_back_kernel(tile, *refs[:7], *refs[-2:]),
        grid=(micro, heads),
        in_specs=[wide, narrow] + shared + [pl.BlockSpec(memory_space=pl.ANY)] * len(ties),
        out_specs=[wide, pl.BlockSpec((1, 2, HD), lambda m, h: (m * heads + h, 0, 0))],
        out_shape=[
            jax.ShapeDtypeStruct((ns, micro, rows, width), bf16),
            jax.ShapeDtypeStruct((micro * heads, 2, HD), f32),
        ],
        compiler_params=pltpu.CompilerParams(vmem_limit_bytes=40 * 2**20),
        cost_estimate=little,
        name="attend_back",
    )(qkv, grad_out, *tables, *ties)


def part_kernel(grad_ref, w_ref, x_ref, inv_ref, *out_refs):
    out_refs, gain_ref = out_refs[:-1], out_refs[-1]
    rows = out_refs[0].shape[0]
    gain = jnp.zeros(gain_ref.shape, f32)
    for b, ref in enumerate(out_refs):
        span = slice(b * rows, (b + 1) * rows)
        wide = dot(grad_ref[span, :], w_ref[...], 1, 1)
        ref[...] = wide.astype(bf16)
        normed = x_ref[span, :].astype(f32) * inv_ref[span, :]
        gain = gain + jnp.sum(wide * normed, axis=0, keepdims=True)
    gain_ref[...] = gain


def part_grads(grad_qkv, w_first, x_all, inv_all, ties=()):
    blocks = grad_qkv.shape[0]
    width = grad_qkv.shape[-1]
    count = grad_qkv.size // width
    block = jax.ShapeDtypeStruct((count // blocks, D), bf16)
    found = call(
        part_kernel,
        "part_grads",
        (D // part,),
        [
            (grad_qkv.reshape(count, width), whole_of((count, width))),
            (w_first, pl.BlockSpec((part, width), lambda d: (d, 0))),
            (x_all.reshape(count, x_all.shape[-1]), pl.BlockSpec((count, part), lambda d: (0, d))),
            (inv_all.reshape(count, 1), whole_of((count, 1))),
        ],
        [(block, pl.BlockSpec((block.shape[0], part), lambda d: (0, d)))] * blocks
        + [(jax.ShapeDtypeStruct((1, D), f32), pl.BlockSpec((1, part), lambda d: (0, d)))],
        ties=ties,
    )
    return found[:-1], found[-1][0]


def proj_kernel(blocks, order_ref, place_ref, h_ref, grad_ref, column_ref, gain_ref, *refs):
    o_refs, out_refs, found_ref = refs[:blocks], refs[blocks:-1], refs[-1]
    k = pl.program_id(0)
    inputs, width = grad_ref.shape[1], column_ref.shape[1]
    owners = found_ref.shape[0] // width
    found_ref[:, :inputs] = dot(h_ref[...], grad_ref[...], 0, 0)
    for j in range(owners):
        place = place_ref[order_ref[k] * owners + j]
        for b in range(blocks):

            @pl.when(place == b)
            def _(b=b, j=j):
                found_ref[j * width : (j + 1) * width, inputs : inputs + width] = dot(
                    o_refs[b][...], column_ref[...], 0, 0
                )

    found_ref[:, inputs + width :] = gain_ref[...]
    for b, ref in enumerate(out_refs):

        @pl.when(k == b)
        def _(ref=ref):
            ref[...] = found_ref[...].astype(bf16)


def proj_grads(h_one, grad_qkv, o_blocks, columns, gains, order, places, ties=()):
    count, inputs = h_one.size // D, grad_qkv.shape[-1]
    width, nf = columns.shape[1], order.shape[0]
    rows, across = D // nf, inputs + width + gains.shape[1]
    result = jax.ShapeDtypeStruct((rows, across), bf16)
    ins = [
        (h_one.reshape(count, D), pl.BlockSpec((count, rows), lambda k, order, _: (0, order[k]))),
        (grad_qkv.reshape(count, inputs), whole_of((count, inputs))),
        (columns, whole_of(columns.shape)),
        (gains, pl.BlockSpec((rows, gains.shape[1]), lambda k, order, _: (order[k], 0))),
    ] + [(v, whole_of(v.shape)) for v in o_blocks]

    def run(*refs):
        lead = 2 + len(ins)
        proj_kernel(len(o_blocks), *refs[:lead], *refs[lead + len(ties) :])

    return pl.pallas_call(
        run,
        grid_spec=pltpu.PrefetchScalarGridSpec(
            num_scalar_prefetch=2,
            grid=(nf,),
            in_specs=[spec for _, spec in ins] + [pl.BlockSpec(memory_space=pl.ANY)] * len(ties),
            out_specs=[whole_of(result.shape)] * nf,
            scratch_shapes=[pltpu.VMEM((rows, across), f32)],
        ),
        out_shape=[result] * nf,
        compiler_params=pltpu.CompilerParams(vmem_limit_bytes=56 * 2**20),
        cost_estimate=little,
        name="proj_grads",
    )(order, places, *[value for value, _ in ins], *ties)


part = 512


def spans(shape, *block):
    block = block or (1,)
    return pl.BlockSpec(
        tuple(block) + tuple(shape[len(block) :]), lambda e, *_: (e,) + (0,) * (len(shape) - 1)
    )


def whole_of(shape):
    return pl.BlockSpec(
        tuple(shape), lambda *_: (0,) * len(shape), pipeline_mode=pl.Buffered(buffer_count=1)
    )


def call(kernel, name, grid, ins, outs, scratch=(), ties=(), aliases={}):
    ties = [t for t in ties if t is not None]
    count = len(ins)

    def run(*refs):
        kernel(*refs[:count], *refs[count + len(ties) :])

    return pl.pallas_call(
        run,
        grid=grid,
        in_specs=[spec for _, spec in ins] + [pl.BlockSpec(memory_space=pl.ANY)] * len(ties),
        out_specs=[spec for _, spec in outs],
        out_shape=[shape for shape, _ in outs],
        scratch_shapes=list(scratch),
        input_output_aliases=aliases,
        compiler_params=pltpu.CompilerParams(vmem_limit_bytes=56 * 2**20),
        cost_estimate=little,
        name=name,
    )(*[value for value, _ in ins], *ties)


def picked(slot_row, capacity):
    place = lax.broadcasted_iota(jnp.int32, (capacity, slot_row.shape[1]), 0)
    return place == slot_row


def slot_weights(slot_row, weight_row, capacity):
    chosen = jnp.where(picked(slot_row, capacity), weight_row, 0.0)
    return jnp.sum(chosen, axis=1, keepdims=True)


def dispatch_kernel(scaled, blocks, *refs):
    value_refs, (slot_ref, weight_ref, w_ref, rows_ref, act_ref) = refs[:blocks], refs[blocks:]
    capacity, half = rows_ref.shape[2], slot_ref.shape[2]
    halves, seen = ([], []), 0
    for ref in value_refs:
        halves[seen // half].append(ref)
        seen += ref.shape[0]
    for h in range(2):
        slot_row = slot_ref[0, h : h + 1, :]
        pick = picked(slot_row, capacity).astype(f32).astype(bf16)
        if scaled:
            scale = slot_weights(slot_row, weight_ref[0, h : h + 1, :], capacity)
        for d in range(0, D, part):
            values = jnp.concatenate(
                [ref[:, d : d + part] for ref in halves[h]], axis=0
            )
            taken = dot(pick, values, 1, 0)
            if scaled:
                taken = taken * scale
            rows_ref[0, h, :, d : d + part] = taken.astype(bf16)
        act_ref[0, h] = dot(rows_ref[0, h], w_ref[0], 1, 0)


def dispatch(
    values, slots, weights, bank, capacity, scaled, ties=(), first=0, count=None, before=()
):
    experts = bank.shape[0]
    count = count or experts
    values = [v.reshape(-1, v.shape[-1]) for v in values]
    rows_shape = (experts, 2, capacity, D)
    act_shape = (experts, 2, capacity, FFE)

    def of(shape):
        return pl.BlockSpec((1,) + shape[1:], lambda e: (first + e,) + (0,) * (len(shape) - 1))

    return call(
        lambda *refs: dispatch_kernel(scaled, len(values), *refs),
        "dispatch",
        (count,),
        [(v, whole_of(v.shape)) for v in values]
        + [(v, of(v.shape)) for v in (slots, weights, bank)],
        [
            (jax.ShapeDtypeStruct(rows_shape, bf16), of(rows_shape)),
            (jax.ShapeDtypeStruct(act_shape, f32), of(act_shape)),
        ],
        ties=tuple(before) + tuple(ties),
        aliases={len(values) + 3 + k: k for k in range(len(before))},
    )


def act_kernel(taken_ref, gate_ref, grad_ref, w_ref, hidden_ref, grad_gate_ref, grad_up_ref):
    for f in range(0, FFE, 256):
        span = slice(f, f + 256)
        up_act = dot(taken_ref[0, 0], w_ref[0, :, span], 1, 0)
        gate_act, grad_hidden = gate_ref[0, 0, :, span], grad_ref[0, 0, :, span]
        gate_sig = jax.nn.sigmoid(gate_act)
        gate_silu = gate_act * gate_sig
        hidden_ref[0, 0, :, span] = (gate_silu * up_act).astype(bf16)
        grad_gate = grad_hidden * up_act * gate_sig * (1.0 + gate_act * (1.0 - gate_sig))
        grad_gate_ref[0, 0, :, span] = grad_gate.astype(bf16)
        grad_up_ref[0, 0, :, span] = (grad_hidden * gate_silu).astype(bf16)


def activate(taken, gate_act, grad_hidden, w_up, ties=()):
    count, _, capacity, _ = taken.shape

    def of(width):
        return pl.BlockSpec((1, 1, capacity, width), lambda e, h: (e, h, 0, 0))

    result = jax.ShapeDtypeStruct(gate_act.shape, bf16)
    return call(
        act_kernel,
        "activate",
        (count, 2),
        [
            (taken, of(D)),
            (gate_act, of(FFE)),
            (grad_hidden, of(FFE)),
            (w_up, spans(w_up.shape)),
        ],
        [(result, of(FFE))] * 3,
        ties=ties,
    )


def bank_kernel(left_ref, right_ref, out_ref):
    rows = left_ref.shape[1] * left_ref.shape[2]
    left, right = left_ref[0].reshape(rows, -1), right_ref[0].reshape(rows, -1)
    out_ref[0] = dot(left, right, 0, 0).astype(bf16)


def bank_grad(left, right, ties=()):
    count, _, capacity, _ = left.shape
    result = jax.ShapeDtypeStruct((count, D, FFE), bf16)
    return call(
        bank_kernel,
        "bank_grad",
        (count, D // part),
        [
            (left, pl.BlockSpec((1, 2, capacity, part), lambda e, d: (e, 0, 0, d))),
            (right, pl.BlockSpec((1, 2, capacity, FFE), lambda e, d: (e, 0, 0, 0))),
        ],
        [(result, pl.BlockSpec((1, part, FFE), lambda e, d: (e, d, 0)))],
        ties=ties,
    )[0]


def combine_kernel(scaled, acts, h, *refs):
    act_refs, w_refs = refs[:acts], refs[acts : 2 * acts]
    column_ref, slot_ref, weight_ref = refs[2 * acts : 2 * acts + 3]
    out_refs, (pick_ref, rows_ref, scale_ref) = refs[2 * acts + 3 : -3], refs[-3:]
    count, _, capacity, _ = act_refs[0].shape
    half, stride = pick_ref.shape[0], rows_ref.shape[0] // count

    @pl.when(pl.program_id(0) == 0)
    def _():
        rows_ref[...] = jnp.zeros_like(rows_ref)
        place = lax.broadcasted_iota(jnp.int32, (half, stride), 1)
        for e in range(count):
            pick = (place == column_ref[e, 0]).astype(f32).astype(bf16)
            pick_ref[:, e * stride : (e + 1) * stride] = pick
            if scaled:
                scale_ref[e] = slot_weights(
                    slot_ref[e, h : h + 1, :], weight_ref[e, h : h + 1, :], capacity
                )

    for e in range(count):
        grads = [dot(a_ref[e, 0], w_ref[e], 1, 1) for a_ref, w_ref in zip(act_refs, w_refs)]
        rows = sum(grads[1:], grads[0])
        if scaled:
            rows = rows * scale_ref[e]
        rows_ref[e * stride : e * stride + capacity, :] = rows.astype(bf16)
    n = out_refs[0].shape[0]
    for b, ref in enumerate(out_refs):
        ref[...] = dot(pick_ref[b * n : (b + 1) * n, :], rows_ref[...], 1, 0).astype(bf16)


def combine(acts, banks, columns, slots, weights, h, blocks, scaled, ties=()):
    count, _, capacity, _ = acts[0].shape
    half = columns.shape[2]
    stride = -(-capacity // 128) * 128
    result = jax.ShapeDtypeStruct((half // blocks, D), bf16)
    once = pl.Buffered(buffer_count=1)
    act = pl.BlockSpec((count, 1, capacity, FFE), lambda d: (0, h, 0, 0), pipeline_mode=once)
    column = pl.BlockSpec((count, 1, half, 1), lambda d: (0, h, 0, 0), pipeline_mode=once)
    return call(
        lambda *refs: combine_kernel(scaled, len(acts), h, *refs),
        "combine",
        (D // part,),
        [(a, act) for a in acts]
        + [(w, pl.BlockSpec((count, part, FFE), lambda d: (0, d, 0))) for w in banks]
        + [(columns, column)]
        + [(v, whole_of(v.shape)) for v in (slots, weights)],
        [(result, pl.BlockSpec((half // blocks, part), lambda d: (0, d)))] * blocks,
        scratch=[
            pltpu.VMEM((half, count * stride), bf16),
            pltpu.VMEM((count * stride, part), bf16),
            pltpu.VMEM((count, capacity, 1), f32),
        ],
        ties=ties,
    )


def body(
    layer_input,
    cotangent,
    segments,
    routes,
    route_weights,
    gain_attention,
    gain_experts,
    query_proj,
    key_proj,
    value_proj,
    output_proj,
    head_gains,
    expert_gate,
    expert_up,
    expert_down,
):
    micro, rows, _ = layer_input.shape
    nf, ns = lax.axis_size("fsdp"), lax.axis_size("seq")
    seq_index = lax.axis_index("seq")
    seq_order = relative_order("seq")
    tokens = micro * rows
    group = rows * ns
    half = group * micro // 2
    heads_local = H // ns
    width = heads_local * HD
    local_experts = expert_gate.shape[0]
    experts = local_experts * ns
    capacity = micro * ns // 2 * min(rows, 3 * rows * TOP // (2 * experts))
    share = D // (nf * ns)

    def spread(value, axis):
        return lax.all_gather(value, "fsdp", axis=axis, tiled=True)

    def gather_tokens(value):
        blocks = jnp.concatenate(ring_gather(value, "seq", split=True), axis=0)
        return blocks.reshape((ns,) + value.shape)

    columns = [
        lax.dynamic_slice_in_dim(w, seq_index * width, width, axis=1).reshape(-1, heads_local, HD)
        for w in (query_proj, key_proj, value_proj)
    ]
    columns = jnp.stack(columns, axis=2).reshape(-1, 3 * width)
    extra = jnp.pad(jnp.stack([gain_attention, gain_experts], axis=1), ((0, 0), (0, HD - 2)))
    w_first = spread(jnp.concatenate([columns, extra], axis=1), 0)
    w_qkv = w_first[:, : 3 * width]
    gain_one = w_first[:, 3 * width].astype(f32)
    gain_two = w_first[:, 3 * width + 1].astype(f32)
    w_down = spread(expert_down, 1)
    w_output = spread(output_proj, 0)
    w_gate = spread(expert_gate, 1)
    w_up = spread(expert_up, 1)

    weight_high = route_weights.astype(bf16)
    weight_low = (route_weights - weight_high.astype(f32)).astype(bf16)
    packed = jnp.concatenate(
        [layer_input, routes.astype(bf16), weight_high, weight_low], axis=-1
    )
    packed = jnp.pad(packed, ((0, 0), (0, 0), (0, HD - 3 * TOP)))
    packed = x_all = gather_tokens(packed)
    x_wide = packed[..., :D].astype(f32)
    inv_all = rms_scale(x_wide)
    h_one = (x_wide * inv_all * gain_one).astype(bf16)
    qkv = jnp.einsum("smtd,de->smte", h_one, w_qkv, preferred_element_type=f32).astype(bf16)

    places = (seq_order[:, None] * rows + jnp.arange(rows)[None, :]).reshape(-1)
    lane = jnp.arange(HD) % (HD // 2)
    frequency = jnp.exp(-jnp.log(rope_base) * (2.0 * lane.astype(f32) / HD))
    angles = places.astype(f32)[:, None] * frequency[None, :]
    sign = jnp.where(jnp.arange(HD) < HD // 2, -1.0, 1.0)
    segment = reorder(segments.reshape(micro, ns, rows), seq_order, axis=1).reshape(micro, group)
    tables = (
        jnp.cos(angles),
        jnp.sin(angles) * sign,
        segment[:, None, :],
        segment[:, :, None],
        head_gains.astype(f32),
    )
    o_heads = attend(qkv, tables)

    inverse_seq = jnp.argsort(seq_order)
    o_heads = reorder(o_heads, inverse_seq, axis=0)
    g_blocks, g_next = ring_gather(
        after(cotangent, packed), "seq", (lambda _: qkv, lambda _: o_heads), True, stop=2
    )
    o_heads = after(o_heads, g_next)
    o_back = lax.all_to_all(o_heads, "seq", split_axis=0, concat_axis=0, tiled=True)
    o_rows = jnp.moveaxis(o_back, 0, 2).reshape(tokens, D)

    x_rows = layer_input.astype(f32).reshape(tokens, D)
    middle = x_rows + jnp.dot(o_rows, w_output, preferred_element_type=f32)
    inv_two = rms_scale(middle)
    normed_two = middle * inv_two
    h_two_own = (normed_two * gain_two).astype(bf16).reshape(micro, rows, D)
    h_blocks = ring_gather(h_two_own, "seq", (), True)

    packed = packed[..., D : D + 3 * TOP].astype(f32)
    packed = packed.reshape(2, half, 3 * TOP)
    route_all = packed[..., :TOP].astype(jnp.int32)
    weight_all = packed[..., TOP : 2 * TOP] + packed[..., 2 * TOP :]
    mine = seq_index * local_experts + jnp.arange(local_experts)
    hit = route_all[:, :, None, :] == mine[None, None, :, None]
    chosen = jnp.any(hit, axis=-1)
    weight_of = jnp.sum(jnp.where(hit, weight_all[:, :, None, :], 0.0), axis=-1)
    block = 128
    counted = chosen.reshape(2, half // block, block, local_experts).astype(f32)
    below = jnp.tril(jnp.ones((block, block), f32), -1)
    inside = jnp.einsum("ab,mkbe->mkae", below, counted)
    sums = jnp.sum(counted, axis=2)
    before = jnp.cumsum(sums, axis=1) - sums
    slot = (inside + before[:, :, None, :]).reshape(2, half, local_experts).astype(jnp.int32)
    slots = jnp.transpose(jnp.where(chosen, slot, -1), (2, 0, 1))
    weights = jnp.transpose(weight_of, (2, 0, 1))
    slot_columns = slots[..., None]

    grad_top = cotangent.astype(f32).reshape(tokens, D)
    done = {}

    def keep(**found):
        done.update(found)
        return next(iter(found.values()))

    def combined(acts, banks, h, scaled, ties=()):
        return combine(acts, banks, slot_columns, slots, weights, h, ns // 2, scaled, ties)

    g_blocks = ring_gather(after(g_next, h_blocks[-1]), "seq", (), True, g_blocks)

    def grad_work(_):
        grad_rows, grad_hidden = dispatch(g_blocks, slots, weights, w_down, capacity, True)
        return keep(grad_rows=grad_rows, grad_hidden=grad_hidden)

    def take_work(_):
        taken, gate_act = dispatch(
            h_blocks, slots, weights, w_gate, capacity, False, (done["grad_rows"],)
        )
        return keep(taken=taken, gate_act=gate_act)

    o_all = ring_gather(
        after(o_heads.reshape(group * micro, width), g_blocks[-1]), "seq", (grad_work, take_work), True
    )
    o_all = o_all[:-2] + [jnp.concatenate(o_all[-2:], axis=0)] if len(o_all) > ns else o_all
    grad_rows, taken = done["grad_rows"], done["taken"]
    hidden, grad_gate_act, grad_up_act = activate(
        taken, done["gate_act"], done["grad_hidden"], w_up, (o_all[-1],)
    )
    first = combined((grad_gate_act, grad_up_act), (w_gate, w_up), 0, False)
    second = combined((grad_gate_act, grad_up_act), (w_gate, w_up), 1, False, (first[0],))

    def down_work(ties):
        return keep(whole_down=bank_grad(grad_rows, hidden, ties))

    def down_then(moved):
        keep(sum_down=after(done["whole_down"], *moved))

    def mixed_work(h):
        def work(ties):
            mixed = combined((hidden,), (w_down,), h, True, ties)
            done.setdefault("mixed", []).extend(mixed)
            return mixed[0]

        return work

    parts = [v.reshape(micro, rows, D) for v in list(first) + list(second)]
    grad_h_two = ring_scatter(
        parts,
        "seq",
        (lambda _: second[0], down_work, mixed_work(0), mixed_work(1)),
        {
            1: down_then,
            3: lambda moved: keep(last=moved),
        },
    ).reshape(tokens, D)

    def bank_sum(whole):
        return lax.psum_scatter(whole, "fsdp", scatter_dimension=1, tiled=True).astype(f32)

    grad_down = bank_sum(done["sum_down"])

    grad_gain_two = jnp.sum(grad_h_two * normed_two, axis=0)
    grad_unit = grad_h_two * gain_two
    grad_middle = grad_top + inv_two * (
        grad_unit - normed_two * jnp.mean(grad_unit * normed_two, axis=-1, keepdims=True)
    )
    grad_attn = grad_middle.astype(bf16)
    grad_o = jnp.einsum("te,de->td", grad_attn, w_output, preferred_element_type=f32).astype(bf16)

    def to_heads(value):
        cut = value.reshape(micro, rows, ns, width)
        return lax.all_to_all(
            jnp.moveaxis(cut, 2, 0), "seq", split_axis=0, concat_axis=0, tiled=True
        )

    whole_gate = bank_grad(taken, grad_gate_act, (grad_o,))
    (do_blocks,) = together((whole_gate,), to_heads(grad_o))
    grad_gate = bank_sum(after(whole_gate, do_blocks))
    do_heads = reorder(do_blocks, seq_order)

    mixed = [v.reshape(micro, rows, D) for v in done["mixed"]]
    k = sizes("seq")[1] + 1 % sizes("seq")[1]
    mixed[k] = after(mixed[k], do_blocks)
    grad_qkv, grad_head = attend_back(qkv, do_heads, tables)
    part_h_one, grad_gain_one = part_grads(grad_qkv, w_first, x_all, inv_all)
    one, columns = together(
        (grad_gain_one,), row_move(mixed, 1, "seq"), to_heads(after(grad_attn, do_blocks))
    )

    total = one
    part_h_one = [v.reshape(micro, rows, D) for v in part_h_one]
    part_h_one[k] = after(part_h_one[k], total)
    gains = jnp.pad(jnp.stack([grad_gain_one, grad_gain_two], axis=1), ((0, 0), (0, HD - 2)))
    whole = proj_grads(
        h_one,
        grad_qkv,
        o_all,
        columns.reshape(micro * group, width),
        gains,
        relative_order("fsdp"),
        inverse_seq,
        (total,),
    )
    left = exchanges()
    head = jnp.sum(after(grad_head, total), axis=0)

    def exchange(head):
        axis, pairs = left.pop(0)
        return lax.ppermute(head, axis, pairs)

    total = ahead(row_sum(total, mixed, 1, "seq"), "seq")
    head = head + exchange(head)
    total, two, one, moved = together(
        (whole[0],),
        total,
        row_move(mixed, 2, "seq"),
        row_move(part_h_one, 1, "seq"),
        exchange(head),
    )
    head = head + moved

    whole_up = bank_grad(taken, grad_up_act, (one,))
    whole = [after(v, one) for v in whole]
    owned = ring_scatter(whole, "fsdp", (None, lambda _: whole_up)).astype(bf16)

    total = ahead(add(row_sum(two, mixed, 2, "seq"), total).astype(bf16), "seq")
    grad_total = ahead(row_sum(one, part_h_one, 1, "seq"), "seq")
    total, grad_total, three, two, owned = together(
        (whole_up,),
        total,
        grad_total,
        row_move(mixed, 3, "seq"),
        row_move(part_h_one, 2, "seq"),
        owned,
    )
    grad_up = bank_sum(after(whole_up, owned))
    owned = lax.all_to_all(
        owned.reshape(ns, share, -1), "seq", split_axis=0, concat_axis=0, tiled=True
    )

    grad_total = add(row_sum(two, part_h_one, 2, "seq"), grad_total).astype(bf16)
    grad_total, zero, moved, owned = together(
        (grad_down,),
        ahead(grad_total, "seq"),
        row_move(part_h_one, 3, "seq"),
        exchange(head),
        owned,
    )
    head = head + moved

    k = 1 % sizes("seq")[1]
    mixed[k], part_h_one[k] = after(mixed[k], owned), after(part_h_one[k], owned)
    total = ahead(add(row_sum(three, mixed, 3, "seq"), total).astype(bf16), "seq")
    grad_total = add(row_sum(zero, part_h_one, 3, "seq"), grad_total).astype(bf16)
    grad_total, zero, moved, last, total = together(
        (grad_gate,),
        ahead(grad_total, "seq"),
        row_move(part_h_one, 0, "seq"),
        exchange(head),
        row_move(mixed, 0, "seq"),
        total,
    )
    head = head + moved
    mixed = add(row_sum(last, mixed, 0, "seq"), total).reshape(tokens, D)
    layer_output = (middle + mixed).astype(bf16).reshape(micro, rows, D)
    while left:
        head = head + exchange(head)
    grad_head_gains = head
    grad_h_one = add(row_sum(zero, part_h_one, 0, "seq"), grad_total).reshape(tokens, D)
    inv_one = rms_scale(x_rows)
    normed_one = x_rows * inv_one
    grad_unit = grad_h_one * gain_one
    input_grad = grad_middle + inv_one * (
        grad_unit - normed_one * jnp.mean(grad_unit * normed_one, axis=-1, keepdims=True)
    )
    input_grad = input_grad.reshape(micro, rows, D)
    owned = owned.astype(f32)
    of_qkv = owned[..., : 3 * width].reshape(ns, share, heads_local, 3, HD)
    grad_query, grad_key, grad_value = (
        jnp.moveaxis(of_qkv[..., k, :], 0, 1).reshape(share, D) for k in range(3)
    )
    grad_output = jnp.moveaxis(owned[..., 3 * width : 4 * width], 0, 1).reshape(share, D)
    of_gains = jnp.sum(owned[..., 4 * width : 4 * width + 2], axis=0)
    return (
        layer_output,
        input_grad,
        of_gains[:, 0],
        of_gains[:, 1],
        grad_query,
        grad_key,
        grad_value,
        grad_output,
        grad_head_gains,
        grad_gate,
        grad_up,
        grad_down,
    )


def solution(mesh):
    placed = (
        P(None, ("fsdp", "seq"), None),
        P(None, ("fsdp", "seq"), None),
        P(None, "fsdp"),
        P(None, ("fsdp", "seq"), None),
        P(None, ("fsdp", "seq"), None),
        P("fsdp"),
        P("fsdp"),
        P("fsdp", None),
        P("fsdp", None),
        P("fsdp", None),
        P("fsdp", None),
        P(),
        P("seq", "fsdp", None),
        P("seq", "fsdp", None),
        P("seq", "fsdp", None),
    )
    return jax.shard_map(
        body,
        mesh=mesh,
        in_specs=placed,
        out_specs=(
            P(None, ("fsdp", "seq"), None),
            P(None, ("fsdp", "seq"), None),
            P(("fsdp", "seq")),
            P(("fsdp", "seq")),
            P(("fsdp", "seq"), None),
            P(("fsdp", "seq"), None),
            P(("fsdp", "seq"), None),
            P(("fsdp", "seq"), None),
            P(),
            P("seq", "fsdp", None),
            P("seq", "fsdp", None),
            P("seq", "fsdp", None),
        ),
        check_vma=False,
    )
```

```python
import math

import jax
import jax.numpy as jnp
from jax import lax
from jax.experimental import pallas as pl
from jax.experimental.pallas import tpu as pltpu
from jax.sharding import PartitionSpec as P

D = 2048
H = 16
HD = 128
FFE = 1024
TOP = 8
SEQ_LEN = 1024

eps = 1e-06
rope_base = 10000.0
masked_score = -1e30
f32 = jnp.float32
little = pl.CostEstimate(flops=1, bytes_accessed=1, transcendentals=0)
bf16 = jnp.bfloat16


def shift(value, axis, outer, inner, by_outer, by_inner):
    pairs = []
    for a in range(outer):
        for b in range(inner):
            there = ((a + by_outer) % outer) * inner + (b + by_inner) % inner
            pairs.append((a * inner + b, there))
    return lax.ppermute(value, axis, pairs)


def sizes(axis):
    count = lax.axis_size(axis)
    return (count // 2, 2) if axis == "fsdp" else (4, count // 4)


def after(value, *others):
    others = [v for v in others if v is not None]
    if not others:
        return value
    anywhere = pl.BlockSpec(memory_space=pl.ANY)
    return pl.pallas_call(
        lambda *refs: None,
        in_specs=[anywhere] * (1 + len(others)),
        out_specs=anywhere,
        out_shape=jax.ShapeDtypeStruct(value.shape, value.dtype),
        input_output_aliases={0: 0},
        cost_estimate=little,
        name="after",
    )(value, *others)


def together(work, *moved):
    moved = list(moved)
    for k in range(len(moved)):
        moved[k] = after(moved[k], *work, *moved[:k], *moved[k + 1 :])
    return moved


def ring_gather(value, axis, work=None, split=False, blocks=(), stop=None):
    outer, inner = sizes(axis)
    blocks, arrived = list(blocks), []
    for a in range(len(blocks) // inner, outer if stop is None else stop):
        row = [value]
        for b in range(1, inner):
            row.append(shift(row[-1], axis, outer, inner, 0, 1))
        moved = row[1:]
        if a + 1 < outer:
            moved.append(shift(value, axis, outer, inner, 1, 0))
        last = split and inner == 2 and a + 1 == outer
        if last:
            cut = value.shape[0] // 2
            moved = [
                shift(value[:cut], axis, outer, inner, 0, 1),
                shift(blocks[-1][cut:], axis, outer, inner, 1, 0),
            ]
        if work is not None:
            moved = together([f(arrived) for f in work[a : a + 1] if f], *moved)
        blocks += [value] + (moved if last else moved[: inner - 1])
        value, arrived = moved[-1], moved
    return blocks if stop is None else (blocks, value)


def row_move(parts, a, axis):
    outer, inner = sizes(axis)
    row = parts[a * inner + 1 % inner]
    for b in range(2, inner):
        row = shift(row, axis, outer, inner, 0, 1)
        row = (row.astype(f32) + parts[a * inner + b].astype(f32)).astype(bf16)
    return shift(row, axis, outer, inner, 0, 1) if inner > 1 else row


def row_sum(moved, parts, a, axis):
    total = moved.astype(f32) + parts[a * sizes(axis)[1]].astype(f32)
    return total.astype(bf16)


def ahead(value, axis):
    return shift(value, axis, *sizes(axis), 1, 0)


def add(one, other):
    return one.astype(f32) + other.astype(f32)


def ring_scatter(parts, axis, work=(), then={}):
    outer, _ = sizes(axis)
    total, arrived = None, []
    for step in range(outer):
        a = (step + 1) % outer
        moved = [row_move(parts, a, axis)]
        if step:
            moved.append(ahead(total, axis))
        moved = together([f(arrived) for f in work[step : step + 1] if f], *moved)
        if step in then:
            then[step](moved)
        arrived = moved
        total = row_sum(moved[0], parts, a, axis)
        if step:
            total = add(total, moved[1])
        if step and step + 1 < outer:
            total = total.astype(bf16)
    return total


def relative_order(axis):
    outer, inner = sizes(axis)
    me = lax.axis_index(axis)
    a, b = me // inner, me % inner
    k = jnp.arange(outer * inner)
    return ((a - k // inner) % outer) * inner + (b - k % inner) % inner


def reorder(value, order, axis=0):
    value = jnp.moveaxis(value, axis, 0)
    value = value.at[order].get(mode="promise_in_bounds", unique_indices=True)
    return jnp.moveaxis(value, 0, axis)


def rms_scale(values):
    return lax.rsqrt(jnp.mean(values * values, axis=-1, keepdims=True) + eps)


def exchanges():
    steps = []
    for axis in ("fsdp", "seq"):
        count = lax.axis_size(axis)
        for k in range(count.bit_length() - 1):
            steps.append((axis, [(i, i ^ (1 << k)) for i in range(count)]))
    return steps


def turn(values, cosine, sine):
    return values * cosine + pltpu.roll(values, HD // 2, 1) * sine


def turn_back(values, cosine, sine):
    return values * cosine - pltpu.roll(values, HD // 2, 1) * sine


def dot(left, right, left_dim, right_dim):
    return lax.dot_general(
        left, right, (((left_dim,), (right_dim,)), ((), ())), preferred_element_type=f32
    )


def attend_kernel(tile, qkv_ref, cos_ref, sin_ref, seg_row_ref, seg_col_ref, gain_ref, o_ref):
    blocks, _, rows, _ = qkv_ref.shape
    group = blocks * rows
    cosine, sine = cos_ref[...], sin_ref[...]

    def turned(part, row):
        raw = qkv_ref[:, 0, :, part * HD : (part + 1) * HD].reshape(group, HD).astype(f32)
        return turn(raw * rms_scale(raw) * gain_ref[row : row + 1, :], cosine, sine).astype(bf16)

    queries, keys = turned(0, 0), turned(1, 1)
    values = qkv_ref[:, 0, :, 2 * HD : 3 * HD].reshape(group, HD)
    seg_row = seg_row_ref[0]
    for start in range(0, group, tile):
        scores = dot(queries[start : start + tile], keys, 1, 1) * (1.0 / math.sqrt(HD))
        allowed = seg_col_ref[0, start : start + tile, :] == seg_row
        scores = jnp.where(allowed, scores, masked_score)
        powered = jnp.exp(scores - jnp.max(scores, axis=-1, keepdims=True))
        scale = 1.0 / jnp.sum(powered, axis=-1, keepdims=True)
        attended = dot((powered * scale).astype(bf16), values, 1, 0).astype(bf16)
        o_ref[start // rows : (start + tile) // rows, 0, :, :] = attended.reshape(
            tile // rows, rows, HD
        )


def attend_back_kernel(
    tile,
    qkv_ref,
    do_ref,
    cos_ref,
    sin_ref,
    seg_row_ref,
    seg_col_ref,
    gain_ref,
    grad_ref,
    grad_gain_ref,
):
    blocks, _, rows, _ = qkv_ref.shape
    group = blocks * rows
    cosine, sine = cos_ref[...], sin_ref[...]
    scaling = 1.0 / math.sqrt(HD)

    def normed(part):
        raw = qkv_ref[:, 0, :, part * HD : (part + 1) * HD].reshape(group, HD).astype(f32)
        inverse = rms_scale(raw)
        return raw * inverse, inverse

    def turned(part):
        return turn(normed(part)[0] * gain_ref[part : part + 1, :], cosine, sine).astype(bf16)

    def finish(part, grad_turned):
        unit, inverse = normed(part)
        grad_scaled = turn_back(grad_turned, cosine, sine)
        grad_gain_ref[0, part : part + 1, :] = jnp.sum(grad_scaled * unit, axis=0, keepdims=True)
        grad_unit = grad_scaled * gain_ref[part : part + 1, :]
        grad_raw = inverse * (
            grad_unit - unit * jnp.mean(grad_unit * unit, axis=-1, keepdims=True)
        )
        return grad_raw

    def put(part, value):
        grad_ref[:, 0, :, part * HD : (part + 1) * HD] = value.astype(bf16).reshape(
            blocks, rows, HD
        )

    queries, keys = turned(0), turned(1)
    values = qkv_ref[:, 0, :, 2 * HD : 3 * HD].reshape(group, HD)
    grad_out = do_ref[:, 0, :, :].reshape(group, HD)
    seg_row = seg_row_ref[0]
    grad_query = []
    grad_key = jnp.zeros((group, HD), f32)
    grad_value = jnp.zeros((group, HD), f32)
    for start in range(0, group, tile):
        part = queries[start : start + tile]
        grad_part = grad_out[start : start + tile]
        scores = dot(part, keys, 1, 1) * scaling
        allowed = seg_col_ref[0, start : start + tile, :] == seg_row
        scores = jnp.where(allowed, scores, masked_score)
        powered = jnp.exp(scores - jnp.max(scores, axis=-1, keepdims=True))
        probabilities = powered * (1.0 / jnp.sum(powered, axis=-1, keepdims=True))
        grad_probs = dot(grad_part, values, 1, 1)
        centre = jnp.sum(probabilities * grad_probs, axis=-1, keepdims=True)
        grad_scores = (probabilities * (grad_probs - centre)).astype(bf16)
        grad_query.append(dot(grad_scores, keys, 1, 0) * scaling)
        grad_key = grad_key + dot(grad_scores, part, 0, 0)
        grad_value = grad_value + dot(probabilities.astype(bf16), grad_part, 0, 0)
    put(0, finish(0, jnp.concatenate(grad_query, axis=0)))
    put(1, finish(1, grad_key * scaling))
    put(2, grad_value)


def attention_specs(ns, micro, rows, heads):
    group = ns * rows
    tile = max(rows, 256)
    return (
        tile,
        pl.BlockSpec((ns, 1, rows, 3 * HD), lambda m, h: (0, m, 0, h)),
        pl.BlockSpec((ns, 1, rows, HD), lambda m, h: (0, m, 0, h)),
        [
            pl.BlockSpec((group, HD), lambda m, h: (0, 0)),
            pl.BlockSpec((group, HD), lambda m, h: (0, 0)),
            pl.BlockSpec((1, 1, group), lambda m, h: (m, 0, 0)),
            pl.BlockSpec((1, group, 1), lambda m, h: (m, 0, 0)),
            pl.BlockSpec((2, HD), lambda m, h: (0, 0)),
        ],
    )


def attend(qkv, tables):
    ns, micro, rows, width = qkv.shape
    heads = width // (3 * HD)
    tile, wide, narrow, shared = attention_specs(ns, micro, rows, heads)
    group = ns * rows
    return pl.pallas_call(
        lambda *refs: attend_kernel(tile, *refs),
        grid=(micro, heads),
        in_specs=[wide] + shared,
        out_specs=narrow,
        out_shape=jax.ShapeDtypeStruct((ns, micro, rows, heads * HD), bf16),
        compiler_params=pltpu.CompilerParams(vmem_limit_bytes=40 * 2**20),
        cost_estimate=little,
        name="attend",
    )(qkv, *tables)


def attend_back(qkv, grad_out, tables, ties=()):
    ns, micro, rows, width = qkv.shape
    heads = width // (3 * HD)
    tile, wide, narrow, shared = attention_specs(ns, micro, rows, heads)
    group = ns * rows
    return pl.pallas_call(
        lambda *refs: attend_back_kernel(tile, *refs[:7], *refs[-2:]),
        grid=(micro, heads),
        in_specs=[wide, narrow] + shared + [pl.BlockSpec(memory_space=pl.ANY)] * len(ties),
        out_specs=[wide, pl.BlockSpec((1, 2, HD), lambda m, h: (m * heads + h, 0, 0))],
        out_shape=[
            jax.ShapeDtypeStruct((ns, micro, rows, width), bf16),
            jax.ShapeDtypeStruct((micro * heads, 2, HD), f32),
        ],
        compiler_params=pltpu.CompilerParams(vmem_limit_bytes=40 * 2**20),
        cost_estimate=little,
        name="attend_back",
    )(qkv, grad_out, *tables, *ties)


def part_kernel(grad_ref, w_ref, x_ref, inv_ref, *out_refs):
    out_refs, gain_ref = out_refs[:-1], out_refs[-1]
    rows = out_refs[0].shape[0]
    gain = jnp.zeros(gain_ref.shape, f32)
    for b, ref in enumerate(out_refs):
        span = slice(b * rows, (b + 1) * rows)
        wide = dot(grad_ref[span, :], w_ref[...], 1, 1)
        ref[...] = wide.astype(bf16)
        normed = x_ref[span, :].astype(f32) * inv_ref[span, :]
        gain = gain + jnp.sum(wide * normed, axis=0, keepdims=True)
    gain_ref[...] = gain


def part_grads(grad_qkv, w_first, x_all, inv_all, ties=()):
    blocks = grad_qkv.shape[0]
    width = grad_qkv.shape[-1]
    count = grad_qkv.size // width
    block = jax.ShapeDtypeStruct((count // blocks, D), bf16)
    found = call(
        part_kernel,
        "part_grads",
        (D // part,),
        [
            (grad_qkv.reshape(count, width), whole_of((count, width))),
            (w_first, pl.BlockSpec((part, width), lambda d: (d, 0))),
            (x_all.reshape(count, x_all.shape[-1]), pl.BlockSpec((count, part), lambda d: (0, d))),
            (inv_all.reshape(count, 1), whole_of((count, 1))),
        ],
        [(block, pl.BlockSpec((block.shape[0], part), lambda d: (0, d)))] * blocks
        + [(jax.ShapeDtypeStruct((1, D), f32), pl.BlockSpec((1, part), lambda d: (0, d)))],
        ties=ties,
    )
    return found[:-1], found[-1][0]


def proj_kernel(blocks, order_ref, place_ref, h_ref, grad_ref, column_ref, gain_ref, *refs):
    o_refs, out_refs, found_ref = refs[:blocks], refs[blocks:-1], refs[-1]
    k = pl.program_id(0)
    inputs, width = grad_ref.shape[1], column_ref.shape[1]
    owners = found_ref.shape[0] // width
    found_ref[:, :inputs] = dot(h_ref[...], grad_ref[...], 0, 0)
    for j in range(owners):
        place = place_ref[order_ref[k] * owners + j]
        for b in range(blocks):

            @pl.when(place == b)
            def _(b=b, j=j):
                found_ref[j * width : (j + 1) * width, inputs : inputs + width] = dot(
                    o_refs[b][...], column_ref[...], 0, 0
                )

    found_ref[:, inputs + width :] = gain_ref[...]
    for b, ref in enumerate(out_refs):

        @pl.when(k == b)
        def _(ref=ref):
            ref[...] = found_ref[...].astype(bf16)


def proj_grads(h_one, grad_qkv, o_blocks, columns, gains, order, places, ties=()):
    count, inputs = h_one.size // D, grad_qkv.shape[-1]
    width, nf = columns.shape[1], order.shape[0]
    rows, across = D // nf, inputs + width + gains.shape[1]
    result = jax.ShapeDtypeStruct((rows, across), bf16)
    ins = [
        (h_one.reshape(count, D), pl.BlockSpec((count, rows), lambda k, order, _: (0, order[k]))),
        (grad_qkv.reshape(count, inputs), whole_of((count, inputs))),
        (columns, whole_of(columns.shape)),
        (gains, pl.BlockSpec((rows, gains.shape[1]), lambda k, order, _: (order[k], 0))),
    ] + [(v, whole_of(v.shape)) for v in o_blocks]

    def run(*refs):
        lead = 2 + len(ins)
        proj_kernel(len(o_blocks), *refs[:lead], *refs[lead + len(ties) :])

    return pl.pallas_call(
        run,
        grid_spec=pltpu.PrefetchScalarGridSpec(
            num_scalar_prefetch=2,
            grid=(nf,),
            in_specs=[spec for _, spec in ins] + [pl.BlockSpec(memory_space=pl.ANY)] * len(ties),
            out_specs=[whole_of(result.shape)] * nf,
            scratch_shapes=[pltpu.VMEM((rows, across), f32)],
        ),
        out_shape=[result] * nf,
        compiler_params=pltpu.CompilerParams(vmem_limit_bytes=56 * 2**20),
        cost_estimate=little,
        name="proj_grads",
    )(order, places, *[value for value, _ in ins], *ties)


part = 512


def spans(shape, *block):
    block = block or (1,)
    return pl.BlockSpec(
        tuple(block) + tuple(shape[len(block) :]), lambda e, *_: (e,) + (0,) * (len(shape) - 1)
    )


def whole_of(shape):
    return pl.BlockSpec(
        tuple(shape), lambda *_: (0,) * len(shape), pipeline_mode=pl.Buffered(buffer_count=1)
    )


def call(kernel, name, grid, ins, outs, scratch=(), ties=(), aliases={}):
    ties = [t for t in ties if t is not None]
    count = len(ins)

    def run(*refs):
        kernel(*refs[:count], *refs[count + len(ties) :])

    return pl.pallas_call(
        run,
        grid=grid,
        in_specs=[spec for _, spec in ins] + [pl.BlockSpec(memory_space=pl.ANY)] * len(ties),
        out_specs=[spec for _, spec in outs],
        out_shape=[shape for shape, _ in outs],
        scratch_shapes=list(scratch),
        input_output_aliases=aliases,
        compiler_params=pltpu.CompilerParams(vmem_limit_bytes=56 * 2**20),
        cost_estimate=little,
        name=name,
    )(*[value for value, _ in ins], *ties)


def picked(slot_row, capacity):
    place = lax.broadcasted_iota(jnp.int32, (capacity, slot_row.shape[1]), 0)
    return place == slot_row


def slot_weights(slot_row, weight_row, capacity):
    chosen = jnp.where(picked(slot_row, capacity), weight_row, 0.0)
    return jnp.sum(chosen, axis=1, keepdims=True)


def dispatch_kernel(scaled, blocks, *refs):
    value_refs, (slot_ref, weight_ref, w_ref, rows_ref, act_ref) = refs[:blocks], refs[blocks:]
    capacity, half = rows_ref.shape[2], slot_ref.shape[2]
    halves, seen = ([], []), 0
    for ref in value_refs:
        halves[seen // half].append(ref)
        seen += ref.shape[0]
    for h in range(2):
        slot_row = slot_ref[0, h : h + 1, :]
        pick = picked(slot_row, capacity).astype(f32).astype(bf16)
        if scaled:
            scale = slot_weights(slot_row, weight_ref[0, h : h + 1, :], capacity)
        for d in range(0, D, part):
            values = jnp.concatenate(
                [ref[:, d : d + part] for ref in halves[h]], axis=0
            )
            taken = dot(pick, values, 1, 0)
            if scaled:
                taken = taken * scale
            rows_ref[0, h, :, d : d + part] = taken.astype(bf16)
        act_ref[0, h] = dot(rows_ref[0, h], w_ref[0], 1, 0)


def dispatch(
    values, slots, weights, bank, capacity, scaled, ties=(), first=0, count=None, before=()
):
    experts = bank.shape[0]
    count = count or experts
    values = [v.reshape(-1, v.shape[-1]) for v in values]
    rows_shape = (experts, 2, capacity, D)
    act_shape = (experts, 2, capacity, FFE)

    def of(shape):
        return pl.BlockSpec((1,) + shape[1:], lambda e: (first + e,) + (0,) * (len(shape) - 1))

    return call(
        lambda *refs: dispatch_kernel(scaled, len(values), *refs),
        "dispatch",
        (count,),
        [(v, whole_of(v.shape)) for v in values]
        + [(v, of(v.shape)) for v in (slots, weights, bank)],
        [
            (jax.ShapeDtypeStruct(rows_shape, bf16), of(rows_shape)),
            (jax.ShapeDtypeStruct(act_shape, f32), of(act_shape)),
        ],
        ties=tuple(before) + tuple(ties),
        aliases={len(values) + 3 + k: k for k in range(len(before))},
    )


def act_kernel(taken_ref, gate_ref, grad_ref, w_ref, hidden_ref, grad_gate_ref, grad_up_ref):
    for f in range(0, FFE, 256):
        span = slice(f, f + 256)
        up_act = dot(taken_ref[0, 0], w_ref[0, :, span], 1, 0)
        gate_act, grad_hidden = gate_ref[0, 0, :, span], grad_ref[0, 0, :, span]
        gate_sig = jax.nn.sigmoid(gate_act)
        gate_silu = gate_act * gate_sig
        hidden_ref[0, 0, :, span] = (gate_silu * up_act).astype(bf16)
        grad_gate = grad_hidden * up_act * gate_sig * (1.0 + gate_act * (1.0 - gate_sig))
        grad_gate_ref[0, 0, :, span] = grad_gate.astype(bf16)
        grad_up_ref[0, 0, :, span] = (grad_hidden * gate_silu).astype(bf16)


def activate(taken, gate_act, grad_hidden, w_up, ties=()):
    count, _, capacity, _ = taken.shape

    def of(width):
        return pl.BlockSpec((1, 1, capacity, width), lambda e, h: (e, h, 0, 0))

    result = jax.ShapeDtypeStruct(gate_act.shape, bf16)
    return call(
        act_kernel,
        "activate",
        (count, 2),
        [
            (taken, of(D)),
            (gate_act, of(FFE)),
            (grad_hidden, of(FFE)),
            (w_up, spans(w_up.shape)),
        ],
        [(result, of(FFE))] * 3,
        ties=ties,
    )


def bank_kernel(left_ref, right_ref, out_ref):
    rows = left_ref.shape[1] * left_ref.shape[2]
    left, right = left_ref[0].reshape(rows, -1), right_ref[0].reshape(rows, -1)
    out_ref[0] = dot(left, right, 0, 0).astype(bf16)


def bank_grad(left, right, ties=(), first=0, count=None):
    capacity = left.shape[2]
    count = count or left.shape[0]
    result = jax.ShapeDtypeStruct((count, D, FFE), bf16)
    return call(
        bank_kernel,
        "bank_grad",
        (count, D // part),
        [
            (left, pl.BlockSpec((1, 2, capacity, part), lambda e, d: (first + e, 0, 0, d))),
            (right, pl.BlockSpec((1, 2, capacity, FFE), lambda e, d: (first + e, 0, 0, 0))),
        ],
        [(result, pl.BlockSpec((1, part, FFE), lambda e, d: (e, d, 0)))],
        ties=ties,
    )[0]


def combine_kernel(scaled, acts, h, *refs):
    act_refs, w_refs = refs[:acts], refs[acts : 2 * acts]
    column_ref, slot_ref, weight_ref = refs[2 * acts : 2 * acts + 3]
    out_refs, (pick_ref, rows_ref, scale_ref) = refs[2 * acts + 3 : -3], refs[-3:]
    count, _, capacity, _ = act_refs[0].shape
    half, stride = pick_ref.shape[0], rows_ref.shape[0] // count

    @pl.when(pl.program_id(0) == 0)
    def _():
        rows_ref[...] = jnp.zeros_like(rows_ref)
        place = lax.broadcasted_iota(jnp.int32, (half, stride), 1)
        for e in range(count):
            pick = (place == column_ref[e, 0]).astype(f32).astype(bf16)
            pick_ref[:, e * stride : (e + 1) * stride] = pick
            if scaled:
                scale_ref[e] = slot_weights(
                    slot_ref[e, h : h + 1, :], weight_ref[e, h : h + 1, :], capacity
                )

    for e in range(count):
        grads = [dot(a_ref[e, 0], w_ref[e], 1, 1) for a_ref, w_ref in zip(act_refs, w_refs)]
        rows = sum(grads[1:], grads[0])
        if scaled:
            rows = rows * scale_ref[e]
        rows_ref[e * stride : e * stride + capacity, :] = rows.astype(bf16)
    n = out_refs[0].shape[0]
    for b, ref in enumerate(out_refs):
        ref[...] = dot(pick_ref[b * n : (b + 1) * n, :], rows_ref[...], 1, 0).astype(bf16)


def combine(acts, banks, columns, slots, weights, h, blocks, scaled, ties=()):
    count, _, capacity, _ = acts[0].shape
    half = columns.shape[2]
    stride = -(-capacity // 128) * 128
    result = jax.ShapeDtypeStruct((half // blocks, D), bf16)
    once = pl.Buffered(buffer_count=1)
    act = pl.BlockSpec((count, 1, capacity, FFE), lambda d: (0, h, 0, 0), pipeline_mode=once)
    column = pl.BlockSpec((count, 1, half, 1), lambda d: (0, h, 0, 0), pipeline_mode=once)
    return call(
        lambda *refs: combine_kernel(scaled, len(acts), h, *refs),
        "combine",
        (D // part,),
        [(a, act) for a in acts]
        + [(w, pl.BlockSpec((count, part, FFE), lambda d: (0, d, 0))) for w in banks]
        + [(columns, column)]
        + [(v, whole_of(v.shape)) for v in (slots, weights)],
        [(result, pl.BlockSpec((half // blocks, part), lambda d: (0, d)))] * blocks,
        scratch=[
            pltpu.VMEM((half, count * stride), bf16),
            pltpu.VMEM((count * stride, part), bf16),
            pltpu.VMEM((count, capacity, 1), f32),
        ],
        ties=ties,
    )


def body(
    layer_input,
    cotangent,
    segments,
    routes,
    route_weights,
    gain_attention,
    gain_experts,
    query_proj,
    key_proj,
    value_proj,
    output_proj,
    head_gains,
    expert_gate,
    expert_up,
    expert_down,
):
    micro, rows, _ = layer_input.shape
    nf, ns = lax.axis_size("fsdp"), lax.axis_size("seq")
    seq_index = lax.axis_index("seq")
    seq_order = relative_order("seq")
    tokens = micro * rows
    group = rows * ns
    half = group * micro // 2
    heads_local = H // ns
    width = heads_local * HD
    local_experts = expert_gate.shape[0]
    experts = local_experts * ns
    capacity = micro * ns // 2 * min(rows, 3 * rows * TOP // (2 * experts))
    share = D // (nf * ns)

    def spread(value, axis):
        return lax.all_gather(value, "fsdp", axis=axis, tiled=True)

    def gather_tokens(value):
        blocks = jnp.concatenate(ring_gather(value, "seq", split=True), axis=0)
        return blocks.reshape((ns,) + value.shape)

    columns = [
        lax.dynamic_slice_in_dim(w, seq_index * width, width, axis=1).reshape(-1, heads_local, HD)
        for w in (query_proj, key_proj, value_proj)
    ]
    columns = jnp.stack(columns, axis=2).reshape(-1, 3 * width)
    extra = jnp.pad(jnp.stack([gain_attention, gain_experts], axis=1), ((0, 0), (0, HD - 2)))
    w_first = spread(jnp.concatenate([columns, extra], axis=1), 0)
    w_qkv = w_first[:, : 3 * width]
    gain_one = w_first[:, 3 * width].astype(f32)
    gain_two = w_first[:, 3 * width + 1].astype(f32)
    w_down = spread(expert_down, 1)
    w_output = spread(output_proj, 0)
    w_gate = spread(expert_gate, 1)
    w_up = spread(expert_up, 1)

    weight_high = route_weights.astype(bf16)
    weight_low = (route_weights - weight_high.astype(f32)).astype(bf16)
    packed = jnp.concatenate(
        [layer_input, routes.astype(bf16), weight_high, weight_low], axis=-1
    )
    packed = jnp.pad(packed, ((0, 0), (0, 0), (0, HD - 3 * TOP)))
    packed = x_all = gather_tokens(packed)
    x_wide = packed[..., :D].astype(f32)
    inv_all = rms_scale(x_wide)
    h_one = (x_wide * inv_all * gain_one).astype(bf16)
    qkv = jnp.einsum("smtd,de->smte", h_one, w_qkv, preferred_element_type=f32).astype(bf16)

    places = (seq_order[:, None] * rows + jnp.arange(rows)[None, :]).reshape(-1)
    lane = jnp.arange(HD) % (HD // 2)
    frequency = jnp.exp(-jnp.log(rope_base) * (2.0 * lane.astype(f32) / HD))
    angles = places.astype(f32)[:, None] * frequency[None, :]
    sign = jnp.where(jnp.arange(HD) < HD // 2, -1.0, 1.0)
    segment = reorder(segments.reshape(micro, ns, rows), seq_order, axis=1).reshape(micro, group)
    tables = (
        jnp.cos(angles),
        jnp.sin(angles) * sign,
        segment[:, None, :],
        segment[:, :, None],
        head_gains.astype(f32),
    )
    o_heads = attend(qkv, tables)

    o_heads = reorder(o_heads, seq_order, axis=0)
    g_blocks, g_next = ring_gather(
        after(cotangent, packed, *tables), "seq", (lambda _: qkv, lambda _: o_heads), True, stop=2
    )
    o_heads = after(o_heads, g_next)
    o_back = lax.all_to_all(o_heads, "seq", split_axis=0, concat_axis=0, tiled=True)
    o_rows = jnp.moveaxis(o_back, 0, 2).reshape(tokens, D)

    x_rows = layer_input.astype(f32).reshape(tokens, D)
    middle = x_rows + jnp.dot(o_rows, w_output, preferred_element_type=f32)
    inv_two = rms_scale(middle)
    normed_two = middle * inv_two
    h_two_own = (normed_two * gain_two).astype(bf16).reshape(micro, rows, D)
    h_blocks = ring_gather(h_two_own, "seq", (), True)

    packed = packed[..., D : D + 3 * TOP].astype(f32)
    packed = packed.reshape(2, half, 3 * TOP)
    route_all = packed[..., :TOP].astype(jnp.int32)
    weight_all = packed[..., TOP : 2 * TOP] + packed[..., 2 * TOP :]
    mine = seq_index * local_experts + jnp.arange(local_experts)
    hit = route_all[:, :, None, :] == mine[None, None, :, None]
    chosen = jnp.any(hit, axis=-1)
    weight_of = jnp.sum(jnp.where(hit, weight_all[:, :, None, :], 0.0), axis=-1)
    block = 128
    counted = chosen.reshape(2, half // block, block, local_experts).astype(f32)
    below = jnp.tril(jnp.ones((block, block), f32), -1)
    inside = jnp.einsum("ab,mkbe->mkae", below, counted)
    sums = jnp.sum(counted, axis=2)
    before = jnp.cumsum(sums, axis=1) - sums
    slot = (inside + before[:, :, None, :]).reshape(2, half, local_experts).astype(jnp.int32)
    slots = jnp.transpose(jnp.where(chosen, slot, -1), (2, 0, 1))
    weights = jnp.transpose(weight_of, (2, 0, 1))
    slot_columns = slots[..., None]

    grad_top = cotangent.astype(f32).reshape(tokens, D)
    done = {}

    def keep(**found):
        done.update(found)
        return next(iter(found.values()))

    def combined(acts, banks, h, scaled, ties=()):
        return combine(acts, banks, slot_columns, slots, weights, h, ns // 2, scaled, ties)

    g_blocks = ring_gather(after(g_next, h_blocks[-1]), "seq", (), True, g_blocks)

    def grad_work(_):
        grad_rows, grad_hidden = dispatch(g_blocks, slots, weights, w_down, capacity, True)
        return keep(grad_rows=grad_rows, grad_hidden=grad_hidden)

    pair = local_experts // 2

    def take_work(first):
        def work(ties):
            takes = dispatch(
                h_blocks,
                slots,
                weights,
                w_gate,
                capacity,
                False,
                tuple(ties) + (done["grad_rows"],),
                first,
                local_experts - pair if first else pair,
                done.get("takes", ()),
            )
            return keep(taken=takes[0], gate_act=takes[1], takes=takes)

        return work

    def act_work(_):
        acts = activate(done["taken"], done["gate_act"], done["grad_hidden"], w_up)
        return keep(tail=acts[0], acts=acts)

    o_all = ring_gather(
        after(o_heads.reshape(group * micro, width), g_blocks[-1]),
        "seq",
        (grad_work, take_work(0), take_work(pair), act_work),
        True,
    )
    o_all = o_all[:-2] + [jnp.concatenate(o_all[-2:], axis=0)] if len(o_all) > ns else o_all
    grad_rows, taken = done["grad_rows"], done["taken"]
    hidden, grad_gate_act, grad_up_act = done["acts"]
    first = combined((grad_gate_act, grad_up_act), (w_gate, w_up), 0, False, (o_all[-1],))
    whole_down = [bank_grad(grad_rows, hidden, (first[0],), 0, pair)]
    second = combined(
        (grad_gate_act, grad_up_act), (w_gate, w_up), 1, False, (whole_down[0],)
    )

    def mixed_work(h):
        def work(ties):
            if h == 0:
                whole_down.append(bank_grad(grad_rows, hidden, ties, pair, local_experts - pair))
                ties = (whole_down[1],)
            mixed = combined((hidden,), (w_down,), h, True, ties)
            done.setdefault("mixed", []).extend(mixed)
            return mixed[0]

        return work

    def gate_work(ties):
        return keep(whole_gate=bank_grad(taken, grad_gate_act, ties))

    parts = [v.reshape(micro, rows, D) for v in list(first) + list(second)]
    grad_h_two = ring_scatter(
        parts,
        "seq",
        (lambda _: second[0], mixed_work(0), mixed_work(1), gate_work),
        {3: lambda moved: keep(sum_gate=after(done["whole_gate"], *moved))},
    ).reshape(tokens, D)

    def bank_sum(whole):
        return lax.psum_scatter(whole, "fsdp", scatter_dimension=1, tiled=True).astype(f32)

    grad_down = jnp.concatenate([bank_sum(v) for v in whole_down], axis=0)
    grad_gate = bank_sum(done["sum_gate"])

    grad_gain_two = jnp.sum(grad_h_two * normed_two, axis=0)
    grad_unit = grad_h_two * gain_two
    grad_middle = grad_top + inv_two * (
        grad_unit - normed_two * jnp.mean(grad_unit * normed_two, axis=-1, keepdims=True)
    )
    grad_attn = grad_middle.astype(bf16)
    grad_o = jnp.einsum("te,de->td", grad_attn, w_output, preferred_element_type=f32).astype(bf16)

    def to_heads(value):
        cut = value.reshape(micro, rows, ns, width)
        return lax.all_to_all(
            jnp.moveaxis(cut, 2, 0), "seq", split_axis=0, concat_axis=0, tiled=True
        )

    whole_up = bank_grad(taken, grad_up_act, (grad_o,))
    (do_blocks,) = together((whole_up,), to_heads(grad_o))
    grad_up = bank_sum(after(whole_up, do_blocks))
    do_heads = reorder(do_blocks, seq_order)

    mixed = [v.reshape(micro, rows, D) for v in done["mixed"]]
    k = sizes("seq")[1] + 1 % sizes("seq")[1]
    mixed[k] = after(mixed[k], do_blocks)
    grad_qkv, grad_head = attend_back(qkv, do_heads, tables)
    part_h_one, grad_gain_one = part_grads(grad_qkv, w_first, x_all, inv_all)
    one, columns = together(
        (grad_gain_one,), row_move(mixed, 1, "seq"), to_heads(after(grad_attn, do_blocks))
    )

    total = one
    part_h_one = [v.reshape(micro, rows, D) for v in part_h_one]
    part_h_one[k] = after(part_h_one[k], total)
    gains = jnp.pad(jnp.stack([grad_gain_one, grad_gain_two], axis=1), ((0, 0), (0, HD - 2)))
    whole = proj_grads(
        h_one,
        grad_qkv,
        o_all,
        columns.reshape(micro * group, width),
        gains,
        relative_order("fsdp"),
        seq_order,
        (total,),
    )
    left = exchanges()
    head = jnp.sum(after(grad_head, total), axis=0)

    def exchange(head):
        axis, pairs = left.pop(0)
        return lax.ppermute(head, axis, pairs)

    total = ahead(row_sum(total, mixed, 1, "seq"), "seq")
    head = head + exchange(head)
    total, two, one, moved = together(
        (whole[0],),
        total,
        row_move(mixed, 2, "seq"),
        row_move(part_h_one, 1, "seq"),
        exchange(head),
    )
    head = head + moved

    whole = [after(v, one) for v in whole]
    owned = ring_scatter(whole, "fsdp").astype(bf16)

    total = ahead(add(row_sum(two, mixed, 2, "seq"), total).astype(bf16), "seq")
    grad_total = ahead(row_sum(one, part_h_one, 1, "seq"), "seq")
    total, grad_total, three, two, owned = together(
        (),
        total,
        grad_total,
        row_move(mixed, 3, "seq"),
        row_move(part_h_one, 2, "seq"),
        owned,
    )
    owned = lax.all_to_all(
        owned.reshape(ns, share, -1), "seq", split_axis=0, concat_axis=0, tiled=True
    )

    grad_total = add(row_sum(two, part_h_one, 2, "seq"), grad_total).astype(bf16)
    grad_total, zero, moved, owned = together(
        (grad_down,),
        ahead(grad_total, "seq"),
        row_move(part_h_one, 3, "seq"),
        exchange(head),
        owned,
    )
    head = head + moved

    k = 1 % sizes("seq")[1]
    mixed[k], part_h_one[k] = after(mixed[k], owned), after(part_h_one[k], owned)
    total = ahead(add(row_sum(three, mixed, 3, "seq"), total).astype(bf16), "seq")
    grad_total = add(row_sum(zero, part_h_one, 3, "seq"), grad_total).astype(bf16)
    grad_total, zero, moved, last, total = together(
        (grad_gate,),
        ahead(grad_total, "seq"),
        row_move(part_h_one, 0, "seq"),
        exchange(head),
        row_move(mixed, 0, "seq"),
        total,
    )
    head = head + moved
    mixed = add(row_sum(last, mixed, 0, "seq"), total).reshape(tokens, D)
    layer_output = (middle + mixed).astype(bf16).reshape(micro, rows, D)
    while left:
        head = head + exchange(head)
    grad_head_gains = head
    grad_h_one = add(row_sum(zero, part_h_one, 0, "seq"), grad_total).reshape(tokens, D)
    inv_one = rms_scale(x_rows)
    normed_one = x_rows * inv_one
    grad_unit = grad_h_one * gain_one
    input_grad = grad_middle + inv_one * (
        grad_unit - normed_one * jnp.mean(grad_unit * normed_one, axis=-1, keepdims=True)
    )
    input_grad = input_grad.reshape(micro, rows, D)
    owned = owned.astype(f32)
    of_qkv = owned[..., : 3 * width].reshape(ns, share, heads_local, 3, HD)
    grad_query, grad_key, grad_value = (
        jnp.moveaxis(of_qkv[..., k, :], 0, 1).reshape(share, D) for k in range(3)
    )
    grad_output = jnp.moveaxis(owned[..., 3 * width : 4 * width], 0, 1).reshape(share, D)
    of_gains = jnp.sum(owned[..., 4 * width : 4 * width + 2], axis=0)
    return (
        layer_output,
        input_grad,
        of_gains[:, 0],
        of_gains[:, 1],
        grad_query,
        grad_key,
        grad_value,
        grad_output,
        grad_head_gains,
        grad_gate,
        grad_up,
        grad_down,
    )


def solution(mesh):
    placed = (
        P(None, ("fsdp", "seq"), None),
        P(None, ("fsdp", "seq"), None),
        P(None, "fsdp"),
        P(None, ("fsdp", "seq"), None),
        P(None, ("fsdp", "seq"), None),
        P("fsdp"),
        P("fsdp"),
        P("fsdp", None),
        P("fsdp", None),
        P("fsdp", None),
        P("fsdp", None),
        P(),
        P("seq", "fsdp", None),
        P("seq", "fsdp", None),
        P("seq", "fsdp", None),
    )
    return jax.shard_map(
        body,
        mesh=mesh,
        in_specs=placed,
        out_specs=(
            P(None, ("fsdp", "seq"), None),
            P(None, ("fsdp", "seq"), None),
            P(("fsdp", "seq")),
            P(("fsdp", "seq")),
            P(("fsdp", "seq"), None),
            P(("fsdp", "seq"), None),
            P(("fsdp", "seq"), None),
            P(("fsdp", "seq"), None),
            P(),
            P("seq", "fsdp", None),
            P("seq", "fsdp", None),
            P("seq", "fsdp", None),
        ),
        check_vma=False,
    )
```

```python
import math

import jax
import jax.numpy as jnp
from jax import lax
from jax.experimental import pallas as pl
from jax.experimental.pallas import tpu as pltpu
from jax.sharding import PartitionSpec as P

D = 2048
H = 16
HD = 128
FFE = 1024
TOP = 8
SEQ_LEN = 1024

eps = 1e-06
rope_base = 10000.0
masked_score = -1e30
f32 = jnp.float32
little = pl.CostEstimate(flops=1, bytes_accessed=1, transcendentals=0)
bf16 = jnp.bfloat16


def shift(value, axis, outer, inner, by_outer, by_inner):
    pairs = []
    for a in range(outer):
        for b in range(inner):
            there = ((a + by_outer) % outer) * inner + (b + by_inner) % inner
            pairs.append((a * inner + b, there))
    return lax.ppermute(value, axis, pairs)


def sizes(axis):
    count = lax.axis_size(axis)
    return (count // 2, 2) if axis == "fsdp" else (4, count // 4)


def after(value, *others):
    others = [v for v in others if v is not None]
    if not others:
        return value
    anywhere = pl.BlockSpec(memory_space=pl.ANY)
    return pl.pallas_call(
        lambda *refs: None,
        in_specs=[anywhere] * (1 + len(others)),
        out_specs=anywhere,
        out_shape=jax.ShapeDtypeStruct(value.shape, value.dtype),
        input_output_aliases={0: 0},
        cost_estimate=little,
        name="after",
    )(value, *others)


def together(work, *moved):
    moved = list(moved)
    for k in range(len(moved)):
        moved[k] = after(moved[k], *work, *moved[:k], *moved[k + 1 :])
    return moved


def ring_gather(value, axis, work=None, split=False, blocks=(), stop=None):
    outer, inner = sizes(axis)
    blocks, arrived = list(blocks), []
    for a in range(len(blocks) // inner, outer if stop is None else stop):
        row = [value]
        for b in range(1, inner):
            row.append(shift(row[-1], axis, outer, inner, 0, 1))
        moved = row[1:]
        if a + 1 < outer:
            moved.append(shift(value, axis, outer, inner, 1, 0))
        last = split and inner == 2 and a + 1 == outer
        if last:
            cut = value.shape[0] // 2
            moved = [
                shift(value[:cut], axis, outer, inner, 0, 1),
                shift(blocks[-1][cut:], axis, outer, inner, 1, 0),
            ]
        if work is not None:
            moved = together([f(arrived) for f in work[a : a + 1] if f], *moved)
        blocks += [value] + (moved if last else moved[: inner - 1])
        value, arrived = moved[-1], moved
    return blocks if stop is None else (blocks, value)


def row_move(parts, a, axis):
    outer, inner = sizes(axis)
    row = parts[a * inner + 1 % inner]
    for b in range(2, inner):
        row = shift(row, axis, outer, inner, 0, 1)
        row = (row.astype(f32) + parts[a * inner + b].astype(f32)).astype(bf16)
    return shift(row, axis, outer, inner, 0, 1) if inner > 1 else row


def row_sum(moved, parts, a, axis):
    total = moved.astype(f32) + parts[a * sizes(axis)[1]].astype(f32)
    return total.astype(bf16)


def ahead(value, axis):
    return shift(value, axis, *sizes(axis), 1, 0)


def add(one, other):
    return one.astype(f32) + other.astype(f32)


def ring_scatter(parts, axis, work=(), then={}, beside={}):
    outer, _ = sizes(axis)
    total, arrived = None, []
    for step in range(outer):
        a = (step + 1) % outer
        moved = [row_move(parts, a, axis)]
        if step:
            moved.append(ahead(total, axis))
        moved += beside.get(step, [])
        moved = together([f(arrived) for f in work[step : step + 1] if f], *moved)
        if step in then:
            then[step](moved)
        arrived = moved
        total = row_sum(moved[0], parts, a, axis)
        if step:
            total = add(total, moved[1])
        if step and step + 1 < outer:
            total = total.astype(bf16)
    return total


def relative_order(axis):
    outer, inner = sizes(axis)
    me = lax.axis_index(axis)
    a, b = me // inner, me % inner
    k = jnp.arange(outer * inner)
    return ((a - k // inner) % outer) * inner + (b - k % inner) % inner


def reorder(value, order, axis=0):
    value = jnp.moveaxis(value, axis, 0)
    value = value.at[order].get(mode="promise_in_bounds", unique_indices=True)
    return jnp.moveaxis(value, 0, axis)


def rms_scale(values):
    return lax.rsqrt(jnp.mean(values * values, axis=-1, keepdims=True) + eps)


def exchanges():
    steps = []
    for axis in ("fsdp", "seq"):
        count = lax.axis_size(axis)
        for k in range(count.bit_length() - 1):
            steps.append((axis, [(i, i ^ (1 << k)) for i in range(count)]))
    return steps


def turn(values, cosine, sine):
    return values * cosine + pltpu.roll(values, HD // 2, 1) * sine


def turn_back(values, cosine, sine):
    return values * cosine - pltpu.roll(values, HD // 2, 1) * sine


def dot(left, right, left_dim, right_dim):
    return lax.dot_general(
        left, right, (((left_dim,), (right_dim,)), ((), ())), preferred_element_type=f32
    )


def attend_kernel(tile, qkv_ref, cos_ref, sin_ref, seg_row_ref, seg_col_ref, gain_ref, o_ref):
    blocks, _, rows, _ = qkv_ref.shape
    group = blocks * rows
    cosine, sine = cos_ref[...], sin_ref[...]

    def turned(part, row):
        raw = qkv_ref[:, 0, :, part * HD : (part + 1) * HD].reshape(group, HD).astype(f32)
        return turn(raw * rms_scale(raw) * gain_ref[row : row + 1, :], cosine, sine).astype(bf16)

    queries, keys = turned(0, 0), turned(1, 1)
    values = qkv_ref[:, 0, :, 2 * HD : 3 * HD].reshape(group, HD)
    seg_row = seg_row_ref[0]
    for start in range(0, group, tile):
        scores = dot(queries[start : start + tile], keys, 1, 1) * (1.0 / math.sqrt(HD))
        allowed = seg_col_ref[0, start : start + tile, :] == seg_row
        scores = jnp.where(allowed, scores, masked_score)
        powered = jnp.exp(scores - jnp.max(scores, axis=-1, keepdims=True))
        scale = 1.0 / jnp.sum(powered, axis=-1, keepdims=True)
        attended = dot((powered * scale).astype(bf16), values, 1, 0).astype(bf16)
        o_ref[start // rows : (start + tile) // rows, 0, :, :] = attended.reshape(
            tile // rows, rows, HD
        )


def attend_back_kernel(
    tile,
    qkv_ref,
    do_ref,
    cos_ref,
    sin_ref,
    seg_row_ref,
    seg_col_ref,
    gain_ref,
    grad_ref,
    grad_gain_ref,
):
    blocks, _, rows, _ = qkv_ref.shape
    group = blocks * rows
    cosine, sine = cos_ref[...], sin_ref[...]
    scaling = 1.0 / math.sqrt(HD)

    def normed(part):
        raw = qkv_ref[:, 0, :, part * HD : (part + 1) * HD].reshape(group, HD).astype(f32)
        inverse = rms_scale(raw)
        return raw * inverse, inverse

    def turned(part):
        return turn(normed(part)[0] * gain_ref[part : part + 1, :], cosine, sine).astype(bf16)

    def finish(part, grad_turned):
        unit, inverse = normed(part)
        grad_scaled = turn_back(grad_turned, cosine, sine)
        grad_gain_ref[0, part : part + 1, :] = jnp.sum(grad_scaled * unit, axis=0, keepdims=True)
        grad_unit = grad_scaled * gain_ref[part : part + 1, :]
        grad_raw = inverse * (
            grad_unit - unit * jnp.mean(grad_unit * unit, axis=-1, keepdims=True)
        )
        return grad_raw

    def put(part, value):
        grad_ref[:, 0, :, part * HD : (part + 1) * HD] = value.astype(bf16).reshape(
            blocks, rows, HD
        )

    queries, keys = turned(0), turned(1)
    values = qkv_ref[:, 0, :, 2 * HD : 3 * HD].reshape(group, HD)
    grad_out = do_ref[:, 0, :, :].reshape(group, HD)
    seg_row = seg_row_ref[0]
    grad_query = []
    grad_key = jnp.zeros((group, HD), f32)
    grad_value = jnp.zeros((group, HD), f32)
    for start in range(0, group, tile):
        part = queries[start : start + tile]
        grad_part = grad_out[start : start + tile]
        scores = dot(part, keys, 1, 1) * scaling
        allowed = seg_col_ref[0, start : start + tile, :] == seg_row
        scores = jnp.where(allowed, scores, masked_score)
        powered = jnp.exp(scores - jnp.max(scores, axis=-1, keepdims=True))
        probabilities = powered * (1.0 / jnp.sum(powered, axis=-1, keepdims=True))
        grad_probs = dot(grad_part, values, 1, 1)
        centre = jnp.sum(probabilities * grad_probs, axis=-1, keepdims=True)
        grad_scores = (probabilities * (grad_probs - centre)).astype(bf16)
        grad_query.append(dot(grad_scores, keys, 1, 0) * scaling)
        grad_key = grad_key + dot(grad_scores, part, 0, 0)
        grad_value = grad_value + dot(probabilities.astype(bf16), grad_part, 0, 0)
    put(0, finish(0, jnp.concatenate(grad_query, axis=0)))
    put(1, finish(1, grad_key * scaling))
    put(2, grad_value)


def attention_specs(ns, micro, rows, heads):
    group = ns * rows
    tile = max(rows, 256)
    return (
        tile,
        pl.BlockSpec((ns, 1, rows, 3 * HD), lambda m, h: (0, m, 0, h)),
        pl.BlockSpec((ns, 1, rows, HD), lambda m, h: (0, m, 0, h)),
        [
            pl.BlockSpec((group, HD), lambda m, h: (0, 0)),
            pl.BlockSpec((group, HD), lambda m, h: (0, 0)),
            pl.BlockSpec((1, 1, group), lambda m, h: (m, 0, 0)),
            pl.BlockSpec((1, group, 1), lambda m, h: (m, 0, 0)),
            pl.BlockSpec((2, HD), lambda m, h: (0, 0)),
        ],
    )


def attend(qkv, tables):
    ns, micro, rows, width = qkv.shape
    heads = width // (3 * HD)
    tile, wide, narrow, shared = attention_specs(ns, micro, rows, heads)
    group = ns * rows
    return pl.pallas_call(
        lambda *refs: attend_kernel(tile, *refs),
        grid=(micro, heads),
        in_specs=[wide] + shared,
        out_specs=narrow,
        out_shape=jax.ShapeDtypeStruct((ns, micro, rows, heads * HD), bf16),
        compiler_params=pltpu.CompilerParams(vmem_limit_bytes=40 * 2**20),
        cost_estimate=little,
        name="attend",
    )(qkv, *tables)


def attend_back(qkv, grad_out, tables, ties=()):
    ns, micro, rows, width = qkv.shape
    heads = width // (3 * HD)
    tile, wide, narrow, shared = attention_specs(ns, micro, rows, heads)
    group = ns * rows
    return pl.pallas_call(
        lambda *refs: attend_back_kernel(tile, *refs[:7], *refs[-2:]),
        grid=(micro, heads),
        in_specs=[wide, narrow] + shared + [pl.BlockSpec(memory_space=pl.ANY)] * len(ties),
        out_specs=[wide, pl.BlockSpec((1, 2, HD), lambda m, h: (m * heads + h, 0, 0))],
        out_shape=[
            jax.ShapeDtypeStruct((ns, micro, rows, width), bf16),
            jax.ShapeDtypeStruct((micro * heads, 2, HD), f32),
        ],
        compiler_params=pltpu.CompilerParams(vmem_limit_bytes=40 * 2**20),
        cost_estimate=little,
        name="attend_back",
    )(qkv, grad_out, *tables, *ties)


def part_kernel(grad_ref, w_ref, x_ref, inv_ref, *out_refs):
    out_refs, gain_ref = out_refs[:-1], out_refs[-1]
    rows = out_refs[0].shape[0]
    gain = jnp.zeros(gain_ref.shape, f32)
    for b, ref in enumerate(out_refs):
        span = slice(b * rows, (b + 1) * rows)
        wide = dot(grad_ref[span, :], w_ref[...], 1, 1)
        ref[...] = wide.astype(bf16)
        normed = x_ref[span, :].astype(f32) * inv_ref[span, :]
        gain = gain + jnp.sum(wide * normed, axis=0, keepdims=True)
    gain_ref[...] = gain


def part_grads(grad_qkv, w_first, x_all, inv_all, ties=()):
    blocks = grad_qkv.shape[0]
    width = grad_qkv.shape[-1]
    count = grad_qkv.size // width
    block = jax.ShapeDtypeStruct((count // blocks, D), bf16)
    found = call(
        part_kernel,
        "part_grads",
        (D // part,),
        [
            (grad_qkv.reshape(count, width), whole_of((count, width))),
            (w_first, pl.BlockSpec((part, width), lambda d: (d, 0))),
            (x_all.reshape(count, x_all.shape[-1]), pl.BlockSpec((count, part), lambda d: (0, d))),
            (inv_all.reshape(count, 1), whole_of((count, 1))),
        ],
        [(block, pl.BlockSpec((block.shape[0], part), lambda d: (0, d)))] * blocks
        + [(jax.ShapeDtypeStruct((1, D), f32), pl.BlockSpec((1, part), lambda d: (0, d)))],
        ties=ties,
    )
    return found[:-1], found[-1][0]


def proj_kernel(blocks, order_ref, place_ref, h_ref, grad_ref, column_ref, gain_ref, *refs):
    o_refs, out_refs, found_ref = refs[:blocks], refs[blocks:-1], refs[-1]
    k = pl.program_id(0)
    inputs, width = grad_ref.shape[1], column_ref.shape[1]
    owners = found_ref.shape[0] // width
    found_ref[:, :inputs] = dot(h_ref[...], grad_ref[...], 0, 0)
    for j in range(owners):
        place = place_ref[order_ref[k] * owners + j]
        for b in range(blocks):

            @pl.when(place == b)
            def _(b=b, j=j):
                found_ref[j * width : (j + 1) * width, inputs : inputs + width] = dot(
                    o_refs[b][...], column_ref[...], 0, 0
                )

    found_ref[:, inputs + width :] = gain_ref[...]
    for b, ref in enumerate(out_refs):

        @pl.when(k == b)
        def _(ref=ref):
            ref[...] = found_ref[...].astype(bf16)


def proj_grads(h_one, grad_qkv, o_blocks, columns, gains, order, places, ties=()):
    count, inputs = h_one.size // D, grad_qkv.shape[-1]
    width, nf = columns.shape[1], order.shape[0]
    rows, across = D // nf, inputs + width + gains.shape[1]
    result = jax.ShapeDtypeStruct((rows, across), bf16)
    ins = [
        (h_one.reshape(count, D), pl.BlockSpec((count, rows), lambda k, order, _: (0, order[k]))),
        (grad_qkv.reshape(count, inputs), whole_of((count, inputs))),
        (columns, whole_of(columns.shape)),
        (gains, pl.BlockSpec((rows, gains.shape[1]), lambda k, order, _: (order[k], 0))),
    ] + [(v, whole_of(v.shape)) for v in o_blocks]

    def run(*refs):
        lead = 2 + len(ins)
        proj_kernel(len(o_blocks), *refs[:lead], *refs[lead + len(ties) :])

    return pl.pallas_call(
        run,
        grid_spec=pltpu.PrefetchScalarGridSpec(
            num_scalar_prefetch=2,
            grid=(nf,),
            in_specs=[spec for _, spec in ins] + [pl.BlockSpec(memory_space=pl.ANY)] * len(ties),
            out_specs=[whole_of(result.shape)] * nf,
            scratch_shapes=[pltpu.VMEM((rows, across), f32)],
        ),
        out_shape=[result] * nf,
        compiler_params=pltpu.CompilerParams(vmem_limit_bytes=56 * 2**20),
        cost_estimate=little,
        name="proj_grads",
    )(order, places, *[value for value, _ in ins], *ties)


part = 512


def spans(shape, *block):
    block = block or (1,)
    return pl.BlockSpec(
        tuple(block) + tuple(shape[len(block) :]), lambda e, *_: (e,) + (0,) * (len(shape) - 1)
    )


def whole_of(shape):
    return pl.BlockSpec(
        tuple(shape), lambda *_: (0,) * len(shape), pipeline_mode=pl.Buffered(buffer_count=1)
    )


def call(kernel, name, grid, ins, outs, scratch=(), ties=(), aliases={}):
    ties = [t for t in ties if t is not None]
    count = len(ins)

    def run(*refs):
        kernel(*refs[:count], *refs[count + len(ties) :])

    return pl.pallas_call(
        run,
        grid=grid,
        in_specs=[spec for _, spec in ins] + [pl.BlockSpec(memory_space=pl.ANY)] * len(ties),
        out_specs=[spec for _, spec in outs],
        out_shape=[shape for shape, _ in outs],
        scratch_shapes=list(scratch),
        input_output_aliases=aliases,
        compiler_params=pltpu.CompilerParams(vmem_limit_bytes=56 * 2**20),
        cost_estimate=little,
        name=name,
    )(*[value for value, _ in ins], *ties)


def picked(slot_row, capacity):
    place = lax.broadcasted_iota(jnp.int32, (capacity, slot_row.shape[1]), 0)
    return place == slot_row


def slot_weights(slot_row, weight_row, capacity):
    chosen = jnp.where(picked(slot_row, capacity), weight_row, 0.0)
    return jnp.sum(chosen, axis=1, keepdims=True)


def dispatch_kernel(scaled, blocks, *refs):
    value_refs, (slot_ref, weight_ref, w_ref, rows_ref, act_ref) = refs[:blocks], refs[blocks:]
    capacity, half = rows_ref.shape[2], slot_ref.shape[2]
    halves, seen = ([], []), 0
    for ref in value_refs:
        halves[seen // half].append(ref)
        seen += ref.shape[0]
    for h in range(2):
        slot_row = slot_ref[0, h : h + 1, :]
        pick = picked(slot_row, capacity).astype(f32).astype(bf16)
        if scaled:
            scale = slot_weights(slot_row, weight_ref[0, h : h + 1, :], capacity)
        for d in range(0, D, part):
            values = jnp.concatenate(
                [ref[:, d : d + part] for ref in halves[h]], axis=0
            )
            taken = dot(pick, values, 1, 0)
            if scaled:
                taken = taken * scale
            rows_ref[0, h, :, d : d + part] = taken.astype(bf16)
        act_ref[0, h] = dot(rows_ref[0, h], w_ref[0], 1, 0)


def dispatch(
    values, slots, weights, bank, capacity, scaled, ties=(), first=0, count=None, before=()
):
    experts = bank.shape[0]
    count = count or experts
    values = [v.reshape(-1, v.shape[-1]) for v in values]
    rows_shape = (experts, 2, capacity, D)
    act_shape = (experts, 2, capacity, FFE)

    def of(shape):
        return pl.BlockSpec((1,) + shape[1:], lambda e: (first + e,) + (0,) * (len(shape) - 1))

    return call(
        lambda *refs: dispatch_kernel(scaled, len(values), *refs),
        "dispatch",
        (count,),
        [(v, whole_of(v.shape)) for v in values]
        + [(v, of(v.shape)) for v in (slots, weights, bank)],
        [
            (jax.ShapeDtypeStruct(rows_shape, bf16), of(rows_shape)),
            (jax.ShapeDtypeStruct(act_shape, f32), of(act_shape)),
        ],
        ties=tuple(before) + tuple(ties),
        aliases={len(values) + 3 + k: k for k in range(len(before))},
    )


def act_kernel(taken_ref, gate_ref, grad_ref, w_ref, hidden_ref, grad_gate_ref, grad_up_ref):
    for f in range(0, FFE, 256):
        span = slice(f, f + 256)
        up_act = dot(taken_ref[0, 0], w_ref[0, :, span], 1, 0)
        gate_act, grad_hidden = gate_ref[0, 0, :, span], grad_ref[0, 0, :, span]
        gate_sig = jax.nn.sigmoid(gate_act)
        gate_silu = gate_act * gate_sig
        hidden_ref[0, 0, :, span] = (gate_silu * up_act).astype(bf16)
        grad_gate = grad_hidden * up_act * gate_sig * (1.0 + gate_act * (1.0 - gate_sig))
        grad_gate_ref[0, 0, :, span] = grad_gate.astype(bf16)
        grad_up_ref[0, 0, :, span] = (grad_hidden * gate_silu).astype(bf16)


def activate(taken, gate_act, grad_hidden, w_up, ties=()):
    count, _, capacity, _ = taken.shape

    def of(width):
        return pl.BlockSpec((1, 1, capacity, width), lambda e, h: (e, h, 0, 0))

    result = jax.ShapeDtypeStruct(gate_act.shape, bf16)
    return call(
        act_kernel,
        "activate",
        (count, 2),
        [
            (taken, of(D)),
            (gate_act, of(FFE)),
            (grad_hidden, of(FFE)),
            (w_up, spans(w_up.shape)),
        ],
        [(result, of(FFE))] * 3,
        ties=ties,
    )


def bank_kernel(left_ref, right_ref, out_ref):
    rows = left_ref.shape[1] * left_ref.shape[2]
    left, right = left_ref[0].reshape(rows, -1), right_ref[0].reshape(rows, -1)
    out_ref[0] = dot(left, right, 0, 0).astype(bf16)


def bank_grad(left, right, ties=(), first=0, count=None):
    capacity = left.shape[2]
    count = count or left.shape[0]
    result = jax.ShapeDtypeStruct((count, D, FFE), bf16)
    return call(
        bank_kernel,
        "bank_grad",
        (count, D // part),
        [
            (left, pl.BlockSpec((1, 2, capacity, part), lambda e, d: (first + e, 0, 0, d))),
            (right, pl.BlockSpec((1, 2, capacity, FFE), lambda e, d: (first + e, 0, 0, 0))),
        ],
        [(result, pl.BlockSpec((1, part, FFE), lambda e, d: (e, d, 0)))],
        ties=ties,
    )[0]


def combine_kernel(scaled, acts, h, *refs):
    act_refs, w_refs = refs[:acts], refs[acts : 2 * acts]
    column_ref, slot_ref, weight_ref = refs[2 * acts : 2 * acts + 3]
    out_refs, (pick_ref, rows_ref, scale_ref) = refs[2 * acts + 3 : -3], refs[-3:]
    count, _, capacity, _ = act_refs[0].shape
    half, stride = pick_ref.shape[0], rows_ref.shape[0] // count

    @pl.when(pl.program_id(0) == 0)
    def _():
        rows_ref[...] = jnp.zeros_like(rows_ref)
        place = lax.broadcasted_iota(jnp.int32, (half, stride), 1)
        for e in range(count):
            pick = (place == column_ref[e, 0]).astype(f32).astype(bf16)
            pick_ref[:, e * stride : (e + 1) * stride] = pick
            if scaled:
                scale_ref[e] = slot_weights(
                    slot_ref[e, h : h + 1, :], weight_ref[e, h : h + 1, :], capacity
                )

    for e in range(count):
        grads = [dot(a_ref[e, 0], w_ref[e], 1, 1) for a_ref, w_ref in zip(act_refs, w_refs)]
        rows = sum(grads[1:], grads[0])
        if scaled:
            rows = rows * scale_ref[e]
        rows_ref[e * stride : e * stride + capacity, :] = rows.astype(bf16)
    n = out_refs[0].shape[0]
    for b, ref in enumerate(out_refs):
        ref[...] = dot(pick_ref[b * n : (b + 1) * n, :], rows_ref[...], 1, 0).astype(bf16)


def combine(acts, banks, columns, slots, weights, h, blocks, scaled, ties=()):
    count, _, capacity, _ = acts[0].shape
    half = columns.shape[2]
    stride = -(-capacity // 128) * 128
    result = jax.ShapeDtypeStruct((half // blocks, D), bf16)
    once = pl.Buffered(buffer_count=1)
    act = pl.BlockSpec((count, 1, capacity, FFE), lambda d: (0, h, 0, 0), pipeline_mode=once)
    column = pl.BlockSpec((count, 1, half, 1), lambda d: (0, h, 0, 0), pipeline_mode=once)
    return call(
        lambda *refs: combine_kernel(scaled, len(acts), h, *refs),
        "combine",
        (D // part,),
        [(a, act) for a in acts]
        + [(w, pl.BlockSpec((count, part, FFE), lambda d: (0, d, 0))) for w in banks]
        + [(columns, column)]
        + [(v, whole_of(v.shape)) for v in (slots, weights)],
        [(result, pl.BlockSpec((half // blocks, part), lambda d: (0, d)))] * blocks,
        scratch=[
            pltpu.VMEM((half, count * stride), bf16),
            pltpu.VMEM((count * stride, part), bf16),
            pltpu.VMEM((count, capacity, 1), f32),
        ],
        ties=ties,
    )


def body(
    layer_input,
    cotangent,
    segments,
    routes,
    route_weights,
    gain_attention,
    gain_experts,
    query_proj,
    key_proj,
    value_proj,
    output_proj,
    head_gains,
    expert_gate,
    expert_up,
    expert_down,
):
    micro, rows, _ = layer_input.shape
    nf, ns = lax.axis_size("fsdp"), lax.axis_size("seq")
    seq_index = lax.axis_index("seq")
    seq_order = relative_order("seq")
    tokens = micro * rows
    group = rows * ns
    half = group * micro // 2
    heads_local = H // ns
    width = heads_local * HD
    local_experts = expert_gate.shape[0]
    experts = local_experts * ns
    capacity = micro * ns // 2 * min(rows, 3 * rows * TOP // (2 * experts))
    share = D // (nf * ns)

    def spread(value, axis):
        return lax.all_gather(value, "fsdp", axis=axis, tiled=True)

    def gather_tokens(value):
        blocks = jnp.concatenate(ring_gather(value, "seq", split=True), axis=0)
        return blocks.reshape((ns,) + value.shape)

    columns = [
        lax.dynamic_slice_in_dim(w, seq_index * width, width, axis=1).reshape(-1, heads_local, HD)
        for w in (query_proj, key_proj, value_proj)
    ]
    columns = jnp.stack(columns, axis=2).reshape(-1, 3 * width)
    extra = jnp.pad(jnp.stack([gain_attention, gain_experts], axis=1), ((0, 0), (0, HD - 2)))
    w_first = spread(jnp.concatenate([columns, extra], axis=1), 0)
    w_qkv = w_first[:, : 3 * width]
    gain_one = w_first[:, 3 * width].astype(f32)
    gain_two = w_first[:, 3 * width + 1].astype(f32)
    w_down = spread(expert_down, 1)
    w_output = spread(output_proj, 0)
    w_gate = spread(expert_gate, 1)
    w_up = spread(expert_up, 1)

    weight_high = route_weights.astype(bf16)
    weight_low = (route_weights - weight_high.astype(f32)).astype(bf16)
    packed = jnp.concatenate(
        [layer_input, routes.astype(bf16), weight_high, weight_low], axis=-1
    )
    packed = jnp.pad(packed, ((0, 0), (0, 0), (0, HD - 3 * TOP)))
    packed = x_all = gather_tokens(packed)
    x_wide = packed[..., :D].astype(f32)
    inv_all = rms_scale(x_wide)
    h_one = (x_wide * inv_all * gain_one).astype(bf16)
    qkv = jnp.einsum("smtd,de->smte", h_one, w_qkv, preferred_element_type=f32).astype(bf16)

    places = (seq_order[:, None] * rows + jnp.arange(rows)[None, :]).reshape(-1)
    lane = jnp.arange(HD) % (HD // 2)
    frequency = jnp.exp(-jnp.log(rope_base) * (2.0 * lane.astype(f32) / HD))
    angles = places.astype(f32)[:, None] * frequency[None, :]
    sign = jnp.where(jnp.arange(HD) < HD // 2, -1.0, 1.0)
    segment = reorder(segments.reshape(micro, ns, rows), seq_order, axis=1).reshape(micro, group)
    tables = (
        jnp.cos(angles),
        jnp.sin(angles) * sign,
        segment[:, None, :],
        segment[:, :, None],
        head_gains.astype(f32),
    )
    o_heads = attend(qkv, tables)

    o_heads = reorder(o_heads, seq_order, axis=0)
    g_blocks, g_next = ring_gather(
        after(cotangent, packed, *tables), "seq", (lambda _: qkv, lambda _: o_heads), True, stop=2
    )
    o_heads = after(o_heads, g_next)
    o_back = lax.all_to_all(o_heads, "seq", split_axis=0, concat_axis=0, tiled=True)
    o_rows = jnp.moveaxis(o_back, 0, 2).reshape(tokens, D)

    x_rows = layer_input.astype(f32).reshape(tokens, D)
    middle = x_rows + jnp.dot(o_rows, w_output, preferred_element_type=f32)
    inv_two = rms_scale(middle)
    normed_two = middle * inv_two
    h_two_own = (normed_two * gain_two).astype(bf16).reshape(micro, rows, D)
    h_blocks = ring_gather(h_two_own, "seq", (), True)

    packed = packed[..., D : D + 3 * TOP].astype(f32)
    packed = packed.reshape(2, half, 3 * TOP)
    route_all = packed[..., :TOP].astype(jnp.int32)
    weight_all = packed[..., TOP : 2 * TOP] + packed[..., 2 * TOP :]
    mine = seq_index * local_experts + jnp.arange(local_experts)
    hit = route_all[:, :, None, :] == mine[None, None, :, None]
    chosen = jnp.any(hit, axis=-1)
    weight_of = jnp.sum(jnp.where(hit, weight_all[:, :, None, :], 0.0), axis=-1)
    block = 128
    counted = chosen.reshape(2, half // block, block, local_experts).astype(f32)
    below = jnp.tril(jnp.ones((block, block), f32), -1)
    inside = jnp.einsum("ab,mkbe->mkae", below, counted)
    sums = jnp.sum(counted, axis=2)
    before = jnp.cumsum(sums, axis=1) - sums
    slot = (inside + before[:, :, None, :]).reshape(2, half, local_experts).astype(jnp.int32)
    slots = jnp.transpose(jnp.where(chosen, slot, -1), (2, 0, 1))
    weights = jnp.transpose(weight_of, (2, 0, 1))
    slot_columns = slots[..., None]

    grad_top = cotangent.astype(f32).reshape(tokens, D)
    done = {}

    def keep(**found):
        done.update(found)
        return next(iter(found.values()))

    def combined(acts, banks, h, scaled, ties=()):
        return combine(acts, banks, slot_columns, slots, weights, h, ns // 2, scaled, ties)

    g_blocks = ring_gather(after(g_next, h_blocks[-1]), "seq", (), True, g_blocks)

    def grad_work(_):
        grad_rows, grad_hidden = dispatch(g_blocks, slots, weights, w_down, capacity, True)
        return keep(grad_rows=grad_rows, grad_hidden=grad_hidden)

    pair = local_experts // 2

    def take_work(first):
        def work(ties):
            takes = dispatch(
                h_blocks,
                slots,
                weights,
                w_gate,
                capacity,
                False,
                tuple(ties) + (done["grad_rows"],),
                first,
                local_experts - pair if first else pair,
                done.get("takes", ()),
            )
            return keep(taken=takes[0], gate_act=takes[1], takes=takes)

        return work

    def act_work(_):
        acts = activate(done["taken"], done["gate_act"], done["grad_hidden"], w_up)
        return keep(tail=acts[0], acts=acts)

    o_all = ring_gather(
        after(o_heads.reshape(group * micro, width), g_blocks[-1]),
        "seq",
        (grad_work, take_work(0), take_work(pair), act_work),
        True,
    )
    o_all = o_all[:-2] + [jnp.concatenate(o_all[-2:], axis=0)] if len(o_all) > ns else o_all
    grad_rows, taken = done["grad_rows"], done["taken"]
    hidden, grad_gate_act, grad_up_act = done["acts"]
    first = combined((grad_gate_act, grad_up_act), (w_gate, w_up), 0, False, (o_all[-1],))
    whole_down = [bank_grad(grad_rows, hidden, (first[0],), 0, pair)]
    mixed = combined((hidden,), (w_down,), 0, True, (whole_down[0],))
    second = combined((grad_gate_act, grad_up_act), (w_gate, w_up), 1, False, (mixed[0],))

    def down_work(ties):
        whole_down.append(bank_grad(grad_rows, hidden, ties, pair, local_experts - pair))
        return whole_down[1]

    def mixed_work(ties):
        found = combined((hidden,), (w_down,), 1, True, ties)
        return keep(tail=found[0], mixed=found)

    def gate_work(ties):
        return keep(whole_gate=bank_grad(taken, grad_gate_act, ties))

    parts = [v.reshape(micro, rows, D) for v in list(first) + list(second)]
    mixed = [v.reshape(micro, rows, D) for v in mixed]
    grad_h_two = ring_scatter(
        parts,
        "seq",
        (lambda _: second[0], down_work, mixed_work, gate_work),
        {
            0: lambda moved: keep(mixed_one=moved[-1]),
            1: lambda moved: keep(sum_down=after(whole_down[1], *moved)),
            3: lambda moved: keep(sum_gate=after(done["whole_gate"], *moved)),
        },
        {0: [row_move(mixed, 1, "seq")]},
    ).reshape(tokens, D)
    mixed += [v.reshape(micro, rows, D) for v in done["mixed"]]

    def bank_sum(whole):
        return lax.psum_scatter(whole, "fsdp", scatter_dimension=1, tiled=True).astype(f32)

    grad_down = jnp.concatenate([bank_sum(whole_down[0]), bank_sum(done["sum_down"])], axis=0)
    grad_gate = bank_sum(done["sum_gate"])

    grad_gain_two = jnp.sum(grad_h_two * normed_two, axis=0)
    grad_unit = grad_h_two * gain_two
    grad_middle = grad_top + inv_two * (
        grad_unit - normed_two * jnp.mean(grad_unit * normed_two, axis=-1, keepdims=True)
    )
    grad_attn = grad_middle.astype(bf16)
    grad_o = jnp.einsum("te,de->td", grad_attn, w_output, preferred_element_type=f32).astype(bf16)

    def to_heads(value):
        cut = value.reshape(micro, rows, ns, width)
        return lax.all_to_all(
            jnp.moveaxis(cut, 2, 0), "seq", split_axis=0, concat_axis=0, tiled=True
        )

    whole_up = bank_grad(taken, grad_up_act, (grad_o,))
    (do_blocks,) = together((whole_up,), to_heads(grad_o))
    grad_up = bank_sum(after(whole_up, do_blocks))
    do_heads = reorder(do_blocks, seq_order)

    inner = sizes("seq")[1]
    one = 1 % inner
    total = row_sum(after(done["mixed_one"], do_blocks), mixed, 1, "seq")
    mixed[2 * inner + one] = after(mixed[2 * inner + one], do_blocks)
    grad_qkv, grad_head = attend_back(qkv, do_heads, tables)
    part_h_one, grad_gain_one = part_grads(grad_qkv, w_first, x_all, inv_all)
    total, two, columns = together(
        (grad_gain_one,),
        ahead(total, "seq"),
        row_move(mixed, 2, "seq"),
        to_heads(after(grad_attn, do_blocks)),
    )

    part_h_one = [v.reshape(micro, rows, D) for v in part_h_one]
    part_h_one[inner + one] = after(part_h_one[inner + one], total)
    mixed[3 * inner + one] = after(mixed[3 * inner + one], total)
    gains = jnp.pad(jnp.stack([grad_gain_one, grad_gain_two], axis=1), ((0, 0), (0, HD - 2)))
    whole = proj_grads(
        h_one,
        grad_qkv,
        o_all,
        columns.reshape(micro * group, width),
        gains,
        relative_order("fsdp"),
        seq_order,
        (total,),
    )
    left = exchanges()
    head = jnp.sum(after(grad_head, total), axis=0)

    def exchange(head):
        axis, pairs = left.pop(0)
        return lax.ppermute(head, axis, pairs)

    total = ahead(add(row_sum(two, mixed, 2, "seq"), total).astype(bf16), "seq")
    head = head + exchange(head)
    total, three, grad_one, moved = together(
        (whole[0],),
        total,
        row_move(mixed, 3, "seq"),
        row_move(part_h_one, 1, "seq"),
        exchange(head),
    )
    head = head + moved

    whole = [after(v, grad_one) for v in whole]
    owned = ring_scatter(whole, "fsdp").astype(bf16)

    mixed[one] = after(mixed[one], grad_one)
    part_h_one[2 * inner + one] = after(part_h_one[2 * inner + one], grad_one)
    total = ahead(add(row_sum(three, mixed, 3, "seq"), total).astype(bf16), "seq")
    grad_total = ahead(row_sum(grad_one, part_h_one, 1, "seq"), "seq")
    total, grad_total, grad_two, zero, owned = together(
        (),
        total,
        grad_total,
        row_move(part_h_one, 2, "seq"),
        row_move(mixed, 0, "seq"),
        owned,
    )
    owned = lax.all_to_all(
        owned.reshape(ns, share, -1), "seq", split_axis=0, concat_axis=0, tiled=True
    )

    part_h_one[3 * inner + one] = after(part_h_one[3 * inner + one], grad_total)
    grad_total = add(row_sum(grad_two, part_h_one, 2, "seq"), grad_total).astype(bf16)
    grad_total, grad_three, moved, owned = together(
        (grad_down,),
        ahead(grad_total, "seq"),
        row_move(part_h_one, 3, "seq"),
        exchange(head),
        owned,
    )
    head = head + moved
    mixed = add(row_sum(zero, mixed, 0, "seq"), total).reshape(tokens, D)
    layer_output = (middle + mixed).astype(bf16).reshape(micro, rows, D)

    part_h_one[one] = after(part_h_one[one], owned)
    grad_total = add(row_sum(grad_three, part_h_one, 3, "seq"), grad_total).astype(bf16)
    grad_total, zero, moved = together(
        (grad_gate,),
        ahead(grad_total, "seq"),
        row_move(part_h_one, 0, "seq"),
        exchange(head),
    )
    head = head + moved
    while left:
        head = head + exchange(head)
    grad_head_gains = head
    grad_h_one = add(row_sum(zero, part_h_one, 0, "seq"), grad_total).reshape(tokens, D)
    inv_one = rms_scale(x_rows)
    normed_one = x_rows * inv_one
    grad_unit = grad_h_one * gain_one
    input_grad = grad_middle + inv_one * (
        grad_unit - normed_one * jnp.mean(grad_unit * normed_one, axis=-1, keepdims=True)
    )
    input_grad = input_grad.reshape(micro, rows, D)
    owned = owned.astype(f32)
    of_qkv = owned[..., : 3 * width].reshape(ns, share, heads_local, 3, HD)
    grad_query, grad_key, grad_value = (
        jnp.moveaxis(of_qkv[..., k, :], 0, 1).reshape(share, D) for k in range(3)
    )
    grad_output = jnp.moveaxis(owned[..., 3 * width : 4 * width], 0, 1).reshape(share, D)
    of_gains = jnp.sum(owned[..., 4 * width : 4 * width + 2], axis=0)
    return (
        layer_output,
        input_grad,
        of_gains[:, 0],
        of_gains[:, 1],
        grad_query,
        grad_key,
        grad_value,
        grad_output,
        grad_head_gains,
        grad_gate,
        grad_up,
        grad_down,
    )


def solution(mesh):
    placed = (
        P(None, ("fsdp", "seq"), None),
        P(None, ("fsdp", "seq"), None),
        P(None, "fsdp"),
        P(None, ("fsdp", "seq"), None),
        P(None, ("fsdp", "seq"), None),
        P("fsdp"),
        P("fsdp"),
        P("fsdp", None),
        P("fsdp", None),
        P("fsdp", None),
        P("fsdp", None),
        P(),
        P("seq", "fsdp", None),
        P("seq", "fsdp", None),
        P("seq", "fsdp", None),
    )
    return jax.shard_map(
        body,
        mesh=mesh,
        in_specs=placed,
        out_specs=(
            P(None, ("fsdp", "seq"), None),
            P(None, ("fsdp", "seq"), None),
            P(("fsdp", "seq")),
            P(("fsdp", "seq")),
            P(("fsdp", "seq"), None),
            P(("fsdp", "seq"), None),
            P(("fsdp", "seq"), None),
            P(("fsdp", "seq"), None),
            P(),
            P("seq", "fsdp", None),
            P("seq", "fsdp", None),
            P("seq", "fsdp", None),
        ),
        check_vma=False,
    )
```

```python
import math

import jax
import jax.numpy as jnp
from jax import lax
from jax.experimental import pallas as pl
from jax.experimental.pallas import tpu as pltpu
from jax.sharding import PartitionSpec as P

D = 2048
H = 16
HD = 128
FFE = 1024
TOP = 8
SEQ_LEN = 1024

eps = 1e-06
rope_base = 10000.0
masked_score = -1e30
f32 = jnp.float32
little = pl.CostEstimate(flops=1, bytes_accessed=1, transcendentals=0)
bf16 = jnp.bfloat16


def shift(value, axis, outer, inner, by_outer, by_inner):
    pairs = []
    for a in range(outer):
        for b in range(inner):
            there = ((a + by_outer) % outer) * inner + (b + by_inner) % inner
            pairs.append((a * inner + b, there))
    return lax.ppermute(value, axis, pairs)


def sizes(axis):
    count = lax.axis_size(axis)
    return (count // 2, 2) if axis == "fsdp" else (4, count // 4)


def after(value, *others):
    others = [v for v in others if v is not None]
    if not others:
        return value
    anywhere = pl.BlockSpec(memory_space=pl.ANY)
    return pl.pallas_call(
        lambda *refs: None,
        in_specs=[anywhere] * (1 + len(others)),
        out_specs=anywhere,
        out_shape=jax.ShapeDtypeStruct(value.shape, value.dtype),
        input_output_aliases={0: 0},
        cost_estimate=little,
        name="after",
    )(value, *others)


def together(work, *moved):
    moved = list(moved)
    for k in range(len(moved)):
        moved[k] = after(moved[k], *work, *moved[:k], *moved[k + 1 :])
    return moved


def ring_gather(value, axis, work=None, split=False, blocks=(), stop=None):
    outer, inner = sizes(axis)
    blocks, arrived = list(blocks), []
    for a in range(len(blocks) // inner, outer if stop is None else stop):
        row = [value]
        for b in range(1, inner):
            row.append(shift(row[-1], axis, outer, inner, 0, 1))
        moved = row[1:]
        if a + 1 < outer:
            moved.append(shift(value, axis, outer, inner, 1, 0))
        last = split and inner == 2 and a + 1 == outer
        if last:
            cut = value.shape[0] // 2
            moved = [
                shift(value[:cut], axis, outer, inner, 0, 1),
                shift(blocks[-1][cut:], axis, outer, inner, 1, 0),
            ]
        if work is not None:
            moved = together([f(arrived) for f in work[a : a + 1] if f], *moved)
        blocks += [value] + (moved if last else moved[: inner - 1])
        value, arrived = moved[-1], moved
    return blocks if stop is None else (blocks, value)


def row_move(parts, a, axis):
    outer, inner = sizes(axis)
    row = parts[a * inner + 1 % inner]
    for b in range(2, inner):
        row = shift(row, axis, outer, inner, 0, 1)
        row = (row.astype(f32) + parts[a * inner + b].astype(f32)).astype(bf16)
    return shift(row, axis, outer, inner, 0, 1) if inner > 1 else row


def row_sum(moved, parts, a, axis):
    total = moved.astype(f32) + parts[a * sizes(axis)[1]].astype(f32)
    return total.astype(bf16)


def ahead(value, axis):
    return shift(value, axis, *sizes(axis), 1, 0)


def add(one, other):
    return one.astype(f32) + other.astype(f32)


def ring_scatter(parts, axis, work=(), then={}, beside={}):
    outer, _ = sizes(axis)
    total, arrived = None, []
    for step in range(outer):
        a = (step + 1) % outer
        moved = [row_move(parts, a, axis)]
        if step:
            moved.append(ahead(total, axis))
        moved += beside.get(step, [])
        moved = together([f(arrived) for f in work[step : step + 1] if f], *moved)
        if step in then:
            then[step](moved)
        arrived = moved
        total = row_sum(moved[0], parts, a, axis)
        if step:
            total = add(total, moved[1])
        if step and step + 1 < outer:
            total = total.astype(bf16)
    return total


def relative_order(axis):
    outer, inner = sizes(axis)
    me = lax.axis_index(axis)
    a, b = me // inner, me % inner
    k = jnp.arange(outer * inner)
    return ((a - k // inner) % outer) * inner + (b - k % inner) % inner


def reorder(value, order, axis=0):
    value = jnp.moveaxis(value, axis, 0)
    value = value.at[order].get(mode="promise_in_bounds", unique_indices=True)
    return jnp.moveaxis(value, 0, axis)


def rms_scale(values):
    return lax.rsqrt(jnp.mean(values * values, axis=-1, keepdims=True) + eps)


def exchanges():
    steps = []
    for axis in ("fsdp", "seq"):
        count = lax.axis_size(axis)
        for k in range(count.bit_length() - 1):
            steps.append((axis, [(i, i ^ (1 << k)) for i in range(count)]))
    return steps


def turn(values, cosine, sine):
    return values * cosine + pltpu.roll(values, HD // 2, 1) * sine


def turn_back(values, cosine, sine):
    return values * cosine - pltpu.roll(values, HD // 2, 1) * sine


def dot(left, right, left_dim, right_dim):
    return lax.dot_general(
        left, right, (((left_dim,), (right_dim,)), ((), ())), preferred_element_type=f32
    )


def attend_kernel(tile, qkv_ref, cos_ref, sin_ref, seg_row_ref, seg_col_ref, gain_ref, o_ref):
    blocks, _, rows, _ = qkv_ref.shape
    group = blocks * rows
    cosine, sine = cos_ref[...], sin_ref[...]

    def turned(part, row):
        raw = qkv_ref[:, 0, :, part * HD : (part + 1) * HD].reshape(group, HD).astype(f32)
        return turn(raw * rms_scale(raw) * gain_ref[row : row + 1, :], cosine, sine).astype(bf16)

    queries, keys = turned(0, 0), turned(1, 1)
    values = qkv_ref[:, 0, :, 2 * HD : 3 * HD].reshape(group, HD)
    seg_row = seg_row_ref[0]
    for start in range(0, group, tile):
        scores = dot(queries[start : start + tile], keys, 1, 1) * (1.0 / math.sqrt(HD))
        allowed = seg_col_ref[0, start : start + tile, :] == seg_row
        scores = jnp.where(allowed, scores, masked_score)
        powered = jnp.exp(scores - jnp.max(scores, axis=-1, keepdims=True))
        scale = 1.0 / jnp.sum(powered, axis=-1, keepdims=True)
        attended = dot((powered * scale).astype(bf16), values, 1, 0).astype(bf16)
        o_ref[start // rows : (start + tile) // rows, 0, :, :] = attended.reshape(
            tile // rows, rows, HD
        )


def attend_back_kernel(
    tile,
    qkv_ref,
    do_ref,
    cos_ref,
    sin_ref,
    seg_row_ref,
    seg_col_ref,
    gain_ref,
    grad_ref,
    grad_gain_ref,
):
    blocks, _, rows, _ = qkv_ref.shape
    group = blocks * rows
    cosine, sine = cos_ref[...], sin_ref[...]
    scaling = 1.0 / math.sqrt(HD)

    def normed(part):
        raw = qkv_ref[:, 0, :, part * HD : (part + 1) * HD].reshape(group, HD).astype(f32)
        inverse = rms_scale(raw)
        return raw * inverse, inverse

    def turned(part):
        return turn(normed(part)[0] * gain_ref[part : part + 1, :], cosine, sine).astype(bf16)

    def finish(part, grad_turned):
        unit, inverse = normed(part)
        grad_scaled = turn_back(grad_turned, cosine, sine)
        grad_gain_ref[0, part : part + 1, :] = jnp.sum(grad_scaled * unit, axis=0, keepdims=True)
        grad_unit = grad_scaled * gain_ref[part : part + 1, :]
        grad_raw = inverse * (
            grad_unit - unit * jnp.mean(grad_unit * unit, axis=-1, keepdims=True)
        )
        return grad_raw

    def put(part, value):
        grad_ref[:, 0, :, part * HD : (part + 1) * HD] = value.astype(bf16).reshape(
            blocks, rows, HD
        )

    queries, keys = turned(0), turned(1)
    values = qkv_ref[:, 0, :, 2 * HD : 3 * HD].reshape(group, HD)
    grad_out = do_ref[:, 0, :, :].reshape(group, HD)
    seg_row = seg_row_ref[0]
    grad_query = []
    grad_key = jnp.zeros((group, HD), f32)
    grad_value = jnp.zeros((group, HD), f32)
    for start in range(0, group, tile):
        part = queries[start : start + tile]
        grad_part = grad_out[start : start + tile]
        scores = dot(part, keys, 1, 1) * scaling
        allowed = seg_col_ref[0, start : start + tile, :] == seg_row
        scores = jnp.where(allowed, scores, masked_score)
        powered = jnp.exp(scores - jnp.max(scores, axis=-1, keepdims=True))
        probabilities = powered * (1.0 / jnp.sum(powered, axis=-1, keepdims=True))
        grad_probs = dot(grad_part, values, 1, 1)
        centre = jnp.sum(probabilities * grad_probs, axis=-1, keepdims=True)
        grad_scores = (probabilities * (grad_probs - centre)).astype(bf16)
        grad_query.append(dot(grad_scores, keys, 1, 0) * scaling)
        grad_key = grad_key + dot(grad_scores, part, 0, 0)
        grad_value = grad_value + dot(probabilities.astype(bf16), grad_part, 0, 0)
    put(0, finish(0, jnp.concatenate(grad_query, axis=0)))
    put(1, finish(1, grad_key * scaling))
    put(2, grad_value)


def attention_specs(ns, micro, rows, heads):
    group = ns * rows
    tile = max(rows, 256)
    return (
        tile,
        pl.BlockSpec((ns, 1, rows, 3 * HD), lambda m, h: (0, m, 0, h)),
        pl.BlockSpec((ns, 1, rows, HD), lambda m, h: (0, m, 0, h)),
        [
            pl.BlockSpec((group, HD), lambda m, h: (0, 0)),
            pl.BlockSpec((group, HD), lambda m, h: (0, 0)),
            pl.BlockSpec((1, 1, group), lambda m, h: (m, 0, 0)),
            pl.BlockSpec((1, group, 1), lambda m, h: (m, 0, 0)),
            pl.BlockSpec((2, HD), lambda m, h: (0, 0)),
        ],
    )


def attend(qkv, tables):
    ns, micro, rows, width = qkv.shape
    heads = width // (3 * HD)
    tile, wide, narrow, shared = attention_specs(ns, micro, rows, heads)
    group = ns * rows
    return pl.pallas_call(
        lambda *refs: attend_kernel(tile, *refs),
        grid=(micro, heads),
        in_specs=[wide] + shared,
        out_specs=narrow,
        out_shape=jax.ShapeDtypeStruct((ns, micro, rows, heads * HD), bf16),
        compiler_params=pltpu.CompilerParams(vmem_limit_bytes=40 * 2**20),
        cost_estimate=little,
        name="attend",
    )(qkv, *tables)


def attend_back(qkv, grad_out, tables, ties=()):
    ns, micro, rows, width = qkv.shape
    heads = width // (3 * HD)
    tile, wide, narrow, shared = attention_specs(ns, micro, rows, heads)
    group = ns * rows
    return pl.pallas_call(
        lambda *refs: attend_back_kernel(tile, *refs[:7], *refs[-2:]),
        grid=(micro, heads),
        in_specs=[wide, narrow] + shared + [pl.BlockSpec(memory_space=pl.ANY)] * len(ties),
        out_specs=[wide, pl.BlockSpec((1, 2, HD), lambda m, h: (m * heads + h, 0, 0))],
        out_shape=[
            jax.ShapeDtypeStruct((ns, micro, rows, width), bf16),
            jax.ShapeDtypeStruct((micro * heads, 2, HD), f32),
        ],
        compiler_params=pltpu.CompilerParams(vmem_limit_bytes=40 * 2**20),
        cost_estimate=little,
        name="attend_back",
    )(qkv, grad_out, *tables, *ties)


def part_kernel(grad_ref, w_ref, x_ref, inv_ref, *out_refs):
    out_refs, gain_ref = out_refs[:-1], out_refs[-1]
    rows = out_refs[0].shape[0]
    gain = jnp.zeros(gain_ref.shape, f32)
    for b, ref in enumerate(out_refs):
        span = slice(b * rows, (b + 1) * rows)
        wide = dot(grad_ref[span, :], w_ref[...], 1, 1)
        ref[...] = wide.astype(bf16)
        normed = x_ref[span, :].astype(f32) * inv_ref[span, :]
        gain = gain + jnp.sum(wide * normed, axis=0, keepdims=True)
    gain_ref[...] = gain


def part_grads(grad_qkv, w_first, x_all, inv_all, ties=()):
    blocks = grad_qkv.shape[0]
    width = grad_qkv.shape[-1]
    count = grad_qkv.size // width
    block = jax.ShapeDtypeStruct((count // blocks, D), bf16)
    found = call(
        part_kernel,
        "part_grads",
        (D // part,),
        [
            (grad_qkv.reshape(count, width), whole_of((count, width))),
            (w_first, pl.BlockSpec((part, width), lambda d: (d, 0))),
            (x_all.reshape(count, x_all.shape[-1]), pl.BlockSpec((count, part), lambda d: (0, d))),
            (inv_all.reshape(count, 1), whole_of((count, 1))),
        ],
        [(block, pl.BlockSpec((block.shape[0], part), lambda d: (0, d)))] * blocks
        + [(jax.ShapeDtypeStruct((1, D), f32), pl.BlockSpec((1, part), lambda d: (0, d)))],
        ties=ties,
    )
    return found[:-1], found[-1][0]


def proj_kernel(blocks, order_ref, place_ref, h_ref, grad_ref, column_ref, gain_ref, *refs):
    o_refs, out_refs, found_ref = refs[:blocks], refs[blocks:-1], refs[-1]
    k = pl.program_id(0)
    inputs, width = grad_ref.shape[1], column_ref.shape[1]
    owners = found_ref.shape[0] // width
    found_ref[:, :inputs] = dot(h_ref[...], grad_ref[...], 0, 0)
    for j in range(owners):
        place = place_ref[order_ref[k] * owners + j]
        for b in range(blocks):

            @pl.when(place == b)
            def _(b=b, j=j):
                found_ref[j * width : (j + 1) * width, inputs : inputs + width] = dot(
                    o_refs[b][...], column_ref[...], 0, 0
                )

    found_ref[:, inputs + width :] = gain_ref[...]
    for b, ref in enumerate(out_refs):

        @pl.when(k == b)
        def _(ref=ref):
            ref[...] = found_ref[...].astype(bf16)


def proj_grads(h_one, grad_qkv, o_blocks, columns, gains, order, places, ties=()):
    count, inputs = h_one.size // D, grad_qkv.shape[-1]
    width, nf = columns.shape[1], order.shape[0]
    rows, across = D // nf, inputs + width + gains.shape[1]
    result = jax.ShapeDtypeStruct((rows, across), bf16)
    ins = [
        (h_one.reshape(count, D), pl.BlockSpec((count, rows), lambda k, order, _: (0, order[k]))),
        (grad_qkv.reshape(count, inputs), whole_of((count, inputs))),
        (columns, whole_of(columns.shape)),
        (gains, pl.BlockSpec((rows, gains.shape[1]), lambda k, order, _: (order[k], 0))),
    ] + [(v, whole_of(v.shape)) for v in o_blocks]

    def run(*refs):
        lead = 2 + len(ins)
        proj_kernel(len(o_blocks), *refs[:lead], *refs[lead + len(ties) :])

    return pl.pallas_call(
        run,
        grid_spec=pltpu.PrefetchScalarGridSpec(
            num_scalar_prefetch=2,
            grid=(nf,),
            in_specs=[spec for _, spec in ins] + [pl.BlockSpec(memory_space=pl.ANY)] * len(ties),
            out_specs=[whole_of(result.shape)] * nf,
            scratch_shapes=[pltpu.VMEM((rows, across), f32)],
        ),
        out_shape=[result] * nf,
        compiler_params=pltpu.CompilerParams(vmem_limit_bytes=56 * 2**20),
        cost_estimate=little,
        name="proj_grads",
    )(order, places, *[value for value, _ in ins], *ties)


part = 512


def spans(shape, *block):
    block = block or (1,)
    return pl.BlockSpec(
        tuple(block) + tuple(shape[len(block) :]), lambda e, *_: (e,) + (0,) * (len(shape) - 1)
    )


def whole_of(shape):
    return pl.BlockSpec(
        tuple(shape), lambda *_: (0,) * len(shape), pipeline_mode=pl.Buffered(buffer_count=1)
    )


def call(kernel, name, grid, ins, outs, scratch=(), ties=(), aliases={}):
    ties = [t for t in ties if t is not None]
    count = len(ins)

    def run(*refs):
        kernel(*refs[:count], *refs[count + len(ties) :])

    return pl.pallas_call(
        run,
        grid=grid,
        in_specs=[spec for _, spec in ins] + [pl.BlockSpec(memory_space=pl.ANY)] * len(ties),
        out_specs=[spec for _, spec in outs],
        out_shape=[shape for shape, _ in outs],
        scratch_shapes=list(scratch),
        input_output_aliases=aliases,
        compiler_params=pltpu.CompilerParams(vmem_limit_bytes=56 * 2**20),
        cost_estimate=little,
        name=name,
    )(*[value for value, _ in ins], *ties)


def picked(slot_row, capacity):
    place = lax.broadcasted_iota(jnp.int32, (capacity, slot_row.shape[1]), 0)
    return place == slot_row


def slot_weights(slot_row, weight_row, capacity):
    chosen = jnp.where(picked(slot_row, capacity), weight_row, 0.0)
    return jnp.sum(chosen, axis=1, keepdims=True)


def dispatch_kernel(scaled, blocks, *refs):
    value_refs, (slot_ref, weight_ref, w_ref, rows_ref, act_ref) = refs[:blocks], refs[blocks:]
    capacity, half = rows_ref.shape[2], slot_ref.shape[2]
    halves, seen = ([], []), 0
    for ref in value_refs:
        halves[seen // half].append(ref)
        seen += ref.shape[0]
    for h in range(2):
        slot_row = slot_ref[0, h : h + 1, :]
        pick = picked(slot_row, capacity).astype(f32).astype(bf16)
        if scaled:
            scale = slot_weights(slot_row, weight_ref[0, h : h + 1, :], capacity)
        for d in range(0, D, part):
            values = jnp.concatenate(
                [ref[:, d : d + part] for ref in halves[h]], axis=0
            )
            taken = dot(pick, values, 1, 0)
            if scaled:
                taken = taken * scale
            rows_ref[0, h, :, d : d + part] = taken.astype(bf16)
        act_ref[0, h] = dot(rows_ref[0, h], w_ref[0], 1, 0)


def dispatch(
    values, slots, weights, bank, capacity, scaled, ties=(), first=0, count=None, before=()
):
    experts = bank.shape[0]
    count = count or experts
    values = [v.reshape(-1, v.shape[-1]) for v in values]
    rows_shape = (experts, 2, capacity, D)
    act_shape = (experts, 2, capacity, FFE)

    def of(shape):
        return pl.BlockSpec((1,) + shape[1:], lambda e: (first + e,) + (0,) * (len(shape) - 1))

    return call(
        lambda *refs: dispatch_kernel(scaled, len(values), *refs),
        "dispatch",
        (count,),
        [(v, whole_of(v.shape)) for v in values]
        + [(v, of(v.shape)) for v in (slots, weights, bank)],
        [
            (jax.ShapeDtypeStruct(rows_shape, bf16), of(rows_shape)),
            (jax.ShapeDtypeStruct(act_shape, f32), of(act_shape)),
        ],
        ties=tuple(before) + tuple(ties),
        aliases={len(values) + 3 + k: k for k in range(len(before))},
    )


def act_kernel(taken_ref, gate_ref, grad_ref, w_ref, hidden_ref, grad_gate_ref, grad_up_ref):
    for f in range(0, FFE, 256):
        span = slice(f, f + 256)
        up_act = dot(taken_ref[0, 0], w_ref[0, :, span], 1, 0)
        gate_act, grad_hidden = gate_ref[0, 0, :, span], grad_ref[0, 0, :, span]
        gate_sig = jax.nn.sigmoid(gate_act)
        gate_silu = gate_act * gate_sig
        hidden_ref[0, 0, :, span] = (gate_silu * up_act).astype(bf16)
        grad_gate = grad_hidden * up_act * gate_sig * (1.0 + gate_act * (1.0 - gate_sig))
        grad_gate_ref[0, 0, :, span] = grad_gate.astype(bf16)
        grad_up_ref[0, 0, :, span] = (grad_hidden * gate_silu).astype(bf16)


def activate(taken, gate_act, grad_hidden, w_up, ties=()):
    count, _, capacity, _ = taken.shape

    def of(width):
        return pl.BlockSpec((1, 1, capacity, width), lambda e, h: (e, h, 0, 0))

    result = jax.ShapeDtypeStruct(gate_act.shape, bf16)
    return call(
        act_kernel,
        "activate",
        (count, 2),
        [
            (taken, of(D)),
            (gate_act, of(FFE)),
            (grad_hidden, of(FFE)),
            (w_up, spans(w_up.shape)),
        ],
        [(result, of(FFE))] * 3,
        ties=ties,
    )


def bank_kernel(left_ref, right_ref, out_ref):
    rows = left_ref.shape[1] * left_ref.shape[2]
    left, right = left_ref[0].reshape(rows, -1), right_ref[0].reshape(rows, -1)
    out_ref[0] = dot(left, right, 0, 0).astype(bf16)


def bank_grad(left, right, ties=(), first=0, count=None):
    capacity = left.shape[2]
    count = count or left.shape[0]
    result = jax.ShapeDtypeStruct((count, D, FFE), bf16)
    return call(
        bank_kernel,
        "bank_grad",
        (count, D // part),
        [
            (left, pl.BlockSpec((1, 2, capacity, part), lambda e, d: (first + e, 0, 0, d))),
            (right, pl.BlockSpec((1, 2, capacity, FFE), lambda e, d: (first + e, 0, 0, 0))),
        ],
        [(result, pl.BlockSpec((1, part, FFE), lambda e, d: (e, d, 0)))],
        ties=ties,
    )[0]


def combine_kernel(scaled, acts, h, *refs):
    act_refs, w_refs = refs[:acts], refs[acts : 2 * acts]
    column_ref, slot_ref, weight_ref = refs[2 * acts : 2 * acts + 3]
    out_refs, (pick_ref, rows_ref, scale_ref) = refs[2 * acts + 3 : -3], refs[-3:]
    count, _, capacity, _ = act_refs[0].shape
    half, stride = pick_ref.shape[0], rows_ref.shape[0] // count

    @pl.when(pl.program_id(0) == 0)
    def _():
        rows_ref[...] = jnp.zeros_like(rows_ref)
        place = lax.broadcasted_iota(jnp.int32, (half, stride), 1)
        for e in range(count):
            pick = (place == column_ref[e, 0]).astype(f32).astype(bf16)
            pick_ref[:, e * stride : (e + 1) * stride] = pick
            if scaled:
                scale_ref[e] = slot_weights(
                    slot_ref[e, h : h + 1, :], weight_ref[e, h : h + 1, :], capacity
                )

    for e in range(count):
        grads = [dot(a_ref[e, 0], w_ref[e], 1, 1) for a_ref, w_ref in zip(act_refs, w_refs)]
        rows = sum(grads[1:], grads[0])
        if scaled:
            rows = rows * scale_ref[e]
        rows_ref[e * stride : e * stride + capacity, :] = rows.astype(bf16)
    n = out_refs[0].shape[0]
    for b, ref in enumerate(out_refs):
        ref[...] = dot(pick_ref[b * n : (b + 1) * n, :], rows_ref[...], 1, 0).astype(bf16)


def combine(acts, banks, columns, slots, weights, h, blocks, scaled, ties=()):
    count, _, capacity, _ = acts[0].shape
    half = columns.shape[2]
    stride = -(-capacity // 128) * 128
    result = jax.ShapeDtypeStruct((half // blocks, D), bf16)
    once = pl.Buffered(buffer_count=1)
    act = pl.BlockSpec((count, 1, capacity, FFE), lambda d: (0, h, 0, 0), pipeline_mode=once)
    column = pl.BlockSpec((count, 1, half, 1), lambda d: (0, h, 0, 0), pipeline_mode=once)
    return call(
        lambda *refs: combine_kernel(scaled, len(acts), h, *refs),
        "combine",
        (D // part,),
        [(a, act) for a in acts]
        + [(w, pl.BlockSpec((count, part, FFE), lambda d: (0, d, 0))) for w in banks]
        + [(columns, column)]
        + [(v, whole_of(v.shape)) for v in (slots, weights)],
        [(result, pl.BlockSpec((half // blocks, part), lambda d: (0, d)))] * blocks,
        scratch=[
            pltpu.VMEM((half, count * stride), bf16),
            pltpu.VMEM((count * stride, part), bf16),
            pltpu.VMEM((count, capacity, 1), f32),
        ],
        ties=ties,
    )


def body(
    layer_input,
    cotangent,
    segments,
    routes,
    route_weights,
    gain_attention,
    gain_experts,
    query_proj,
    key_proj,
    value_proj,
    output_proj,
    head_gains,
    expert_gate,
    expert_up,
    expert_down,
):
    micro, rows, _ = layer_input.shape
    nf, ns = lax.axis_size("fsdp"), lax.axis_size("seq")
    seq_index = lax.axis_index("seq")
    seq_order = relative_order("seq")
    tokens = micro * rows
    group = rows * ns
    half = group * micro // 2
    heads_local = H // ns
    width = heads_local * HD
    local_experts = expert_gate.shape[0]
    experts = local_experts * ns
    capacity = micro * ns // 2 * min(rows, 3 * rows * TOP // (2 * experts))
    share = D // (nf * ns)

    def spread(value, axis):
        return lax.all_gather(value, "fsdp", axis=axis, tiled=True)

    def gather_tokens(value):
        blocks = jnp.concatenate(ring_gather(value, "seq", split=True), axis=0)
        return blocks.reshape((ns,) + value.shape)

    columns = [
        lax.dynamic_slice_in_dim(w, seq_index * width, width, axis=1).reshape(-1, heads_local, HD)
        for w in (query_proj, key_proj, value_proj)
    ]
    columns = jnp.stack(columns, axis=2).reshape(-1, 3 * width)
    extra = jnp.pad(jnp.stack([gain_attention, gain_experts], axis=1), ((0, 0), (0, HD - 2)))
    w_first = spread(jnp.concatenate([columns, extra], axis=1), 0)
    w_qkv = w_first[:, : 3 * width]
    gain_one = w_first[:, 3 * width].astype(f32)
    gain_two = w_first[:, 3 * width + 1].astype(f32)
    w_down = spread(expert_down, 1)
    w_output = spread(output_proj, 0)
    w_gate = spread(expert_gate, 1)
    w_up = spread(expert_up, 1)

    weight_high = route_weights.astype(bf16)
    weight_low = (route_weights - weight_high.astype(f32)).astype(bf16)
    packed = jnp.concatenate(
        [layer_input, routes.astype(bf16), weight_high, weight_low], axis=-1
    )
    packed = jnp.pad(packed, ((0, 0), (0, 0), (0, HD - 3 * TOP)))
    packed = x_all = gather_tokens(packed)
    x_wide = packed[..., :D].astype(f32)
    inv_all = rms_scale(x_wide)
    h_one = (x_wide * inv_all * gain_one).astype(bf16)
    qkv = jnp.einsum("smtd,de->smte", h_one, w_qkv, preferred_element_type=f32).astype(bf16)

    places = (seq_order[:, None] * rows + jnp.arange(rows)[None, :]).reshape(-1)
    lane = jnp.arange(HD) % (HD // 2)
    frequency = jnp.exp(-jnp.log(rope_base) * (2.0 * lane.astype(f32) / HD))
    angles = places.astype(f32)[:, None] * frequency[None, :]
    sign = jnp.where(jnp.arange(HD) < HD // 2, -1.0, 1.0)
    segment = reorder(segments.reshape(micro, ns, rows), seq_order, axis=1).reshape(micro, group)
    tables = (
        jnp.cos(angles),
        jnp.sin(angles) * sign,
        segment[:, None, :],
        segment[:, :, None],
        head_gains.astype(f32),
    )
    o_heads = attend(qkv, tables)

    o_heads = reorder(o_heads, seq_order, axis=0)
    g_blocks, g_next = ring_gather(
        after(cotangent, packed, *tables), "seq", (lambda _: qkv, lambda _: o_heads), True, stop=2
    )
    o_heads = after(o_heads, g_next)
    o_back = lax.all_to_all(o_heads, "seq", split_axis=0, concat_axis=0, tiled=True)
    o_rows = jnp.moveaxis(o_back, 0, 2).reshape(tokens, D)

    x_rows = layer_input.astype(f32).reshape(tokens, D)
    middle = x_rows + jnp.dot(o_rows, w_output, preferred_element_type=f32)
    inv_two = rms_scale(middle)
    normed_two = middle * inv_two
    h_two_own = (normed_two * gain_two).astype(bf16).reshape(micro, rows, D)
    h_blocks = ring_gather(h_two_own, "seq", (), True)

    packed = packed[..., D : D + 3 * TOP].astype(f32)
    packed = packed.reshape(2, half, 3 * TOP)
    route_all = packed[..., :TOP].astype(jnp.int32)
    weight_all = packed[..., TOP : 2 * TOP] + packed[..., 2 * TOP :]
    mine = seq_index * local_experts + jnp.arange(local_experts)
    hit = route_all[:, :, None, :] == mine[None, None, :, None]
    chosen = jnp.any(hit, axis=-1)
    weight_of = jnp.sum(jnp.where(hit, weight_all[:, :, None, :], 0.0), axis=-1)
    block = 128
    counted = chosen.reshape(2, half // block, block, local_experts).astype(f32)
    below = jnp.tril(jnp.ones((block, block), f32), -1)
    inside = jnp.einsum("ab,mkbe->mkae", below, counted)
    sums = jnp.sum(counted, axis=2)
    before = jnp.cumsum(sums, axis=1) - sums
    slot = (inside + before[:, :, None, :]).reshape(2, half, local_experts).astype(jnp.int32)
    slots = jnp.transpose(jnp.where(chosen, slot, -1), (2, 0, 1))
    weights = jnp.transpose(weight_of, (2, 0, 1))
    slot_columns = slots[..., None]

    grad_top = cotangent.astype(f32).reshape(tokens, D)
    done = {}

    def keep(**found):
        done.update(found)
        return next(iter(found.values()))

    def combined(acts, banks, h, scaled, ties=()):
        return combine(acts, banks, slot_columns, slots, weights, h, ns // 2, scaled, ties)

    g_blocks = ring_gather(after(g_next, h_blocks[-1]), "seq", (), True, g_blocks)

    def grad_work(_):
        grad_rows, grad_hidden = dispatch(g_blocks, slots, weights, w_down, capacity, True)
        return keep(grad_rows=grad_rows, grad_hidden=grad_hidden)

    pair = local_experts // 2

    def take_work(first):
        def work(ties):
            takes = dispatch(
                h_blocks,
                slots,
                weights,
                w_gate,
                capacity,
                False,
                tuple(ties) + (done["grad_rows"],),
                first,
                local_experts - pair if first else pair,
                done.get("takes", ()),
            )
            return keep(taken=takes[0], gate_act=takes[1], takes=takes)

        return work

    def act_work(_):
        acts = activate(done["taken"], done["gate_act"], done["grad_hidden"], w_up)
        return keep(tail=acts[0], acts=acts)

    o_all = ring_gather(
        after(o_heads.reshape(group * micro, width), g_blocks[-1]),
        "seq",
        (grad_work, take_work(0), take_work(pair), act_work),
        True,
    )
    o_all = o_all[:-2] + [jnp.concatenate(o_all[-2:], axis=0)] if len(o_all) > ns else o_all
    grad_rows, taken = done["grad_rows"], done["taken"]
    hidden, grad_gate_act, grad_up_act = done["acts"]
    first = combined((grad_gate_act, grad_up_act), (w_gate, w_up), 0, False, (o_all[-1],))
    whole_down = [bank_grad(grad_rows, hidden, (first[0],), 0, pair)]
    mixed = combined((hidden,), (w_down,), 0, True, (whole_down[0],))
    second = combined((grad_gate_act, grad_up_act), (w_gate, w_up), 1, False, (mixed[0],))

    def down_work(ties):
        whole_down.append(bank_grad(grad_rows, hidden, ties, pair, local_experts - pair))
        return whole_down[1]

    def mixed_work(ties):
        found = combined((hidden,), (w_down,), 1, True, ties)
        return keep(tail=found[0], mixed=found)

    def gate_work(ties):
        return keep(whole_gate=bank_grad(taken, grad_gate_act, ties))

    parts = [v.reshape(micro, rows, D) for v in list(first) + list(second)]
    mixed = [v.reshape(micro, rows, D) for v in mixed]
    grad_h_two = ring_scatter(
        parts,
        "seq",
        (lambda _: second[0], down_work, mixed_work, gate_work),
        {
            0: lambda moved: keep(mixed_one=moved[-1]),
            1: lambda moved: keep(sum_down=after(whole_down[1], *moved)),
            3: lambda moved: keep(sum_gate=after(done["whole_gate"], *moved)),
        },
        {0: [row_move(mixed, 1, "seq")]},
    ).reshape(tokens, D)
    mixed += [v.reshape(micro, rows, D) for v in done["mixed"]]

    def bank_sum(whole):
        return lax.psum_scatter(whole, "fsdp", scatter_dimension=1, tiled=True).astype(f32)

    grad_down = jnp.concatenate([bank_sum(whole_down[0]), bank_sum(done["sum_down"])], axis=0)
    grad_gate = bank_sum(done["sum_gate"])

    grad_gain_two = jnp.sum(grad_h_two * normed_two, axis=0)
    grad_unit = grad_h_two * gain_two
    grad_middle = grad_top + inv_two * (
        grad_unit - normed_two * jnp.mean(grad_unit * normed_two, axis=-1, keepdims=True)
    )
    grad_attn = grad_middle.astype(bf16)
    grad_o = jnp.einsum("te,de->td", grad_attn, w_output, preferred_element_type=f32).astype(bf16)

    def to_heads(value):
        cut = value.reshape(micro, rows, ns, width)
        return lax.all_to_all(
            jnp.moveaxis(cut, 2, 0), "seq", split_axis=0, concat_axis=0, tiled=True
        )

    whole_up = bank_grad(taken, grad_up_act, (grad_o,))
    (do_blocks,) = together((whole_up,), to_heads(grad_o))
    grad_up = bank_sum(after(whole_up, do_blocks))
    do_heads = reorder(do_blocks, seq_order)

    inner = sizes("seq")[1]
    one = 1 % inner
    total = row_sum(after(done["mixed_one"], do_blocks), mixed, 1, "seq")
    mixed[2 * inner + one] = after(mixed[2 * inner + one], do_blocks)
    grad_qkv, grad_head = attend_back(qkv, do_heads, tables)
    part_h_one, grad_gain_one = part_grads(grad_qkv, w_first, x_all, inv_all)
    total, two, columns = together(
        (grad_gain_one,),
        ahead(total, "seq"),
        row_move(mixed, 2, "seq"),
        to_heads(after(grad_attn, do_blocks)),
    )

    part_h_one = [v.reshape(micro, rows, D) for v in part_h_one]
    part_h_one[inner + one] = after(part_h_one[inner + one], total)
    gains = jnp.pad(jnp.stack([grad_gain_one, grad_gain_two], axis=1), ((0, 0), (0, HD - 2)))
    whole = proj_grads(
        h_one,
        grad_qkv,
        o_all,
        columns.reshape(micro * group, width),
        gains,
        relative_order("fsdp"),
        seq_order,
        (total,),
    )
    left = exchanges()
    head = jnp.sum(after(grad_head, total), axis=0)

    def exchange(head):
        axis, pairs = left.pop(0)
        return lax.ppermute(head, axis, pairs)

    total = ahead(add(row_sum(two, mixed, 2, "seq"), total).astype(bf16), "seq")
    head = head + exchange(head)
    total, three, grad_one, moved = together(
        (whole[0],),
        total,
        row_move(mixed, 3, "seq"),
        row_move(part_h_one, 1, "seq"),
        exchange(head),
    )
    head = head + moved

    whole = [after(v, grad_one) for v in whole]
    owned = ring_scatter(whole, "fsdp").astype(bf16)

    total = ahead(add(row_sum(three, mixed, 3, "seq"), total).astype(bf16), "seq")
    grad_total = ahead(row_sum(grad_one, part_h_one, 1, "seq"), "seq")
    total, grad_total, grad_two, zero, owned = together(
        (),
        total,
        grad_total,
        row_move(part_h_one, 2, "seq"),
        row_move(mixed, 0, "seq"),
        owned,
    )
    owned = lax.all_to_all(
        owned.reshape(ns, share, -1), "seq", split_axis=0, concat_axis=0, tiled=True
    )

    part_h_one[3 * inner + one] = after(part_h_one[3 * inner + one], grad_total)
    grad_total = add(row_sum(grad_two, part_h_one, 2, "seq"), grad_total).astype(bf16)
    grad_total, grad_three, moved, owned = together(
        (grad_down,),
        ahead(grad_total, "seq"),
        row_move(part_h_one, 3, "seq"),
        exchange(head),
        owned,
    )
    head = head + moved
    mixed = add(row_sum(zero, mixed, 0, "seq"), total).reshape(tokens, D)
    layer_output = (middle + mixed).astype(bf16).reshape(micro, rows, D)

    part_h_one[one] = after(part_h_one[one], owned)
    grad_total = add(row_sum(grad_three, part_h_one, 3, "seq"), grad_total).astype(bf16)
    grad_total, zero, moved = together(
        (grad_gate,),
        ahead(grad_total, "seq"),
        row_move(part_h_one, 0, "seq"),
        exchange(head),
    )
    head = head + moved
    while left:
        head = head + exchange(head)
    grad_head_gains = head
    grad_h_one = add(row_sum(zero, part_h_one, 0, "seq"), grad_total).reshape(tokens, D)
    inv_one = rms_scale(x_rows)
    normed_one = x_rows * inv_one
    grad_unit = grad_h_one * gain_one
    input_grad = grad_middle + inv_one * (
        grad_unit - normed_one * jnp.mean(grad_unit * normed_one, axis=-1, keepdims=True)
    )
    input_grad = input_grad.reshape(micro, rows, D)
    owned = owned.astype(f32)
    of_qkv = owned[..., : 3 * width].reshape(ns, share, heads_local, 3, HD)
    grad_query, grad_key, grad_value = (
        jnp.moveaxis(of_qkv[..., k, :], 0, 1).reshape(share, D) for k in range(3)
    )
    grad_output = jnp.moveaxis(owned[..., 3 * width : 4 * width], 0, 1).reshape(share, D)
    of_gains = jnp.sum(owned[..., 4 * width : 4 * width + 2], axis=0)
    return (
        layer_output,
        input_grad,
        of_gains[:, 0],
        of_gains[:, 1],
        grad_query,
        grad_key,
        grad_value,
        grad_output,
        grad_head_gains,
        grad_gate,
        grad_up,
        grad_down,
    )


def solution(mesh):
    placed = (
        P(None, ("fsdp", "seq"), None),
        P(None, ("fsdp", "seq"), None),
        P(None, "fsdp"),
        P(None, ("fsdp", "seq"), None),
        P(None, ("fsdp", "seq"), None),
        P("fsdp"),
        P("fsdp"),
        P("fsdp", None),
        P("fsdp", None),
        P("fsdp", None),
        P("fsdp", None),
        P(),
        P("seq", "fsdp", None),
        P("seq", "fsdp", None),
        P("seq", "fsdp", None),
    )
    return jax.shard_map(
        body,
        mesh=mesh,
        in_specs=placed,
        out_specs=(
            P(None, ("fsdp", "seq"), None),
            P(None, ("fsdp", "seq"), None),
            P(("fsdp", "seq")),
            P(("fsdp", "seq")),
            P(("fsdp", "seq"), None),
            P(("fsdp", "seq"), None),
            P(("fsdp", "seq"), None),
            P(("fsdp", "seq"), None),
            P(),
            P("seq", "fsdp", None),
            P("seq", "fsdp", None),
            P("seq", "fsdp", None),
        ),
        check_vma=False,
    )
```

```python
import math

import jax
import jax.numpy as jnp
from jax import lax
from jax.experimental import pallas as pl
from jax.experimental.pallas import tpu as pltpu
from jax.sharding import PartitionSpec as P

D = 2048
H = 16
HD = 128
FFE = 1024
TOP = 8
SEQ_LEN = 1024

eps = 1e-06
rope_base = 10000.0
masked_score = -1e30
f32 = jnp.float32
little = pl.CostEstimate(flops=1, bytes_accessed=1, transcendentals=0)
bf16 = jnp.bfloat16


def shift(value, axis, outer, inner, by_outer, by_inner):
    pairs = []
    for a in range(outer):
        for b in range(inner):
            there = ((a + by_outer) % outer) * inner + (b + by_inner) % inner
            pairs.append((a * inner + b, there))
    return lax.ppermute(value, axis, pairs)


def sizes(axis):
    count = lax.axis_size(axis)
    return (count // 2, 2) if axis == "fsdp" else (4, count // 4)


def after(value, *others):
    others = [v for v in others if v is not None]
    if not others:
        return value
    anywhere = pl.BlockSpec(memory_space=pl.ANY)
    return pl.pallas_call(
        lambda *refs: None,
        in_specs=[anywhere] * (1 + len(others)),
        out_specs=anywhere,
        out_shape=jax.ShapeDtypeStruct(value.shape, value.dtype),
        input_output_aliases={0: 0},
        cost_estimate=little,
        name="after",
    )(value, *others)


def together(work, *moved):
    moved = list(moved)
    for k in range(len(moved)):
        moved[k] = after(moved[k], *work, *moved[:k], *moved[k + 1 :])
    return moved


def ring_gather(value, axis, work=None, split=False, blocks=(), stop=None):
    outer, inner = sizes(axis)
    blocks, arrived = list(blocks), []
    for a in range(len(blocks) // inner, outer if stop is None else stop):
        row = [value]
        for b in range(1, inner):
            row.append(shift(row[-1], axis, outer, inner, 0, 1))
        moved = row[1:]
        if a + 1 < outer:
            moved.append(shift(value, axis, outer, inner, 1, 0))
        last = split and inner == 2 and a + 1 == outer
        if last:
            cut = value.shape[0] // 2
            moved = [
                shift(value[:cut], axis, outer, inner, 0, 1),
                shift(blocks[-1][cut:], axis, outer, inner, 1, 0),
            ]
        if work is not None:
            moved = together([f(arrived) for f in work[a : a + 1] if f], *moved)
        blocks += [value] + (moved if last else moved[: inner - 1])
        value, arrived = moved[-1], moved
    return blocks if stop is None else (blocks, value)


def row_move(parts, a, axis):
    outer, inner = sizes(axis)
    row = parts[a * inner + 1 % inner]
    for b in range(2, inner):
        row = shift(row, axis, outer, inner, 0, 1)
        row = (row.astype(f32) + parts[a * inner + b].astype(f32)).astype(bf16)
    return shift(row, axis, outer, inner, 0, 1) if inner > 1 else row


def row_sum(moved, parts, a, axis):
    total = moved.astype(f32) + parts[a * sizes(axis)[1]].astype(f32)
    return total.astype(bf16)


def ahead(value, axis):
    return shift(value, axis, *sizes(axis), 1, 0)


def add(one, other):
    return one.astype(f32) + other.astype(f32)


def ring_scatter(parts, axis, work=(), then={}, beside={}):
    outer, _ = sizes(axis)
    total, arrived = None, []
    for step in range(outer):
        a = (step + 1) % outer
        moved = [row_move(parts, a, axis)]
        if step:
            moved.append(ahead(total, axis))
        moved += beside.get(step, [])
        moved = together([f(arrived) for f in work[step : step + 1] if f], *moved)
        if step in then:
            then[step](moved)
        arrived = moved
        total = row_sum(moved[0], parts, a, axis)
        if step:
            total = add(total, moved[1])
        if step and step + 1 < outer:
            total = total.astype(bf16)
    return total


def relative_order(axis):
    outer, inner = sizes(axis)
    me = lax.axis_index(axis)
    a, b = me // inner, me % inner
    k = jnp.arange(outer * inner)
    return ((a - k // inner) % outer) * inner + (b - k % inner) % inner


def reorder(value, order, axis=0):
    value = jnp.moveaxis(value, axis, 0)
    value = value.at[order].get(mode="promise_in_bounds", unique_indices=True)
    return jnp.moveaxis(value, 0, axis)


def rms_scale(values):
    return lax.rsqrt(jnp.mean(values * values, axis=-1, keepdims=True) + eps)


def exchanges():
    steps = []
    for axis in ("fsdp", "seq"):
        count = lax.axis_size(axis)
        for k in range(count.bit_length() - 1):
            steps.append((axis, [(i, i ^ (1 << k)) for i in range(count)]))
    return steps


def turn(values, cosine, sine):
    return values * cosine + pltpu.roll(values, HD // 2, 1) * sine


def turn_back(values, cosine, sine):
    return values * cosine - pltpu.roll(values, HD // 2, 1) * sine


def dot(left, right, left_dim, right_dim):
    return lax.dot_general(
        left, right, (((left_dim,), (right_dim,)), ((), ())), preferred_element_type=f32
    )


def attend_kernel(tile, qkv_ref, cos_ref, sin_ref, seg_row_ref, seg_col_ref, gain_ref, o_ref):
    blocks, _, rows, _ = qkv_ref.shape
    group = blocks * rows
    cosine, sine = cos_ref[...], sin_ref[...]

    def turned(part, row):
        raw = qkv_ref[:, 0, :, part * HD : (part + 1) * HD].reshape(group, HD).astype(f32)
        return turn(raw * rms_scale(raw) * gain_ref[row : row + 1, :], cosine, sine).astype(bf16)

    queries, keys = turned(0, 0), turned(1, 1)
    values = qkv_ref[:, 0, :, 2 * HD : 3 * HD].reshape(group, HD)
    seg_row = seg_row_ref[0]
    for start in range(0, group, tile):
        scores = dot(queries[start : start + tile], keys, 1, 1) * (1.0 / math.sqrt(HD))
        allowed = seg_col_ref[0, start : start + tile, :] == seg_row
        scores = jnp.where(allowed, scores, masked_score)
        powered = jnp.exp(scores - jnp.max(scores, axis=-1, keepdims=True))
        scale = 1.0 / jnp.sum(powered, axis=-1, keepdims=True)
        attended = dot((powered * scale).astype(bf16), values, 1, 0).astype(bf16)
        o_ref[start // rows : (start + tile) // rows, 0, :, :] = attended.reshape(
            tile // rows, rows, HD
        )


def attend_back_kernel(
    tile,
    qkv_ref,
    do_ref,
    order_ref,
    cos_ref,
    sin_ref,
    seg_row_ref,
    seg_col_ref,
    gain_ref,
    grad_ref,
    grad_gain_ref,
):
    blocks, _, rows, _ = qkv_ref.shape
    group = blocks * rows
    cosine, sine = cos_ref[...], sin_ref[...]
    scaling = 1.0 / math.sqrt(HD)

    def normed(part):
        raw = qkv_ref[:, 0, :, part * HD : (part + 1) * HD].reshape(group, HD).astype(f32)
        inverse = rms_scale(raw)
        return raw * inverse, inverse

    def turned(part):
        return turn(normed(part)[0] * gain_ref[part : part + 1, :], cosine, sine).astype(bf16)

    def finish(part, grad_turned):
        unit, inverse = normed(part)
        grad_scaled = turn_back(grad_turned, cosine, sine)
        grad_gain_ref[0, part : part + 1, :] = jnp.sum(grad_scaled * unit, axis=0, keepdims=True)
        grad_unit = grad_scaled * gain_ref[part : part + 1, :]
        grad_raw = inverse * (
            grad_unit - unit * jnp.mean(grad_unit * unit, axis=-1, keepdims=True)
        )
        return grad_raw

    def put(part, value):
        grad_ref[:, 0, :, part * HD : (part + 1) * HD] = value.astype(bf16).reshape(
            blocks, rows, HD
        )

    queries, keys = turned(0), turned(1)
    values = qkv_ref[:, 0, :, 2 * HD : 3 * HD].reshape(group, HD)
    grad_out = jnp.concatenate([do_ref[order_ref[k], 0] for k in range(blocks)], axis=0)
    seg_row = seg_row_ref[0]
    grad_query = []
    grad_key = jnp.zeros((group, HD), f32)
    grad_value = jnp.zeros((group, HD), f32)
    for start in range(0, group, tile):
        part = queries[start : start + tile]
        grad_part = grad_out[start : start + tile]
        scores = dot(part, keys, 1, 1) * scaling
        allowed = seg_col_ref[0, start : start + tile, :] == seg_row
        scores = jnp.where(allowed, scores, masked_score)
        powered = jnp.exp(scores - jnp.max(scores, axis=-1, keepdims=True))
        probabilities = powered * (1.0 / jnp.sum(powered, axis=-1, keepdims=True))
        grad_probs = dot(grad_part, values, 1, 1)
        centre = jnp.sum(probabilities * grad_probs, axis=-1, keepdims=True)
        grad_scores = (probabilities * (grad_probs - centre)).astype(bf16)
        grad_query.append(dot(grad_scores, keys, 1, 0) * scaling)
        grad_key = grad_key + dot(grad_scores, part, 0, 0)
        grad_value = grad_value + dot(probabilities.astype(bf16), grad_part, 0, 0)
    put(0, finish(0, jnp.concatenate(grad_query, axis=0)))
    put(1, finish(1, grad_key * scaling))
    put(2, grad_value)


def attention_specs(ns, micro, rows, heads):
    group = ns * rows
    tile = max(rows, 256)
    return (
        tile,
        pl.BlockSpec((ns, 1, rows, 3 * HD), lambda m, h: (0, m, 0, h)),
        pl.BlockSpec((ns, 1, rows, HD), lambda m, h: (0, m, 0, h)),
        [
            pl.BlockSpec((group, HD), lambda m, h: (0, 0)),
            pl.BlockSpec((group, HD), lambda m, h: (0, 0)),
            pl.BlockSpec((1, 1, group), lambda m, h: (m, 0, 0)),
            pl.BlockSpec((1, group, 1), lambda m, h: (m, 0, 0)),
            pl.BlockSpec((2, HD), lambda m, h: (0, 0)),
        ],
    )


def attend(qkv, tables):
    ns, micro, rows, width = qkv.shape
    heads = width // (3 * HD)
    tile, wide, narrow, shared = attention_specs(ns, micro, rows, heads)
    group = ns * rows
    return pl.pallas_call(
        lambda *refs: attend_kernel(tile, *refs),
        grid=(micro, heads),
        in_specs=[wide] + shared,
        out_specs=narrow,
        out_shape=jax.ShapeDtypeStruct((ns, micro, rows, heads * HD), bf16),
        compiler_params=pltpu.CompilerParams(vmem_limit_bytes=40 * 2**20),
        cost_estimate=little,
        name="attend",
    )(qkv, *tables)


def attend_back(qkv, grad_out, order, tables):
    ns, micro, rows, width = qkv.shape
    heads = width // (3 * HD)
    tile, wide, narrow, shared = attention_specs(ns, micro, rows, heads)
    group = ns * rows
    return pl.pallas_call(
        lambda *refs: attend_back_kernel(tile, *refs),
        grid=(micro, heads),
        in_specs=[wide, narrow, pl.BlockSpec(memory_space=pltpu.SMEM)] + shared,
        out_specs=[wide, pl.BlockSpec((1, 2, HD), lambda m, h: (m * heads + h, 0, 0))],
        out_shape=[
            jax.ShapeDtypeStruct((ns, micro, rows, width), bf16),
            jax.ShapeDtypeStruct((micro * heads, 2, HD), f32),
        ],
        compiler_params=pltpu.CompilerParams(vmem_limit_bytes=40 * 2**20),
        cost_estimate=little,
        name="attend_back",
    )(qkv, grad_out, order, *tables)


def part_kernel(grad_ref, w_ref, x_ref, inv_ref, *out_refs):
    out_refs, gain_ref = out_refs[:-1], out_refs[-1]
    rows = out_refs[0].shape[0]
    gain = jnp.zeros(gain_ref.shape, f32)
    for b, ref in enumerate(out_refs):
        span = slice(b * rows, (b + 1) * rows)
        wide = dot(grad_ref[span, :], w_ref[...], 1, 1)
        ref[...] = wide.astype(bf16)
        normed = x_ref[span, :].astype(f32) * inv_ref[span, :]
        gain = gain + jnp.sum(wide * normed, axis=0, keepdims=True)
    gain_ref[...] = gain


def part_grads(grad_qkv, w_first, x_all, inv_all, ties=()):
    blocks = grad_qkv.shape[0]
    width = grad_qkv.shape[-1]
    count = grad_qkv.size // width
    block = jax.ShapeDtypeStruct((count // blocks, D), bf16)
    found = call(
        part_kernel,
        "part_grads",
        (D // part,),
        [
            (grad_qkv.reshape(count, width), whole_of((count, width))),
            (w_first, pl.BlockSpec((part, width), lambda d: (d, 0))),
            (x_all.reshape(count, x_all.shape[-1]), pl.BlockSpec((count, part), lambda d: (0, d))),
            (inv_all.reshape(count, 1), whole_of((count, 1))),
        ],
        [(block, pl.BlockSpec((block.shape[0], part), lambda d: (0, d)))] * blocks
        + [(jax.ShapeDtypeStruct((1, D), f32), pl.BlockSpec((1, part), lambda d: (0, d)))],
        ties=ties,
    )
    return found[:-1], found[-1][0]


def proj_kernel(blocks, order_ref, place_ref, h_ref, grad_ref, column_ref, gain_ref, *refs):
    o_refs, out_refs, found_ref = refs[:blocks], refs[blocks:-1], refs[-1]
    k = pl.program_id(0)
    inputs, width = grad_ref.shape[1], column_ref.shape[1]
    owners = found_ref.shape[0] // width
    found_ref[:, :inputs] = dot(h_ref[...], grad_ref[...], 0, 0)
    for j in range(owners):
        place = place_ref[order_ref[k] * owners + j]
        for b in range(blocks):

            @pl.when(place == b)
            def _(b=b, j=j):
                found_ref[j * width : (j + 1) * width, inputs : inputs + width] = dot(
                    o_refs[b][...], column_ref[...], 0, 0
                )

    found_ref[:, inputs + width :] = gain_ref[...]
    for b, ref in enumerate(out_refs):

        @pl.when(k == b)
        def _(ref=ref):
            ref[...] = found_ref[...].astype(bf16)


def proj_grads(h_one, grad_qkv, o_blocks, columns, gains, order, places, ties=()):
    count, inputs = h_one.size // D, grad_qkv.shape[-1]
    width, nf = columns.shape[1], order.shape[0]
    rows, across = D // nf, inputs + width + gains.shape[1]
    result = jax.ShapeDtypeStruct((rows, across), bf16)
    ins = [
        (h_one.reshape(count, D), pl.BlockSpec((count, rows), lambda k, order, _: (0, order[k]))),
        (grad_qkv.reshape(count, inputs), whole_of((count, inputs))),
        (columns, whole_of(columns.shape)),
        (gains, pl.BlockSpec((rows, gains.shape[1]), lambda k, order, _: (order[k], 0))),
    ] + [(v, whole_of(v.shape)) for v in o_blocks]

    def run(*refs):
        lead = 2 + len(ins)
        proj_kernel(len(o_blocks), *refs[:lead], *refs[lead + len(ties) :])

    return pl.pallas_call(
        run,
        grid_spec=pltpu.PrefetchScalarGridSpec(
            num_scalar_prefetch=2,
            grid=(nf,),
            in_specs=[spec for _, spec in ins] + [pl.BlockSpec(memory_space=pl.ANY)] * len(ties),
            out_specs=[whole_of(result.shape)] * nf,
            scratch_shapes=[pltpu.VMEM((rows, across), f32)],
        ),
        out_shape=[result] * nf,
        compiler_params=pltpu.CompilerParams(vmem_limit_bytes=56 * 2**20),
        cost_estimate=little,
        name="proj_grads",
    )(order, places, *[value for value, _ in ins], *ties)


part = 512


def spans(shape, *block):
    block = block or (1,)
    return pl.BlockSpec(
        tuple(block) + tuple(shape[len(block) :]), lambda e, *_: (e,) + (0,) * (len(shape) - 1)
    )


def whole_of(shape):
    return pl.BlockSpec(
        tuple(shape), lambda *_: (0,) * len(shape), pipeline_mode=pl.Buffered(buffer_count=1)
    )


def call(kernel, name, grid, ins, outs, scratch=(), ties=(), aliases={}):
    ties = [t for t in ties if t is not None]
    count = len(ins)

    def run(*refs):
        kernel(*refs[:count], *refs[count + len(ties) :])

    return pl.pallas_call(
        run,
        grid=grid,
        in_specs=[spec for _, spec in ins] + [pl.BlockSpec(memory_space=pl.ANY)] * len(ties),
        out_specs=[spec for _, spec in outs],
        out_shape=[shape for shape, _ in outs],
        scratch_shapes=list(scratch),
        input_output_aliases=aliases,
        compiler_params=pltpu.CompilerParams(vmem_limit_bytes=56 * 2**20),
        cost_estimate=little,
        name=name,
    )(*[value for value, _ in ins], *ties)


def picked(slot_row, capacity):
    place = lax.broadcasted_iota(jnp.int32, (capacity, slot_row.shape[1]), 0)
    return place == slot_row


def slot_weights(slot_row, weight_row, capacity):
    chosen = jnp.where(picked(slot_row, capacity), weight_row, 0.0)
    return jnp.sum(chosen, axis=1, keepdims=True)


def dispatch_kernel(scaled, blocks, *refs):
    value_refs, (slot_ref, weight_ref, w_ref, rows_ref, act_ref) = refs[:blocks], refs[blocks:]
    capacity, half = rows_ref.shape[2], slot_ref.shape[2]
    halves, seen = ([], []), 0
    for ref in value_refs:
        halves[seen // half].append(ref)
        seen += ref.shape[0]
    for h in range(2):
        slot_row = slot_ref[0, h : h + 1, :]
        pick = picked(slot_row, capacity).astype(f32).astype(bf16)
        if scaled:
            scale = slot_weights(slot_row, weight_ref[0, h : h + 1, :], capacity)
        for d in range(0, D, part):
            values = jnp.concatenate(
                [ref[:, d : d + part] for ref in halves[h]], axis=0
            )
            taken = dot(pick, values, 1, 0)
            if scaled:
                taken = taken * scale
            rows_ref[0, h, :, d : d + part] = taken.astype(bf16)
        act_ref[0, h] = dot(rows_ref[0, h], w_ref[0], 1, 0)


def dispatch(
    values, slots, weights, bank, capacity, scaled, ties=(), first=0, count=None, before=()
):
    experts = bank.shape[0]
    count = count or experts
    values = [v.reshape(-1, v.shape[-1]) for v in values]
    rows_shape = (experts, 2, capacity, D)
    act_shape = (experts, 2, capacity, FFE)

    def of(shape):
        return pl.BlockSpec((1,) + shape[1:], lambda e: (first + e,) + (0,) * (len(shape) - 1))

    return call(
        lambda *refs: dispatch_kernel(scaled, len(values), *refs),
        "dispatch",
        (count,),
        [(v, whole_of(v.shape)) for v in values]
        + [(v, of(v.shape)) for v in (slots, weights, bank)],
        [
            (jax.ShapeDtypeStruct(rows_shape, bf16), of(rows_shape)),
            (jax.ShapeDtypeStruct(act_shape, f32), of(act_shape)),
        ],
        ties=tuple(before) + tuple(ties),
        aliases={len(values) + 3 + k: k for k in range(len(before))},
    )


def act_kernel(taken_ref, gate_ref, grad_ref, w_ref, hidden_ref, grad_gate_ref, grad_up_ref):
    for f in range(0, FFE, 256):
        span = slice(f, f + 256)
        up_act = dot(taken_ref[0, 0], w_ref[0, :, span], 1, 0)
        gate_act, grad_hidden = gate_ref[0, 0, :, span], grad_ref[0, 0, :, span]
        gate_sig = jax.nn.sigmoid(gate_act)
        gate_silu = gate_act * gate_sig
        hidden_ref[0, 0, :, span] = (gate_silu * up_act).astype(bf16)
        grad_gate = grad_hidden * up_act * gate_sig * (1.0 + gate_act * (1.0 - gate_sig))
        grad_gate_ref[0, 0, :, span] = grad_gate.astype(bf16)
        grad_up_ref[0, 0, :, span] = (grad_hidden * gate_silu).astype(bf16)


def activate(taken, gate_act, grad_hidden, w_up, ties=()):
    count, _, capacity, _ = taken.shape

    def of(width):
        return pl.BlockSpec((1, 1, capacity, width), lambda e, h: (e, h, 0, 0))

    result = jax.ShapeDtypeStruct(gate_act.shape, bf16)
    return call(
        act_kernel,
        "activate",
        (count, 2),
        [
            (taken, of(D)),
            (gate_act, of(FFE)),
            (grad_hidden, of(FFE)),
            (w_up, spans(w_up.shape)),
        ],
        [(result, of(FFE))] * 3,
        ties=ties,
    )


def bank_kernel(left_ref, right_ref, out_ref):
    rows = left_ref.shape[1] * left_ref.shape[2]
    left, right = left_ref[0].reshape(rows, -1), right_ref[0].reshape(rows, -1)
    out_ref[0] = dot(left, right, 0, 0).astype(bf16)


def bank_grad(left, right, ties=(), first=0, count=None):
    capacity = left.shape[2]
    count = count or left.shape[0]
    result = jax.ShapeDtypeStruct((count, D, FFE), bf16)
    return call(
        bank_kernel,
        "bank_grad",
        (count, D // part),
        [
            (left, pl.BlockSpec((1, 2, capacity, part), lambda e, d: (first + e, 0, 0, d))),
            (right, pl.BlockSpec((1, 2, capacity, FFE), lambda e, d: (first + e, 0, 0, 0))),
        ],
        [(result, pl.BlockSpec((1, part, FFE), lambda e, d: (e, d, 0)))],
        ties=ties,
    )[0]


def combine_kernel(scaled, acts, h, *refs):
    act_refs, w_refs = refs[:acts], refs[acts : 2 * acts]
    column_ref, slot_ref, weight_ref = refs[2 * acts : 2 * acts + 3]
    out_refs, (pick_ref, rows_ref, scale_ref) = refs[2 * acts + 3 : -3], refs[-3:]
    count, _, capacity, _ = act_refs[0].shape
    half, stride = pick_ref.shape[0], rows_ref.shape[0] // count

    @pl.when(pl.program_id(0) == 0)
    def _():
        rows_ref[...] = jnp.zeros_like(rows_ref)
        place = lax.broadcasted_iota(jnp.int32, (half, stride), 1)
        for e in range(count):
            pick = (place == column_ref[e, 0]).astype(f32).astype(bf16)
            pick_ref[:, e * stride : (e + 1) * stride] = pick
            if scaled:
                scale_ref[e] = slot_weights(
                    slot_ref[e, h : h + 1, :], weight_ref[e, h : h + 1, :], capacity
                )

    for e in range(count):
        grads = [dot(a_ref[e, 0], w_ref[e], 1, 1) for a_ref, w_ref in zip(act_refs, w_refs)]
        rows = sum(grads[1:], grads[0])
        if scaled:
            rows = rows * scale_ref[e]
        rows_ref[e * stride : e * stride + capacity, :] = rows.astype(bf16)
    n = out_refs[0].shape[0]
    for b, ref in enumerate(out_refs):
        ref[...] = dot(pick_ref[b * n : (b + 1) * n, :], rows_ref[...], 1, 0).astype(bf16)


def combine(acts, banks, columns, slots, weights, h, blocks, scaled, ties=()):
    count, _, capacity, _ = acts[0].shape
    half = columns.shape[2]
    stride = -(-capacity // 128) * 128
    result = jax.ShapeDtypeStruct((half // blocks, D), bf16)
    once = pl.Buffered(buffer_count=1)
    act = pl.BlockSpec((count, 1, capacity, FFE), lambda d: (0, h, 0, 0), pipeline_mode=once)
    column = pl.BlockSpec((count, 1, half, 1), lambda d: (0, h, 0, 0), pipeline_mode=once)
    return call(
        lambda *refs: combine_kernel(scaled, len(acts), h, *refs),
        "combine",
        (D // part,),
        [(a, act) for a in acts]
        + [(w, pl.BlockSpec((count, part, FFE), lambda d: (0, d, 0))) for w in banks]
        + [(columns, column)]
        + [(v, whole_of(v.shape)) for v in (slots, weights)],
        [(result, pl.BlockSpec((half // blocks, part), lambda d: (0, d)))] * blocks,
        scratch=[
            pltpu.VMEM((half, count * stride), bf16),
            pltpu.VMEM((count * stride, part), bf16),
            pltpu.VMEM((count, capacity, 1), f32),
        ],
        ties=ties,
    )


def body(
    layer_input,
    cotangent,
    segments,
    routes,
    route_weights,
    gain_attention,
    gain_experts,
    query_proj,
    key_proj,
    value_proj,
    output_proj,
    head_gains,
    expert_gate,
    expert_up,
    expert_down,
):
    micro, rows, _ = layer_input.shape
    nf, ns = lax.axis_size("fsdp"), lax.axis_size("seq")
    seq_index = lax.axis_index("seq")
    seq_order = relative_order("seq")
    tokens = micro * rows
    group = rows * ns
    half = group * micro // 2
    heads_local = H // ns
    width = heads_local * HD
    local_experts = expert_gate.shape[0]
    experts = local_experts * ns
    capacity = micro * ns // 2 * min(rows, 3 * rows * TOP // (2 * experts))
    share = D // (nf * ns)

    def spread(value, axis):
        return lax.all_gather(value, "fsdp", axis=axis, tiled=True)

    def gather_tokens(value):
        blocks = jnp.concatenate(ring_gather(value, "seq", split=True), axis=0)
        return blocks.reshape((ns,) + value.shape)

    columns = [
        lax.dynamic_slice_in_dim(w, seq_index * width, width, axis=1).reshape(-1, heads_local, HD)
        for w in (query_proj, key_proj, value_proj)
    ]
    columns = jnp.stack(columns, axis=2).reshape(-1, 3 * width)
    extra = jnp.pad(jnp.stack([gain_attention, gain_experts], axis=1), ((0, 0), (0, HD - 2)))
    w_first = spread(jnp.concatenate([columns, extra], axis=1), 0)
    w_qkv = w_first[:, : 3 * width]
    gain_one = w_first[:, 3 * width].astype(f32)
    gain_two = w_first[:, 3 * width + 1].astype(f32)
    w_down = spread(expert_down, 1)
    w_output = spread(output_proj, 0)
    w_gate = spread(expert_gate, 1)
    w_up = spread(expert_up, 1)

    weight_high = route_weights.astype(bf16)
    weight_low = (route_weights - weight_high.astype(f32)).astype(bf16)
    packed = jnp.concatenate(
        [layer_input, routes.astype(bf16), weight_high, weight_low], axis=-1
    )
    packed = jnp.pad(packed, ((0, 0), (0, 0), (0, HD - 3 * TOP)))
    packed = x_all = gather_tokens(packed)
    x_wide = packed[..., :D].astype(f32)
    inv_all = rms_scale(x_wide)
    h_one = (x_wide * inv_all * gain_one).astype(bf16)
    qkv = jnp.einsum("smtd,de->smte", h_one, w_qkv, preferred_element_type=f32).astype(bf16)

    places = (seq_order[:, None] * rows + jnp.arange(rows)[None, :]).reshape(-1)
    lane = jnp.arange(HD) % (HD // 2)
    frequency = jnp.exp(-jnp.log(rope_base) * (2.0 * lane.astype(f32) / HD))
    angles = places.astype(f32)[:, None] * frequency[None, :]
    sign = jnp.where(jnp.arange(HD) < HD // 2, -1.0, 1.0)
    segment = reorder(segments.reshape(micro, ns, rows), seq_order, axis=1).reshape(micro, group)
    tables = (
        jnp.cos(angles),
        jnp.sin(angles) * sign,
        segment[:, None, :],
        segment[:, :, None],
        head_gains.astype(f32),
    )
    o_heads = attend(qkv, tables)

    o_heads = reorder(o_heads, seq_order, axis=0)
    g_blocks, g_next = ring_gather(
        after(cotangent, packed, *tables), "seq", (lambda _: qkv, lambda _: o_heads), True, stop=2
    )
    o_heads = after(o_heads, g_next)
    o_back = lax.all_to_all(o_heads, "seq", split_axis=0, concat_axis=0, tiled=True)
    o_rows = jnp.moveaxis(o_back, 0, 2).reshape(tokens, D)

    x_rows = layer_input.astype(f32).reshape(tokens, D)
    middle = x_rows + jnp.dot(o_rows, w_output, preferred_element_type=f32)
    inv_two = rms_scale(middle)
    normed_two = middle * inv_two
    h_two_own = (normed_two * gain_two).astype(bf16).reshape(micro, rows, D)
    h_blocks = ring_gather(h_two_own, "seq", (), True)

    packed = packed[..., D : D + 3 * TOP].astype(f32)
    packed = packed.reshape(2, half, 3 * TOP)
    route_all = packed[..., :TOP].astype(jnp.int32)
    weight_all = packed[..., TOP : 2 * TOP] + packed[..., 2 * TOP :]
    mine = seq_index * local_experts + jnp.arange(local_experts)
    hit = route_all[:, :, None, :] == mine[None, None, :, None]
    chosen = jnp.any(hit, axis=-1)
    weight_of = jnp.sum(jnp.where(hit, weight_all[:, :, None, :], 0.0), axis=-1)
    block = 128
    counted = chosen.reshape(2, half // block, block, local_experts).astype(f32)
    below = jnp.tril(jnp.ones((block, block), f32), -1)
    inside = jnp.einsum("ab,mkbe->mkae", below, counted)
    sums = jnp.sum(counted, axis=2)
    before = jnp.cumsum(sums, axis=1) - sums
    slot = (inside + before[:, :, None, :]).reshape(2, half, local_experts).astype(jnp.int32)
    slots = jnp.transpose(jnp.where(chosen, slot, -1), (2, 0, 1))
    weights = jnp.transpose(weight_of, (2, 0, 1))
    slot_columns = slots[..., None]

    grad_top = cotangent.astype(f32).reshape(tokens, D)
    done = {}

    def keep(**found):
        done.update(found)
        return next(iter(found.values()))

    def combined(acts, banks, h, scaled, ties=()):
        return combine(acts, banks, slot_columns, slots, weights, h, ns // 2, scaled, ties)

    g_blocks = ring_gather(after(g_next, h_blocks[-1]), "seq", (), True, g_blocks)

    def grad_work(_):
        grad_rows, grad_hidden = dispatch(g_blocks, slots, weights, w_down, capacity, True)
        return keep(grad_rows=grad_rows, grad_hidden=grad_hidden)

    pair = local_experts // 2

    def take_work(first):
        def work(ties):
            takes = dispatch(
                h_blocks,
                slots,
                weights,
                w_gate,
                capacity,
                False,
                tuple(ties) + (done["grad_rows"],),
                first,
                local_experts - pair if first else pair,
                done.get("takes", ()),
            )
            return keep(taken=takes[0], gate_act=takes[1], takes=takes)

        return work

    def act_work(_):
        acts = activate(done["taken"], done["gate_act"], done["grad_hidden"], w_up)
        return keep(tail=acts[0], acts=acts)

    o_all = ring_gather(
        after(o_heads.reshape(group * micro, width), g_blocks[-1]),
        "seq",
        (grad_work, take_work(0), take_work(pair), act_work),
        True,
    )
    o_all = o_all[:-2] + [jnp.concatenate(o_all[-2:], axis=0)] if len(o_all) > ns else o_all
    grad_rows, taken = done["grad_rows"], done["taken"]
    hidden, grad_gate_act, grad_up_act = done["acts"]
    first = combined((grad_gate_act, grad_up_act), (w_gate, w_up), 0, False, (o_all[-1],))
    whole_down = [bank_grad(grad_rows, hidden, (first[0],), 0, pair)]
    mixed = combined((hidden,), (w_down,), 0, True, (whole_down[0],))
    second = combined((grad_gate_act, grad_up_act), (w_gate, w_up), 1, False, (mixed[0],))

    def down_work(ties):
        whole_down.append(bank_grad(grad_rows, hidden, ties, pair, local_experts - pair))
        return whole_down[1]

    def mixed_work(ties):
        found = combined((hidden,), (w_down,), 1, True, ties)
        return keep(tail=found[0], mixed=found)

    def gate_work(ties):
        return keep(whole_gate=bank_grad(taken, grad_gate_act, ties))

    parts = [v.reshape(micro, rows, D) for v in list(first) + list(second)]
    mixed = [v.reshape(micro, rows, D) for v in mixed]
    grad_h_two = ring_scatter(
        parts,
        "seq",
        (lambda _: second[0], down_work, mixed_work, gate_work),
        {
            0: lambda moved: keep(mixed_one=moved[-1]),
            1: lambda moved: keep(sum_down=after(whole_down[1], *moved)),
            3: lambda moved: keep(sum_gate=after(done["whole_gate"], *moved)),
        },
        {0: [row_move(mixed, 1, "seq")]},
    ).reshape(tokens, D)
    mixed += [v.reshape(micro, rows, D) for v in done["mixed"]]

    def bank_sum(whole):
        return lax.psum_scatter(whole, "fsdp", scatter_dimension=1, tiled=True).astype(f32)

    grad_down = jnp.concatenate([bank_sum(whole_down[0]), bank_sum(done["sum_down"])], axis=0)
    grad_gate = bank_sum(done["sum_gate"])

    grad_gain_two = jnp.sum(grad_h_two * normed_two, axis=0)
    grad_unit = grad_h_two * gain_two
    grad_middle = grad_top + inv_two * (
        grad_unit - normed_two * jnp.mean(grad_unit * normed_two, axis=-1, keepdims=True)
    )
    grad_attn = grad_middle.astype(bf16)
    grad_o = jnp.einsum("te,de->td", grad_attn, w_output, preferred_element_type=f32).astype(bf16)

    def to_heads(value):
        cut = value.reshape(micro, rows, ns, width)
        return lax.all_to_all(
            jnp.moveaxis(cut, 2, 0), "seq", split_axis=0, concat_axis=0, tiled=True
        )

    whole_up = bank_grad(taken, grad_up_act, (grad_o,))
    (do_blocks,) = together((whole_up,), to_heads(grad_o))
    grad_up = bank_sum(after(whole_up, do_blocks))

    inner = sizes("seq")[1]
    one = 1 % inner
    total = after(row_sum(done["mixed_one"], mixed, 1, "seq"), do_blocks)
    mixed[2 * inner + one] = after(mixed[2 * inner + one], do_blocks)
    grad_qkv, grad_head = attend_back(qkv, do_blocks, seq_order, tables)
    part_h_one, grad_gain_one = part_grads(grad_qkv, w_first, x_all, inv_all)
    total, two, columns = together(
        (grad_gain_one,),
        ahead(total, "seq"),
        row_move(mixed, 2, "seq"),
        to_heads(after(grad_attn, do_blocks)),
    )

    part_h_one = [v.reshape(micro, rows, D) for v in part_h_one]
    part_h_one[inner + one] = after(part_h_one[inner + one], total)
    gains = jnp.pad(jnp.stack([grad_gain_one, grad_gain_two], axis=1), ((0, 0), (0, HD - 2)))
    whole = proj_grads(
        h_one,
        grad_qkv,
        o_all,
        columns.reshape(micro * group, width),
        gains,
        relative_order("fsdp"),
        seq_order,
        (total,),
    )
    left = exchanges()
    head = jnp.sum(after(grad_head, total), axis=0)

    def exchange(head):
        axis, pairs = left.pop(0)
        return lax.ppermute(head, axis, pairs)

    total = ahead(add(row_sum(two, mixed, 2, "seq"), total).astype(bf16), "seq")
    head = head + exchange(head)
    total, three, grad_one, moved = together(
        (whole[0],),
        total,
        row_move(mixed, 3, "seq"),
        row_move(part_h_one, 1, "seq"),
        exchange(head),
    )
    head = head + moved

    whole = [after(v, grad_one) for v in whole]
    owned = ring_scatter(whole, "fsdp").astype(bf16)

    total = ahead(add(row_sum(three, mixed, 3, "seq"), total).astype(bf16), "seq")
    grad_total = ahead(row_sum(grad_one, part_h_one, 1, "seq"), "seq")
    total, grad_total, grad_two, zero, moved, owned = together(
        (),
        total,
        grad_total,
        row_move(part_h_one, 2, "seq"),
        row_move(mixed, 0, "seq"),
        exchange(head),
        owned,
    )
    head = head + moved
    owned = lax.all_to_all(
        owned.reshape(ns, share, -1), "seq", split_axis=0, concat_axis=0, tiled=True
    )

    part_h_one[3 * inner + one] = after(part_h_one[3 * inner + one], grad_total)
    grad_total = add(row_sum(grad_two, part_h_one, 2, "seq"), grad_total).astype(bf16)
    grad_total, grad_three, moved, owned = together(
        (grad_down,),
        ahead(grad_total, "seq"),
        row_move(part_h_one, 3, "seq"),
        exchange(head),
        owned,
    )
    head = head + moved
    mixed = add(row_sum(zero, mixed, 0, "seq"), total).reshape(tokens, D)
    layer_output = (middle + mixed).astype(bf16).reshape(micro, rows, D)

    part_h_one[one] = after(part_h_one[one], owned)
    grad_total = add(row_sum(grad_three, part_h_one, 3, "seq"), grad_total).astype(bf16)
    grad_total, zero, moved = together(
        (grad_gate, grad_up),
        ahead(grad_total, "seq"),
        row_move(part_h_one, 0, "seq"),
        exchange(head),
    )
    head = head + moved
    while left:
        head = head + exchange(head)
    grad_head_gains = head
    grad_h_one = add(row_sum(zero, part_h_one, 0, "seq"), grad_total).reshape(tokens, D)
    inv_one = rms_scale(x_rows)
    normed_one = x_rows * inv_one
    grad_unit = grad_h_one * gain_one
    input_grad = grad_middle + inv_one * (
        grad_unit - normed_one * jnp.mean(grad_unit * normed_one, axis=-1, keepdims=True)
    )
    input_grad = input_grad.reshape(micro, rows, D)
    owned = owned.astype(f32)
    of_qkv = owned[..., : 3 * width].reshape(ns, share, heads_local, 3, HD)
    grad_query, grad_key, grad_value = (
        jnp.moveaxis(of_qkv[..., k, :], 0, 1).reshape(share, D) for k in range(3)
    )
    grad_output = jnp.moveaxis(owned[..., 3 * width : 4 * width], 0, 1).reshape(share, D)
    of_gains = jnp.sum(owned[..., 4 * width : 4 * width + 2], axis=0)
    return (
        layer_output,
        input_grad,
        of_gains[:, 0],
        of_gains[:, 1],
        grad_query,
        grad_key,
        grad_value,
        grad_output,
        grad_head_gains,
        grad_gate,
        grad_up,
        grad_down,
    )


def solution(mesh):
    placed = (
        P(None, ("fsdp", "seq"), None),
        P(None, ("fsdp", "seq"), None),
        P(None, "fsdp"),
        P(None, ("fsdp", "seq"), None),
        P(None, ("fsdp", "seq"), None),
        P("fsdp"),
        P("fsdp"),
        P("fsdp", None),
        P("fsdp", None),
        P("fsdp", None),
        P("fsdp", None),
        P(),
        P("seq", "fsdp", None),
        P("seq", "fsdp", None),
        P("seq", "fsdp", None),
    )
    return jax.shard_map(
        body,
        mesh=mesh,
        in_specs=placed,
        out_specs=(
            P(None, ("fsdp", "seq"), None),
            P(None, ("fsdp", "seq"), None),
            P(("fsdp", "seq")),
            P(("fsdp", "seq")),
            P(("fsdp", "seq"), None),
            P(("fsdp", "seq"), None),
            P(("fsdp", "seq"), None),
            P(("fsdp", "seq"), None),
            P(),
            P("seq", "fsdp", None),
            P("seq", "fsdp", None),
            P("seq", "fsdp", None),
        ),
        check_vma=False,
    )
```

```python
import math

import jax
import jax.numpy as jnp
from jax import lax
from jax.experimental import pallas as pl
from jax.experimental.pallas import tpu as pltpu
from jax.sharding import PartitionSpec as P

D = 2048
H = 16
HD = 128
FFE = 1024
TOP = 8
SEQ_LEN = 1024

eps = 1e-06
rope_base = 10000.0
masked_score = -1e30
f32 = jnp.float32
little = pl.CostEstimate(flops=1, bytes_accessed=1, transcendentals=0)
bf16 = jnp.bfloat16


def shift(value, axis, outer, inner, by_outer, by_inner):
    pairs = []
    for a in range(outer):
        for b in range(inner):
            there = ((a + by_outer) % outer) * inner + (b + by_inner) % inner
            pairs.append((a * inner + b, there))
    return lax.ppermute(value, axis, pairs)


def sizes(axis):
    count = lax.axis_size(axis)
    return (count // 2, 2) if axis == "fsdp" else (4, count // 4)


def after(value, *others):
    others = [v for v in others if v is not None]
    if not others:
        return value
    anywhere = pl.BlockSpec(memory_space=pl.ANY)
    return pl.pallas_call(
        lambda *refs: None,
        in_specs=[anywhere] * (1 + len(others)),
        out_specs=anywhere,
        out_shape=jax.ShapeDtypeStruct(value.shape, value.dtype),
        input_output_aliases={0: 0},
        cost_estimate=little,
        name="after",
    )(value, *others)


def together(work, *moved):
    moved = list(moved)
    for k in range(len(moved)):
        moved[k] = after(moved[k], *work, *moved[:k], *moved[k + 1 :])
    return moved


def ring_gather(value, axis, work=None, split=False, blocks=(), stop=None):
    outer, inner = sizes(axis)
    blocks, arrived = list(blocks), []
    for a in range(len(blocks) // inner, outer if stop is None else stop):
        row = [value]
        for b in range(1, inner):
            row.append(shift(row[-1], axis, outer, inner, 0, 1))
        moved = row[1:]
        if a + 1 < outer:
            moved.append(shift(value, axis, outer, inner, 1, 0))
        last = split and inner == 2 and a + 1 == outer
        if last:
            cut = value.shape[0] // 2
            moved = [
                shift(value[:cut], axis, outer, inner, 0, 1),
                shift(blocks[-1][cut:], axis, outer, inner, 1, 0),
            ]
        if work is not None:
            moved = together([f(arrived) for f in work[a : a + 1] if f], *moved)
        blocks += [value] + (moved if last else moved[: inner - 1])
        value, arrived = moved[-1], moved
    return blocks if stop is None else (blocks, value)


def row_move(parts, a, axis):
    outer, inner = sizes(axis)
    row = parts[a * inner + 1 % inner]
    for b in range(2, inner):
        row = shift(row, axis, outer, inner, 0, 1)
        row = (row.astype(f32) + parts[a * inner + b].astype(f32)).astype(bf16)
    return shift(row, axis, outer, inner, 0, 1) if inner > 1 else row


def row_sum(moved, parts, a, axis):
    total = moved.astype(f32) + parts[a * sizes(axis)[1]].astype(f32)
    return total.astype(bf16)


def ahead(value, axis):
    return shift(value, axis, *sizes(axis), 1, 0)


def add(one, other):
    return one.astype(f32) + other.astype(f32)


def ring_scatter(parts, axis, work=(), then={}):
    outer, _ = sizes(axis)
    total, arrived = None, []
    for step in range(outer):
        a = (step + 1) % outer
        moved = [row_move(parts, a, axis)]
        if step:
            moved.append(ahead(total, axis))
        moved = together([f(arrived) for f in work[step : step + 1] if f], *moved)
        if step in then:
            then[step](moved)
        arrived = moved
        total = row_sum(moved[0], parts, a, axis)
        if step:
            total = add(total, moved[1])
        if step and step + 1 < outer:
            total = total.astype(bf16)
    return total


def relative_order(axis):
    outer, inner = sizes(axis)
    me = lax.axis_index(axis)
    a, b = me // inner, me % inner
    k = jnp.arange(outer * inner)
    return ((a - k // inner) % outer) * inner + (b - k % inner) % inner


def reorder(value, order, axis=0):
    value = jnp.moveaxis(value, axis, 0)
    value = value.at[order].get(mode="promise_in_bounds", unique_indices=True)
    return jnp.moveaxis(value, 0, axis)


def rms_scale(values):
    return lax.rsqrt(jnp.mean(values * values, axis=-1, keepdims=True) + eps)


def exchanges():
    steps = []
    for axis in ("fsdp", "seq"):
        count = lax.axis_size(axis)
        for k in range(count.bit_length() - 1):
            steps.append((axis, [(i, i ^ (1 << k)) for i in range(count)]))
    return steps


def turn(values, cosine, sine):
    return values * cosine + pltpu.roll(values, HD // 2, 1) * sine


def turn_back(values, cosine, sine):
    return values * cosine - pltpu.roll(values, HD // 2, 1) * sine


def dot(left, right, left_dim, right_dim):
    return lax.dot_general(
        left, right, (((left_dim,), (right_dim,)), ((), ())), preferred_element_type=f32
    )


def attend_kernel(tile, qkv_ref, cos_ref, sin_ref, seg_row_ref, seg_col_ref, gain_ref, o_ref):
    blocks, _, rows, _ = qkv_ref.shape
    group = blocks * rows
    cosine, sine = cos_ref[...], sin_ref[...]

    def turned(part, row):
        raw = qkv_ref[:, 0, :, part * HD : (part + 1) * HD].reshape(group, HD).astype(f32)
        return turn(raw * rms_scale(raw) * gain_ref[row : row + 1, :], cosine, sine).astype(bf16)

    queries, keys = turned(0, 0), turned(1, 1)
    values = qkv_ref[:, 0, :, 2 * HD : 3 * HD].reshape(group, HD)
    seg_row = seg_row_ref[0]
    for start in range(0, group, tile):
        scores = dot(queries[start : start + tile], keys, 1, 1) * (1.0 / math.sqrt(HD))
        allowed = seg_col_ref[0, start : start + tile, :] == seg_row
        scores = jnp.where(allowed, scores, masked_score)
        powered = jnp.exp(scores - jnp.max(scores, axis=-1, keepdims=True))
        scale = 1.0 / jnp.sum(powered, axis=-1, keepdims=True)
        attended = dot((powered * scale).astype(bf16), values, 1, 0).astype(bf16)
        o_ref[start // rows : (start + tile) // rows, 0, :, :] = attended.reshape(
            tile // rows, rows, HD
        )


def attend_back_kernel(
    tile,
    qkv_ref,
    do_ref,
    order_ref,
    cos_ref,
    sin_ref,
    seg_row_ref,
    seg_col_ref,
    gain_ref,
    grad_ref,
    grad_gain_ref,
):
    blocks, _, rows, _ = qkv_ref.shape
    group = blocks * rows
    cosine, sine = cos_ref[...], sin_ref[...]
    scaling = 1.0 / math.sqrt(HD)

    def normed(part):
        raw = qkv_ref[:, 0, :, part * HD : (part + 1) * HD].reshape(group, HD).astype(f32)
        inverse = rms_scale(raw)
        return raw * inverse, inverse

    def turned(part):
        return turn(normed(part)[0] * gain_ref[part : part + 1, :], cosine, sine).astype(bf16)

    def finish(part, grad_turned):
        unit, inverse = normed(part)
        grad_scaled = turn_back(grad_turned, cosine, sine)
        grad_gain_ref[0, part : part + 1, :] = jnp.sum(grad_scaled * unit, axis=0, keepdims=True)
        grad_unit = grad_scaled * gain_ref[part : part + 1, :]
        grad_raw = inverse * (
            grad_unit - unit * jnp.mean(grad_unit * unit, axis=-1, keepdims=True)
        )
        return grad_raw

    def put(part, value):
        grad_ref[:, 0, :, part * HD : (part + 1) * HD] = value.astype(bf16).reshape(
            blocks, rows, HD
        )

    queries, keys = turned(0), turned(1)
    values = qkv_ref[:, 0, :, 2 * HD : 3 * HD].reshape(group, HD)
    grad_out = jnp.concatenate([do_ref[order_ref[k], 0] for k in range(blocks)], axis=0)
    seg_row = seg_row_ref[0]
    grad_query = []
    grad_key = jnp.zeros((group, HD), f32)
    grad_value = jnp.zeros((group, HD), f32)
    for start in range(0, group, tile):
        part = queries[start : start + tile]
        grad_part = grad_out[start : start + tile]
        scores = dot(part, keys, 1, 1) * scaling
        allowed = seg_col_ref[0, start : start + tile, :] == seg_row
        scores = jnp.where(allowed, scores, masked_score)
        powered = jnp.exp(scores - jnp.max(scores, axis=-1, keepdims=True))
        probabilities = powered * (1.0 / jnp.sum(powered, axis=-1, keepdims=True))
        grad_probs = dot(grad_part, values, 1, 1)
        centre = jnp.sum(probabilities * grad_probs, axis=-1, keepdims=True)
        grad_scores = (probabilities * (grad_probs - centre)).astype(bf16)
        grad_query.append(dot(grad_scores, keys, 1, 0) * scaling)
        grad_key = grad_key + dot(grad_scores, part, 0, 0)
        grad_value = grad_value + dot(probabilities.astype(bf16), grad_part, 0, 0)
    put(0, finish(0, jnp.concatenate(grad_query, axis=0)))
    put(1, finish(1, grad_key * scaling))
    put(2, grad_value)


def attention_specs(ns, micro, rows, heads):
    group = ns * rows
    tile = max(rows, 256)
    return (
        tile,
        pl.BlockSpec((ns, 1, rows, 3 * HD), lambda m, h: (0, m, 0, h)),
        pl.BlockSpec((ns, 1, rows, HD), lambda m, h: (0, m, 0, h)),
        [
            pl.BlockSpec((group, HD), lambda m, h: (0, 0)),
            pl.BlockSpec((group, HD), lambda m, h: (0, 0)),
            pl.BlockSpec((1, 1, group), lambda m, h: (m, 0, 0)),
            pl.BlockSpec((1, group, 1), lambda m, h: (m, 0, 0)),
            pl.BlockSpec((2, HD), lambda m, h: (0, 0)),
        ],
    )


def attend(qkv, tables):
    ns, micro, rows, width = qkv.shape
    heads = width // (3 * HD)
    tile, wide, narrow, shared = attention_specs(ns, micro, rows, heads)
    group = ns * rows
    return pl.pallas_call(
        lambda *refs: attend_kernel(tile, *refs),
        grid=(micro, heads),
        in_specs=[wide] + shared,
        out_specs=narrow,
        out_shape=jax.ShapeDtypeStruct((ns, micro, rows, heads * HD), bf16),
        compiler_params=pltpu.CompilerParams(vmem_limit_bytes=40 * 2**20),
        cost_estimate=little,
        name="attend",
    )(qkv, *tables)


def attend_back(qkv, grad_out, order, tables):
    ns, micro, rows, width = qkv.shape
    heads = width // (3 * HD)
    tile, wide, narrow, shared = attention_specs(ns, micro, rows, heads)
    group = ns * rows
    return pl.pallas_call(
        lambda *refs: attend_back_kernel(tile, *refs),
        grid=(micro, heads),
        in_specs=[wide, narrow, pl.BlockSpec(memory_space=pltpu.SMEM)] + shared,
        out_specs=[wide, pl.BlockSpec((1, 2, HD), lambda m, h: (m * heads + h, 0, 0))],
        out_shape=[
            jax.ShapeDtypeStruct((ns, micro, rows, width), bf16),
            jax.ShapeDtypeStruct((micro * heads, 2, HD), f32),
        ],
        compiler_params=pltpu.CompilerParams(vmem_limit_bytes=40 * 2**20),
        cost_estimate=little,
        name="attend_back",
    )(qkv, grad_out, order, *tables)


def part_kernel(grad_ref, w_ref, x_ref, inv_ref, *out_refs):
    out_refs, gain_ref = out_refs[:-1], out_refs[-1]
    rows = out_refs[0].shape[0]
    gain = jnp.zeros(gain_ref.shape, f32)
    for b, ref in enumerate(out_refs):
        span = slice(b * rows, (b + 1) * rows)
        wide = dot(grad_ref[span, :], w_ref[...], 1, 1)
        ref[...] = wide.astype(bf16)
        normed = x_ref[span, :].astype(f32) * inv_ref[span, :]
        gain = gain + jnp.sum(wide * normed, axis=0, keepdims=True)
    gain_ref[...] = gain


def part_grads(grad_qkv, w_first, x_all, inv_all, ties=()):
    blocks = grad_qkv.shape[0]
    width = grad_qkv.shape[-1]
    count = grad_qkv.size // width
    block = jax.ShapeDtypeStruct((count // blocks, D), bf16)
    found = call(
        part_kernel,
        "part_grads",
        (D // part,),
        [
            (grad_qkv.reshape(count, width), whole_of((count, width))),
            (w_first, pl.BlockSpec((part, width), lambda d: (d, 0))),
            (x_all.reshape(count, x_all.shape[-1]), pl.BlockSpec((count, part), lambda d: (0, d))),
            (inv_all.reshape(count, 1), whole_of((count, 1))),
        ],
        [(block, pl.BlockSpec((block.shape[0], part), lambda d: (0, d)))] * blocks
        + [(jax.ShapeDtypeStruct((1, D), f32), pl.BlockSpec((1, part), lambda d: (0, d)))],
        ties=ties,
    )
    return found[:-1], found[-1][0]


def proj_kernel(blocks, order_ref, place_ref, h_ref, grad_ref, column_ref, gain_ref, *refs):
    o_refs, out_refs, found_ref = refs[:blocks], refs[blocks:-1], refs[-1]
    k = pl.program_id(0)
    inputs, width = grad_ref.shape[1], column_ref.shape[1]
    owners = found_ref.shape[0] // width
    found_ref[:, :inputs] = dot(h_ref[...], grad_ref[...], 0, 0)
    for j in range(owners):
        place = place_ref[order_ref[k] * owners + j]
        for b in range(blocks):

            @pl.when(place == b)
            def _(b=b, j=j):
                found_ref[j * width : (j + 1) * width, inputs : inputs + width] = dot(
                    o_refs[b][...], column_ref[...], 0, 0
                )

    found_ref[:, inputs + width :] = gain_ref[...]
    for b, ref in enumerate(out_refs):

        @pl.when(k == b)
        def _(ref=ref):
            ref[...] = found_ref[...].astype(bf16)


def proj_grads(h_one, grad_qkv, o_blocks, columns, gains, order, places, ties=()):
    count, inputs = h_one.size // D, grad_qkv.shape[-1]
    width, nf = columns.shape[1], order.shape[0]
    rows, across = D // nf, inputs + width + gains.shape[1]
    result = jax.ShapeDtypeStruct((rows, across), bf16)
    ins = [
        (h_one.reshape(count, D), pl.BlockSpec((count, rows), lambda k, order, _: (0, order[k]))),
        (grad_qkv.reshape(count, inputs), whole_of((count, inputs))),
        (columns, whole_of(columns.shape)),
        (gains, pl.BlockSpec((rows, gains.shape[1]), lambda k, order, _: (order[k], 0))),
    ] + [(v, whole_of(v.shape)) for v in o_blocks]

    def run(*refs):
        lead = 2 + len(ins)
        proj_kernel(len(o_blocks), *refs[:lead], *refs[lead + len(ties) :])

    return pl.pallas_call(
        run,
        grid_spec=pltpu.PrefetchScalarGridSpec(
            num_scalar_prefetch=2,
            grid=(nf,),
            in_specs=[spec for _, spec in ins] + [pl.BlockSpec(memory_space=pl.ANY)] * len(ties),
            out_specs=[whole_of(result.shape)] * nf,
            scratch_shapes=[pltpu.VMEM((rows, across), f32)],
        ),
        out_shape=[result] * nf,
        compiler_params=pltpu.CompilerParams(vmem_limit_bytes=56 * 2**20),
        cost_estimate=little,
        name="proj_grads",
    )(order, places, *[value for value, _ in ins], *ties)


part = 512


def spans(shape, *block):
    block = block or (1,)
    return pl.BlockSpec(
        tuple(block) + tuple(shape[len(block) :]), lambda e, *_: (e,) + (0,) * (len(shape) - 1)
    )


def whole_of(shape):
    return pl.BlockSpec(
        tuple(shape), lambda *_: (0,) * len(shape), pipeline_mode=pl.Buffered(buffer_count=1)
    )


def call(kernel, name, grid, ins, outs, scratch=(), ties=(), aliases={}):
    ties = [t for t in ties if t is not None]
    count = len(ins)

    def run(*refs):
        kernel(*refs[:count], *refs[count + len(ties) :])

    return pl.pallas_call(
        run,
        grid=grid,
        in_specs=[spec for _, spec in ins] + [pl.BlockSpec(memory_space=pl.ANY)] * len(ties),
        out_specs=[spec for _, spec in outs],
        out_shape=[shape for shape, _ in outs],
        scratch_shapes=list(scratch),
        input_output_aliases=aliases,
        compiler_params=pltpu.CompilerParams(vmem_limit_bytes=56 * 2**20),
        cost_estimate=little,
        name=name,
    )(*[value for value, _ in ins], *ties)


def picked(slot_row, capacity):
    place = lax.broadcasted_iota(jnp.int32, (capacity, slot_row.shape[1]), 0)
    return place == slot_row


def slot_weights(slot_row, weight_row, capacity):
    chosen = jnp.where(picked(slot_row, capacity), weight_row, 0.0)
    return jnp.sum(chosen, axis=1, keepdims=True)


def dispatch_kernel(scaled, blocks, *refs):
    value_refs, (slot_ref, weight_ref, w_ref, rows_ref, act_ref) = refs[:blocks], refs[blocks:]
    capacity, half = rows_ref.shape[2], slot_ref.shape[2]
    halves, seen = ([], []), 0
    for ref in value_refs:
        halves[seen // half].append(ref)
        seen += ref.shape[0]
    for h in range(2):
        slot_row = slot_ref[0, h : h + 1, :]
        pick = picked(slot_row, capacity).astype(f32).astype(bf16)
        if scaled:
            scale = slot_weights(slot_row, weight_ref[0, h : h + 1, :], capacity)
        for d in range(0, D, part):
            values = jnp.concatenate(
                [ref[:, d : d + part] for ref in halves[h]], axis=0
            )
            taken = dot(pick, values, 1, 0)
            if scaled:
                taken = taken * scale
            rows_ref[0, h, :, d : d + part] = taken.astype(bf16)
        act_ref[0, h] = dot(rows_ref[0, h], w_ref[0], 1, 0)


def dispatch(
    values, slots, weights, bank, capacity, scaled, ties=(), first=0, count=None, before=()
):
    experts = bank.shape[0]
    count = count or experts
    values = [v.reshape(-1, v.shape[-1]) for v in values]
    rows_shape = (experts, 2, capacity, D)
    act_shape = (experts, 2, capacity, FFE)

    def of(shape):
        return pl.BlockSpec((1,) + shape[1:], lambda e: (first + e,) + (0,) * (len(shape) - 1))

    return call(
        lambda *refs: dispatch_kernel(scaled, len(values), *refs),
        "dispatch",
        (count,),
        [(v, whole_of(v.shape)) for v in values]
        + [(v, of(v.shape)) for v in (slots, weights, bank)],
        [
            (jax.ShapeDtypeStruct(rows_shape, bf16), of(rows_shape)),
            (jax.ShapeDtypeStruct(act_shape, f32), of(act_shape)),
        ],
        ties=tuple(before) + tuple(ties),
        aliases={len(values) + 3 + k: k for k in range(len(before))},
    )


def act_kernel(taken_ref, gate_ref, grad_ref, w_ref, hidden_ref, grad_gate_ref, grad_up_ref):
    for f in range(0, FFE, 256):
        span = slice(f, f + 256)
        up_act = dot(taken_ref[0, 0], w_ref[0, :, span], 1, 0)
        gate_act, grad_hidden = gate_ref[0, 0, :, span], grad_ref[0, 0, :, span]
        gate_sig = jax.nn.sigmoid(gate_act)
        gate_silu = gate_act * gate_sig
        hidden_ref[0, 0, :, span] = (gate_silu * up_act).astype(bf16)
        grad_gate = grad_hidden * up_act * gate_sig * (1.0 + gate_act * (1.0 - gate_sig))
        grad_gate_ref[0, 0, :, span] = grad_gate.astype(bf16)
        grad_up_ref[0, 0, :, span] = (grad_hidden * gate_silu).astype(bf16)


def activate(taken, gate_act, grad_hidden, w_up, ties=()):
    count, _, capacity, _ = taken.shape

    def of(width):
        return pl.BlockSpec((1, 1, capacity, width), lambda e, h: (e, h, 0, 0))

    result = jax.ShapeDtypeStruct(gate_act.shape, bf16)
    return call(
        act_kernel,
        "activate",
        (count, 2),
        [
            (taken, of(D)),
            (gate_act, of(FFE)),
            (grad_hidden, of(FFE)),
            (w_up, spans(w_up.shape)),
        ],
        [(result, of(FFE))] * 3,
        ties=ties,
    )


def bank_kernel(left_ref, right_ref, out_ref):
    rows = left_ref.shape[1] * left_ref.shape[2]
    left, right = left_ref[0].reshape(rows, -1), right_ref[0].reshape(rows, -1)
    out_ref[0] = dot(left, right, 0, 0).astype(bf16)


def bank_grad(left, right, ties=(), first=0, count=None):
    capacity = left.shape[2]
    count = count or left.shape[0]
    result = jax.ShapeDtypeStruct((count, D, FFE), bf16)
    return call(
        bank_kernel,
        "bank_grad",
        (count, D // part),
        [
            (left, pl.BlockSpec((1, 2, capacity, part), lambda e, d: (first + e, 0, 0, d))),
            (right, pl.BlockSpec((1, 2, capacity, FFE), lambda e, d: (first + e, 0, 0, 0))),
        ],
        [(result, pl.BlockSpec((1, part, FFE), lambda e, d: (e, d, 0)))],
        ties=ties,
    )[0]


def combine_kernel(scaled, acts, h, *refs):
    act_refs, w_refs = refs[:acts], refs[acts : 2 * acts]
    column_ref, slot_ref, weight_ref = refs[2 * acts : 2 * acts + 3]
    out_refs, (pick_ref, rows_ref, scale_ref) = refs[2 * acts + 3 : -3], refs[-3:]
    count, _, capacity, _ = act_refs[0].shape
    half, stride = pick_ref.shape[0], rows_ref.shape[0] // count

    @pl.when(pl.program_id(0) == 0)
    def _():
        rows_ref[...] = jnp.zeros_like(rows_ref)
        place = lax.broadcasted_iota(jnp.int32, (half, stride), 1)
        for e in range(count):
            pick = (place == column_ref[e, 0]).astype(f32).astype(bf16)
            pick_ref[:, e * stride : (e + 1) * stride] = pick
            if scaled:
                scale_ref[e] = slot_weights(
                    slot_ref[e, h : h + 1, :], weight_ref[e, h : h + 1, :], capacity
                )

    for e in range(count):
        grads = [dot(a_ref[e, 0], w_ref[e], 1, 1) for a_ref, w_ref in zip(act_refs, w_refs)]
        rows = sum(grads[1:], grads[0])
        if scaled:
            rows = rows * scale_ref[e]
        rows_ref[e * stride : e * stride + capacity, :] = rows.astype(bf16)
    n = out_refs[0].shape[0]
    for b, ref in enumerate(out_refs):
        ref[...] = dot(pick_ref[b * n : (b + 1) * n, :], rows_ref[...], 1, 0).astype(bf16)


def combine(acts, banks, columns, slots, weights, h, blocks, scaled, ties=()):
    count, _, capacity, _ = acts[0].shape
    half = columns.shape[2]
    stride = -(-capacity // 128) * 128
    result = jax.ShapeDtypeStruct((half // blocks, D), bf16)
    once = pl.Buffered(buffer_count=1)
    act = pl.BlockSpec((count, 1, capacity, FFE), lambda d: (0, h, 0, 0), pipeline_mode=once)
    column = pl.BlockSpec((count, 1, half, 1), lambda d: (0, h, 0, 0), pipeline_mode=once)
    return call(
        lambda *refs: combine_kernel(scaled, len(acts), h, *refs),
        "combine",
        (D // part,),
        [(a, act) for a in acts]
        + [(w, pl.BlockSpec((count, part, FFE), lambda d: (0, d, 0))) for w in banks]
        + [(columns, column)]
        + [(v, whole_of(v.shape)) for v in (slots, weights)],
        [(result, pl.BlockSpec((half // blocks, part), lambda d: (0, d)))] * blocks,
        scratch=[
            pltpu.VMEM((half, count * stride), bf16),
            pltpu.VMEM((count * stride, part), bf16),
            pltpu.VMEM((count, capacity, 1), f32),
        ],
        ties=ties,
    )


def body(
    layer_input,
    cotangent,
    segments,
    routes,
    route_weights,
    gain_attention,
    gain_experts,
    query_proj,
    key_proj,
    value_proj,
    output_proj,
    head_gains,
    expert_gate,
    expert_up,
    expert_down,
):
    micro, rows, _ = layer_input.shape
    nf, ns = lax.axis_size("fsdp"), lax.axis_size("seq")
    seq_index = lax.axis_index("seq")
    seq_order = relative_order("seq")
    tokens = micro * rows
    group = rows * ns
    half = group * micro // 2
    heads_local = H // ns
    width = heads_local * HD
    local_experts = expert_gate.shape[0]
    experts = local_experts * ns
    capacity = micro * ns // 2 * min(rows, 3 * rows * TOP // (2 * experts))
    share = D // (nf * ns)

    def spread(value, axis):
        return lax.all_gather(value, "fsdp", axis=axis, tiled=True)

    def gather_tokens(value):
        blocks = jnp.concatenate(ring_gather(value, "seq", split=True), axis=0)
        return blocks.reshape((ns,) + value.shape)

    columns = [
        lax.dynamic_slice_in_dim(w, seq_index * width, width, axis=1).reshape(-1, heads_local, HD)
        for w in (query_proj, key_proj, value_proj)
    ]
    columns = jnp.stack(columns, axis=2).reshape(-1, 3 * width)
    extra = jnp.pad(jnp.stack([gain_attention, gain_experts], axis=1), ((0, 0), (0, HD - 2)))
    w_first = spread(jnp.concatenate([columns, extra], axis=1), 0)
    w_qkv = w_first[:, : 3 * width]
    gain_one = w_first[:, 3 * width].astype(f32)
    gain_two = w_first[:, 3 * width + 1].astype(f32)
    w_down = spread(expert_down, 1)
    w_output = spread(output_proj, 0)
    w_gate = spread(expert_gate, 1)
    w_up = spread(expert_up, 1)

    weight_high = route_weights.astype(bf16)
    weight_low = (route_weights - weight_high.astype(f32)).astype(bf16)
    packed = jnp.concatenate(
        [layer_input, routes.astype(bf16), weight_high, weight_low], axis=-1
    )
    packed = jnp.pad(packed, ((0, 0), (0, 0), (0, HD - 3 * TOP)))
    packed = x_all = gather_tokens(packed)
    x_wide = packed[..., :D].astype(f32)
    inv_all = rms_scale(x_wide)
    h_one = (x_wide * inv_all * gain_one).astype(bf16)
    qkv = jnp.einsum("smtd,de->smte", h_one, w_qkv, preferred_element_type=f32).astype(bf16)

    places = (seq_order[:, None] * rows + jnp.arange(rows)[None, :]).reshape(-1)
    lane = jnp.arange(HD) % (HD // 2)
    frequency = jnp.exp(-jnp.log(rope_base) * (2.0 * lane.astype(f32) / HD))
    angles = places.astype(f32)[:, None] * frequency[None, :]
    sign = jnp.where(jnp.arange(HD) < HD // 2, -1.0, 1.0)
    segment = reorder(segments.reshape(micro, ns, rows), seq_order, axis=1).reshape(micro, group)
    tables = (
        jnp.cos(angles),
        jnp.sin(angles) * sign,
        segment[:, None, :],
        segment[:, :, None],
        head_gains.astype(f32),
    )
    o_heads = attend(qkv, tables)

    o_heads = reorder(o_heads, seq_order, axis=0)
    g_blocks, g_next = ring_gather(
        after(cotangent, packed, *tables), "seq", (lambda _: qkv, lambda _: o_heads), True, stop=2
    )
    o_heads = after(o_heads, g_next)
    o_back = lax.all_to_all(o_heads, "seq", split_axis=0, concat_axis=0, tiled=True)
    o_rows = jnp.moveaxis(o_back, 0, 2).reshape(tokens, D)

    x_rows = layer_input.astype(f32).reshape(tokens, D)
    middle = x_rows + jnp.dot(o_rows, w_output, preferred_element_type=f32)
    inv_two = rms_scale(middle)
    normed_two = middle * inv_two
    h_two_own = (normed_two * gain_two).astype(bf16).reshape(micro, rows, D)
    h_blocks = ring_gather(h_two_own, "seq", (), True)

    packed = packed[..., D : D + 3 * TOP].astype(f32)
    packed = packed.reshape(2, half, 3 * TOP)
    route_all = packed[..., :TOP].astype(jnp.int32)
    weight_all = packed[..., TOP : 2 * TOP] + packed[..., 2 * TOP :]
    mine = seq_index * local_experts + jnp.arange(local_experts)
    hit = route_all[:, :, None, :] == mine[None, None, :, None]
    chosen = jnp.any(hit, axis=-1)
    weight_of = jnp.sum(jnp.where(hit, weight_all[:, :, None, :], 0.0), axis=-1)
    block = 128
    counted = chosen.reshape(2, half // block, block, local_experts).astype(f32)
    below = jnp.tril(jnp.ones((block, block), f32), -1)
    inside = jnp.einsum("ab,mkbe->mkae", below, counted)
    sums = jnp.sum(counted, axis=2)
    before = jnp.cumsum(sums, axis=1) - sums
    slot = (inside + before[:, :, None, :]).reshape(2, half, local_experts).astype(jnp.int32)
    slots = jnp.transpose(jnp.where(chosen, slot, -1), (2, 0, 1))
    weights = jnp.transpose(weight_of, (2, 0, 1))
    slot_columns = slots[..., None]

    grad_top = cotangent.astype(f32).reshape(tokens, D)
    done = {}

    def keep(**found):
        done.update(found)
        return next(iter(found.values()))

    def combined(acts, banks, h, scaled, ties=()):
        return combine(acts, banks, slot_columns, slots, weights, h, ns // 2, scaled, ties)

    g_blocks = ring_gather(after(g_next, h_blocks[-1]), "seq", (), True, g_blocks)

    def grad_work(_):
        grad_rows, grad_hidden = dispatch(g_blocks, slots, weights, w_down, capacity, True)
        return keep(grad_rows=grad_rows, grad_hidden=grad_hidden)

    pair = local_experts // 2

    def take_work(first):
        def work(ties):
            takes = dispatch(
                h_blocks,
                slots,
                weights,
                w_gate,
                capacity,
                False,
                tuple(ties) + (done["grad_rows"],),
                first,
                local_experts - pair if first else pair,
                done.get("takes", ()),
            )
            return keep(taken=takes[0], gate_act=takes[1], takes=takes)

        return work

    def act_work(_):
        acts = activate(done["taken"], done["gate_act"], done["grad_hidden"], w_up)
        return keep(tail=acts[0], acts=acts)

    o_all = ring_gather(
        after(o_heads.reshape(group * micro, width), g_blocks[-1]),
        "seq",
        (grad_work, take_work(0), take_work(pair), act_work),
        True,
    )
    o_all = o_all[:-2] + [jnp.concatenate(o_all[-2:], axis=0)] if len(o_all) > ns else o_all
    grad_rows, taken = done["grad_rows"], done["taken"]
    hidden, grad_gate_act, grad_up_act = done["acts"]
    first = combined((grad_gate_act, grad_up_act), (w_gate, w_up), 0, False, (o_all[-1],))
    whole_down = [bank_grad(grad_rows, hidden, (first[0],), 0, pair)]
    second = combined(
        (grad_gate_act, grad_up_act), (w_gate, w_up), 1, False, (whole_down[0],)
    )

    def mixed_work(h):
        def work(ties):
            mixed = combined((hidden,), (w_down,), h, True, ties)
            done.setdefault("mixed", []).extend(mixed)
            return mixed[0]

        return work

    def down_work(ties):
        whole_down.append(bank_grad(grad_rows, hidden, ties, pair, local_experts - pair))
        return whole_down[1]

    parts = [v.reshape(micro, rows, D) for v in list(first) + list(second)]
    grad_h_two = ring_scatter(
        parts,
        "seq",
        (lambda _: second[0], down_work, mixed_work(0), mixed_work(1)),
        {1: lambda moved: keep(sum_down=after(whole_down[1], *moved))},
    ).reshape(tokens, D)

    def bank_sum(whole):
        return lax.psum_scatter(whole, "fsdp", scatter_dimension=1, tiled=True).astype(f32)

    grad_down = jnp.concatenate([bank_sum(whole_down[0]), bank_sum(done["sum_down"])], axis=0)

    grad_gain_two = jnp.sum(grad_h_two * normed_two, axis=0)
    grad_unit = grad_h_two * gain_two
    grad_middle = grad_top + inv_two * (
        grad_unit - normed_two * jnp.mean(grad_unit * normed_two, axis=-1, keepdims=True)
    )
    grad_attn = grad_middle.astype(bf16)
    grad_o = jnp.einsum("te,de->td", grad_attn, w_output, preferred_element_type=f32).astype(bf16)

    def to_heads(value):
        cut = value.reshape(micro, rows, ns, width)
        return lax.all_to_all(
            jnp.moveaxis(cut, 2, 0), "seq", split_axis=0, concat_axis=0, tiled=True
        )

    whole_gate = bank_grad(taken, grad_gate_act, (grad_o,))
    (do_blocks,) = together((whole_gate,), to_heads(grad_o))
    grad_gate = bank_sum(after(whole_gate, do_blocks))

    mixed = [v.reshape(micro, rows, D) for v in done["mixed"]]
    k = sizes("seq")[1] + 1 % sizes("seq")[1]
    mixed[k] = after(mixed[k], do_blocks)
    grad_qkv, grad_head = attend_back(qkv, do_blocks, seq_order, tables)
    part_h_one, grad_gain_one = part_grads(grad_qkv, w_first, x_all, inv_all)
    one, columns = together(
        (grad_gain_one,), row_move(mixed, 1, "seq"), to_heads(after(grad_attn, do_blocks))
    )

    total = one
    part_h_one = [v.reshape(micro, rows, D) for v in part_h_one]
    part_h_one[k] = after(part_h_one[k], total)
    gains = jnp.pad(jnp.stack([grad_gain_one, grad_gain_two], axis=1), ((0, 0), (0, HD - 2)))
    whole = proj_grads(
        h_one,
        grad_qkv,
        o_all,
        columns.reshape(micro * group, width),
        gains,
        relative_order("fsdp"),
        seq_order,
        (total,),
    )
    left = exchanges()
    head = jnp.sum(after(grad_head, total), axis=0)

    def exchange(head):
        axis, pairs = left.pop(0)
        return lax.ppermute(head, axis, pairs)

    total = ahead(row_sum(total, mixed, 1, "seq"), "seq")
    head = head + exchange(head)
    total, two, one, moved = together(
        (whole[0],),
        total,
        row_move(mixed, 2, "seq"),
        row_move(part_h_one, 1, "seq"),
        exchange(head),
    )
    head = head + moved

    whole = [after(v, one) for v in whole]
    whole_up = bank_grad(taken, grad_up_act, (one,))
    owned = ring_scatter(whole, "fsdp", (None, lambda _: whole_up)).astype(bf16)

    total = ahead(add(row_sum(two, mixed, 2, "seq"), total).astype(bf16), "seq")
    grad_total = ahead(row_sum(one, part_h_one, 1, "seq"), "seq")
    total, grad_total, three, two, owned = together(
        (whole_up,),
        total,
        grad_total,
        row_move(mixed, 3, "seq"),
        row_move(part_h_one, 2, "seq"),
        owned,
    )
    grad_up = bank_sum(after(whole_up, owned))
    owned = lax.all_to_all(
        owned.reshape(ns, share, -1), "seq", split_axis=0, concat_axis=0, tiled=True
    )

    grad_total = add(row_sum(two, part_h_one, 2, "seq"), grad_total).astype(bf16)
    grad_total, zero, moved, owned = together(
        (grad_down,),
        ahead(grad_total, "seq"),
        row_move(part_h_one, 3, "seq"),
        exchange(head),
        owned,
    )
    head = head + moved

    k = 1 % sizes("seq")[1]
    mixed[k], part_h_one[k] = after(mixed[k], owned), after(part_h_one[k], owned)
    total = ahead(add(row_sum(three, mixed, 3, "seq"), total).astype(bf16), "seq")
    grad_total = add(row_sum(zero, part_h_one, 3, "seq"), grad_total).astype(bf16)
    grad_total, zero, moved, last, total = together(
        (grad_gate,),
        ahead(grad_total, "seq"),
        row_move(part_h_one, 0, "seq"),
        exchange(head),
        row_move(mixed, 0, "seq"),
        total,
    )
    head = head + moved
    mixed = add(row_sum(last, mixed, 0, "seq"), total).reshape(tokens, D)
    layer_output = (middle + mixed).astype(bf16).reshape(micro, rows, D)
    while left:
        head = head + exchange(head)
    grad_head_gains = head
    grad_h_one = add(row_sum(zero, part_h_one, 0, "seq"), grad_total).reshape(tokens, D)
    inv_one = rms_scale(x_rows)
    normed_one = x_rows * inv_one
    grad_unit = grad_h_one * gain_one
    input_grad = grad_middle + inv_one * (
        grad_unit - normed_one * jnp.mean(grad_unit * normed_one, axis=-1, keepdims=True)
    )
    input_grad = input_grad.reshape(micro, rows, D)
    owned = owned.astype(f32)
    of_qkv = owned[..., : 3 * width].reshape(ns, share, heads_local, 3, HD)
    grad_query, grad_key, grad_value = (
        jnp.moveaxis(of_qkv[..., k, :], 0, 1).reshape(share, D) for k in range(3)
    )
    grad_output = jnp.moveaxis(owned[..., 3 * width : 4 * width], 0, 1).reshape(share, D)
    of_gains = jnp.sum(owned[..., 4 * width : 4 * width + 2], axis=0)
    return (
        layer_output,
        input_grad,
        of_gains[:, 0],
        of_gains[:, 1],
        grad_query,
        grad_key,
        grad_value,
        grad_output,
        grad_head_gains,
        grad_gate,
        grad_up,
        grad_down,
    )


def solution(mesh):
    placed = (
        P(None, ("fsdp", "seq"), None),
        P(None, ("fsdp", "seq"), None),
        P(None, "fsdp"),
        P(None, ("fsdp", "seq"), None),
        P(None, ("fsdp", "seq"), None),
        P("fsdp"),
        P("fsdp"),
        P("fsdp", None),
        P("fsdp", None),
        P("fsdp", None),
        P("fsdp", None),
        P(),
        P("seq", "fsdp", None),
        P("seq", "fsdp", None),
        P("seq", "fsdp", None),
    )
    return jax.shard_map(
        body,
        mesh=mesh,
        in_specs=placed,
        out_specs=(
            P(None, ("fsdp", "seq"), None),
            P(None, ("fsdp", "seq"), None),
            P(("fsdp", "seq")),
            P(("fsdp", "seq")),
            P(("fsdp", "seq"), None),
            P(("fsdp", "seq"), None),
            P(("fsdp", "seq"), None),
            P(("fsdp", "seq"), None),
            P(),
            P("seq", "fsdp", None),
            P("seq", "fsdp", None),
            P("seq", "fsdp", None),
        ),
        check_vma=False,
    )
```
